32 devices in a mesh: dp: 2 (over core), pass: 4 (over z), mp: 4 (over y, x).
Axes of the slice: x: 2, y: 2, z: 4, core: 2. Of those that a mesh axis runs over, the one named last changes fastest.
Arguments:
- tokens: bfloat16 [2560, 768], P(('dp', 'pass')), may hold values from -18 to 18
- encoded: bfloat16 [256, 512, 768], P(('dp', 'pass'), 'mp'), may hold values from -6 to 6
- seg_lens: int32 [256, 2], P('dp'), may hold values from 192 to 256, as said below
- owners: int32 [256, 2], P('dp'), may hold values from 0 to 15, as said below
- answer_lens: int32 [128], P(('dp', 'pass')), may hold values from 2 to 20, as said below
- gain_self: float32 [768], replicated, may hold values from 0.5 to 1.5
- gain_cross: float32 [768], replicated, may hold values from 0.5 to 1.5
- gain_ffn: float32 [768], replicated, may hold values from 0.5 to 1.5
- rel_bias: float32 [32, 12], P(None, 'mp'), may hold values from -4 to 4
- wq_self: bfloat16 [768, 768], P(None, 'mp'), may hold values from -0.02734375 to 0.02734375
- wk_self: bfloat16 [768, 768], P(None, 'mp'), may hold values from -0.21875 to 0.21875
- wv_self: bfloat16 [768, 768], P(None, 'mp'), may hold values from -0.21875 to 0.21875
- wo_self: bfloat16 [768, 768], P('mp'), may hold values from -0.625 to 0.625
- wq_cross: bfloat16 [768, 768], P(None, 'mp'), may hold values from -0.02734375 to 0.02734375
- wk_cross: bfloat16 [768, 768], P(None, 'mp'), may hold values from -0.21875 to 0.21875
- wv_cross: bfloat16 [768, 768], P(None, 'mp'), may hold values from -0.21875 to 0.21875
- wo_cross: bfloat16 [768, 768], P('mp'), may hold values from -4 to 4
- w_in: bfloat16 [768, 3072], P(None, 'mp'), may hold values from -0.21875 to 0.21875
- w_out: bfloat16 [3072, 768], P('mp'), may hold values from -0.109375 to 0.109375
- out_grad: bfloat16 [2560, 768], P(('dp', 'pass')), may hold values from -6 to 6
Outputs:
- output: bfloat16 [2560, 768], P(('dp', 'pass'))
- grad_tokens: bfloat16 [2560, 768], P(('dp', 'pass'))
- gradient_of_encoded: bfloat16 [256, 512, 768], P(('dp', 'pass'), 'mp')
- grad_gain_self: float32 [768], replicated
- grad_gain_cross: float32 [768], replicated
- grad_gain_ffn: float32 [768], replicated
- grad_rel_bias: float32 [32, 12], P(None, 'mp')
- grad_wq_self: float32 [768, 768], P(None, 'mp')
- grad_wk_self: float32 [768, 768], P(None, 'mp')
- grad_wv_self: float32 [768, 768], P(None, 'mp')
- grad_wo_self: float32 [768, 768], P('mp')
- grad_wq_cross: float32 [768, 768], P(None, 'mp')
- grad_wk_cross: float32 [768, 768], P(None, 'mp')
- grad_wv_cross: float32 [768, 768], P(None, 'mp')
- grad_wo_cross: float32 [768, 768], P('mp')
- grad_w_in: float32 [768, 3072], P(None, 'mp')
- grad_w_out: float32 [3072, 768], P('mp')
The draws below stay inside these ranges and needn't reach their ends.
Inputs may be any that keep to these rules, and one draw needn't show every extreme that they name: `seg_lens`: the two passages of a row fill it from its first position; some passage has exactly 256 tokens. `owners`: every question of a group owns 1 to 7 passages of that group; in every group one question owns exactly 7. `answer_lens`: some question has exactly 20.
All inputs are finite; a program needn't handle non-finite values.
Results may differ from the reference program's by a relative error of at most 0.02.
Values may be sent and summed in bfloat16 or wider, within the bound.
A program may use at most 320 MiB of HBM per device.

```python
import math
import jax
import jax.numpy as jnp
import numpy as np
from jax import lax

MODEL_WIDTH = 768
HEADS = 12
HD = 64
FF = 3072
BUCKETS = 32
ANS = 20
PLEN = 256
QDEV = 16
PACKED_ROW_LEN = 512
PMAX = 7
KEYS = 1792
GROUP_ROWS = 32
ROWS_PER_PASS = 8
QUESTIONS = 128
TOKENS = 2560
PACKED_ROWS = 256
N_DP = 2
N_PASS = 4


def draw_tokens(key, part):
    key = jax.random.fold_in(key, 11)
    key_rows, key_vals = jax.random.split(key, 2)
    row_scale = jnp.exp(jax.random.uniform(key_rows, (TOKENS, 1), jnp.float32, -1.15, 1.15))
    values = jnp.clip(jax.random.normal(key_vals, (TOKENS, MODEL_WIDTH), jnp.float32), -5.0, 5.0)
    return (values * row_scale).astype(jnp.bfloat16)


def draw_seg_lens(key, part):
    key = jax.random.fold_in(key, 23)
    key_vals, key_spot = jax.random.split(key)
    lengths = jax.random.randint(key_vals, (PACKED_ROWS * 2,), PLEN * 3 // 4, PLEN + 1, jnp.int32)
    chosen_spot = jax.random.randint(key_spot, (), 0, PACKED_ROWS * 2, jnp.int32)
    lengths = lengths.at[chosen_spot].set(PLEN)
    return lengths.reshape(PACKED_ROWS, 2)


def draw_owners(key, part):
    key = jax.random.fold_in(key, 37)
    group_count = N_DP * N_PASS
    slot_count = 2 * GROUP_ROWS
    spare_count = QDEV * (PMAX - 1)

    def one_group(number):
        group_key = jax.random.fold_in(key, number)
        key_order, key_star, key_slots = jax.random.split(group_key, 3)
        tickets = jax.random.permutation(key_order, spare_count).astype(jnp.int32)
        asked_for = (tickets // (PMAX - 1)).astype(jnp.int32)
        favoured = jax.random.randint(key_star, (), 0, QDEV, jnp.int32)
        places = jnp.arange(spare_count, dtype=jnp.int32)
        priority = jnp.where(asked_for == favoured, places - spare_count, places)
        arranged = asked_for[jnp.argsort(priority)]
        listed = jnp.concatenate([jnp.arange(QDEV, dtype=jnp.int32), arranged[:slot_count - QDEV]])
        return jax.random.permutation(key_slots, listed)
    owners = jax.vmap(one_group)(jnp.arange(group_count, dtype=jnp.int32))
    owners = owners.reshape(N_DP, N_PASS, N_PASS, ROWS_PER_PASS, 2)
    return jnp.transpose(owners, (0, 2, 1, 3, 4)).reshape(PACKED_ROWS, 2).astype(jnp.int32)


def draw_answer_lens(key, part):
    key = jax.random.fold_in(key, 51)
    key_vals, key_spot = jax.random.split(key)
    lengths = jax.random.randint(key_vals, (QUESTIONS,), 2, ANS + 1, jnp.int32)
    chosen_spot = jax.random.randint(key_spot, (), 0, QUESTIONS, jnp.int32)
    return lengths.at[chosen_spot].set(ANS)


def steps_of(key, extent, cuts, smallest, largest):
    gain, own = 1.0, jax.random.fold_in(key, 6)
    for position, parts in cuts:
        heights = jnp.exp(jax.random.uniform(jax.random.fold_in(own, position), (parts,), jnp.float32, smallest / len(cuts), largest / len(cuts)))
        gain = gain * jnp.repeat(heights, extent[position] // parts).reshape([-1 if axis == position else 1 for axis in range(len(extent))])
    return gain


def noise(key, dims, deviation, bound, pieces=(), kind=jnp.bfloat16):
    array = deviation * jax.random.normal(key, dims, jnp.float32)
    if pieces:
        array = array * steps_of(key, dims, pieces, -0.22, 0.18)
    return jnp.clip(array, -bound, bound).astype(kind)


def setup_inputs(seed: int = 0) -> dict:
    key_list = jax.random.split(jax.random.key(seed), 21)
    return {
        "tokens": draw_tokens(jax.random.fold_in(key_list[20], 71), 0),
        "encoded": noise(key_list[1], (PACKED_ROWS, PACKED_ROW_LEN, MODEL_WIDTH), 1.0, 6.0, ((0, 8), (1, 4))),
        "seg_lens": draw_seg_lens(jax.random.fold_in(key_list[20], 71), 0),
        "owners": draw_owners(jax.random.fold_in(key_list[20], 71), 0),
        "answer_lens": draw_answer_lens(jax.random.fold_in(key_list[20], 71), 0),
        "gain_self": jnp.clip(1.0 + 0.1 * jax.random.normal(key_list[5], (MODEL_WIDTH,), jnp.float32), 0.5, 1.5),
        "gain_cross": jnp.clip(1.0 + 0.1 * jax.random.normal(key_list[6], (MODEL_WIDTH,), jnp.float32), 0.5, 1.5),
        "gain_ffn": jnp.clip(1.0 + 0.1 * jax.random.normal(key_list[7], (MODEL_WIDTH,), jnp.float32), 0.5, 1.5),
        "rel_bias": noise(key_list[8], (BUCKETS, HEADS), 1.0, 4.0, ((1, 4),), jnp.float32),
        "wq_self": noise(key_list[9], (MODEL_WIDTH, MODEL_WIDTH), (MODEL_WIDTH * HD) ** -0.5, 0.02734375, ((1, 4),)),
        "wk_self": noise(key_list[10], (MODEL_WIDTH, MODEL_WIDTH), MODEL_WIDTH ** -0.5, 0.21875, ((1, 4),)),
        "wv_self": noise(key_list[11], (MODEL_WIDTH, MODEL_WIDTH), MODEL_WIDTH ** -0.5, 0.21875, ((1, 4),)),
        "wo_self": noise(key_list[12], (MODEL_WIDTH, MODEL_WIDTH), (MODEL_WIDTH // 8) ** -0.5, 0.625, ((0, 4),)),
        "wq_cross": noise(key_list[13], (MODEL_WIDTH, MODEL_WIDTH), (MODEL_WIDTH * HD) ** -0.5, 0.02734375, ((1, 4),)),
        "wk_cross": noise(key_list[14], (MODEL_WIDTH, MODEL_WIDTH), MODEL_WIDTH ** -0.5, 0.21875, ((1, 4),)),
        "wv_cross": noise(key_list[15], (MODEL_WIDTH, MODEL_WIDTH), MODEL_WIDTH ** -0.5, 0.21875, ((1, 4),)),
        "wo_cross": noise(key_list[16], (MODEL_WIDTH, MODEL_WIDTH), 2 ** -0.5, 4.0, ((0, 4),)),
        "w_in": noise(key_list[17], (MODEL_WIDTH, FF), MODEL_WIDTH ** -0.5, 0.21875, ((1, 4),)),
        "w_out": noise(key_list[18], (FF, MODEL_WIDTH), FF ** -0.5, 0.109375, ((0, 4),)),
        "out_grad": noise(key_list[19], (TOKENS, MODEL_WIDTH), 1.0, 6.0, ((0, 8),)),
    }


EPSILON = 1e-06
NEGATIVE = -1e+30

@jax.custom_vjp
def low(v):
    return lax.optimization_barrier(v.astype(jnp.bfloat16)).astype(jnp.float32)

@jax.custom_vjp
def low_back(v):
    return v

def low_keep(v):
    return (low(v), None)

def low_pass(kept, grad):
    return (grad,)

def back_keep(v):
    return (v, None)

def back_low(kept, grad):
    return (low(grad),)
low.defvjp(low_keep, low_pass)
low_back.defvjp(back_keep, back_low)

def lowq(values):
    return low(low_back(values))

def wide_dot(left, right):
    return jnp.dot(left, right, precision=lax.Precision.HIGHEST, preferred_element_type=jnp.float32)

def rms_norm(values, gains):
    inverse = lax.rsqrt(lax.optimization_barrier(jnp.mean(values * values, axis=-1, keepdims=True)) + EPSILON)
    return values * inverse * gains

def bucket_table(length, buckets):
    exact_half = buckets // 2
    result = np.zeros((length, length), np.int32)
    for target in range(length):
        for source in range(length):
            distance = max(target - source, 0)
            if distance < exact_half:
                result[target, source] = distance
            else:
                spread = int(math.log(distance / exact_half) / math.log(128 / exact_half) * (buckets - exact_half))
                result[target, source] = min(exact_half + spread, buckets - 1)
    return result

def passage_slots(lens_group, owners_group, questions, most, span):
    owner_flat = owners_group.reshape(-1).astype(jnp.int32)
    slot_total = owner_flat.shape[0]
    slot_order = jnp.arange(slot_total, dtype=jnp.int32)
    before = (owner_flat[None, :] == owner_flat[:, None]) & (slot_order[None, :] < slot_order[:, None])
    ranking = lax.optimization_barrier(jnp.sum(before.astype(jnp.int32), axis=1)).astype(jnp.int32)
    asked_for = jnp.arange(questions, dtype=jnp.int32)
    places = jnp.arange(most, dtype=jnp.int32)
    chosen = (owner_flat[:, None, None] == asked_for[None, :, None]) & (ranking[:, None, None] == places[None, None, :])
    picked = lax.optimization_barrier(jnp.sum(jnp.where(chosen, slot_order[:, None, None], 0), axis=0)).astype(jnp.int32)
    present = jnp.any(chosen, axis=0)
    length_flat = lens_group.reshape(-1).astype(jnp.int32)
    packed_row_index = (picked // 2).astype(jnp.int32)
    offset = (picked % 2 * lens_group[:, 0].astype(jnp.int32)[packed_row_index]).astype(jnp.int32)
    length = length_flat[picked]
    within = jnp.arange(span, dtype=jnp.int32)
    token_position = (offset[:, :, None] + within[None, None, :]).astype(jnp.int32)
    usable = present[:, :, None] & (within[None, None, :] < length[:, :, None])
    return (packed_row_index, token_position, usable)

def attention(queries, keys_in, valued, bias_full, allowed):
    scores = jnp.einsum('qihd,qjhd->qhij', queries, keys_in, precision=lax.Precision.HIGHEST) + bias_full
    scores = jnp.where(allowed, low_back(scores), NEGATIVE)
    chances = low(jax.nn.softmax(scores, axis=-1))
    return lowq(jnp.einsum('qhij,qjhd->qihd', chances, valued, precision=lax.Precision.HIGHEST))

def group_layer(tokens, encoded, seg_lens, owners, answer_lens, weights):
    gain_self, gain_cross, gain_ffn, rel_bias, wq_self, wk_self, wv_self, wo_self, wq_cross, wk_cross, wv_cross, wo_cross, w_in, w_out = weights
    normed_self = low(rms_norm(tokens, gain_self))
    q_self = lowq(wide_dot(normed_self, wq_self)).reshape(QDEV, ANS, HEADS, HD)
    k_self = lowq(wide_dot(normed_self, wk_self)).reshape(QDEV, ANS, HEADS, HD)
    v_self = lowq(wide_dot(normed_self, wv_self)).reshape(QDEV, ANS, HEADS, HD)
    bucket_map = jnp.asarray(bucket_table(ANS, BUCKETS))
    bias_full = jnp.transpose(rel_bias[bucket_map], (2, 0, 1))[None]
    positions = jnp.arange(ANS, dtype=jnp.int32)
    causal = positions[None, :] <= positions[:, None]
    alive_keys = positions[None, :] < answer_lens[:, None]
    allowed = causal[None, None] & alive_keys[:, None, None, :]
    mixed_self = attention(q_self, k_self, v_self, bias_full, allowed).reshape(QDEV * ANS, MODEL_WIDTH)
    h_one = tokens + low_back(wide_dot(mixed_self, wo_self))
    normed_cross = low(rms_norm(h_one, gain_cross))
    q_cross = lowq(wide_dot(normed_cross, wq_cross)).reshape(QDEV, ANS, HEADS, HD)
    flat_encoded_rows = encoded.reshape(GROUP_ROWS * PACKED_ROW_LEN, MODEL_WIDTH)
    k_all = lowq(wide_dot(flat_encoded_rows, wk_cross))
    v_all = lowq(wide_dot(flat_encoded_rows, wv_cross))
    packed_row_index, token_position, usable = passage_slots(seg_lens, owners, QDEV, PMAX, PLEN)
    flattened_keys = (packed_row_index[:, :, None] * PACKED_ROW_LEN + token_position).reshape(-1).astype(jnp.int32)
    k_cross = jnp.take(k_all, flattened_keys, axis=0).reshape(QDEV, KEYS, HEADS, HD)
    v_cross = jnp.take(v_all, flattened_keys, axis=0).reshape(QDEV, KEYS, HEADS, HD)
    allowed_cross = usable.reshape(QDEV, 1, 1, KEYS)
    mixed_cross = attention(q_cross, k_cross, v_cross, 0.0, allowed_cross).reshape(QDEV * ANS, MODEL_WIDTH)
    h_two = h_one + low_back(wide_dot(mixed_cross, wo_cross))
    normed_ffn = low(rms_norm(h_two, gain_ffn))
    pre_act = low_back(wide_dot(normed_ffn, w_in))
    hidden = lowq(jax.nn.gelu(pre_act, approximate=False))
    return h_two + low_back(wide_dot(hidden, w_out))

def reference(tokens, encoded, seg_lens, owners, answer_lens, gain_self, gain_cross, gain_ffn, rel_bias, wq_self, wk_self, wv_self, wo_self, wq_cross, wk_cross, wv_cross, wo_cross, w_in, w_out, out_grad):
    group_count = N_DP * N_PASS
    weights_f = tuple((weight.astype(jnp.float32) for weight in (gain_self, gain_cross, gain_ffn, rel_bias, wq_self, wk_self, wv_self, wo_self, wq_cross, wk_cross, wv_cross, wo_cross, w_in, w_out)))
    tokens_f = tokens.astype(jnp.float32).reshape(group_count, QDEV * ANS, MODEL_WIDTH)
    encoded_float = jnp.transpose(encoded.astype(jnp.float32).reshape(N_DP, N_PASS, N_PASS, ROWS_PER_PASS, PACKED_ROW_LEN, MODEL_WIDTH), (0, 2, 1, 3, 4, 5)).reshape(group_count, GROUP_ROWS, PACKED_ROW_LEN, MODEL_WIDTH)
    lens_g = jnp.transpose(seg_lens.reshape(N_DP, N_PASS, N_PASS, ROWS_PER_PASS, 2), (0, 2, 1, 3, 4)).reshape(group_count, GROUP_ROWS, 2)
    owners_g = jnp.transpose(owners.reshape(N_DP, N_PASS, N_PASS, ROWS_PER_PASS, 2), (0, 2, 1, 3, 4)).reshape(group_count, GROUP_ROWS, 2)
    answers_g = answer_lens.reshape(group_count, QDEV)

    def full_layer(tokens_in, encoded_in, weights_in):

        def one_group(packed):
            tok_group, enc_group, lens_group, own_group, ans_group = packed
            return group_layer(tok_group, enc_group, lens_group, own_group, ans_group, weights_in)
        return lax.map(jax.checkpoint(one_group), (tokens_in, encoded_in, lens_g, owners_g, answers_g))
    result, pullback = jax.vjp(full_layer, tokens_f, encoded_float, weights_f)
    grad_in, encoded_gradient, grad_weights = pullback(out_grad.astype(jnp.float32).reshape(group_count, QDEV * ANS, MODEL_WIDTH))
    output = result.reshape(TOKENS, MODEL_WIDTH).astype(jnp.bfloat16)
    grad_tokens = grad_in.reshape(TOKENS, MODEL_WIDTH).astype(jnp.bfloat16)
    gradient_of_encoded = jnp.transpose(encoded_gradient.reshape(N_DP, N_PASS, N_PASS, ROWS_PER_PASS, PACKED_ROW_LEN, MODEL_WIDTH), (0, 2, 1, 3, 4, 5)).reshape(PACKED_ROWS, PACKED_ROW_LEN, MODEL_WIDTH).astype(jnp.bfloat16)
    return (output, grad_tokens, gradient_of_encoded, grad_weights[0], grad_weights[1], grad_weights[2], grad_weights[3], grad_weights[4], grad_weights[5], grad_weights[6], grad_weights[7], grad_weights[8], grad_weights[9], grad_weights[10], grad_weights[11], grad_weights[12], grad_weights[13])
```

```python
import functools
import math

import jax
import jax.numpy as jnp
import numpy as np
from jax import lax
from jax.experimental import pallas as pl
from jax.experimental.pallas import tpu as pltpu
from jax.sharding import PartitionSpec as P

MODEL_WIDTH = 768
HD = 64
BUCKETS = 32
ANS = 20
PADT = 24
LANES = 128
STATW = MODEL_WIDTH + LANES
QUAD = 4
QW = QUAD * HD
GROUP_ROWS = 32

EPSILON = 1e-06
NEGATIVE = -1e30
MESH = pl.DeviceIdType.MESH
VMEM_LIMIT = 56 << 20
F32 = jnp.float32
BF16 = jnp.bfloat16


def bucket_table(length, buckets):
    exact_half = buckets // 2
    result = np.zeros((length, length), np.int32)
    for target in range(length):
        for source in range(length):
            distance = max(target - source, 0)
            if distance < exact_half:
                result[target, source] = distance
            else:
                spread = int(
                    math.log(distance / exact_half)
                    / math.log(128 / exact_half)
                    * (buckets - exact_half)
                )
                result[target, source] = min(exact_half + spread, buckets - 1)
    return result


def dot_nn(a, b):
    return lax.dot_general(a, b, (((1,), (0,)), ((), ())), preferred_element_type=F32)


def dot_nt(a, b):
    return lax.dot_general(a, b, (((1,), (1,)), ((), ())), preferred_element_type=F32)


def dot_tn(a, b):
    return lax.dot_general(a, b, (((0,), (0,)), ((), ())), preferred_element_type=F32)


def rms_inverse(v):
    return lax.rsqrt(jnp.mean(v * v, axis=-1, keepdims=True) + EPSILON)


def rms_back(v, gains, ga):
    w = rms_inverse(v)
    gain_grad = jnp.sum(ga * v * w, axis=0, keepdims=True)
    gg = gains * ga
    gv = w * gg - v * (w * w * w) * jnp.mean(gg * v, axis=-1, keepdims=True)
    return gv, gain_grad


def local_call(kernel, outs, *ins, scratch=(), flops=0):
    return pl.pallas_call(
        kernel,
        out_shape=[jax.ShapeDtypeStruct(shape, dtype) for shape, dtype in outs],
        in_specs=[pl.BlockSpec(memory_space=pltpu.VMEM) for _ in ins],
        out_specs=[pl.BlockSpec(memory_space=pltpu.VMEM) for _ in outs],
        scratch_shapes=list(scratch),
        compiler_params=pltpu.CompilerParams(vmem_limit_bytes=VMEM_LIMIT),
        cost_estimate=pl.CostEstimate(
            flops=flops,
            bytes_accessed=sum(math.prod(x.shape) * x.dtype.itemsize for x in ins),
            transcendentals=0,
        ),
    )(*ins)


def place(**kw):
    return tuple(kw[a] if a in kw else lax.axis_index(a) for a in ("dp", "pass", "mp"))


def greet(peers):
    barrier = pltpu.get_barrier_semaphore()
    for peer in peers:
        pl.semaphore_signal(barrier, inc=1, device_id=peer, device_id_type=MESH)
    pl.semaphore_wait(barrier, len(peers))


def remote(src, dst, send, recv, peer):
    return pltpu.make_async_remote_copy(
        src_ref=src, dst_ref=dst, send_sem=send, recv_sem=recv, device_id=peer, device_id_type=MESH
    )


def gather_mp_kernel(x_ref, o_ref, send, recv, here):
    n, me = lax.axis_size("mp"), lax.axis_index("mp")
    peers = [place(mp=lax.rem(me + k, n)) for k in range(1, n)]
    own = pltpu.make_async_copy(x_ref, o_ref.at[me], here)
    own.start()
    greet(peers)
    copies = [
        remote(x_ref, o_ref.at[me], send.at[k], recv.at[k], peer) for k, peer in enumerate(peers)
    ]
    for copy in copies:
        copy.start()
    for copy in copies:
        copy.wait()
    own.wait()


def gather_mp(x, collective_id):
    n = lax.axis_size("mp")
    return pl.pallas_call(
        gather_mp_kernel,
        out_shape=jax.ShapeDtypeStruct((n,) + x.shape, x.dtype),
        in_specs=[pl.BlockSpec(memory_space=pltpu.VMEM)],
        out_specs=pl.BlockSpec(memory_space=pltpu.VMEM),
        scratch_shapes=[
            pltpu.SemaphoreType.DMA((n - 1,)),
            pltpu.SemaphoreType.DMA((n - 1,)),
            pltpu.SemaphoreType.DMA,
        ],
        compiler_params=pltpu.CompilerParams(
            collective_id=collective_id, has_side_effects=True, vmem_limit_bytes=VMEM_LIMIT
        ),
    )(x)


def gather_both_kernel(x_ref, o_ref, zsend, zrecv, msend, mrecv, here):
    pn, pm = lax.axis_size("pass"), lax.axis_index("pass")
    mn, mm = lax.axis_size("mp"), lax.axis_index("mp")
    zpeers = [place(**{"pass": lax.rem(pm + k, pn)}) for k in range(1, pn)]
    mpeers = [place(mp=lax.rem(mm + k, mn)) for k in range(1, mn)]
    own = pltpu.make_async_copy(x_ref, o_ref.at[pm, mm], here)
    own.start()
    greet(zpeers + mpeers)
    zcopies, mcopies = [], []
    for k, peer in enumerate(zpeers):
        copy = remote(x_ref, o_ref.at[pm, mm], zsend.at[k], zrecv.at[k], peer)
        copy.start()
        zcopies.append(copy)
    for k, peer in enumerate(mpeers):
        copy = remote(x_ref, o_ref.at[pm, mm], msend.at[0, k], mrecv.at[0, k], peer)
        copy.start()
        mcopies.append(copy)
    for j, zcopy in enumerate(zcopies):
        zcopy.wait_recv()
        source = lax.rem(pm - (j + 1) + pn, pn)
        for k, peer in enumerate(mpeers):
            copy = remote(
                o_ref.at[source, mm],
                o_ref.at[source, mm],
                msend.at[j + 1, k],
                mrecv.at[j + 1, k],
                peer,
            )
            copy.start()
            mcopies.append(copy)
    for copy in mcopies:
        copy.wait()
    for copy in zcopies:
        copy.wait_send()
    own.wait()


def gather_both(x, collective_id):
    pn, mn = lax.axis_size("pass"), lax.axis_size("mp")
    return pl.pallas_call(
        gather_both_kernel,
        out_shape=jax.ShapeDtypeStruct((pn, mn) + x.shape, x.dtype),
        in_specs=[pl.BlockSpec(memory_space=pltpu.VMEM)],
        out_specs=pl.BlockSpec(memory_space=pltpu.VMEM),
        scratch_shapes=[
            pltpu.SemaphoreType.DMA((pn - 1,)),
            pltpu.SemaphoreType.DMA((pn - 1,)),
            pltpu.SemaphoreType.DMA((pn, mn - 1)),
            pltpu.SemaphoreType.DMA((pn, mn - 1)),
            pltpu.SemaphoreType.DMA,
        ],
        compiler_params=pltpu.CompilerParams(
            collective_id=collective_id, has_side_effects=True, vmem_limit_bytes=VMEM_LIMIT
        ),
    )(x)


def spread(chunks, axis):
    n, me = lax.axis_size(axis), lax.axis_index(axis)
    got = [lax.dynamic_index_in_dim(chunks, me, 0, False)]
    for k in range(1, n):
        chunk = lax.dynamic_index_in_dim(chunks, lax.rem(me + k, n), 0, False)
        got.append(lax.ppermute(chunk, axis, [(i, (i + k) % n) for i in range(n)]))
    return got


def in_order(got, axis):
    n, me = lax.axis_size(axis), lax.axis_index(axis)
    out = jnp.zeros((n,) + got[0].shape, got[0].dtype)
    for k, x in enumerate(got):
        out = lax.dynamic_update_index_in_dim(out, x, lax.rem(me - k + n, n), 0)
    return out


def gather_weights(shard):
    n, me, core = lax.axis_size("mp"), lax.axis_index("mp"), lax.axis_index("dp")
    w, rows, width = shard.shape
    half = rows // 2
    mine = lax.dynamic_slice_in_dim(shard, core * half, half, 1)
    got = [mine]
    for k in range(1, n):
        got.append(lax.ppermute(mine, "mp", [(i, (i + k) % n) for i in range(n)]))
    other = [lax.ppermute(x, "dp", [(0, 1), (1, 0)]) for x in got]
    out = jnp.zeros((w, n, 2, half, width), shard.dtype)
    for k in range(n):
        source = lax.rem(me - k + n, n)
        out = lax.dynamic_update_slice(out, got[k][:, None, None], (0, source, core, 0, 0))
        out = lax.dynamic_update_slice(out, other[k][:, None, None], (0, source, 1 - core, 0, 0))
    return out.reshape(w, n * rows, width)


def self_forward_kernel(
    heads, x_ref, gain_ref, wq_ref, wk_ref, wv_ref, wo_ref, bias_ref, alive_ref,
    term_ref, a1_ref, qkv_ref, p_ref, o1_ref,
):
    x = x_ref[...].astype(F32)
    a1 = (x * rms_inverse(x) * gain_ref[...]).astype(BF16)
    a1_ref[...] = a1
    cols = heads * HD
    for k, w_ref in enumerate((wq_ref, wk_ref, wv_ref)):
        qkv_ref[k] = dot_nn(a1, w_ref[...]).astype(BF16)
    blocks, size = alive_ref.shape[0], alive_ref.shape[2]
    row = lax.broadcasted_iota(jnp.int32, (size, size), 0)
    col = lax.broadcasted_iota(jnp.int32, (size, size), 1)
    near = (col <= row) & (lax.div(col, ANS) == lax.div(row, ANS))
    for b in range(blocks):
        allowed = near & (alive_ref[b] > 0)
        rows = pl.ds(b * size, size)
        q, k, v = qkv_ref[0, rows, :], qkv_ref[1, rows, :], qkv_ref[2, rows, :]
        for h in range(heads):
            part = slice(h * HD, (h + 1) * HD)
            s = jnp.where(allowed, dot_nt(q[:, part], k[:, part]) + bias_ref[h], NEGATIVE)
            e = jnp.exp(s - jnp.max(s, axis=-1, keepdims=True))
            p = e / jnp.sum(e, axis=-1, keepdims=True)
            p_ref[b * heads + h] = p
            o1_ref[rows, part] = dot_nn(p.astype(BF16), v[:, part]).astype(BF16)
    term_ref[...] = dot_nn(o1_ref[...], wo_ref[...]).astype(BF16)


def self_backward_kernel(
    heads, gsa_ref, wq_ref, wk_ref, wv_ref, wo_ref, a1_ref, qkv_ref, p_ref, o1_ref,
    ga1_ref, gw_ref, score_ref, gqkv_ref,
):
    gsa = gsa_ref[...]
    go1 = dot_nt(gsa, wo_ref[...]).astype(BF16)
    size = p_ref.shape[1]
    blocks = p_ref.shape[0] // heads
    for h in range(heads):
        part = slice(h * HD, (h + 1) * HD)
        total = jnp.zeros((size, size), F32)
        for b in range(blocks):
            rows = pl.ds(b * size, size)
            q, k, v = qkv_ref[0, rows, part], qkv_ref[1, rows, part], qkv_ref[2, rows, part]
            p = p_ref[b * heads + h]
            go = go1[b * size : (b + 1) * size, part]
            gp = dot_nt(go, v)
            gs = (p * (gp - jnp.sum(gp * p, axis=-1, keepdims=True))).astype(BF16)
            total = total + gs.astype(F32)
            gqkv_ref[0, rows, part] = dot_nn(gs, k).astype(BF16)
            gqkv_ref[1, rows, part] = dot_tn(gs, q).astype(BF16)
            gqkv_ref[2, rows, part] = dot_tn(p.astype(BF16), go).astype(BF16)
        score_ref[h] = total
    ga1 = dot_nt(gqkv_ref[0], wq_ref[...])
    ga1 = ga1 + dot_nt(gqkv_ref[1], wk_ref[...])
    ga1 = ga1 + dot_nt(gqkv_ref[2], wv_ref[...])
    ga1_ref[...] = ga1.astype(BF16)
    for k in range(3):
        gw_ref[k] = dot_tn(gqkv_ref[k], a1_ref[...])
    gw_ref[3] = dot_tn(o1_ref[...], gsa)


def head_lanes():
    lane = lax.broadcasted_iota(jnp.int32, (QUAD, 1, QW), 2)
    return lax.div(lane, HD) == lax.broadcasted_iota(jnp.int32, (QUAD, 1, QW), 0)


def pad_questions(dst_ref, values):
    questions = dst_ref.shape[0]
    for q in range(questions):
        dst_ref[q, 0:ANS, :] = values[q * ANS : (q + 1) * ANS, :]
        dst_ref[q, ANS:PADT, :] = jnp.zeros((PADT - ANS, values.shape[1]), F32)


def masked_heads(ref, owners, cols, lanes):
    parts = []
    for q in owners:
        parts.append(jnp.where(lanes, ref[q, :, cols][None], 0.0))
    return jnp.concatenate(parts, axis=0).reshape(2 * QUAD * PADT, QW).astype(BF16)


def fold_heads(x, lanes):
    y = x.reshape(2, QUAD, PADT, QW)
    return jnp.sum(jnp.where(lanes[None], y, 0.0), axis=1)


def segment_mask(meta_ref, row, keys):
    lane = lax.broadcasted_iota(jnp.int32, (1, keys), 1)
    parts = []
    for s in range(2):
        first, last = meta_ref[row, 2 + 2 * s], meta_ref[row, 3 + 2 * s]
        parts.append(((lane >= first) & (lane < last)).astype(F32)[None])
    mask = jnp.concatenate(parts, axis=0)
    mask = jnp.broadcast_to(mask, (2, QUAD * PADT, keys)).reshape(2 * QUAD * PADT, keys)
    return mask > 0.5


def split_three(x):
    hi = x.astype(BF16).astype(F32)
    mid = (x - hi).astype(BF16).astype(F32)
    return hi, mid, x - hi - mid


def cross_forward_kernel(
    rows_per, keys, meta_ref, a2_ref, wq_ref, kv_ref, out_ref, q_pad, o_acc, m_acc, l_acc, flat
):
    g = pl.program_id(0)
    q2 = dot_nt(a2_ref[0], wq_ref[...]).astype(BF16).astype(F32)
    pad_questions(q_pad, q2)
    o_acc[...] = jnp.zeros_like(o_acc)
    m_acc[...] = jnp.full_like(m_acc, NEGATIVE)
    l_acc[...] = jnp.zeros_like(l_acc)
    lanes = head_lanes()
    quads = MODEL_WIDTH // QW

    def one_row(r, carry):
        row = g * rows_per + r
        owners = [meta_ref[row, 0], meta_ref[row, 1]]
        at = pl.ds(pl.multiple_of(r * keys, keys), keys)
        mask = segment_mask(meta_ref, row, keys)
        for c in range(quads):
            cols = slice(c * QW, (c + 1) * QW)
            k = kv_ref[at, c * QW : (c + 1) * QW]
            v = kv_ref[at, MODEL_WIDTH + c * QW : MODEL_WIDTH + (c + 1) * QW]
            qm = masked_heads(q_pad, owners, cols, lanes)
            s = jnp.where(mask, dot_nt(qm, k), NEGATIVE)
            top = jnp.max(s, axis=-1, keepdims=True)
            p = jnp.where(mask, jnp.exp(s - top), 0.0)
            o = fold_heads(dot_nn(p.astype(BF16), v), lanes)
            total = jnp.sum(p, axis=-1, keepdims=True)
            m_new = fold_heads(jnp.broadcast_to(top, (2 * QUAD * PADT, QW)), lanes)
            l_new = fold_heads(jnp.broadcast_to(total, (2 * QUAD * PADT, QW)), lanes)
            for s_at, q in enumerate(owners):
                m_old = m_acc[q, :, cols]
                m_both = jnp.maximum(m_old, m_new[s_at])
                a, b = jnp.exp(m_old - m_both), jnp.exp(m_new[s_at] - m_both)
                o_acc[q, :, cols] = a * o_acc[q, :, cols] + b * o[s_at]
                l_acc[q, :, cols] = a * l_acc[q, :, cols] + b * l_new[s_at]
                m_acc[q, :, cols] = m_both
        return carry

    lax.fori_loop(0, rows_per, one_row, 0)
    questions = q_pad.shape[0]
    pick_row = lax.broadcasted_iota(jnp.int32, (MODEL_WIDTH, LANES), 0)
    pick_col = lax.broadcasted_iota(jnp.int32, (MODEL_WIDTH, LANES), 1)
    pick = (pick_row == pick_col * HD).astype(F32)
    for q in range(questions):
        l = l_acc[q]
        some = l > 0.0
        safe = jnp.where(some, l, 1.0)
        o = o_acc[q] / safe
        lse = jnp.where(some, m_acc[q] + jnp.log(safe), NEGATIVE)
        lse = lax.dot_general(
            lse, pick, (((1,), (0,)), ((), ())),
            preferred_element_type=F32, precision=lax.Precision.HIGHEST,
        )
        hi, mid, low = split_three(lse)
        stat = hi + pltpu.roll(mid, 16, 1) + pltpu.roll(low, 32, 1)
        flat[q * ANS : (q + 1) * ANS, :MODEL_WIDTH] = o[:ANS]
        flat[q * ANS : (q + 1) * ANS, MODEL_WIDTH:] = stat[:ANS]
    chunk = out_ref.shape[2]
    for m in range(out_ref.shape[0]):
        out_ref[m, 0] = flat[m * chunk : (m + 1) * chunk, :].astype(BF16)


def cross_forward(meta, a2_all, wq, kv, mp_parts):
    groups, n_tokens, _ = a2_all.shape
    rows_per = GROUP_ROWS // groups
    keys = kv.shape[0] // GROUP_ROWS
    questions = n_tokens // ANS
    block = rows_per * keys
    padded = pltpu.VMEM((questions, PADT, MODEL_WIDTH), F32)
    return pl.pallas_call(
        functools.partial(cross_forward_kernel, rows_per, keys),
        grid_spec=pltpu.PrefetchScalarGridSpec(
            num_scalar_prefetch=1,
            grid=(groups,),
            in_specs=[
                pl.BlockSpec((1, n_tokens, MODEL_WIDTH), lambda g, meta: (g, 0, 0)),
                pl.BlockSpec((MODEL_WIDTH, MODEL_WIDTH), lambda g, meta: (0, 0)),
                pl.BlockSpec((block, 2 * MODEL_WIDTH), lambda g, meta: (g, 0)),
            ],
            out_specs=pl.BlockSpec(
                (mp_parts, 1, n_tokens // mp_parts, STATW), lambda g, meta: (0, g, 0, 0)
            ),
            scratch_shapes=[padded, padded, padded, padded, pltpu.VMEM((n_tokens, STATW), F32)],
        ),
        out_shape=jax.ShapeDtypeStruct((mp_parts, groups, n_tokens // mp_parts, STATW), BF16),
        compiler_params=pltpu.CompilerParams(vmem_limit_bytes=VMEM_LIMIT),
    )(meta, a2_all, wq, kv)


def cross_backward_kernel(
    rows_per, keys, meta_ref, a2_ref, gc_ref, wq_ref, wo_ref, kv_ref, gq_ref, gkv_ref,
    q_pad, go_pad, gq_acc, lse_pad, delta_pad, flat,
):
    g = pl.program_id(0)
    pad_questions(q_pad, dot_nt(a2_ref[0], wq_ref[...]).astype(BF16).astype(F32))
    pad_questions(go_pad, dot_nt(gc_ref[0, :, :MODEL_WIDTH], wo_ref[...]).astype(BF16).astype(F32))
    stat = gc_ref[0, :, MODEL_WIDTH:].astype(F32)
    lse = stat + pltpu.roll(stat, LANES - 16, 1) + pltpu.roll(stat, LANES - 32, 1)
    pad_questions(lse_pad, lse)
    pad_questions(delta_pad, pltpu.roll(lse, LANES - 48, 1))
    gq_acc[...] = jnp.zeros_like(gq_acc)
    lanes = head_lanes()
    quads = MODEL_WIDTH // QW

    def columns(ref, owners, c):
        parts = []
        for q in owners:
            for h in range(QUAD):
                at = c * QUAD + h
                parts.append(ref[q, :, at : at + 1])
        return jnp.concatenate(parts, axis=0)

    def one_row(r, carry):
        row = g * rows_per + r
        owners = [meta_ref[row, 0], meta_ref[row, 1]]
        at = pl.ds(pl.multiple_of(r * keys, keys), keys)
        mask = segment_mask(meta_ref, row, keys)
        for c in range(quads):
            cols = slice(c * QW, (c + 1) * QW)
            vcols = slice(MODEL_WIDTH + c * QW, MODEL_WIDTH + (c + 1) * QW)
            k, v = kv_ref[at, cols], kv_ref[at, vcols]
            qm = masked_heads(q_pad, owners, cols, lanes)
            gom = masked_heads(go_pad, owners, cols, lanes)
            s = dot_nt(qm, k) - columns(lse_pad, owners, c)
            p = jnp.exp(jnp.where(mask, s, NEGATIVE))
            gp = dot_nt(gom, v) - columns(delta_pad, owners, c)
            gs = (p * gp).astype(BF16)
            gq = fold_heads(dot_nn(gs, k), lanes)
            for s_at, q in enumerate(owners):
                gq_acc[q, :, cols] = gq_acc[q, :, cols] + gq[s_at]
            gkv_ref[at, cols] = dot_tn(gs, qm).astype(BF16)
            gkv_ref[at, vcols] = dot_tn(p.astype(BF16), gom).astype(BF16)
        return carry

    lax.fori_loop(0, rows_per, one_row, 0)
    for q in range(q_pad.shape[0]):
        flat[q * ANS : (q + 1) * ANS, :] = gq_acc[q, :ANS, :]
    chunk = gq_ref.shape[2]
    for m in range(gq_ref.shape[0]):
        gq_ref[m, 0] = flat[m * chunk : (m + 1) * chunk, :].astype(BF16)


def cross_backward(meta, a2_all, gc_all, wq, wo, kv, mp_parts):
    groups, n_tokens, _ = a2_all.shape
    rows_per = GROUP_ROWS // groups
    keys = kv.shape[0] // GROUP_ROWS
    questions = n_tokens // ANS
    block = rows_per * keys
    padded = pltpu.VMEM((questions, PADT, MODEL_WIDTH), F32)
    small = pltpu.VMEM((questions, PADT, LANES), F32)
    whole = pl.BlockSpec((MODEL_WIDTH, MODEL_WIDTH), lambda g, meta: (0, 0))
    return pl.pallas_call(
        functools.partial(cross_backward_kernel, rows_per, keys),
        grid_spec=pltpu.PrefetchScalarGridSpec(
            num_scalar_prefetch=1,
            grid=(groups,),
            in_specs=[
                pl.BlockSpec((1, n_tokens, MODEL_WIDTH), lambda g, meta: (g, 0, 0)),
                pl.BlockSpec((1, n_tokens, STATW), lambda g, meta: (g, 0, 0)),
                whole,
                whole,
                pl.BlockSpec((block, 2 * MODEL_WIDTH), lambda g, meta: (g, 0)),
            ],
            out_specs=[
                pl.BlockSpec(
                    (mp_parts, 1, n_tokens // mp_parts, MODEL_WIDTH), lambda g, meta: (0, g, 0, 0)
                ),
                pl.BlockSpec((block, 2 * MODEL_WIDTH), lambda g, meta: (g, 0)),
            ],
            scratch_shapes=[
                padded, padded, padded, small, small, pltpu.VMEM((n_tokens, MODEL_WIDTH), F32)
            ],
        ),
        out_shape=[
            jax.ShapeDtypeStruct((mp_parts, groups, n_tokens // mp_parts, MODEL_WIDTH), BF16),
            jax.ShapeDtypeStruct(kv.shape, BF16),
        ],
        compiler_params=pltpu.CompilerParams(vmem_limit_bytes=VMEM_LIMIT),
    )(meta, a2_all, gc_all, wq, wo, kv)


def widen(w):
    row = lax.broadcasted_iota(jnp.int32, (LANES, MODEL_WIDTH), 0)
    col = lax.broadcasted_iota(jnp.int32, (LANES, MODEL_WIDTH), 1)
    each = (row == lax.div(col, HD)).astype(BF16)
    hi = w.astype(BF16)
    low = (w - hi.astype(F32)).astype(BF16)
    return dot_nn(hi, each) + dot_nn(low, each)


def combined(refs):
    lses = []
    for ref in refs:
        stat = ref[:, MODEL_WIDTH:].astype(F32)
        lses.append(stat + pltpu.roll(stat, LANES - 16, 1) + pltpu.roll(stat, LANES - 32, 1))
    top = functools.reduce(jnp.maximum, lses)
    weights = [jnp.exp(x - top) for x in lses]
    total = functools.reduce(jnp.add, weights)
    out = 0.0
    for ref, weight in zip(refs, weights):
        out = out + widen(weight / total) * ref[:, :MODEL_WIDTH].astype(F32)
    lane = lax.broadcasted_iota(jnp.int32, total.shape, 1)
    lse = jnp.where(lane < MODEL_WIDTH // HD, top + jnp.log(total), 0.0)
    return out, lse


def packed_stat(lse, at=0):
    hi, mid, low = split_three(lse)
    parts = [hi if at == 0 else pltpu.roll(hi, at, 1)]
    parts += [pltpu.roll(mid, at + 16, 1), pltpu.roll(low, at + 32, 1)]
    return parts[0] + parts[1] + parts[2]


def combine_kernel(*refs):
    out_ref = refs[-1]
    out, lse = combined(refs[:-1])
    out_ref[:, :MODEL_WIDTH] = out.astype(BF16)
    out_ref[:, MODEL_WIDTH:] = packed_stat(lse).astype(BF16)


def home_cross_query_kernel(n, *refs):
    parts, (x_ref, gain_ref, h_ref, a_ref) = refs[:n], refs[n:]
    h = x_ref[...].astype(F32)
    for ref in parts:
        h = h + ref[...].astype(F32)
    h_ref[...] = h
    a_ref[...] = (h * rms_inverse(h) * gain_ref[...]).astype(BF16)


def home_cross_out_kernel(n, *refs):
    parts, rest = refs[:n], refs[n:]
    h_ref, wo_ref, gain_ref, h2_ref, a3_ref, o_ref, blocks_ref, lse_ref = rest
    o, lse = combined(parts)
    o_ref[...] = o
    lse_ref[...] = lse
    low = o.astype(BF16)
    width = blocks_ref.shape[2]
    for k in range(blocks_ref.shape[0]):
        blocks_ref[k] = low[:, k * width : (k + 1) * width]
    h = h_ref[...] + dot_nn(low, wo_ref[...])
    h2_ref[...] = h
    a3_ref[...] = (h * rms_inverse(h) * gain_ref[...]).astype(BF16)


def home_ffn_back_kernel(n, *refs):
    parts, rest = refs[:n], refs[n:]
    gy_ref, h_ref, gain_ref, wo_ref, o_ref, lse_ref, gh_ref, gc_ref, gain_out_ref = rest
    ga = parts[0][...].astype(F32)
    for ref in parts[1:]:
        ga = ga + ref[...].astype(F32)
    gv, gain_grad = rms_back(h_ref[...], gain_ref[...], ga)
    gain_out_ref[...] = gain_grad
    gh = gy_ref[...].astype(F32) + gv
    gh_ref[...] = gh
    gc = gh.astype(BF16)
    go = dot_nt(gc, wo_ref[...]).astype(BF16).astype(F32)
    row = lax.broadcasted_iota(jnp.int32, (MODEL_WIDTH, LANES), 0)
    col = lax.broadcasted_iota(jnp.int32, (MODEL_WIDTH, LANES), 1)
    each = (lax.div(row, HD) == col).astype(F32)
    delta = lax.dot_general(
        go * o_ref[...], each, (((1,), (0,)), ((), ())),
        preferred_element_type=F32, precision=lax.Precision.HIGHEST,
    )
    gc_ref[:, :MODEL_WIDTH] = gc
    gc_ref[:, MODEL_WIDTH:] = (packed_stat(lse_ref[...]) + packed_stat(delta, 48)).astype(BF16)


def home_query_back_kernel(n, *refs):
    parts, rest = refs[:n], refs[n:]
    gh2_ref, h_ref, gain_ref, wq_ref, gh1_ref, gsa_ref, blocks_ref, gain_out_ref = rest
    gq = parts[0][...].astype(F32)
    for ref in parts[1:]:
        gq = gq + ref[...].astype(F32)
    low = gq.astype(BF16)
    width = blocks_ref.shape[2]
    for k in range(blocks_ref.shape[0]):
        blocks_ref[k] = low[:, k * width : (k + 1) * width]
    gv, gain_grad = rms_back(h_ref[...], gain_ref[...], dot_nn(low, wq_ref[...]))
    gain_out_ref[...] = gain_grad
    gh = gh2_ref[...] + gv
    gh1_ref[...] = gh
    gsa_ref[...] = gh.astype(BF16)


def home_last_kernel(n, *refs):
    parts, (x_ref, gain_ref, gh1_ref, out_ref, gain_out_ref) = refs[:n], refs[n:]
    ga = parts[0][...].astype(F32)
    for ref in parts[1:]:
        ga = ga + ref[...].astype(F32)
    gv, gain_grad = rms_back(x_ref[...].astype(F32), gain_ref[...], ga)
    gain_out_ref[...] = gain_grad
    out_ref[...] = (gh1_ref[...] + gv).astype(BF16)


def add_kernel(*refs):
    total = refs[0][...].astype(F32)
    for ref in refs[1:-1]:
        total = total + ref[...].astype(F32)
    refs[-1][...] = total.astype(refs[-1].dtype)


def ffn_kernel(a3_ref, w_in_ref, w_out_ref, gy_ref, term_ref, ga3_ref, gw_in_ref, gw_out_ref):
    a3, gy = a3_ref[...], gy_ref[...]
    u = dot_nn(a3, w_in_ref[...])
    cdf = 0.5 * (1.0 + lax.erf(u * np.float32(math.sqrt(0.5))))
    pdf = np.float32(1.0 / math.sqrt(2.0 * math.pi)) * jnp.exp(-0.5 * u * u)
    e = (u * cdf).astype(BF16)
    term_ref[...] = dot_nn(e, w_out_ref[...]).astype(BF16)
    ge = dot_nt(gy, w_out_ref[...]).astype(BF16).astype(F32)
    gu = (ge * (cdf + u * pdf)).astype(BF16)
    ga3_ref[...] = dot_nt(gu, w_in_ref[...]).astype(BF16)
    gw_in_ref[...] = dot_tn(gu, a3).astype(BF16)
    gw_out_ref[...] = dot_tn(e, gy).astype(BF16)


def on_device(
    tokens,
    encoded,
    seg_lens,
    owners,
    answer_lens,
    gain_self,
    gain_cross,
    gain_ffn,
    rel_bias,
    wq_self,
    wk_self,
    wv_self,
    wo_self,
    wq_cross,
    wk_cross,
    wv_cross,
    wo_cross,
    w_in,
    w_out,
    out_grad,
):
    groups, mp_parts = lax.axis_size("pass"), lax.axis_size("mp")
    pass_at, mp_at = lax.axis_index("pass"), lax.axis_index("mp")
    heads = rel_bias.shape[1]
    head_cols = heads * HD
    quarter = encoded.shape[1]
    n_tokens = tokens.shape[0]
    chunk = n_tokens // mp_parts
    block_questions = chunk // ANS
    gain_self, gain_cross, gain_ffn = gain_self[None], gain_cross[None], gain_ffn[None]

    lens_here = lax.dynamic_index_in_dim(
        seg_lens.reshape(groups, GROUP_ROWS, 2), pass_at, 0, keepdims=False
    )
    owners_here = lax.dynamic_index_in_dim(
        owners.reshape(groups, GROUP_ROWS, 2), pass_at, 0, keepdims=False
    )
    first = lens_here[:, :1] - mp_at * quarter
    last = first + lens_here[:, 1:]
    meta = jnp.concatenate([owners_here, jnp.zeros_like(first), first, first, last], axis=1)

    wkv = gather_weights(jnp.stack([wk_cross.T, wv_cross.T])).reshape(2 * MODEL_WIDTH, MODEL_WIDTH)
    wqo = gather_weights(jnp.stack([wq_cross.T, wo_cross]))
    wq_full, wo_full = wqo[0], wqo[1]
    flat_encoded = encoded.reshape(GROUP_ROWS * quarter, MODEL_WIDTH)
    kv = dot_nt(flat_encoded, wkv).astype(BF16)

    tokens_home = lax.dynamic_slice_in_dim(tokens, mp_at * chunk, chunk, 0)
    gy_home = lax.dynamic_slice_in_dim(out_grad, mp_at * chunk, chunk, 0)

    table = np.eye(BUCKETS, dtype=np.float32)[bucket_table(ANS, BUCKETS)]
    bias = jnp.einsum("ijb,bh->hij", table, rel_bias, precision=lax.Precision.HIGHEST)
    bias = jnp.tile(bias, (1, block_questions, block_questions))
    alive = (jnp.arange(ANS, dtype=jnp.int32)[None, :] < answer_lens[:, None]).astype(jnp.int32)
    alive = alive.reshape(mp_parts, 1, chunk)
    term, a1, qkv, p1, o1 = local_call(
        functools.partial(self_forward_kernel, heads),
        [
            ((n_tokens, MODEL_WIDTH), BF16),
            ((n_tokens, MODEL_WIDTH), BF16),
            ((3, n_tokens, head_cols), BF16),
            ((mp_parts * heads, chunk, chunk), F32),
            ((n_tokens, head_cols), BF16),
        ],
        tokens, gain_self, wq_self, wk_self, wv_self, wo_self, bias, alive,
    )
    home = (chunk, MODEL_WIDTH)
    got = spread(term.reshape(mp_parts, chunk, MODEL_WIDTH), "mp")
    h_one, a2 = local_call(
        functools.partial(home_cross_query_kernel, mp_parts),
        [(home, F32), (home, BF16)],
        *got, tokens_home, gain_cross,
    )
    a2_all = gather_both(a2, 0).reshape(groups, n_tokens, MODEL_WIDTH)

    partial = cross_forward(meta, a2_all, wq_full, kv, mp_parts)
    got = spread(partial.reshape(mp_parts, groups * chunk, STATW), "mp")
    (partial,) = local_call(combine_kernel, [((groups * chunk, STATW), BF16)], *got)
    got = spread(partial.reshape(groups, chunk, STATW), "pass")
    h_two, a3, o2, o2_blocks, lse = local_call(
        functools.partial(home_cross_out_kernel, groups),
        [
            (home, F32),
            (home, BF16),
            (home, F32),
            ((mp_parts, chunk, head_cols), BF16),
            ((chunk, LANES), F32),
        ],
        *got, h_one, wo_full, gain_ffn,
    )
    a3_all = gather_mp(a3, 1).reshape(n_tokens, MODEL_WIDTH)
    hidden = w_in.shape[1]
    term, ga3, gw_in, gw_out = local_call(
        ffn_kernel,
        [
            ((n_tokens, MODEL_WIDTH), BF16),
            ((n_tokens, MODEL_WIDTH), BF16),
            ((hidden, MODEL_WIDTH), BF16),
            ((hidden, MODEL_WIDTH), BF16),
        ],
        a3_all, w_in, w_out, out_grad,
    )
    ffn_grads = lax.psum(jnp.concatenate([gw_in, gw_out], axis=0), ("dp", "pass"))
    got = spread(ga3.reshape(mp_parts, chunk, MODEL_WIDTH), "mp")
    gh_two, gc, gain_ffn_grad = local_call(
        functools.partial(home_ffn_back_kernel, mp_parts),
        [(home, F32), ((chunk, STATW), BF16), ((1, MODEL_WIDTH), F32)],
        *got, gy_home, h_two, gain_ffn, wo_full, o2, lse,
    )
    gc_all = gather_both(gc, 2).reshape(groups, n_tokens, STATW)
    got = spread(term.reshape(mp_parts, chunk, MODEL_WIDTH), "mp")
    (out_home,) = local_call(add_kernel, [(home, BF16)], *got, h_two)
    output = gather_mp(out_home, 3).reshape(n_tokens, MODEL_WIDTH)

    gq, gkv = cross_backward(meta, a2_all, gc_all, wq_full, wo_full, kv, mp_parts)
    got = spread(gq.reshape(mp_parts, groups * chunk, MODEL_WIDTH), "mp")
    (gq,) = local_call(add_kernel, [((groups * chunk, MODEL_WIDTH), BF16)], *got)
    got = spread(gq.reshape(groups, chunk, MODEL_WIDTH), "pass")
    gh_one, gsa, gq_blocks, gain_cross_grad = local_call(
        functools.partial(home_query_back_kernel, groups),
        [
            (home, F32),
            (home, BF16),
            ((mp_parts, chunk, head_cols), BF16),
            ((1, MODEL_WIDTH), F32),
        ],
        *got, gh_two, h_one, gain_cross, wq_full,
    )
    gsa_all = gather_mp(gsa, 4).reshape(n_tokens, MODEL_WIDTH)

    gradient_of_encoded = (
        dot_nn(gkv, wkv).astype(BF16).reshape(GROUP_ROWS, quarter, MODEL_WIDTH)
    )
    gw_kv = dot_tn(gkv, flat_encoded).astype(BF16).reshape(2, mp_parts, head_cols, MODEL_WIDTH)
    got = spread(jnp.swapaxes(gw_kv, 0, 1), "mp")
    gw_kv = functools.reduce(jnp.add, [x.astype(F32) for x in got])
    o2_own = in_order(spread(o2_blocks, "mp"), "mp").reshape(n_tokens, head_cols)
    gq_own = in_order(spread(gq_blocks, "mp"), "mp").reshape(n_tokens, head_cols)
    gc_own = lax.dynamic_index_in_dim(gc_all, pass_at, 0, False)[:, :MODEL_WIDTH]
    a2_own = lax.dynamic_index_in_dim(a2_all, pass_at, 0, False)
    gw_o = dot_tn(o2_own, gc_own)
    gw_q = dot_tn(gq_own, a2_own)

    ga1, gw_self, scores, _ = local_call(
        functools.partial(self_backward_kernel, heads),
        [
            ((n_tokens, MODEL_WIDTH), BF16),
            ((4, head_cols, MODEL_WIDTH), F32),
            ((heads, chunk, chunk), F32),
            ((3, n_tokens, head_cols), BF16),
        ],
        gsa_all, wq_self, wk_self, wv_self, wo_self, a1, qkv, p1, o1,
    )
    got = spread(ga1.reshape(mp_parts, chunk, MODEL_WIDTH), "mp")
    grad_home, gain_self_grad = local_call(
        functools.partial(home_last_kernel, mp_parts),
        [(home, BF16), ((1, MODEL_WIDTH), F32)],
        *got, tokens_home, gain_self, gh_one,
    )
    grad_tokens = gather_mp(grad_home, 5).reshape(n_tokens, MODEL_WIDTH)

    scores = jnp.sum(
        scores.reshape(heads, block_questions, ANS, block_questions, ANS), axis=(1, 3)
    )
    bias_grad = jnp.einsum("hij,ijb->bh", scores, table, precision=lax.Precision.HIGHEST)
    rest = jnp.concatenate([gw_self, gw_kv, gw_q[None], gw_o[None]], axis=0).astype(BF16)
    rest = lax.psum(rest, ("dp", "pass")).astype(F32)
    bias_grad = lax.psum(bias_grad, ("dp", "pass"))
    gains = lax.psum(
        jnp.concatenate([gain_self_grad, gain_cross_grad, gain_ffn_grad], axis=0),
        ("dp", "pass", "mp"),
    )
    ffn_grads = ffn_grads.astype(F32)
    return (
        output,
        grad_tokens,
        gradient_of_encoded,
        gains[0],
        gains[1],
        gains[2],
        bias_grad,
        rest[0].T,
        rest[1].T,
        rest[2].T,
        rest[3],
        rest[6].T,
        rest[4].T,
        rest[5].T,
        rest[7],
        ffn_grads[:hidden].T,
        ffn_grads[hidden:],
    )


def solution(mesh):
    tokens_in = P(("dp", "pass"), None)
    encoded_in = P(("dp", "pass"), "mp", None)
    by_column, by_row = P(None, "mp"), P("mp", None)
    weights = (by_column, by_column, by_column, by_row)
    return jax.shard_map(
        on_device,
        mesh=mesh,
        in_specs=(
            tokens_in, encoded_in, P("dp", None), P("dp", None), P(("dp", "pass")),
            P(), P(), P(), by_column,
            *weights, *weights, by_column, by_row, tokens_in,
        ),
        out_specs=(
            tokens_in, tokens_in, encoded_in, P(), P(), P(), by_column,
            *weights, *weights, by_column, by_row,
        ),
        check_vma=False,
    )
```

```python
import functools
import math

import jax
import jax.numpy as jnp
import numpy as np
from jax import lax
from jax.experimental import pallas as pl
from jax.experimental.pallas import tpu as pltpu
from jax.sharding import PartitionSpec as P

MODEL_WIDTH = 768
HD = 64
BUCKETS = 32
ANS = 20
PADT = 24
LANES = 128
STATW = MODEL_WIDTH + LANES
QUAD = 4
QW = QUAD * HD
GROUP_ROWS = 32

EPSILON = 1e-06
NEGATIVE = -1e30
MESH = pl.DeviceIdType.MESH
VMEM_LIMIT = 56 << 20
F32 = jnp.float32
BF16 = jnp.bfloat16


def bucket_table(length, buckets):
    exact_half = buckets // 2
    result = np.zeros((length, length), np.int32)
    for target in range(length):
        for source in range(length):
            distance = max(target - source, 0)
            if distance < exact_half:
                result[target, source] = distance
            else:
                spread = int(
                    math.log(distance / exact_half)
                    / math.log(128 / exact_half)
                    * (buckets - exact_half)
                )
                result[target, source] = min(exact_half + spread, buckets - 1)
    return result


def dot_nn(a, b):
    return lax.dot_general(a, b, (((1,), (0,)), ((), ())), preferred_element_type=F32)


def dot_nt(a, b):
    return lax.dot_general(a, b, (((1,), (1,)), ((), ())), preferred_element_type=F32)


def dot_tn(a, b):
    return lax.dot_general(a, b, (((0,), (0,)), ((), ())), preferred_element_type=F32)


def rms_inverse(v):
    return lax.rsqrt(jnp.mean(v * v, axis=-1, keepdims=True) + EPSILON)


def rms_back(v, gains, ga):
    w = rms_inverse(v)
    gain_grad = jnp.sum(ga * v * w, axis=0, keepdims=True)
    gg = gains * ga
    gv = w * gg - v * (w * w * w) * jnp.mean(gg * v, axis=-1, keepdims=True)
    return gv, gain_grad


def local_call(kernel, outs, *ins, scratch=(), flops=0):
    return pl.pallas_call(
        kernel,
        out_shape=[jax.ShapeDtypeStruct(shape, dtype) for shape, dtype in outs],
        in_specs=[pl.BlockSpec(memory_space=pltpu.VMEM) for _ in ins],
        out_specs=[pl.BlockSpec(memory_space=pltpu.VMEM) for _ in outs],
        scratch_shapes=list(scratch),
        compiler_params=pltpu.CompilerParams(vmem_limit_bytes=VMEM_LIMIT),
        cost_estimate=pl.CostEstimate(
            flops=flops,
            bytes_accessed=sum(math.prod(x.shape) * x.dtype.itemsize for x in ins),
            transcendentals=0,
        ),
    )(*ins)


def place(**kw):
    return tuple(kw[a] if a in kw else lax.axis_index(a) for a in ("dp", "pass", "mp"))


def other(axis, k):
    n = lax.axis_size(axis)
    at = lax.rem(lax.axis_index(axis) + k, n)
    return at, place(**{axis: at})


def others(axis):
    return [(k - 1, *other(axis, k)) for k in range(1, lax.axis_size(axis))]


def greet(axes):
    barrier = pltpu.get_barrier_semaphore()
    peers = [peer for axis in axes for _, _, peer in others(axis)]
    for peer in peers:
        pl.semaphore_signal(barrier, inc=1, device_id=peer, device_id_type=MESH)
    pl.semaphore_wait(barrier, len(peers))


def remote(src, dst, send, recv, peer):
    return pltpu.make_async_remote_copy(
        src_ref=src, dst_ref=dst, send_sem=send, recv_sem=recv, device_id=peer, device_id_type=MESH
    )


def begin(copies):
    for copy in copies:
        copy.start()
    return copies


def finish(copies):
    for copy in copies:
        copy.wait()


def deal(source, slots, sems, axis):
    return begin([
        remote(source(at), slots.at[k], sems.at[0, k], sems.at[1, k], peer)
        for k, at, peer in others(axis)
    ])


def share(ref, sems, axis):
    return begin([remote(ref, ref, sems.at[0, k], sems.at[1, k], peer) for k, _, peer in others(axis)])


def share_both(all_ref, zsems, msems):
    pn, pm, mm = lax.axis_size("pass"), lax.axis_index("pass"), lax.axis_index("mp")
    zcopies = share(all_ref.at[pm, mm], zsems, "pass")
    mcopies = share(all_ref.at[pm, mm], msems.at[0], "mp")

    def forward(j):
        zcopies[j].wait_recv()
        source = lax.rem(pm - (j + 1) + pn, pn)
        mcopies.extend(share(all_ref.at[source, mm], msems.at[j + 1], "mp"))

    def end():
        finish(mcopies)
        for copy in zcopies:
            copy.wait_send()

    return forward, end


def pair_sems(n):
    return pltpu.SemaphoreType.DMA((2, n))


def many_sems(m, n):
    return pltpu.SemaphoreType.DMA((m, 2, n))


def remote_call(kernel, collective_id, outs, *ins, spaces=None, out_spaces=None, scratch=()):
    vmem = pltpu.VMEM
    spaces = spaces or {}
    out_spaces = out_spaces or {}
    return pl.pallas_call(
        kernel,
        out_shape=[jax.ShapeDtypeStruct(shape, dtype) for shape, dtype in outs],
        in_specs=[pl.BlockSpec(memory_space=spaces.get(i, vmem)) for i in range(len(ins))],
        out_specs=[pl.BlockSpec(memory_space=out_spaces.get(i, vmem)) for i in range(len(outs))],
        scratch_shapes=list(scratch),
        compiler_params=pltpu.CompilerParams(
            collective_id=collective_id, has_side_effects=True, vmem_limit_bytes=VMEM_LIMIT
        ),
    )(*ins)


def home_rows(ref, chunk):
    at = pl.multiple_of(lax.axis_index("mp") * chunk, 16)
    return ref[pl.ds(at, chunk), :]


def total_of(first, slots):
    total = first.astype(F32)
    for k in range(slots.shape[0]):
        total = total + slots[k].astype(F32)
    return total


def bucket_grid(size):
    row = lax.broadcasted_iota(jnp.int32, (size, size), 0)
    col = lax.broadcasted_iota(jnp.int32, (size, size), 1)
    near = (col <= row) & (lax.div(col, ANS) == lax.div(row, ANS))
    table = bucket_table(ANS, BUCKETS)
    grid = jnp.full((size, size), -1, jnp.int32)
    for distance in range(ANS):
        grid = jnp.where(near & (row - col == distance), int(table[distance, 0]), grid)
    return grid, near, sorted({int(b) for b in table.reshape(-1)})


def self_forward(
    heads, x_ref, gain_ref, wq_ref, wk_ref, wv_ref, wo_ref, bias_ref, lens_ref,
    a1_ref, qkv_ref, p_ref, o1_ref, term_ref,
):
    x = x_ref[...].astype(F32)
    a1 = (x * rms_inverse(x) * gain_ref[0:1, :]).astype(BF16)
    a1_ref[...] = a1
    for k, w_ref in enumerate((wq_ref, wk_ref, wv_ref)):
        qkv_ref[k] = dot_nt(a1, w_ref[...]).astype(BF16)
    blocks, size = term_ref.shape[0], term_ref.shape[1]
    grid, near, used = bucket_grid(size)
    biases = []
    for h in range(heads):
        bias = jnp.full((size, size), NEGATIVE, F32)
        for b in used:
            bias = jnp.where(grid == b, bias_ref[h, b], bias)
        biases.append(bias)
    lane = lax.broadcasted_iota(jnp.int32, (1, size), 1)
    for b in range(blocks):
        alive = jnp.zeros((1, size), jnp.int32)
        for q in range(size // ANS):
            inside = (lane >= q * ANS) & (lane < q * ANS + lens_ref[b * (size // ANS) + q])
            alive = jnp.where(inside, 1, alive)
        allowed = near & (alive > 0)
        rows = pl.ds(b * size, size)
        q, k, v = qkv_ref[0, rows, :], qkv_ref[1, rows, :], qkv_ref[2, rows, :]
        for h in range(heads):
            part = slice(h * HD, (h + 1) * HD)
            s = jnp.where(allowed, dot_nt(q[:, part], k[:, part]) + biases[h], NEGATIVE)
            e = jnp.exp(s - jnp.max(s, axis=-1, keepdims=True))
            p = e / jnp.sum(e, axis=-1, keepdims=True)
            p_ref[b * heads + h] = p
            o1_ref[rows, part] = dot_nn(p.astype(BF16), v[:, part]).astype(BF16)
    for b in range(blocks):
        term_ref[b] = dot_nn(o1_ref[pl.ds(b * size, size), :], wo_ref[...]).astype(BF16)


KV_STEPS = 8


def front_kernel(
    heads, x_ref, gain_ref, wq_ref, wk_ref, wv_ref, wo_ref, bias_ref, lens_ref,
    wkc_ref, wvc_ref, wqc_ref, woc_ref, enc_ref,
    a2_ref, h_ref, a1_ref, qkv_ref, p_ref, o1_ref, wkv_ref, wq_out_ref, wo_out_ref, kv_ref,
    term, slots, enc, kv_slots, wsems, dsems, rsems, zsems, msems, own_sems, enc_sem, kv_sems,
):
    core, mm, pm = lax.axis_index("dp"), lax.axis_index("mp"), lax.axis_index("pass")
    mn, pn = lax.axis_size("mp"), lax.axis_size("pass")
    width = wkc_ref.shape[0]
    half = width // 2
    chunk = h_ref.shape[0]
    load = pltpu.make_async_copy(enc_ref, enc, enc_sem)
    load.start()
    pieces = [
        (wkc_ref, wkv_ref.at[0]), (wvc_ref, wkv_ref.at[1]), (wqc_ref, wq_out_ref), (woc_ref, wo_out_ref)
    ]

    def rows_of(source, which):
        return pl.ds(pl.multiple_of(source * width + which * half, 16), half)

    mine = pl.ds(pl.multiple_of(core * half, 16), half)
    owns = []
    for i, (shard, full) in enumerate(pieces):
        at = pl.ds(pl.multiple_of(mm * width, 16), width)
        own = pltpu.make_async_copy(shard, full.at[at], own_sems.at[i])
        own.start()
        owns.append(own)
    greet(("dp", "pass", "mp"))

    def send_weight(i):
        shard, full = pieces[i]
        return begin([
            remote(shard.at[mine], full.at[rows_of(mm, core)], wsems.at[i, 0, k], wsems.at[i, 1, k], peer)
            for k, _, peer in others("mp")
        ])

    def pass_weight(i, copies):
        full = pieces[i][1]
        out = []
        for k, copy in enumerate(copies):
            copy.wait_recv()
            at = rows_of(lax.rem(mm - (k + 1) + mn, mn), core)
            out.append(
                remote(full.at[at], full.at[at], dsems.at[i, 0, k], dsems.at[i, 1, k], other("dp", 1)[1])
            )
        return begin(out)

    sent = [send_weight(0), send_weight(1)]
    self_forward(
        heads, x_ref, gain_ref, wq_ref, wk_ref, wv_ref, wo_ref, bias_ref, lens_ref,
        a1_ref, qkv_ref, p_ref, o1_ref, term,
    )
    dealt = deal(lambda at: term.at[at], slots, rsems, "mp")
    passed = [pass_weight(i, sent[i]) for i in range(2)]
    for copy in dealt:
        copy.wait_recv()
    h = home_rows(x_ref, chunk).astype(F32) + total_of(term[mm], slots)
    h_ref[...] = h
    a2_ref[pm, mm] = (h * rms_inverse(h) * gain_ref[1:2, :]).astype(BF16)
    forward, end = share_both(a2_ref, zsems, msems)
    sent += [send_weight(2), send_weight(3)]
    for copies in passed:
        for copy in copies:
            copy.wait_recv()
    for own in owns:
        own.wait()
    load.wait()
    rows = enc.shape[0] // KV_STEPS

    def store(step):
        slot = lax.rem(step, 2)
        at = pl.ds(pl.multiple_of(step * rows, rows), rows)
        return pltpu.make_async_copy(kv_slots.at[slot], kv_ref.at[at], kv_sems.at[slot])

    def project(step, carry):
        slot = lax.rem(step, 2)

        @pl.when(step >= 2)
        def _():
            store(step - 2).wait()

        x = enc[pl.ds(pl.multiple_of(step * rows, rows), rows), :]
        for i in range(2):
            kv_slots[slot, :, i * MODEL_WIDTH : (i + 1) * MODEL_WIDTH] = dot_nt(x, wkv_ref[i]).astype(BF16)
        store(step).start()
        return carry

    done = 0
    for j in range(pn - 1):
        upto = KV_STEPS * (j + 1) // (pn - 1)
        if upto > done:
            lax.fori_loop(done, upto, project, 0)
            done = upto
        forward(j)
    for i in range(2, 4):
        passed.append(pass_weight(i, sent[i]))
    for step in (KV_STEPS - 2, KV_STEPS - 1):
        store(step).wait()
    end()
    for copy in dealt:
        copy.wait_send()
    for copies in sent:
        for copy in copies:
            copy.wait_send()
    for i, copies in enumerate(passed):
        for copy in copies:
            copy.wait_send()
            if i >= 2:
                copy.wait_recv()


def head_lanes():
    lane = lax.broadcasted_iota(jnp.int32, (QUAD, 1, QW), 2)
    return lax.div(lane, HD) == lax.broadcasted_iota(jnp.int32, (QUAD, 1, QW), 0)


def pad_questions(dst_ref, values):
    questions = dst_ref.shape[0]
    for q in range(questions):
        dst_ref[q, 0:ANS, :] = values[q * ANS : (q + 1) * ANS, :]
        dst_ref[q, ANS:PADT, :] = jnp.zeros((PADT - ANS, values.shape[1]), F32)


def masked_heads(ref, owners, cols, lanes):
    parts = []
    for q in owners:
        parts.append(jnp.where(lanes, ref[q, :, cols][None], 0.0))
    return jnp.concatenate(parts, axis=0).reshape(2 * QUAD * PADT, QW).astype(BF16)


def fold_heads(x, lanes):
    y = x.reshape(2, QUAD, PADT, QW)
    return jnp.sum(jnp.where(lanes[None], y, 0.0), axis=1)


def segment_mask(meta_ref, row, keys):
    lane = lax.broadcasted_iota(jnp.int32, (1, keys), 1)
    parts = []
    for s in range(2):
        first, last = meta_ref[row, 2 + 2 * s], meta_ref[row, 3 + 2 * s]
        parts.append(((lane >= first) & (lane < last)).astype(F32)[None])
    mask = jnp.concatenate(parts, axis=0)
    mask = jnp.broadcast_to(mask, (2, QUAD * PADT, keys)).reshape(2 * QUAD * PADT, keys)
    return mask > 0.5


def split_three(x):
    hi = x.astype(BF16).astype(F32)
    mid = (x - hi).astype(BF16).astype(F32)
    return hi, mid, x - hi - mid


def cross_forward_kernel(
    rows_per, keys, meta_ref, a2_ref, wq_ref, kv_ref, out_ref, q_pad, o_acc, m_acc, l_acc, flat
):
    g = pl.program_id(0)
    q2 = dot_nt(a2_ref[0], wq_ref[...]).astype(BF16).astype(F32)
    pad_questions(q_pad, q2)
    o_acc[...] = jnp.zeros_like(o_acc)
    m_acc[...] = jnp.full_like(m_acc, NEGATIVE)
    l_acc[...] = jnp.zeros_like(l_acc)
    lanes = head_lanes()
    quads = MODEL_WIDTH // QW

    def one_row(r, carry):
        row = g * rows_per + r
        owners = [meta_ref[row, 0], meta_ref[row, 1]]
        at = pl.ds(pl.multiple_of(r * keys, keys), keys)
        mask = segment_mask(meta_ref, row, keys)
        for c in range(quads):
            cols = slice(c * QW, (c + 1) * QW)
            k = kv_ref[at, c * QW : (c + 1) * QW]
            v = kv_ref[at, MODEL_WIDTH + c * QW : MODEL_WIDTH + (c + 1) * QW]
            qm = masked_heads(q_pad, owners, cols, lanes)
            s = jnp.where(mask, dot_nt(qm, k), NEGATIVE)
            top = jnp.max(s, axis=-1, keepdims=True)
            p = jnp.where(mask, jnp.exp(s - top), 0.0)
            o = fold_heads(dot_nn(p.astype(BF16), v), lanes)
            total = jnp.sum(p, axis=-1, keepdims=True)
            m_new = fold_heads(jnp.broadcast_to(top, (2 * QUAD * PADT, QW)), lanes)
            l_new = fold_heads(jnp.broadcast_to(total, (2 * QUAD * PADT, QW)), lanes)
            for s_at, q in enumerate(owners):
                m_old = m_acc[q, :, cols]
                m_both = jnp.maximum(m_old, m_new[s_at])
                a, b = jnp.exp(m_old - m_both), jnp.exp(m_new[s_at] - m_both)
                o_acc[q, :, cols] = a * o_acc[q, :, cols] + b * o[s_at]
                l_acc[q, :, cols] = a * l_acc[q, :, cols] + b * l_new[s_at]
                m_acc[q, :, cols] = m_both
        return carry

    lax.fori_loop(0, rows_per, one_row, 0)
    questions = q_pad.shape[0]
    pick_row = lax.broadcasted_iota(jnp.int32, (MODEL_WIDTH, LANES), 0)
    pick_col = lax.broadcasted_iota(jnp.int32, (MODEL_WIDTH, LANES), 1)
    pick = (pick_row == pick_col * HD).astype(F32)
    for q in range(questions):
        l = l_acc[q]
        some = l > 0.0
        safe = jnp.where(some, l, 1.0)
        o = o_acc[q] / safe
        lse = jnp.where(some, m_acc[q] + jnp.log(safe), NEGATIVE)
        lse = lax.dot_general(
            lse, pick, (((1,), (0,)), ((), ())),
            preferred_element_type=F32, precision=lax.Precision.HIGHEST,
        )
        hi, mid, low = split_three(lse)
        stat = hi + pltpu.roll(mid, 16, 1) + pltpu.roll(low, 32, 1)
        flat[q * ANS : (q + 1) * ANS, :MODEL_WIDTH] = o[:ANS]
        flat[q * ANS : (q + 1) * ANS, MODEL_WIDTH:] = stat[:ANS]
    chunk = out_ref.shape[2]
    for m in range(out_ref.shape[0]):
        out_ref[m, 0] = flat[m * chunk : (m + 1) * chunk, :].astype(BF16)


def cross_forward(meta, a2_all, wq, kv, mp_parts):
    groups, n_tokens, _ = a2_all.shape
    rows_per = GROUP_ROWS // groups
    keys = kv.shape[0] // GROUP_ROWS
    questions = n_tokens // ANS
    block = rows_per * keys
    padded = pltpu.VMEM((questions, PADT, MODEL_WIDTH), F32)
    return pl.pallas_call(
        functools.partial(cross_forward_kernel, rows_per, keys),
        grid_spec=pltpu.PrefetchScalarGridSpec(
            num_scalar_prefetch=1,
            grid=(groups,),
            in_specs=[
                pl.BlockSpec((1, n_tokens, MODEL_WIDTH), lambda g, meta: (g, 0, 0)),
                pl.BlockSpec((MODEL_WIDTH, MODEL_WIDTH), lambda g, meta: (0, 0)),
                pl.BlockSpec((block, 2 * MODEL_WIDTH), lambda g, meta: (g, 0)),
            ],
            out_specs=pl.BlockSpec(
                (mp_parts, 1, n_tokens // mp_parts, STATW), lambda g, meta: (0, g, 0, 0)
            ),
            scratch_shapes=[padded, padded, padded, padded, pltpu.VMEM((n_tokens, STATW), F32)],
        ),
        out_shape=jax.ShapeDtypeStruct((mp_parts, groups, n_tokens // mp_parts, STATW), BF16),
        compiler_params=pltpu.CompilerParams(vmem_limit_bytes=VMEM_LIMIT),
    )(meta, a2_all, wq, kv)


def cross_backward_kernel(
    rows_per, keys, meta_ref, a2_ref, gc_ref, wq_ref, wo_ref, kv_ref, gq_ref, gkv_ref,
    q_pad, go_pad, gq_acc, lse_pad, delta_pad, flat,
):
    g = pl.program_id(0)
    pad_questions(q_pad, dot_nt(a2_ref[0], wq_ref[...]).astype(BF16).astype(F32))
    pad_questions(go_pad, dot_nt(gc_ref[0, :, :MODEL_WIDTH], wo_ref[...]).astype(BF16).astype(F32))
    stat = gc_ref[0, :, MODEL_WIDTH:].astype(F32)
    lse = stat + pltpu.roll(stat, LANES - 16, 1) + pltpu.roll(stat, LANES - 32, 1)
    pad_questions(lse_pad, lse)
    pad_questions(delta_pad, pltpu.roll(lse, LANES - 48, 1))
    gq_acc[...] = jnp.zeros_like(gq_acc)
    lanes = head_lanes()
    quads = MODEL_WIDTH // QW

    def columns(ref, owners, c):
        parts = []
        for q in owners:
            for h in range(QUAD):
                at = c * QUAD + h
                parts.append(ref[q, :, at : at + 1])
        return jnp.concatenate(parts, axis=0)

    def one_row(r, carry):
        row = g * rows_per + r
        owners = [meta_ref[row, 0], meta_ref[row, 1]]
        at = pl.ds(pl.multiple_of(r * keys, keys), keys)
        mask = segment_mask(meta_ref, row, keys)
        for c in range(quads):
            cols = slice(c * QW, (c + 1) * QW)
            vcols = slice(MODEL_WIDTH + c * QW, MODEL_WIDTH + (c + 1) * QW)
            k, v = kv_ref[at, cols], kv_ref[at, vcols]
            qm = masked_heads(q_pad, owners, cols, lanes)
            gom = masked_heads(go_pad, owners, cols, lanes)
            s = dot_nt(qm, k) - columns(lse_pad, owners, c)
            p = jnp.exp(jnp.where(mask, s, NEGATIVE))
            gp = dot_nt(gom, v) - columns(delta_pad, owners, c)
            gs = (p * gp).astype(BF16)
            gq = fold_heads(dot_nn(gs, k), lanes)
            for s_at, q in enumerate(owners):
                gq_acc[q, :, cols] = gq_acc[q, :, cols] + gq[s_at]
            gkv_ref[at, cols] = dot_tn(gs, qm).astype(BF16)
            gkv_ref[at, vcols] = dot_tn(p.astype(BF16), gom).astype(BF16)
        return carry

    lax.fori_loop(0, rows_per, one_row, 0)
    for q in range(q_pad.shape[0]):
        flat[q * ANS : (q + 1) * ANS, :] = gq_acc[q, :ANS, :]
    chunk = gq_ref.shape[2]
    for m in range(gq_ref.shape[0]):
        gq_ref[m, 0] = flat[m * chunk : (m + 1) * chunk, :].astype(BF16)


def cross_backward(meta, a2_all, gc_all, wq, wo, kv, mp_parts):
    groups, n_tokens, _ = a2_all.shape
    rows_per = GROUP_ROWS // groups
    keys = kv.shape[0] // GROUP_ROWS
    questions = n_tokens // ANS
    block = rows_per * keys
    padded = pltpu.VMEM((questions, PADT, MODEL_WIDTH), F32)
    small = pltpu.VMEM((questions, PADT, LANES), F32)
    whole = pl.BlockSpec((MODEL_WIDTH, MODEL_WIDTH), lambda g, meta: (0, 0))
    return pl.pallas_call(
        functools.partial(cross_backward_kernel, rows_per, keys),
        grid_spec=pltpu.PrefetchScalarGridSpec(
            num_scalar_prefetch=1,
            grid=(groups,),
            in_specs=[
                pl.BlockSpec((1, n_tokens, MODEL_WIDTH), lambda g, meta: (g, 0, 0)),
                pl.BlockSpec((1, n_tokens, STATW), lambda g, meta: (g, 0, 0)),
                whole,
                whole,
                pl.BlockSpec((block, 2 * MODEL_WIDTH), lambda g, meta: (g, 0)),
            ],
            out_specs=[
                pl.BlockSpec(
                    (mp_parts, 1, n_tokens // mp_parts, MODEL_WIDTH), lambda g, meta: (0, g, 0, 0)
                ),
                pl.BlockSpec((block, 2 * MODEL_WIDTH), lambda g, meta: (g, 0)),
            ],
            scratch_shapes=[
                padded, padded, padded, small, small, pltpu.VMEM((n_tokens, MODEL_WIDTH), F32)
            ],
        ),
        out_shape=[
            jax.ShapeDtypeStruct((mp_parts, groups, n_tokens // mp_parts, MODEL_WIDTH), BF16),
            jax.ShapeDtypeStruct(kv.shape, BF16),
        ],
        compiler_params=pltpu.CompilerParams(vmem_limit_bytes=VMEM_LIMIT),
    )(meta, a2_all, gc_all, wq, wo, kv)


def widen(w):
    row = lax.broadcasted_iota(jnp.int32, (LANES, MODEL_WIDTH), 0)
    col = lax.broadcasted_iota(jnp.int32, (LANES, MODEL_WIDTH), 1)
    each = (row == lax.div(col, HD)).astype(BF16)
    hi = w.astype(BF16)
    low = (w - hi.astype(F32)).astype(BF16)
    return dot_nn(hi, each) + dot_nn(low, each)


def combined(parts):
    lses = []
    for part in parts:
        stat = part[:, MODEL_WIDTH:].astype(F32)
        lses.append(stat + pltpu.roll(stat, LANES - 16, 1) + pltpu.roll(stat, LANES - 32, 1))
    top = functools.reduce(jnp.maximum, lses)
    weights = [jnp.exp(x - top) for x in lses]
    total = functools.reduce(jnp.add, weights)
    out = 0.0
    for part, weight in zip(parts, weights):
        out = out + widen(weight / total) * part[:, :MODEL_WIDTH].astype(F32)
    lane = lax.broadcasted_iota(jnp.int32, total.shape, 1)
    lse = jnp.where(lane < MODEL_WIDTH // HD, top + jnp.log(total), 0.0)
    return out, lse


def packed_stat(lse, at=0):
    hi, mid, low = split_three(lse)
    parts = [hi if at == 0 else pltpu.roll(hi, at, 1)]
    parts += [pltpu.roll(mid, at + 16, 1), pltpu.roll(low, at + 32, 1)]
    return parts[0] + parts[1] + parts[2]


def deal_groups(source, slots, sems):
    pn, pm = lax.axis_size("pass"), lax.axis_index("pass")
    for step in range(pn):
        group = lax.rem(pm + 1 + step, pn)
        deal(lambda at: source.at[at, group], slots.at[step], sems.at[step], "mp")


def groups_home(source, slots, held, zslots, msems, zsems, add):
    pn, pm, mm = lax.axis_size("pass"), lax.axis_index("pass"), lax.axis_index("mp")

    def arrived(step):
        group = lax.rem(pm + 1 + step, pn)
        for k, at, peer in others("mp"):
            remote(
                source.at[at, group], slots.at[step, k], msems.at[step, 0, k], msems.at[step, 1, k], peer
            ).wait()
        held[step] = add([source[mm, group]] + [slots[step, k] for k in range(slots.shape[1])])

    def to_home(step):
        at, peer = other("pass", step + 1)
        return remote(
            held.at[step], zslots.at[step], zsems.at[0, step], zsems.at[1, step], peer
        )

    def one(step, carry):
        arrived(step)
        to_home(step).start()
        return carry

    if pn <= 4:
        for step in range(pn - 1):
            one(step, 0)
    else:
        lax.fori_loop(0, pn - 1, one, 0)
    arrived(pn - 1)
    for step in range(pn - 1):
        to_home(step).wait()
    return [held[pn - 1]] + [zslots[k] for k in range(pn - 1)]


def cross_out_kernel(
    part_ref, h_ref, wo_ref, gain_ref, h2_ref, a3_ref, o_ref, own_ref, lse_ref,
    slots, held, zslots, blocks, msems, zsems, asems, bsems,
):
    mm = lax.axis_index("mp")
    greet(("pass", "mp"))
    deal_groups(part_ref, slots, msems)

    def add(parts):
        out, lse = combined(parts)
        return jnp.concatenate([out, packed_stat(lse)], axis=1).astype(BF16)

    o, lse = combined(groups_home(part_ref, slots, held, zslots, msems, zsems, add))
    low = o.astype(BF16)
    h = h_ref[...] + dot_nn(low, wo_ref[...])
    a3_ref[mm] = (h * rms_inverse(h) * gain_ref[2:3, :]).astype(BF16)
    copies = share(a3_ref.at[mm], asems, "mp")
    h2_ref[...] = h
    o_ref[...] = o
    lse_ref[...] = lse
    width = blocks.shape[2]
    for k in range(blocks.shape[0]):
        blocks[k] = low[:, k * width : (k + 1) * width]
    own_ref[mm] = blocks[mm]
    copies += begin([
        remote(blocks.at[at], own_ref.at[mm], bsems.at[0, k], bsems.at[1, k], peer)
        for k, at, peer in others("mp")
    ])
    finish(copies)


def ffn_back_kernel(
    ga_ref, gy_ref, h_ref, gain_ref, wo_ref, o_ref, lse_ref, gh_ref, gc_ref, gain_out_ref,
    slots, rsems, zsems, msems,
):
    mm, pm = lax.axis_index("mp"), lax.axis_index("pass")
    greet(("pass", "mp"))
    dealt = deal(lambda at: ga_ref.at[at], slots, rsems, "mp")
    finish(dealt)
    gv, gain_grad = rms_back(h_ref[...], gain_ref[2:3, :], total_of(ga_ref[mm], slots))
    gain_out_ref[...] = gain_grad
    gh = home_rows(gy_ref, h_ref.shape[0]).astype(F32) + gv
    gh_ref[...] = gh
    gc = gh.astype(BF16)
    go = dot_nt(gc, wo_ref[...]).astype(BF16).astype(F32)
    row = lax.broadcasted_iota(jnp.int32, (MODEL_WIDTH, LANES), 0)
    col = lax.broadcasted_iota(jnp.int32, (MODEL_WIDTH, LANES), 1)
    each = (lax.div(row, HD) == col).astype(F32)
    delta = lax.dot_general(
        go * o_ref[...], each, (((1,), (0,)), ((), ())),
        preferred_element_type=F32, precision=lax.Precision.HIGHEST,
    )
    stat = packed_stat(lse_ref[...]) + packed_stat(delta, 48)
    gc_ref[pm, mm] = jnp.concatenate([gc, stat.astype(BF16)], axis=1)
    forward, end = share_both(gc_ref, zsems, msems)
    for j in range(lax.axis_size("pass") - 1):
        forward(j)
    end()


def query_back_kernel(
    gq_ref, gh2_ref, h_ref, gain_ref, wq_ref, gh1_ref, gsa_ref, own_ref, gain_out_ref,
    slots, held, zslots, blocks, msems, zsems, asems, bsems,
):
    mm = lax.axis_index("mp")
    greet(("pass", "mp"))
    deal_groups(gq_ref, slots, msems)

    def add(parts):
        return functools.reduce(jnp.add, [part.astype(F32) for part in parts]).astype(BF16)

    parts = groups_home(gq_ref, slots, held, zslots, msems, zsems, add)
    low = add(parts)
    gv, gain_grad = rms_back(h_ref[...], gain_ref[1:2, :], dot_nn(low, wq_ref[...]))
    gh = gh2_ref[...] + gv
    gsa_ref[mm] = gh.astype(BF16)
    copies = share(gsa_ref.at[mm], asems, "mp")
    gain_out_ref[...] = gain_grad
    gh1_ref[...] = gh
    width = blocks.shape[2]
    for k in range(blocks.shape[0]):
        blocks[k] = low[:, k * width : (k + 1) * width]
    own_ref[mm] = blocks[mm]
    copies += begin([
        remote(blocks.at[at], own_ref.at[mm], bsems.at[0, k], bsems.at[1, k], peer)
        for k, at, peer in others("mp")
    ])
    finish(copies)


def self_backward_kernel(
    heads, gsa_ref, wq_ref, wk_ref, wv_ref, wo_ref, a1_ref, qkv_ref, p_ref, o1_ref,
    a2_ref, gq_ref, gc_ref, o2_ref, ga1_ref, gw_ref, bias_ref, gqkv_ref,
):
    gsa = gsa_ref[...]
    go1 = dot_nt(gsa, wo_ref[...]).astype(BF16)
    size = p_ref.shape[1]
    blocks = p_ref.shape[0] // heads
    grid, _, used = bucket_grid(size)
    at_row = lax.broadcasted_iota(jnp.int32, bias_ref.shape, 0)
    at_lane = lax.broadcasted_iota(jnp.int32, bias_ref.shape, 1)
    bias = jnp.zeros(bias_ref.shape, F32)
    for h in range(heads):
        part = slice(h * HD, (h + 1) * HD)
        total = jnp.zeros((size, size), F32)
        for b in range(blocks):
            rows = pl.ds(b * size, size)
            q, k, v = qkv_ref[0, rows, part], qkv_ref[1, rows, part], qkv_ref[2, rows, part]
            p = p_ref[b * heads + h]
            go = go1[b * size : (b + 1) * size, part]
            gp = dot_nt(go, v)
            gs = (p * (gp - jnp.sum(gp * p, axis=-1, keepdims=True))).astype(BF16)
            total = total + gs.astype(F32)
            gqkv_ref[0, rows, part] = dot_nn(gs, k).astype(BF16)
            gqkv_ref[1, rows, part] = dot_tn(gs, q).astype(BF16)
            gqkv_ref[2, rows, part] = dot_tn(p.astype(BF16), go).astype(BF16)
        for b in used:
            value = jnp.sum(jnp.where(grid == b, total, 0.0), keepdims=True)
            bias = jnp.where((at_row == h) & (at_lane == b), value, bias)
    bias_ref[...] = bias
    ga1 = dot_nn(gqkv_ref[0], wq_ref[...])
    ga1 = ga1 + dot_nn(gqkv_ref[1], wk_ref[...])
    ga1 = ga1 + dot_nn(gqkv_ref[2], wv_ref[...])
    ga1_ref[...] = ga1.astype(BF16)
    for k in range(3):
        gw_ref[k] = dot_tn(gqkv_ref[k], a1_ref[...]).astype(BF16)
    gw_ref[3] = dot_tn(o1_ref[...], gsa).astype(BF16)
    gw_ref[4] = dot_tn(gq_ref[...], a2_ref[...]).astype(BF16)
    gw_ref[5] = dot_tn(o2_ref[...], gc_ref[:, :MODEL_WIDTH]).astype(BF16)


def sum_rows(rows, groups):
    return -(-rows // (groups * 16)) * 16


class GroupSum:
    def __init__(self, y, zslots, out, zsems, asems, dsems):
        self.y, self.zslots, self.out = y, zslots, out
        self.zsems, self.asems, self.dsems = zsems, asems, dsems
        self.core, self.pm = lax.axis_index("dp"), lax.axis_index("pass")
        self.rows = zslots.shape[1]

    def part(self, at):
        return pl.ds(pl.multiple_of(at * self.rows, 16), self.rows)

    def spread(self):
        self.copies = deal(lambda at: self.y.at[self.part(at)], self.zslots, self.zsems, "pass")

    def gather(self):
        finish(self.copies)
        total = total_of(self.y[self.part(self.pm), :], self.zslots)
        self.out[self.core, self.part(self.pm), :] = total.astype(BF16)
        self.copies = share(self.out.at[self.core, self.part(self.pm)], self.asems, "pass")

    def swap(self):
        finish(self.copies)
        self.copies = share(self.out.at[self.core], self.dsems, "dp")

    def end(self):
        finish(self.copies)


def fill_tail(y, used):
    if y.shape[0] > used:
        y[used:, :] = jnp.zeros((y.shape[0] - used, y.shape[1]), y.dtype)


def last_kernel(
    ga_ref, term_ref, x_ref, gh_ref, h2_ref, gain_ref, gw_kv_ref, gw_ref, gains_ref, bias_ref,
    out_ref, gx_ref, sum_a_ref, sum_b_ref, small_ref,
    ga_slots, term_slots, kv_core, kv_half, kv_slots, core_slots, y_a, y_b, z_a, z_b,
    small, small_dp, small_z, small_m,
    ga_sems, term_sems, kv_dsems, kv_msems, core_sems, gx_sems, out_sems,
    za_sems, aa_sems, da_sems, zb_sems, ab_sems, db_sems, sd_sems, sz_sems, sm_sems,
):
    core, mm, pm = lax.axis_index("dp"), lax.axis_index("mp"), lax.axis_index("pass")
    chunk = gh_ref.shape[0]
    width = gw_ref.shape[1]
    half = width // 2
    mine = pl.ds(pl.multiple_of(core * half, 16), half)
    theirs = pl.ds(pl.multiple_of((1 - core) * half, 16), half)
    greet(("dp", "pass", "mp"))
    ga_copies = deal(lambda at: ga_ref.at[at], ga_slots, ga_sems, "mp")
    peer = other("dp", 1)[1]
    kv_copy = remote(gw_kv_ref.at[:, :, theirs], kv_core, kv_dsems.at[0], kv_dsems.at[1], peer)
    kv_copy.start()
    core_copy = remote(gw_ref.at[:, theirs], core_slots, core_sems.at[0], core_sems.at[1], peer)
    core_copy.start()
    core_copy.wait()
    for i in range(gw_ref.shape[0]):
        total = gw_ref[i, mine, :].astype(F32) + core_slots[i].astype(F32)
        y_a[i * half : (i + 1) * half, :] = total.astype(BF16)
    fill_tail(y_a, gw_ref.shape[0] * half)
    sum_a = GroupSum(y_a, z_a, sum_a_ref, za_sems, aa_sems, da_sems)
    sum_a.spread()
    finish(ga_copies)
    gv, gain_grad = rms_back(
        home_rows(x_ref, chunk).astype(F32), gain_ref[0:1, :], total_of(ga_ref[mm], ga_slots)
    )
    gx_ref[mm] = (gh_ref[...] + gv).astype(BF16)
    gx_copies = share(gx_ref.at[mm], gx_sems, "mp")
    small[...] = jnp.zeros_like(small)
    small[0:1, :] = gain_grad
    small[1:3, :] = gains_ref[...]
    small[8:16, :LANES] = bias_ref[...]
    sd = begin([remote(small, small_dp, sd_sems.at[0], sd_sems.at[1], peer)])
    kv_copy.wait()
    for i in range(2):
        for k in range(kv_half.shape[0]):
            total = gw_kv_ref[i, k, mine, :].astype(F32) + kv_core[i, k].astype(F32)
            kv_half[k, i] = total.astype(BF16)
    kv_copies = deal(lambda at: kv_half.at[at], kv_slots, kv_msems, "mp")
    term_copies = deal(lambda at: term_ref.at[at], term_slots, term_sems, "mp")
    finish(sd)
    small_z[pm] = small[...] + small_dp[...]
    sz = share(small_z.at[pm], sz_sems, "pass")
    finish(kv_copies)
    for i in range(2):
        total = kv_half[mm, i].astype(F32)
        for k in range(kv_slots.shape[0]):
            total = total + kv_slots[k, i].astype(F32)
        y_b[i * half : (i + 1) * half, :] = total.astype(BF16)
    fill_tail(y_b, 2 * half)
    sum_b = GroupSum(y_b, z_b, sum_b_ref, zb_sems, ab_sems, db_sems)
    sum_b.spread()
    finish(term_copies)
    out_ref[mm] = (h2_ref[...] + total_of(term_ref[mm], term_slots)).astype(BF16)
    out_copies = share(out_ref.at[mm], out_sems, "mp")
    finish(sz)
    total = small_z[0]
    for k in range(1, small_z.shape[0]):
        total = total + small_z[k]
    small_m[mm] = total
    sm = share(small_m.at[mm], sm_sems, "mp")
    sum_a.gather()
    sum_b.gather()
    finish(sm)
    gains = small_m[0]
    for k in range(1, small_m.shape[0]):
        gains = gains + small_m[k]
    small_ref[0:8, :] = gains[0:8]
    small_ref[8:16, :] = total[8:16]
    finish(gx_copies)
    finish(out_copies)
    sum_a.swap()
    sum_b.swap()
    sum_a.end()
    sum_b.end()


def ffn_kernel(a3_ref, w_in_ref, w_out_ref, gy_ref, term_ref, ga3_ref, gw_in_ref, gw_out_ref):
    a3, gy = a3_ref[...], gy_ref[...]
    u = dot_nn(a3, w_in_ref[...])
    cdf = 0.5 * (1.0 + lax.erf(u * np.float32(math.sqrt(0.5))))
    pdf = np.float32(1.0 / math.sqrt(2.0 * math.pi)) * jnp.exp(-0.5 * u * u)
    e = (u * cdf).astype(BF16)
    term_ref[...] = dot_nn(e, w_out_ref[...]).astype(BF16)
    ge = dot_nt(gy, w_out_ref[...]).astype(BF16).astype(F32)
    gu = (ge * (cdf + u * pdf)).astype(BF16)
    ga3_ref[...] = dot_nt(gu, w_in_ref[...]).astype(BF16)
    gw_in_ref[...] = dot_tn(a3, gu).astype(BF16)
    gw_out_ref[...] = dot_tn(e, gy).astype(BF16)


def on_device(
    tokens,
    encoded,
    seg_lens,
    owners,
    answer_lens,
    gain_self,
    gain_cross,
    gain_ffn,
    rel_bias,
    wq_self,
    wk_self,
    wv_self,
    wo_self,
    wq_cross,
    wk_cross,
    wv_cross,
    wo_cross,
    w_in,
    w_out,
    out_grad,
):
    groups, mp_parts = lax.axis_size("pass"), lax.axis_size("mp")
    pass_at, mp_at = lax.axis_index("pass"), lax.axis_index("mp")
    heads = rel_bias.shape[1]
    head_cols = heads * HD
    half = head_cols // 2
    quarter = encoded.shape[1]
    n_tokens = tokens.shape[0]
    chunk = n_tokens // mp_parts
    hidden = w_in.shape[1]
    keys = GROUP_ROWS * quarter
    near, far = mp_parts - 1, groups - 1
    gains = jnp.stack([gain_self, gain_cross, gain_ffn])

    lens_here = lax.dynamic_index_in_dim(
        seg_lens.reshape(groups, GROUP_ROWS, 2), pass_at, 0, keepdims=False
    )
    owners_here = lax.dynamic_index_in_dim(
        owners.reshape(groups, GROUP_ROWS, 2), pass_at, 0, keepdims=False
    )
    first = lens_here[:, :1] - mp_at * quarter
    last = first + lens_here[:, 1:]
    meta = jnp.concatenate([owners_here, jnp.zeros_like(first), first, first, last], axis=1)

    flat_encoded = encoded.reshape(keys, MODEL_WIDTH)
    home = (chunk, MODEL_WIDTH)
    dealt = (mp_parts, chunk, MODEL_WIDTH)
    square = (MODEL_WIDTH, MODEL_WIDTH)
    smem = pltpu.SMEM
    a2_all, h_one, a1, qkv, p1, o1, wkv, wq_full, wo_full, kv = remote_call(
        functools.partial(front_kernel, heads),
        0,
        [
            ((groups, *dealt), BF16),
            (home, F32),
            ((n_tokens, MODEL_WIDTH), BF16),
            ((3, n_tokens, head_cols), BF16),
            ((mp_parts * heads, chunk, chunk), F32),
            ((n_tokens, head_cols), BF16),
            ((2, *square), BF16),
            (square, BF16),
            (square, BF16),
            ((keys, 2 * MODEL_WIDTH), BF16),
        ],
        tokens, gains, wq_self.T, wk_self.T, wv_self.T, wo_self, rel_bias.T, answer_lens,
        wk_cross.T, wv_cross.T, wq_cross.T, wo_cross, flat_encoded,
        spaces={6: smem, 7: smem, 12: pl.ANY},
        out_spaces={9: pl.ANY},
        scratch=[
            pltpu.VMEM(dealt, BF16),
            pltpu.VMEM((near, *home), BF16),
            pltpu.VMEM((keys, MODEL_WIDTH), BF16),
            pltpu.VMEM((2, keys // KV_STEPS, 2 * MODEL_WIDTH), BF16),
            many_sems(4, near),
            many_sems(4, near),
            pair_sems(near),
            pair_sems(far),
            many_sems(groups, near),
            pltpu.SemaphoreType.DMA((4,)),
            pltpu.SemaphoreType.DMA,
            pltpu.SemaphoreType.DMA((2,)),
        ],
    )
    a2_all = a2_all.reshape(groups, n_tokens, MODEL_WIDTH)

    def home_scratch(width):
        return [
            pltpu.VMEM((groups, near, chunk, width), BF16),
            pltpu.VMEM((groups, chunk, width), BF16),
            pltpu.VMEM((far, chunk, width), BF16),
            pltpu.VMEM((mp_parts, chunk, head_cols), BF16),
            many_sems(groups, near),
            pair_sems(far),
            pair_sems(near),
            pair_sems(near),
        ]

    partial = cross_forward(meta, a2_all, wq_full, kv, mp_parts)
    h_two, a3, o2, o2_own, lse = remote_call(
        cross_out_kernel,
        1,
        [
            (home, F32),
            (dealt, BF16),
            (home, F32),
            ((mp_parts, chunk, head_cols), BF16),
            ((chunk, LANES), F32),
        ],
        partial, h_one, wo_full, gains,
        scratch=home_scratch(STATW),
    )
    term, ga3, gw_in, gw_out = local_call(
        ffn_kernel,
        [
            ((n_tokens, MODEL_WIDTH), BF16),
            ((n_tokens, MODEL_WIDTH), BF16),
            ((MODEL_WIDTH, hidden), BF16),
            ((hidden, MODEL_WIDTH), BF16),
        ],
        a3.reshape(n_tokens, MODEL_WIDTH), w_in, w_out, out_grad,
    )
    gw_in, gw_out = lax.psum((gw_in, gw_out), ("dp", "pass"))
    gh_two, gc_all, gain_ffn_grad = remote_call(
        ffn_back_kernel,
        2,
        [(home, F32), ((groups, mp_parts, chunk, STATW), BF16), ((1, MODEL_WIDTH), F32)],
        ga3.reshape(dealt), out_grad, h_two, gains, wo_full, o2, lse,
        scratch=[
            pltpu.VMEM((near, *home), BF16), pair_sems(near), pair_sems(far), many_sems(groups, near)
        ],
    )
    gc_all = gc_all.reshape(groups, n_tokens, STATW)

    gq, gkv = cross_backward(meta, a2_all, gc_all, wq_full, wo_full, kv, mp_parts)
    gh_one, gsa, gq_own, gain_cross_grad = remote_call(
        query_back_kernel,
        3,
        [
            (home, F32),
            (dealt, BF16),
            ((mp_parts, chunk, head_cols), BF16),
            ((1, MODEL_WIDTH), F32),
        ],
        gq, gh_two, h_one, gains, wq_full,
        scratch=home_scratch(MODEL_WIDTH),
    )
    gradient_of_encoded = (
        dot_nn(gkv, wkv.reshape(2 * MODEL_WIDTH, MODEL_WIDTH))
        .astype(BF16)
        .reshape(GROUP_ROWS, quarter, MODEL_WIDTH)
    )
    gw_kv = dot_tn(gkv, flat_encoded).astype(BF16).reshape(2, mp_parts, head_cols, MODEL_WIDTH)
    gc_own = lax.dynamic_index_in_dim(gc_all, pass_at, 0, False)
    a2_own = lax.dynamic_index_in_dim(a2_all, pass_at, 0, False)
    ga1, gw, bias_grad, _ = local_call(
        functools.partial(self_backward_kernel, heads),
        [
            ((n_tokens, MODEL_WIDTH), BF16),
            ((6, head_cols, MODEL_WIDTH), BF16),
            ((8, LANES), F32),
            ((3, n_tokens, head_cols), BF16),
        ],
        gsa.reshape(n_tokens, MODEL_WIDTH), wq_self.T, wk_self.T, wv_self.T, wo_self,
        a1, qkv, p1, o1, a2_own, gq_own.reshape(n_tokens, head_cols), gc_own,
        o2_own.reshape(n_tokens, head_cols),
    )

    rows_a, rows_b = sum_rows(6 * half, groups), sum_rows(2 * half, groups)
    small = pltpu.VMEM((16, MODEL_WIDTH), F32)
    output, grad_tokens, sum_a, sum_b, small_sums = remote_call(
        last_kernel,
        4,
        [
            (dealt, BF16),
            (dealt, BF16),
            ((2, groups * rows_a, MODEL_WIDTH), BF16),
            ((2, groups * rows_b, MODEL_WIDTH), BF16),
            ((16, MODEL_WIDTH), F32),
        ],
        ga1.reshape(dealt), term.reshape(dealt), tokens, gh_one, h_two, gains, gw_kv, gw,
        jnp.concatenate([gain_cross_grad, gain_ffn_grad], axis=0), bias_grad,
        scratch=[
            pltpu.VMEM((near, *home), BF16),
            pltpu.VMEM((near, *home), BF16),
            pltpu.VMEM((2, mp_parts, half, MODEL_WIDTH), BF16),
            pltpu.VMEM((mp_parts, 2, half, MODEL_WIDTH), BF16),
            pltpu.VMEM((near, 2, half, MODEL_WIDTH), BF16),
            pltpu.VMEM((6, half, MODEL_WIDTH), BF16),
            pltpu.VMEM((groups * rows_a, MODEL_WIDTH), BF16),
            pltpu.VMEM((groups * rows_b, MODEL_WIDTH), BF16),
            pltpu.VMEM((far, rows_a, MODEL_WIDTH), BF16),
            pltpu.VMEM((far, rows_b, MODEL_WIDTH), BF16),
            small,
            small,
            pltpu.VMEM((groups, 16, MODEL_WIDTH), F32),
            pltpu.VMEM((mp_parts, 16, MODEL_WIDTH), F32),
            pair_sems(near),
            pair_sems(near),
            pltpu.SemaphoreType.DMA((2,)),
            pair_sems(near),
            pltpu.SemaphoreType.DMA((2,)),
            pair_sems(near),
            pair_sems(near),
            pair_sems(far), pair_sems(far), pair_sems(1),
            pair_sems(far), pair_sems(far), pair_sems(1),
            pltpu.SemaphoreType.DMA((2,)),
            pair_sems(far),
            pair_sems(near),
        ],
    )
    sum_a = sum_a[:, : 6 * half].reshape(2, 6, half, MODEL_WIDTH)
    sum_b = sum_b[:, : 2 * half].reshape(2, 2, half, MODEL_WIDTH)

    def weight(sums, at):
        return sums[:, at].reshape(head_cols, MODEL_WIDTH).astype(F32)

    return (
        output.reshape(n_tokens, MODEL_WIDTH),
        grad_tokens.reshape(n_tokens, MODEL_WIDTH),
        gradient_of_encoded,
        small_sums[0],
        small_sums[1],
        small_sums[2],
        small_sums[8 : 8 + heads, :BUCKETS].T,
        weight(sum_a, 0).T,
        weight(sum_a, 1).T,
        weight(sum_a, 2).T,
        weight(sum_a, 3),
        weight(sum_a, 4).T,
        weight(sum_b, 0).T,
        weight(sum_b, 1).T,
        weight(sum_a, 5),
        gw_in.astype(F32),
        gw_out.astype(F32),
    )


def solution(mesh):
    tokens_in = P(("dp", "pass"), None)
    encoded_in = P(("dp", "pass"), "mp", None)
    by_column, by_row = P(None, "mp"), P("mp", None)
    weights = (by_column, by_column, by_column, by_row)
    return jax.shard_map(
        on_device,
        mesh=mesh,
        in_specs=(
            tokens_in, encoded_in, P("dp", None), P("dp", None), P(("dp", "pass")),
            P(), P(), P(), by_column,
            *weights, *weights, by_column, by_row, tokens_in,
        ),
        out_specs=(
            tokens_in, tokens_in, encoded_in, P(), P(), P(), by_column,
            *weights, *weights, by_column, by_row,
        ),
        check_vma=False,
    )
```

```python
import functools
import math

import jax
import jax.numpy as jnp
import numpy as np
from jax import lax
from jax.experimental import pallas as pl
from jax.experimental.pallas import tpu as pltpu
from jax.sharding import PartitionSpec as P

MODEL_WIDTH = 768
HD = 64
BUCKETS = 32
ANS = 20
PADT = 24
LANES = 128
STATW = MODEL_WIDTH + LANES
GROUP_ROWS = 32

EPSILON = 1e-06
NEGATIVE = -1e30
MESH = pl.DeviceIdType.MESH
VMEM_LIMIT = 60 << 20
F32 = jnp.float32
BF16 = jnp.bfloat16


def bucket_table(length, buckets):
    exact_half = buckets // 2
    result = np.zeros((length, length), np.int32)
    for target in range(length):
        for source in range(length):
            distance = max(target - source, 0)
            if distance < exact_half:
                result[target, source] = distance
            else:
                spread = int(
                    math.log(distance / exact_half)
                    / math.log(128 / exact_half)
                    * (buckets - exact_half)
                )
                result[target, source] = min(exact_half + spread, buckets - 1)
    return result


def dot_nn(a, b):
    return lax.dot_general(a, b, (((1,), (0,)), ((), ())), preferred_element_type=F32)


def dot_nt(a, b):
    return lax.dot_general(a, b, (((1,), (1,)), ((), ())), preferred_element_type=F32)


def dot_tn(a, b):
    return lax.dot_general(a, b, (((0,), (0,)), ((), ())), preferred_element_type=F32)


def rms_inverse(v):
    return lax.rsqrt(jnp.mean(v * v, axis=-1, keepdims=True) + EPSILON)


def rms_back(v, gains, ga):
    w = rms_inverse(v)
    gain_grad = jnp.sum(ga * v * w, axis=0, keepdims=True)
    gg = gains * ga
    gv = w * gg - v * (w * w * w) * jnp.mean(gg * v, axis=-1, keepdims=True)
    return gv, gain_grad


def local_call(kernel, outs, *ins, scratch=(), flops=0):
    return pl.pallas_call(
        kernel,
        out_shape=[jax.ShapeDtypeStruct(shape, dtype) for shape, dtype in outs],
        in_specs=[pl.BlockSpec(memory_space=pltpu.VMEM) for _ in ins],
        out_specs=[pl.BlockSpec(memory_space=pltpu.VMEM) for _ in outs],
        scratch_shapes=list(scratch),
        compiler_params=pltpu.CompilerParams(vmem_limit_bytes=VMEM_LIMIT),
        cost_estimate=pl.CostEstimate(
            flops=flops,
            bytes_accessed=sum(math.prod(x.shape) * x.dtype.itemsize for x in ins),
            transcendentals=0,
        ),
    )(*ins)


def place(**kw):
    return tuple(kw[a] if a in kw else lax.axis_index(a) for a in ("dp", "pass", "mp"))


def other(axis, k):
    n = lax.axis_size(axis)
    at = lax.rem(lax.axis_index(axis) + k, n)
    return at, place(**{axis: at})


def others(axis):
    return [(k - 1, *other(axis, k)) for k in range(1, lax.axis_size(axis))]


def greet(axes):
    barrier = pltpu.get_barrier_semaphore()
    peers = [peer for axis in axes for _, _, peer in others(axis)]
    for peer in peers:
        pl.semaphore_signal(barrier, inc=1, device_id=peer, device_id_type=MESH)
    pl.semaphore_wait(barrier, len(peers))


def remote(src, dst, send, recv, peer):
    return pltpu.make_async_remote_copy(
        src_ref=src, dst_ref=dst, send_sem=send, recv_sem=recv, device_id=peer, device_id_type=MESH
    )


def begin(copies):
    for copy in copies:
        copy.start()
    return copies


def finish(copies):
    for copy in copies:
        copy.wait()


def deal(source, slots, sems, axis):
    return begin([
        remote(source(at), slots.at[k], sems.at[0, k], sems.at[1, k], peer)
        for k, at, peer in others(axis)
    ])


def share(ref, sems, axis):
    return begin([remote(ref, ref, sems.at[0, k], sems.at[1, k], peer) for k, _, peer in others(axis)])


def share_both(all_ref, zsems, msems):
    pn, pm, mm = lax.axis_size("pass"), lax.axis_index("pass"), lax.axis_index("mp")
    zcopies = share(all_ref.at[pm, mm], zsems, "pass")
    mcopies = share(all_ref.at[pm, mm], msems.at[0], "mp")

    def forward(j):
        zcopies[j].wait_recv()
        source = lax.rem(pm - (j + 1) + pn, pn)
        mcopies.extend(share(all_ref.at[source, mm], msems.at[j + 1], "mp"))

    def end():
        finish(mcopies)
        for copy in zcopies:
            copy.wait_send()

    return forward, end


def pair_sems(n):
    return pltpu.SemaphoreType.DMA((2, n))


def many_sems(m, n):
    return pltpu.SemaphoreType.DMA((m, 2, n))


def remote_call(kernel, collective_id, outs, *ins, spaces=None, out_spaces=None, scratch=()):
    vmem = pltpu.VMEM
    spaces = spaces or {}
    out_spaces = out_spaces or {}
    return pl.pallas_call(
        kernel,
        out_shape=[jax.ShapeDtypeStruct(shape, dtype) for shape, dtype in outs],
        in_specs=[pl.BlockSpec(memory_space=spaces.get(i, vmem)) for i in range(len(ins))],
        out_specs=[pl.BlockSpec(memory_space=out_spaces.get(i, vmem)) for i in range(len(outs))],
        scratch_shapes=list(scratch),
        compiler_params=pltpu.CompilerParams(
            collective_id=collective_id, has_side_effects=True, vmem_limit_bytes=VMEM_LIMIT
        ),
    )(*ins)


def home_rows(ref, chunk):
    at = pl.multiple_of(lax.axis_index("mp") * chunk, 16)
    return ref[pl.ds(at, chunk), :]


def total_of(first, slots):
    total = first.astype(F32)
    for k in range(slots.shape[0]):
        total = total + slots[k].astype(F32)
    return total


def bucket_grid(size):
    row = lax.broadcasted_iota(jnp.int32, (size, size), 0)
    col = lax.broadcasted_iota(jnp.int32, (size, size), 1)
    near = (col <= row) & (lax.div(col, ANS) == lax.div(row, ANS))
    table = bucket_table(ANS, BUCKETS)
    grid = jnp.full((size, size), -1, jnp.int32)
    for distance in range(ANS):
        grid = jnp.where(near & (row - col == distance), int(table[distance, 0]), grid)
    return grid, near, sorted({int(b) for b in table.reshape(-1)})


def self_forward(
    heads, x_ref, gain_ref, wq_ref, wk_ref, wv_ref, wo_ref, bias_ref, lens_ref,
    a1_ref, qkv_ref, p_ref, o1_ref, term_ref,
):
    x = x_ref[...].astype(F32)
    a1 = (x * rms_inverse(x) * gain_ref[0:1, :]).astype(BF16)
    a1_ref[...] = a1
    for k, w_ref in enumerate((wq_ref, wk_ref, wv_ref)):
        qkv_ref[k] = dot_nt(a1, w_ref[...]).astype(BF16)
    blocks, size = term_ref.shape[0], term_ref.shape[1]
    grid, near, used = bucket_grid(size)
    biases = []
    for h in range(heads):
        bias = jnp.full((size, size), NEGATIVE, F32)
        for b in used:
            bias = jnp.where(grid == b, bias_ref[h, b], bias)
        biases.append(bias)
    lane = lax.broadcasted_iota(jnp.int32, (1, size), 1)
    for b in range(blocks):
        alive = jnp.zeros((1, size), jnp.int32)
        for q in range(size // ANS):
            inside = (lane >= q * ANS) & (lane < q * ANS + lens_ref[b * (size // ANS) + q])
            alive = jnp.where(inside, 1, alive)
        allowed = near & (alive > 0)
        rows = pl.ds(b * size, size)
        q, k, v = qkv_ref[0, rows, :], qkv_ref[1, rows, :], qkv_ref[2, rows, :]
        for h in range(heads):
            part = slice(h * HD, (h + 1) * HD)
            s = jnp.where(allowed, dot_nt(q[:, part], k[:, part]) + biases[h], NEGATIVE)
            e = jnp.exp(s - jnp.max(s, axis=-1, keepdims=True))
            p = e / jnp.sum(e, axis=-1, keepdims=True)
            p_ref[b * heads + h] = p
            o1_ref[rows, part] = dot_nn(p.astype(BF16), v[:, part]).astype(BF16)
    for b in range(blocks):
        term_ref[b] = dot_nn(o1_ref[pl.ds(b * size, size), :], wo_ref[...]).astype(BF16)


KV_STEPS = 8


def front_kernel(
    heads, x_ref, gain_ref, wq_ref, wk_ref, wv_ref, wo_ref, bias_ref, lens_ref,
    wkc_ref, wvc_ref, wqc_ref, woc_ref, enc_ref,
    a2_ref, h_ref, a1_ref, qkv_ref, p_ref, o1_ref, wkv_ref, wq_out_ref, wo_out_ref, kv_ref,
    term, slots, enc, kv_slots, wsems, dsems, rsems, zsems, msems, own_sems, enc_sem, kv_sems,
):
    core, mm, pm = lax.axis_index("dp"), lax.axis_index("mp"), lax.axis_index("pass")
    mn, pn = lax.axis_size("mp"), lax.axis_size("pass")
    width = wkc_ref.shape[0]
    half = width // 2
    chunk = h_ref.shape[0]
    load = pltpu.make_async_copy(enc_ref, enc, enc_sem)
    load.start()
    pieces = [
        (wkc_ref, wkv_ref.at[0]), (wvc_ref, wkv_ref.at[1]), (wqc_ref, wq_out_ref), (woc_ref, wo_out_ref)
    ]

    def rows_of(source, which):
        return pl.ds(pl.multiple_of(source * width + which * half, 16), half)

    mine = pl.ds(pl.multiple_of(core * half, 16), half)
    owns = []
    for i, (shard, full) in enumerate(pieces):
        at = pl.ds(pl.multiple_of(mm * width, 16), width)
        own = pltpu.make_async_copy(shard, full.at[at], own_sems.at[i])
        own.start()
        owns.append(own)
    greet(("dp", "pass", "mp"))

    def send_weight(i):
        shard, full = pieces[i]
        return begin([
            remote(shard.at[mine], full.at[rows_of(mm, core)], wsems.at[i, 0, k], wsems.at[i, 1, k], peer)
            for k, _, peer in others("mp")
        ])

    def pass_weight(i, copies):
        full = pieces[i][1]
        out = []
        for k, copy in enumerate(copies):
            copy.wait_recv()
            at = rows_of(lax.rem(mm - (k + 1) + mn, mn), core)
            out.append(
                remote(full.at[at], full.at[at], dsems.at[i, 0, k], dsems.at[i, 1, k], other("dp", 1)[1])
            )
        return begin(out)

    sent = [send_weight(0), send_weight(1)]
    self_forward(
        heads, x_ref, gain_ref, wq_ref, wk_ref, wv_ref, wo_ref, bias_ref, lens_ref,
        a1_ref, qkv_ref, p_ref, o1_ref, term,
    )
    dealt = deal(lambda at: term.at[at], slots, rsems, "mp")
    passed = [pass_weight(i, sent[i]) for i in range(2)]
    for copy in dealt:
        copy.wait_recv()
    h = home_rows(x_ref, chunk).astype(F32) + total_of(term[mm], slots)
    h_ref[...] = h
    a2_ref[pm, mm] = (h * rms_inverse(h) * gain_ref[1:2, :]).astype(BF16)
    forward, end = share_both(a2_ref, zsems, msems)
    sent += [send_weight(2), send_weight(3)]
    for copies in passed:
        for copy in copies:
            copy.wait_recv()
    for own in owns:
        own.wait()
    load.wait()
    rows = enc.shape[0] // KV_STEPS

    def store(step):
        slot = lax.rem(step, 2)
        at = pl.ds(pl.multiple_of(step * rows, rows), rows)
        return pltpu.make_async_copy(kv_slots.at[slot], kv_ref.at[at], kv_sems.at[slot])

    def project(step, carry):
        slot = lax.rem(step, 2)

        @pl.when(step >= 2)
        def _():
            store(step - 2).wait()

        x = enc[pl.ds(pl.multiple_of(step * rows, rows), rows), :]
        for i in range(2):
            kv_slots[slot, :, i * MODEL_WIDTH : (i + 1) * MODEL_WIDTH] = dot_nt(x, wkv_ref[i]).astype(BF16)
        store(step).start()
        return carry

    done = 0
    for j in range(pn - 1):
        upto = KV_STEPS * (j + 1) // (pn - 1)
        if upto > done:
            lax.fori_loop(done, upto, project, 0)
            done = upto
        forward(j)
    for i in range(2, 4):
        passed.append(pass_weight(i, sent[i]))
    for step in (KV_STEPS - 2, KV_STEPS - 1):
        store(step).wait()
    end()
    for copy in dealt:
        copy.wait_send()
    for copies in sent:
        for copy in copies:
            copy.wait_send()
    for i, copies in enumerate(passed):
        for copy in copies:
            copy.wait_send()
            if i >= 2:
                copy.wait_recv()


PAIR = 2 * HD
PAIRS = MODEL_WIDTH // PAIR
PROWS = 2 * PADT
FLOOR = -1e29


def low_lanes(shape):
    return lax.broadcasted_iota(jnp.int32, shape, len(shape) - 1) < HD


def pair_rows(dst_ref, pad_ref, values, stat=None, stat_at=0):
    questions = dst_ref.shape[0]
    low = low_lanes((1, PADT, PAIR))
    for q in range(questions):
        rows = slice(q * ANS, (q + 1) * ANS)
        pad_ref[q, 0:ANS, :MODEL_WIDTH] = values[rows, :]
        pad_ref[q, ANS:PADT, :] = jnp.zeros((PADT - ANS, pad_ref.shape[2]), F32)
        if stat is not None:
            pad_ref[q, 0:ANS, MODEL_WIDTH:] = stat[rows, :]
    lane = lax.broadcasted_iota(jnp.int32, (1, 1, LANES), 2)
    for c in range(PAIRS):
        x = pad_ref[:, :, c * PAIR : (c + 1) * PAIR]
        both = jnp.concatenate([jnp.where(low, x, 0.0), jnp.where(low, 0.0, x)], axis=1)
        dst_ref[:, c, :, :PAIR] = both.astype(BF16)
        if stat is not None:
            s = pad_ref[:, :, MODEL_WIDTH:]
            parts = []
            for h in (2 * c, 2 * c + 1):
                at = lane - (stat_at + h)
                parts.append(s * ((at == 0) | (at == 16) | (at == 32)).astype(F32))
            dst_ref[:, c, :, PAIR:] = jnp.concatenate(parts, axis=1).astype(BF16)


def segment_mask(lens_ref, row, keys):
    lane = lax.broadcasted_iota(jnp.int32, (PROWS, keys), 1)
    cut = lens_ref[0, row] - lax.axis_index("mp") * keys
    return [lane < cut, (lane >= cut) & (lane < cut + lens_ref[1, row])]


def masked(scores, mask):
    return jnp.concatenate(
        [jnp.where(mask[s], scores[s * PROWS : (s + 1) * PROWS], NEGATIVE) for s in range(2)], axis=0
    )


def fold_pair(x, s, low):
    at = s * PROWS
    return jnp.where(low, x[at : at + PADT], x[at + PADT : at + PROWS])


def split_three(x):
    hi = x.astype(BF16).astype(F32)
    mid = (x - hi).astype(BF16).astype(F32)
    return hi, mid, x - hi - mid


def staged(rows_per, stages):
    depth = len(stages)
    for i in range(rows_per + depth - 1):
        for k in reversed(range(depth)):
            if 0 <= i - k < rows_per:
                stages[k](i - k, (i - k) % 2)


def cross_forward_kernel(
    rows_per, keys, lens_ref, owners_ref, a2_ref, wq_ref, kv_ref, out_ref,
    q_rows, pad, s_buf, p_buf, t_buf, o_acc, m_acc, l_acc, flat,
):
    g = pl.program_id(0)
    pair_rows(q_rows, pad, dot_nt(a2_ref[0], wq_ref[...]).astype(BF16).astype(F32))
    o_acc[...] = jnp.zeros_like(o_acc)
    m_acc[...] = jnp.full_like(m_acc, FLOOR)
    l_acc[...] = jnp.zeros_like(l_acc)
    low = low_lanes((PADT, PAIR))
    ones = jnp.ones((keys, PAIR), BF16)

    def row_of(r):
        return lax.axis_index("pass") * GROUP_ROWS + g * rows_per + r

    def owners_of(r):
        return [owners_ref[0, row_of(r)], owners_ref[1, row_of(r)]]

    def scores(r, slot):
        owners = owners_of(r)
        mask = segment_mask(lens_ref, row_of(r), keys)
        for c in range(PAIRS):
            k = kv_ref[r * keys : (r + 1) * keys, c * PAIR : (c + 1) * PAIR]
            qm = jnp.concatenate([q_rows[q, c] for q in owners], axis=0)
            s_buf[slot, c] = masked(dot_nt(qm, k), mask)

    def chances(r, slot):
        for c in range(PAIRS):
            s = s_buf[slot, c]
            top = jnp.maximum(jnp.max(s, axis=-1, keepdims=True), FLOOR)
            p_buf[slot, c] = jnp.exp(s - top).astype(BF16)
            top = jnp.broadcast_to(top, (2 * PROWS, PAIR))
            for i in range(2):
                t_buf[slot, c, i] = fold_pair(top, i, low)

    def values(r, slot):
        owners = owners_of(r)
        new = []
        for c in range(PAIRS):
            v = kv_ref[r * keys : (r + 1) * keys, MODEL_WIDTH + c * PAIR : MODEL_WIDTH + (c + 1) * PAIR]
            both = dot_nn(p_buf[slot, c], jnp.concatenate([v, ones], axis=1))
            new.append([
                (fold_pair(both[:, :PAIR], i, low), fold_pair(both[:, PAIR:], i, low)) for i in range(2)
            ])
        for i, q in enumerate(owners):
            for c in range(PAIRS):
                cols = slice(c * PAIR, (c + 1) * PAIR)
                o, l = new[c][i]
                m_old, m_new = m_acc[q, :, cols], t_buf[slot, c, i]
                m_both = jnp.maximum(m_old, m_new)
                a, b = jnp.exp(m_old - m_both), jnp.exp(m_new - m_both)
                o_acc[q, :, cols] = a * o_acc[q, :, cols] + b * o
                l_acc[q, :, cols] = a * l_acc[q, :, cols] + b * l
                m_acc[q, :, cols] = m_both

    staged(rows_per, [scores, chances, values])
    questions = q_rows.shape[0]
    lane = lax.broadcasted_iota(jnp.int32, (PADT, LANES), 1)
    for q in range(questions):
        l = l_acc[q]
        some = l > 0.0
        safe = jnp.where(some, l, 1.0)
        o = o_acc[q] / safe
        lse = jnp.where(some, m_acc[q] + jnp.log(safe), NEGATIVE)
        few = jnp.zeros((PADT, LANES), F32)
        for h in range(MODEL_WIDTH // HD):
            few = jnp.where(lane == h, lse[:, h * HD : h * HD + 1], few)
        hi, mid, rest = split_three(few)
        stat = hi + pltpu.roll(mid, 16, 1) + pltpu.roll(rest, 32, 1)
        flat[q * ANS : (q + 1) * ANS, :MODEL_WIDTH] = o[:ANS]
        flat[q * ANS : (q + 1) * ANS, MODEL_WIDTH:] = stat[:ANS]
    chunk = out_ref.shape[2]
    for m in range(out_ref.shape[0]):
        out_ref[m, 0] = flat[m * chunk : (m + 1) * chunk, :].astype(BF16)


def cross_forward(lens, owners, a2_all, wq, kv, mp_parts):
    groups, n_tokens, _ = a2_all.shape
    rows_per = GROUP_ROWS // groups
    keys = kv.shape[0] // GROUP_ROWS
    questions = n_tokens // ANS
    block = rows_per * keys
    padded = pltpu.VMEM((questions, PADT, MODEL_WIDTH), F32)
    return pl.pallas_call(
        functools.partial(cross_forward_kernel, rows_per, keys),
        grid_spec=pltpu.PrefetchScalarGridSpec(
            num_scalar_prefetch=2,
            grid=(groups,),
            in_specs=[
                pl.BlockSpec((1, n_tokens, MODEL_WIDTH), lambda g, *_: (g, 0, 0)),
                pl.BlockSpec((MODEL_WIDTH, MODEL_WIDTH), lambda g, *_: (0, 0)),
                pl.BlockSpec((block, 2 * MODEL_WIDTH), lambda g, *_: (g, 0)),
            ],
            out_specs=pl.BlockSpec(
                (mp_parts, 1, n_tokens // mp_parts, STATW), lambda g, *_: (0, g, 0, 0)
            ),
            scratch_shapes=[
                pltpu.VMEM((questions, PAIRS, PROWS, PAIR), BF16),
                padded,
                pltpu.VMEM((2, PAIRS, 2 * PROWS, keys), F32),
                pltpu.VMEM((2, PAIRS, 2 * PROWS, keys), BF16),
                pltpu.VMEM((2, PAIRS, 2, PADT, PAIR), F32),
                padded,
                padded,
                padded,
                pltpu.VMEM((n_tokens, STATW), F32),
            ],
        ),
        out_shape=jax.ShapeDtypeStruct((mp_parts, groups, n_tokens // mp_parts, STATW), BF16),
        compiler_params=pltpu.CompilerParams(vmem_limit_bytes=VMEM_LIMIT),
    )(lens, owners, a2_all, wq, kv)


def cross_backward_kernel(
    rows_per, keys, lens_ref, owners_ref, a2_ref, gc_ref, wq_ref, wo_ref, kv_ref, gq_ref, gkv_ref,
    q_rows, go_rows, pad, s_buf, gp_buf, p_buf, gs_buf, gq_acc, flat,
):
    g = pl.program_id(0)
    stat = gc_ref[0, :, MODEL_WIDTH:].astype(F32)
    q2 = dot_nt(a2_ref[0], wq_ref[...]).astype(BF16).astype(F32)
    pair_rows(q_rows, pad, q2, stat, 0)
    go2 = dot_nt(gc_ref[0, :, :MODEL_WIDTH], wo_ref[...]).astype(BF16).astype(F32)
    pair_rows(go_rows, pad, go2, stat, 48)
    gq_acc[...] = jnp.zeros_like(gq_acc)
    low = low_lanes((PADT, PAIR))
    minus = jnp.full((keys, LANES), -1.0, BF16)

    def row_of(r):
        return lax.axis_index("pass") * GROUP_ROWS + g * rows_per + r

    def owners_of(r):
        return [owners_ref[0, row_of(r)], owners_ref[1, row_of(r)]]

    def tile(r, c, off):
        return kv_ref[r * keys : (r + 1) * keys, off + c * PAIR : off + (c + 1) * PAIR]

    def scores(r, slot):
        owners = owners_of(r)
        mask = segment_mask(lens_ref, row_of(r), keys)
        for c in range(PAIRS):
            qm = jnp.concatenate([q_rows[q, c] for q in owners], axis=0)
            gom = jnp.concatenate([go_rows[q, c] for q in owners], axis=0)
            s = dot_nt(qm, jnp.concatenate([tile(r, c, 0), minus], axis=1))
            s_buf[slot, c] = masked(s, mask)
            gp_buf[slot, c] = dot_nt(gom, jnp.concatenate([tile(r, c, MODEL_WIDTH), minus], axis=1))

    def chances(r, slot):
        for c in range(PAIRS):
            p = jnp.exp(s_buf[slot, c])
            p_buf[slot, c] = p.astype(BF16)
            gs_buf[slot, c] = (p * gp_buf[slot, c]).astype(BF16)

    def grads(r, slot):
        owners = owners_of(r)
        new = []
        rows = slice(r * keys, (r + 1) * keys)
        for c in range(PAIRS):
            gs, p = gs_buf[slot, c], p_buf[slot, c]
            qm = jnp.concatenate([q_rows[q, c, :, :PAIR] for q in owners], axis=0)
            gom = jnp.concatenate([go_rows[q, c, :, :PAIR] for q in owners], axis=0)
            gkv_ref[rows, c * PAIR : (c + 1) * PAIR] = dot_tn(gs, qm).astype(BF16)
            gkv_ref[rows, MODEL_WIDTH + c * PAIR : MODEL_WIDTH + (c + 1) * PAIR] = dot_tn(p, gom).astype(BF16)
            gq = dot_nn(gs, tile(r, c, 0))
            new.append([fold_pair(gq, i, low) for i in range(2)])
        for i, q in enumerate(owners):
            for c in range(PAIRS):
                cols = slice(c * PAIR, (c + 1) * PAIR)
                gq_acc[q, :, cols] = gq_acc[q, :, cols] + new[c][i]

    staged(rows_per, [scores, chances, grads])
    for q in range(q_rows.shape[0]):
        flat[q * ANS : (q + 1) * ANS, :] = gq_acc[q, :ANS, :]
    chunk = gq_ref.shape[2]
    for m in range(gq_ref.shape[0]):
        gq_ref[m, 0] = flat[m * chunk : (m + 1) * chunk, :].astype(BF16)


def cross_backward(lens, owners, a2_all, gc_all, wq, wo, kv, mp_parts):
    groups, n_tokens, _ = a2_all.shape
    rows_per = GROUP_ROWS // groups
    keys = kv.shape[0] // GROUP_ROWS
    questions = n_tokens // ANS
    block = rows_per * keys
    rows = pltpu.VMEM((questions, PAIRS, PROWS, PAIR + LANES), BF16)
    whole = pl.BlockSpec((MODEL_WIDTH, MODEL_WIDTH), lambda g, *_: (0, 0))
    return pl.pallas_call(
        functools.partial(cross_backward_kernel, rows_per, keys),
        grid_spec=pltpu.PrefetchScalarGridSpec(
            num_scalar_prefetch=2,
            grid=(groups,),
            in_specs=[
                pl.BlockSpec((1, n_tokens, MODEL_WIDTH), lambda g, *_: (g, 0, 0)),
                pl.BlockSpec((1, n_tokens, STATW), lambda g, *_: (g, 0, 0)),
                whole,
                whole,
                pl.BlockSpec((block, 2 * MODEL_WIDTH), lambda g, *_: (g, 0)),
            ],
            out_specs=[
                pl.BlockSpec(
                    (mp_parts, 1, n_tokens // mp_parts, MODEL_WIDTH), lambda g, *_: (0, g, 0, 0)
                ),
                pl.BlockSpec((block, 2 * MODEL_WIDTH), lambda g, *_: (g, 0)),
            ],
            scratch_shapes=[
                rows,
                rows,
                pltpu.VMEM((questions, PADT, STATW), F32),
                pltpu.VMEM((2, PAIRS, 2 * PROWS, keys), F32),
                pltpu.VMEM((2, PAIRS, 2 * PROWS, keys), F32),
                pltpu.VMEM((2, PAIRS, 2 * PROWS, keys), BF16),
                pltpu.VMEM((2, PAIRS, 2 * PROWS, keys), BF16),
                pltpu.VMEM((questions, PADT, MODEL_WIDTH), F32),
                pltpu.VMEM((n_tokens, MODEL_WIDTH), F32),
            ],
        ),
        out_shape=[
            jax.ShapeDtypeStruct((mp_parts, groups, n_tokens // mp_parts, MODEL_WIDTH), BF16),
            jax.ShapeDtypeStruct(kv.shape, BF16),
        ],
        compiler_params=pltpu.CompilerParams(vmem_limit_bytes=VMEM_LIMIT),
    )(lens, owners, a2_all, gc_all, wq, wo, kv)


def widen(w):
    row = lax.broadcasted_iota(jnp.int32, (LANES, MODEL_WIDTH), 0)
    col = lax.broadcasted_iota(jnp.int32, (LANES, MODEL_WIDTH), 1)
    each = (row == lax.div(col, HD)).astype(BF16)
    hi = w.astype(BF16)
    low = (w - hi.astype(F32)).astype(BF16)
    return dot_nn(hi, each) + dot_nn(low, each)


def combined(parts):
    lses = []
    for part in parts:
        stat = part[:, MODEL_WIDTH:].astype(F32)
        lses.append(stat + pltpu.roll(stat, LANES - 16, 1) + pltpu.roll(stat, LANES - 32, 1))
    top = functools.reduce(jnp.maximum, lses)
    weights = [jnp.exp(x - top) for x in lses]
    total = functools.reduce(jnp.add, weights)
    out = 0.0
    for part, weight in zip(parts, weights):
        out = out + widen(weight / total) * part[:, :MODEL_WIDTH].astype(F32)
    lane = lax.broadcasted_iota(jnp.int32, total.shape, 1)
    lse = jnp.where(lane < MODEL_WIDTH // HD, top + jnp.log(total), 0.0)
    return out, lse


def packed_stat(lse, at=0):
    hi, mid, low = split_three(lse)
    parts = [hi if at == 0 else pltpu.roll(hi, at, 1)]
    parts += [pltpu.roll(mid, at + 16, 1), pltpu.roll(low, at + 32, 1)]
    return parts[0] + parts[1] + parts[2]


def deal_groups(source, slots, sems):
    pn, pm = lax.axis_size("pass"), lax.axis_index("pass")
    for step in range(pn):
        group = lax.rem(pm + 1 + step, pn)
        deal(lambda at: source.at[at, group], slots.at[step], sems.at[step], "mp")


def groups_home(source, slots, held, zslots, msems, zsems, add):
    pn, pm, mm = lax.axis_size("pass"), lax.axis_index("pass"), lax.axis_index("mp")

    def arrived(step):
        group = lax.rem(pm + 1 + step, pn)
        for k, at, peer in others("mp"):
            remote(
                source.at[at, group], slots.at[step, k], msems.at[step, 0, k], msems.at[step, 1, k], peer
            ).wait()
        held[step] = add([source[mm, group]] + [slots[step, k] for k in range(slots.shape[1])])

    def to_home(step):
        at, peer = other("pass", step + 1)
        return remote(
            held.at[step], zslots.at[step], zsems.at[0, step], zsems.at[1, step], peer
        )

    def one(step, carry):
        arrived(step)
        to_home(step).start()
        return carry

    if pn <= 4:
        for step in range(pn - 1):
            one(step, 0)
    else:
        lax.fori_loop(0, pn - 1, one, 0)
    arrived(pn - 1)
    for step in range(pn - 1):
        to_home(step).wait()
    return [held[pn - 1]] + [zslots[k] for k in range(pn - 1)]


def cross_out_kernel(
    part_ref, h_ref, wo_ref, gain_ref, h2_ref, a3_ref, o_ref, own_ref, lse_ref,
    slots, held, zslots, blocks, msems, zsems, asems, bsems,
):
    mm = lax.axis_index("mp")
    greet(("pass", "mp"))
    deal_groups(part_ref, slots, msems)

    def add(parts):
        out, lse = combined(parts)
        return jnp.concatenate([out, packed_stat(lse)], axis=1).astype(BF16)

    o, lse = combined(groups_home(part_ref, slots, held, zslots, msems, zsems, add))
    low = o.astype(BF16)
    h = h_ref[...] + dot_nn(low, wo_ref[...])
    a3_ref[mm] = (h * rms_inverse(h) * gain_ref[2:3, :]).astype(BF16)
    copies = share(a3_ref.at[mm], asems, "mp")
    h2_ref[...] = h
    o_ref[...] = o
    lse_ref[...] = lse
    width = blocks.shape[2]
    for k in range(blocks.shape[0]):
        blocks[k] = low[:, k * width : (k + 1) * width]
    own_ref[mm] = blocks[mm]
    copies += begin([
        remote(blocks.at[at], own_ref.at[mm], bsems.at[0, k], bsems.at[1, k], peer)
        for k, at, peer in others("mp")
    ])
    finish(copies)


def ffn_back_kernel(
    ga_ref, gy_ref, h_ref, gain_ref, wo_ref, o_ref, lse_ref, gh_ref, gc_ref, gain_out_ref,
    slots, rsems, zsems, msems,
):
    mm, pm = lax.axis_index("mp"), lax.axis_index("pass")
    greet(("pass", "mp"))
    dealt = deal(lambda at: ga_ref.at[at], slots, rsems, "mp")
    finish(dealt)
    gv, gain_grad = rms_back(h_ref[...], gain_ref[2:3, :], total_of(ga_ref[mm], slots))
    gain_out_ref[...] = gain_grad
    gh = home_rows(gy_ref, h_ref.shape[0]).astype(F32) + gv
    gh_ref[...] = gh
    gc = gh.astype(BF16)
    go = dot_nt(gc, wo_ref[...]).astype(BF16).astype(F32)
    row = lax.broadcasted_iota(jnp.int32, (MODEL_WIDTH, LANES), 0)
    col = lax.broadcasted_iota(jnp.int32, (MODEL_WIDTH, LANES), 1)
    each = (lax.div(row, HD) == col).astype(F32)
    delta = lax.dot_general(
        go * o_ref[...], each, (((1,), (0,)), ((), ())),
        preferred_element_type=F32, precision=lax.Precision.HIGHEST,
    )
    stat = packed_stat(lse_ref[...]) + packed_stat(delta, 48)
    gc_ref[pm, mm] = jnp.concatenate([gc, stat.astype(BF16)], axis=1)
    forward, end = share_both(gc_ref, zsems, msems)
    for j in range(lax.axis_size("pass") - 1):
        forward(j)
    end()


def sum_rows(rows, groups):
    return -(-rows // (groups * 16)) * 16


class GroupSum:
    def __init__(self, y, zslots, out, sems):
        self.y, self.zslots, self.out = y, zslots, out
        self.zsems, self.asems, self.dsems = sems.at[0], sems.at[1], sems.at[2]
        self.core, self.pm = lax.axis_index("dp"), lax.axis_index("pass")
        self.rows = zslots.shape[1]

    def part(self, at):
        return pl.ds(pl.multiple_of(at * self.rows, 16), self.rows)

    def spread(self):
        self.copies = deal(lambda at: self.y.at[self.part(at)], self.zslots, self.zsems, "pass")

    def gather(self):
        finish(self.copies)
        total = total_of(self.y[self.part(self.pm), :], self.zslots)
        self.out[self.core, self.part(self.pm), :] = total.astype(BF16)
        self.copies = share(self.out.at[self.core, self.part(self.pm)], self.asems, "pass")

    def swap(self):
        finish(self.copies)
        self.copies = share(self.out.at[self.core], self.dsems, "dp")

    def end(self):
        finish(self.copies)


def fill_tail(y, used):
    if y.shape[0] > used:
        y[used:, :] = jnp.zeros((y.shape[0] - used, y.shape[1]), y.dtype)


def self_backward(
    heads, gsa, wq_ref, wk_ref, wv_ref, wo_ref, qkv_ref, p_ref, ga1_ref, gqkv_ref, bias_ref
):
    go1 = dot_nt(gsa, wo_ref[...]).astype(BF16)
    blocks, size = ga1_ref.shape[0], ga1_ref.shape[1]
    grid, _, used = bucket_grid(size)
    at_row = lax.broadcasted_iota(jnp.int32, bias_ref.shape, 0)
    at_lane = lax.broadcasted_iota(jnp.int32, bias_ref.shape, 1)
    totals = []
    for h in range(heads):
        part = slice(h * HD, (h + 1) * HD)
        total = jnp.zeros((size, size), F32)
        for b in range(blocks):
            rows = pl.ds(b * size, size)
            q, k, v = qkv_ref[0, rows, part], qkv_ref[1, rows, part], qkv_ref[2, rows, part]
            p = p_ref[b * heads + h]
            go = go1[b * size : (b + 1) * size, part]
            gp = dot_nt(go, v)
            gs = (p * (gp - jnp.sum(gp * p, axis=-1, keepdims=True))).astype(BF16)
            total = total + gs.astype(F32)
            gqkv_ref[0, rows, part] = dot_nn(gs, k).astype(BF16)
            gqkv_ref[1, rows, part] = dot_tn(gs, q).astype(BF16)
            gqkv_ref[2, rows, part] = dot_tn(p.astype(BF16), go).astype(BF16)
        totals.append(total)
    ga1 = dot_nn(gqkv_ref[0], wq_ref[...])
    ga1 = ga1 + dot_nn(gqkv_ref[1], wk_ref[...])
    ga1 = ga1 + dot_nn(gqkv_ref[2], wv_ref[...])
    for b in range(blocks):
        ga1_ref[b] = ga1[b * size : (b + 1) * size].astype(BF16)

    def bias_sums():
        bias = jnp.zeros(bias_ref.shape, F32)
        for h, total in enumerate(totals):
            for b in used:
                value = jnp.sum(jnp.where(grid == b, total, 0.0), keepdims=True)
                bias = jnp.where((at_row == h) & (at_lane == b), value, bias)
        bias_ref[...] = bias

    return bias_sums


def finish_kernel(
    heads, gq_ref, gkv_ref, enc_ref, wkv_ref, gh2_ref, h_ref, gain_ref, wq_ref,
    ws_q_ref, ws_k_ref, ws_v_ref, ws_o_ref, a1_ref, qkv_ref, p_ref, o1_ref,
    a2_ref, gc_ref, o2_ref, term_ref, x_ref, h2_ref, ffn_gain_ref,
    out_ref, gx_ref, sum_c_ref, sum_k_ref, sum_s_ref, small_ref, genc_ref,
    held, slots, zslots, gkv_in, enc_in, genc_out, gw_acc, gw_kv, gw_c, gw_s,
    blocks, gq_own, gsa_all, ga1, gqkv, bias, a2_own, gc_own,
    ga_slots, term_slots, kv_core, kv_half, kv_slots, core_c, core_s,
    y_c, y_k, y_s, z_c, z_k, z_s, small, small_dp, small_z, small_m,
    msems, gzsems, asems, bsems, load_sems, in_sems, genc_sems,
    ga_sems, term_sems, kv_dsems, kv_msems, cc_sems, cs_sems, gx_sems, out_sems,
    zc_sems, zk_sems, zs_sems, sd_sems, sz_sems, sm_sems,
):
    core, mm, pm = lax.axis_index("dp"), lax.axis_index("mp"), lax.axis_index("pass")
    pn = lax.axis_size("pass")
    chunk = h_ref.shape[0]
    width = o1_ref.shape[1]
    half = width // 2
    mine = pl.ds(pl.multiple_of(core * half, 16), half)
    theirs = pl.ds(pl.multiple_of((1 - core) * half, 16), half)
    peer = other("dp", 1)[1]
    loads = begin([
        pltpu.make_async_copy(gq_ref.at[mm], held, load_sems.at[0]),
        pltpu.make_async_copy(a2_ref.at[pm], a2_own, load_sems.at[1]),
        pltpu.make_async_copy(gc_ref.at[pm], gc_own, load_sems.at[2]),
    ])
    rows = gkv_in.shape[1]
    steps = gkv_ref.shape[0] // rows

    def step_rows(step):
        return pl.ds(pl.multiple_of(step * rows, rows), rows)

    def fetch(step, slot):
        return [
            pltpu.make_async_copy(gkv_ref.at[step_rows(step)], gkv_in.at[slot], in_sems.at[slot, 0]),
            pltpu.make_async_copy(enc_ref.at[step_rows(step)], enc_in.at[slot], in_sems.at[slot, 1]),
        ]

    def store(step, slot):
        return pltpu.make_async_copy(genc_out.at[slot], genc_ref.at[step_rows(step)], genc_sems.at[slot])

    begin(fetch(0, 0))
    greet(("dp", "pass", "mp"))
    for step in range(pn):
        group = lax.rem(pm + 1 + step, pn)
        deal(lambda at: gq_ref.at[at, group], slots.at[step], msems.at[step], "mp")
    finish(loads)

    def to_home(step):
        at, to = other("pass", step + 1)
        return remote(held.at[at], zslots.at[step], gzsems.at[0, step], gzsems.at[1, step], to)

    def arrived(step, carry):
        group = lax.rem(pm + 1 + step, pn)
        for k, at, to in others("mp"):
            remote(
                gq_ref.at[at, group], slots.at[step, k], msems.at[step, 0, k], msems.at[step, 1, k], to
            ).wait()
        total = held[group].astype(F32)
        for k in range(slots.shape[1]):
            total = total + slots[step, k].astype(F32)
        held[group] = total.astype(BF16)

        @pl.when(step < pn - 1)
        def _():
            to_home(step).start()

        return carry

    gw_acc[...] = jnp.zeros_like(gw_acc)

    def work(step, carry):
        slot = lax.rem(step, 2)

        @pl.when(step + 1 < steps)
        def _():
            begin(fetch(step + 1, 1 - slot))

        finish(fetch(step, slot))

        @pl.when(step >= 2)
        def _():
            store(step - 2, slot).wait()

        genc_out[slot] = dot_nn(gkv_in[slot], wkv_ref[...]).astype(BF16)
        store(step, slot).start()
        for i in range(2):
            part = slice(i * MODEL_WIDTH, (i + 1) * MODEL_WIDTH)
            gw_acc[part, :] += dot_tn(gkv_in[slot, :, part], enc_in[slot])
        lax.fori_loop(lax.div(step * pn, steps), lax.div((step + 1) * pn, steps), arrived, 0)
        return carry

    lax.fori_loop(0, steps, work, 0)
    for step in range(pn - 1):
        to_home(step).wait()
    low = total_of(held[pm], zslots).astype(BF16)
    gv, cross_gain = rms_back(h_ref[...], gain_ref[1:2, :], dot_nn(low, wq_ref[...]))
    gh1 = gh2_ref[...] + gv
    gsa_all[mm] = gh1.astype(BF16)
    gsa_copies = share(gsa_all.at[mm], asems, "mp")
    for k in range(blocks.shape[0]):
        blocks[k] = low[:, k * width : (k + 1) * width]
    gq_own[mm] = blocks[mm]
    block_copies = begin([
        remote(blocks.at[at], gq_own.at[mm], bsems.at[0, k], bsems.at[1, k], to)
        for k, at, to in others("mp")
    ])
    parts = blocks.shape[0]
    for i in range(2):
        for k in range(parts):
            at = (i * parts + k) * width
            gw_kv[i, k] = gw_acc[at : at + width, :].astype(BF16)
    kv_copy = remote(gw_kv.at[:, :, theirs], kv_core, kv_dsems.at[0], kv_dsems.at[1], peer)
    kv_copy.start()
    for step in (steps - 2, steps - 1):
        store(step, step % 2).wait()
    total = jnp.zeros((width, MODEL_WIDTH), F32)
    for k in range(parts):
        total = total + dot_tn(o2_ref[k], gc_own[k, :, :MODEL_WIDTH])
    gw_c[0] = total.astype(BF16)
    kv_copy.wait()
    for i in range(2):
        for k in range(parts):
            kv_half[k, i] = (gw_kv[i, k, mine, :].astype(F32) + kv_core[i, k].astype(F32)).astype(BF16)
    kv_copies = deal(lambda at: kv_half.at[at], kv_slots, kv_msems, "mp")
    finish(gsa_copies)
    gsa = jnp.concatenate([gsa_all[k] for k in range(parts)], axis=0)
    bias_sums = self_backward(
        heads, gsa, ws_q_ref, ws_k_ref, ws_v_ref, ws_o_ref, qkv_ref, p_ref, ga1, gqkv, bias
    )
    ga_copies = deal(lambda at: ga1.at[at], ga_slots, ga_sems, "mp")
    finish(block_copies)
    total = jnp.zeros((width, MODEL_WIDTH), F32)
    for k in range(parts):
        total = total + dot_tn(gq_own[k], a2_own[k])
    gw_c[1] = total.astype(BF16)
    c_copy = remote(gw_c.at[:, theirs], core_c, cc_sems.at[0], cc_sems.at[1], peer)
    c_copy.start()
    for k in range(3):
        gw_s[k] = dot_tn(gqkv[k], a1_ref[...]).astype(BF16)
    gw_s[3] = dot_tn(o1_ref[...], gsa).astype(BF16)
    s_copy = remote(gw_s.at[:, theirs], core_s, cs_sems.at[0], cs_sems.at[1], peer)
    s_copy.start()

    def both_cores(copy, gw, got, y):
        copy.wait()
        for i in range(gw.shape[0]):
            y[i * half : (i + 1) * half, :] = (gw[i, mine, :].astype(F32) + got[i].astype(F32)).astype(BF16)
        fill_tail(y, gw.shape[0] * half)

    both_cores(c_copy, gw_c, core_c, y_c)
    sum_c = GroupSum(y_c, z_c, sum_c_ref, zc_sems)
    sum_c.spread()
    both_cores(s_copy, gw_s, core_s, y_s)
    sum_s = GroupSum(y_s, z_s, sum_s_ref, zs_sems)
    sum_s.spread()
    finish(ga_copies)
    gv, self_gain = rms_back(
        home_rows(x_ref, chunk).astype(F32), gain_ref[0:1, :], total_of(ga1[mm], ga_slots)
    )
    gx_ref[mm] = (gh1 + gv).astype(BF16)
    gx_copies = share(gx_ref.at[mm], gx_sems, "mp")
    term_copies = deal(lambda at: term_ref.at[at], term_slots, term_sems, "mp")
    bias_sums()
    small[...] = jnp.zeros_like(small)
    small[0:1, :] = self_gain
    small[1:2, :] = cross_gain
    small[2:3, :] = ffn_gain_ref[...]
    small[8:16, :LANES] = bias[...]
    sd = begin([remote(small, small_dp, sd_sems.at[0], sd_sems.at[1], peer)])
    finish(kv_copies)
    for i in range(2):
        total = kv_half[mm, i].astype(F32)
        for k in range(kv_slots.shape[0]):
            total = total + kv_slots[k, i].astype(F32)
        y_k[i * half : (i + 1) * half, :] = total.astype(BF16)
    fill_tail(y_k, 2 * half)
    sum_k = GroupSum(y_k, z_k, sum_k_ref, zk_sems)
    sum_k.spread()
    finish(sd)
    small_z[pm] = small[...] + small_dp[...]
    sz = share(small_z.at[pm], sz_sems, "pass")
    sum_c.gather()
    finish(term_copies)
    out_ref[mm] = (h2_ref[...] + total_of(term_ref[mm], term_slots)).astype(BF16)
    out_copies = share(out_ref.at[mm], out_sems, "mp")
    sum_s.gather()
    finish(sz)
    total = small_z[0]
    for k in range(1, small_z.shape[0]):
        total = total + small_z[k]
    small_m[mm] = total
    sm = share(small_m.at[mm], sm_sems, "mp")
    sum_k.gather()
    sum_c.swap()
    finish(sm)
    gains = small_m[0]
    for k in range(1, small_m.shape[0]):
        gains = gains + small_m[k]
    small_ref[0:8, :] = gains[0:8]
    small_ref[8:16, :] = total[8:16]
    finish(gx_copies)
    finish(out_copies)
    sum_s.swap()
    sum_k.swap()
    sum_c.end()
    sum_s.end()
    sum_k.end()


def widen_kernel(c_ref, k_ref, s_ref, in_ref, out_ref, *refs):
    half = refs[0].shape[0] // 2
    outs, wide, wide_in, wide_out, sems = refs[:10], refs[10], refs[11], refs[12], refs[13]
    sources = [(s_ref, 0), (s_ref, 1), (s_ref, 2), (s_ref, 3), (c_ref, 1), (k_ref, 0), (k_ref, 1), (c_ref, 0)]
    copies = []
    for n, (ref, i) in enumerate(sources):
        for core in range(2):
            wide[n, core * half : (core + 1) * half, :] = ref[core, i * half : (i + 1) * half, :].astype(F32)
        copies.append(pltpu.make_async_copy(wide.at[n], outs[n], sems.at[n]))
        copies[-1].start()
    for n, (ref, buffer) in enumerate(((in_ref, wide_in), (out_ref, wide_out))):
        buffer[...] = ref[...].astype(F32)
        copies.append(pltpu.make_async_copy(buffer, outs[8 + n], sems.at[8 + n]))
        copies[-1].start()
    for copy in copies:
        copy.wait()


def ffn_kernel(a3_ref, w_in_ref, w_out_ref, gy_ref, term_ref, ga3_ref, gw_in_ref, gw_out_ref):
    a3, gy = a3_ref[...], gy_ref[...]
    u = dot_nn(a3, w_in_ref[...])
    cdf = 0.5 * (1.0 + lax.erf(u * np.float32(math.sqrt(0.5))))
    pdf = np.float32(1.0 / math.sqrt(2.0 * math.pi)) * jnp.exp(-0.5 * u * u)
    e = (u * cdf).astype(BF16)
    term_ref[...] = dot_nn(e, w_out_ref[...]).astype(BF16)
    ge = dot_nt(gy, w_out_ref[...]).astype(BF16).astype(F32)
    gu = (ge * (cdf + u * pdf)).astype(BF16)
    ga3_ref[...] = dot_nt(gu, w_in_ref[...]).astype(BF16)
    gw_in_ref[...] = dot_tn(a3, gu).astype(BF16)
    gw_out_ref[...] = dot_tn(e, gy).astype(BF16)


def on_device(
    tokens,
    encoded,
    seg_lens,
    owners,
    answer_lens,
    gain_self,
    gain_cross,
    gain_ffn,
    rel_bias,
    wq_self,
    wk_self,
    wv_self,
    wo_self,
    wq_cross,
    wk_cross,
    wv_cross,
    wo_cross,
    w_in,
    w_out,
    out_grad,
):
    groups, mp_parts = lax.axis_size("pass"), lax.axis_size("mp")
    heads = rel_bias.shape[1]
    head_cols = heads * HD
    half = head_cols // 2
    quarter = encoded.shape[1]
    n_tokens = tokens.shape[0]
    chunk = n_tokens // mp_parts
    hidden = w_in.shape[1]
    keys = GROUP_ROWS * quarter
    near, far = mp_parts - 1, groups - 1
    gains = jnp.stack([gain_self, gain_cross, gain_ffn])

    lens, owners = seg_lens.T, owners.T
    flat_encoded = encoded.reshape(keys, MODEL_WIDTH)
    home = (chunk, MODEL_WIDTH)
    dealt = (mp_parts, chunk, MODEL_WIDTH)
    square = (MODEL_WIDTH, MODEL_WIDTH)
    smem = pltpu.SMEM
    a2_all, h_one, a1, qkv, p1, o1, wkv, wq_full, wo_full, kv = remote_call(
        functools.partial(front_kernel, heads),
        0,
        [
            ((groups, *dealt), BF16),
            (home, F32),
            ((n_tokens, MODEL_WIDTH), BF16),
            ((3, n_tokens, head_cols), BF16),
            ((mp_parts * heads, chunk, chunk), F32),
            ((n_tokens, head_cols), BF16),
            ((2, *square), BF16),
            (square, BF16),
            (square, BF16),
            ((keys, 2 * MODEL_WIDTH), BF16),
        ],
        tokens, gains, wq_self.T, wk_self.T, wv_self.T, wo_self, rel_bias.T, answer_lens,
        wk_cross.T, wv_cross.T, wq_cross.T, wo_cross, flat_encoded,
        spaces={6: smem, 7: smem, 12: pl.ANY},
        out_spaces={9: pl.ANY},
        scratch=[
            pltpu.VMEM(dealt, BF16),
            pltpu.VMEM((near, *home), BF16),
            pltpu.VMEM((keys, MODEL_WIDTH), BF16),
            pltpu.VMEM((2, keys // KV_STEPS, 2 * MODEL_WIDTH), BF16),
            many_sems(4, near),
            many_sems(4, near),
            pair_sems(near),
            pair_sems(far),
            many_sems(groups, near),
            pltpu.SemaphoreType.DMA((4,)),
            pltpu.SemaphoreType.DMA,
            pltpu.SemaphoreType.DMA((2,)),
        ],
    )
    a2_all = a2_all.reshape(groups, n_tokens, MODEL_WIDTH)

    def home_scratch(width):
        return [
            pltpu.VMEM((groups, near, chunk, width), BF16),
            pltpu.VMEM((groups, chunk, width), BF16),
            pltpu.VMEM((far, chunk, width), BF16),
            pltpu.VMEM((mp_parts, chunk, head_cols), BF16),
            many_sems(groups, near),
            pair_sems(far),
            pair_sems(near),
            pair_sems(near),
        ]

    partial = cross_forward(lens, owners, a2_all, wq_full, kv, mp_parts)
    h_two, a3, o2, o2_own, lse = remote_call(
        cross_out_kernel,
        1,
        [
            (home, F32),
            (dealt, BF16),
            (home, F32),
            ((mp_parts, chunk, head_cols), BF16),
            ((chunk, LANES), F32),
        ],
        partial, h_one, wo_full, gains,
        scratch=home_scratch(STATW),
    )
    term, ga3, gw_in, gw_out = local_call(
        ffn_kernel,
        [
            ((n_tokens, MODEL_WIDTH), BF16),
            ((n_tokens, MODEL_WIDTH), BF16),
            ((MODEL_WIDTH, hidden), BF16),
            ((hidden, MODEL_WIDTH), BF16),
        ],
        a3.reshape(n_tokens, MODEL_WIDTH), w_in, w_out, out_grad,
    )
    gw_in, gw_out = lax.psum((gw_in, gw_out), ("dp", "pass"))
    gh_two, gc_all, gain_ffn_grad = remote_call(
        ffn_back_kernel,
        2,
        [(home, F32), ((groups, mp_parts, chunk, STATW), BF16), ((1, MODEL_WIDTH), F32)],
        ga3.reshape(dealt), out_grad, h_two, gains, wo_full, o2, lse,
        scratch=[
            pltpu.VMEM((near, *home), BF16), pair_sems(near), pair_sems(far), many_sems(groups, near)
        ],
    )
    gq, gkv = cross_backward(
        lens, owners, a2_all, gc_all.reshape(groups, n_tokens, STATW), wq_full, wo_full, kv, mp_parts
    )
    rows = {"c": sum_rows(2 * half, groups), "k": sum_rows(2 * half, groups), "s": sum_rows(4 * half, groups)}
    small = pltpu.VMEM((16, MODEL_WIDTH), F32)
    own = (mp_parts, chunk, head_cols)
    step = keys // (KV_STEPS if groups <= KV_STEPS else 2 * KV_STEPS)
    hbm = pl.ANY
    pair = pltpu.SemaphoreType.DMA((2,))
    output, grad_tokens, sum_c, sum_k, sum_s, small_sums, genc = remote_call(
        functools.partial(finish_kernel, heads),
        3,
        [
            (dealt, BF16),
            (dealt, BF16),
            *[((2, groups * rows[k], MODEL_WIDTH), BF16) for k in "cks"],
            ((16, MODEL_WIDTH), F32),
            ((keys, MODEL_WIDTH), BF16),
        ],
        gq, gkv, flat_encoded, wkv.reshape(2 * MODEL_WIDTH, MODEL_WIDTH), gh_two, h_one, gains, wq_full,
        wq_self.T, wk_self.T, wv_self.T, wo_self, a1, qkv, p1, o1,
        a2_all.reshape(groups, *dealt), gc_all, o2_own, term.reshape(dealt), tokens, h_two, gain_ffn_grad,
        spaces={0: hbm, 1: hbm, 2: hbm, 16: hbm, 17: hbm},
        out_spaces={6: hbm},
        scratch=[
            pltpu.VMEM((groups, *home), BF16),
            pltpu.VMEM((groups, near, *home), BF16),
            pltpu.VMEM((far, *home), BF16),
            pltpu.VMEM((2, step, 2 * MODEL_WIDTH), BF16),
            pltpu.VMEM((2, step, MODEL_WIDTH), BF16),
            pltpu.VMEM((2, step, MODEL_WIDTH), BF16),
            pltpu.VMEM((2 * MODEL_WIDTH, MODEL_WIDTH), F32),
            pltpu.VMEM((2, mp_parts, head_cols, MODEL_WIDTH), BF16),
            pltpu.VMEM((2, head_cols, MODEL_WIDTH), BF16),
            pltpu.VMEM((4, head_cols, MODEL_WIDTH), BF16),
            pltpu.VMEM(own, BF16),
            pltpu.VMEM(own, BF16),
            pltpu.VMEM(dealt, BF16),
            pltpu.VMEM(dealt, BF16),
            pltpu.VMEM((3, n_tokens, head_cols), BF16),
            pltpu.VMEM((8, LANES), F32),
            pltpu.VMEM(dealt, BF16),
            pltpu.VMEM((mp_parts, chunk, STATW), BF16),
            pltpu.VMEM((near, *home), BF16),
            pltpu.VMEM((near, *home), BF16),
            pltpu.VMEM((2, mp_parts, half, MODEL_WIDTH), BF16),
            pltpu.VMEM((mp_parts, 2, half, MODEL_WIDTH), BF16),
            pltpu.VMEM((near, 2, half, MODEL_WIDTH), BF16),
            pltpu.VMEM((2, half, MODEL_WIDTH), BF16),
            pltpu.VMEM((4, half, MODEL_WIDTH), BF16),
            *[pltpu.VMEM((groups * rows[k], MODEL_WIDTH), BF16) for k in "cks"],
            *[pltpu.VMEM((far, rows[k], MODEL_WIDTH), BF16) for k in "cks"],
            small,
            small,
            pltpu.VMEM((groups, 16, MODEL_WIDTH), F32),
            pltpu.VMEM((mp_parts, 16, MODEL_WIDTH), F32),
            many_sems(groups, near),
            pair_sems(far),
            pair_sems(near),
            pair_sems(near),
            pltpu.SemaphoreType.DMA((3,)),
            pltpu.SemaphoreType.DMA((2, 2)),
            pair,
            pair_sems(near),
            pair_sems(near),
            pair,
            pair_sems(near),
            pair,
            pair,
            pair_sems(near),
            pair_sems(near),
            many_sems(3, far),
            many_sems(3, far),
            many_sems(3, far),
            pair,
            pair_sems(far),
            pair_sems(near),
        ],
    )
    grads = pl.pallas_call(
        widen_kernel,
        out_shape=[jax.ShapeDtypeStruct((head_cols, MODEL_WIDTH), F32)] * 8
        + [jax.ShapeDtypeStruct(gw_in.shape, F32), jax.ShapeDtypeStruct(gw_out.shape, F32)],
        in_specs=[pl.BlockSpec(memory_space=pltpu.VMEM)] * 5,
        out_specs=[pl.BlockSpec(memory_space=hbm)] * 10,
        scratch_shapes=[
            pltpu.VMEM((8, head_cols, MODEL_WIDTH), F32),
            pltpu.VMEM(gw_in.shape, F32),
            pltpu.VMEM(gw_out.shape, F32),
            pltpu.SemaphoreType.DMA((10,)),
        ],
        compiler_params=pltpu.CompilerParams(vmem_limit_bytes=VMEM_LIMIT),
    )(sum_c, sum_k, sum_s, gw_in, gw_out)

    return (
        output.reshape(n_tokens, MODEL_WIDTH),
        grad_tokens.reshape(n_tokens, MODEL_WIDTH),
        genc.reshape(GROUP_ROWS, quarter, MODEL_WIDTH),
        small_sums[0],
        small_sums[1],
        small_sums[2],
        small_sums[8 : 8 + heads, :BUCKETS].T,
        *[grads[i].T for i in range(3)],
        grads[3],
        *[grads[i].T for i in range(4, 7)],
        *grads[7:],
    )


def solution(mesh):
    tokens_in = P(("dp", "pass"), None)
    encoded_in = P(("dp", "pass"), "mp", None)
    by_column, by_row = P(None, "mp"), P("mp", None)
    weights = (by_column, by_column, by_column, by_row)
    return jax.shard_map(
        on_device,
        mesh=mesh,
        in_specs=(
            tokens_in, encoded_in, P("dp", None), P("dp", None), P(("dp", "pass")),
            P(), P(), P(), by_column,
            *weights, *weights, by_column, by_row, tokens_in,
        ),
        out_specs=(
            tokens_in, tokens_in, encoded_in, P(), P(), P(), by_column,
            *weights, *weights, by_column, by_row,
        ),
        check_vma=False,
    )
```

```python
import functools
import math

import jax
import jax.numpy as jnp
import numpy as np
from jax import lax
from jax.experimental import pallas as pl
from jax.experimental.pallas import tpu as pltpu
from jax.sharding import PartitionSpec as P

MODEL_WIDTH = 768
HD = 64
BUCKETS = 32
ANS = 20
PADT = 24
LANES = 128
STATW = MODEL_WIDTH + LANES
GROUP_ROWS = 32

EPSILON = 1e-06
NEGATIVE = -1e30
MESH = pl.DeviceIdType.MESH
VMEM_LIMIT = 61 << 20
F32 = jnp.float32
BF16 = jnp.bfloat16


def bucket_table(length, buckets):
    exact_half = buckets // 2
    result = np.zeros((length, length), np.int32)
    for target in range(length):
        for source in range(length):
            distance = max(target - source, 0)
            if distance < exact_half:
                result[target, source] = distance
            else:
                spread = int(
                    math.log(distance / exact_half)
                    / math.log(128 / exact_half)
                    * (buckets - exact_half)
                )
                result[target, source] = min(exact_half + spread, buckets - 1)
    return result


def dot_nn(a, b):
    return lax.dot_general(a, b, (((1,), (0,)), ((), ())), preferred_element_type=F32)


def dot_nt(a, b):
    return lax.dot_general(a, b, (((1,), (1,)), ((), ())), preferred_element_type=F32)


def dot_tn(a, b):
    return lax.dot_general(a, b, (((0,), (0,)), ((), ())), preferred_element_type=F32)


def rms_inverse(v):
    return lax.rsqrt(jnp.mean(v * v, axis=-1, keepdims=True) + EPSILON)


def rms_back(v, gains, ga):
    w = rms_inverse(v)
    gain_grad = jnp.sum(ga * v * w, axis=0, keepdims=True)
    gg = gains * ga
    gv = w * gg - v * (w * w * w) * jnp.mean(gg * v, axis=-1, keepdims=True)
    return gv, gain_grad


def local_call(kernel, outs, *ins, scratch=(), flops=0):
    return pl.pallas_call(
        kernel,
        out_shape=[jax.ShapeDtypeStruct(shape, dtype) for shape, dtype in outs],
        in_specs=[pl.BlockSpec(memory_space=pltpu.VMEM) for _ in ins],
        out_specs=[pl.BlockSpec(memory_space=pltpu.VMEM) for _ in outs],
        scratch_shapes=list(scratch),
        compiler_params=pltpu.CompilerParams(vmem_limit_bytes=VMEM_LIMIT),
        cost_estimate=pl.CostEstimate(
            flops=flops,
            bytes_accessed=sum(math.prod(x.shape) * x.dtype.itemsize for x in ins),
            transcendentals=0,
        ),
    )(*ins)


def place(**kw):
    return tuple(kw[a] if a in kw else lax.axis_index(a) for a in ("dp", "pass", "mp"))


def other(axis, k):
    n = lax.axis_size(axis)
    at = lax.rem(lax.axis_index(axis) + k, n)
    return at, place(**{axis: at})


def others(axis):
    return [(k - 1, *other(axis, k)) for k in range(1, lax.axis_size(axis))]


def greet(axes):
    barrier = pltpu.get_barrier_semaphore()
    peers = [peer for axis in axes for _, _, peer in others(axis)]
    for peer in peers:
        pl.semaphore_signal(barrier, inc=1, device_id=peer, device_id_type=MESH)
    pl.semaphore_wait(barrier, len(peers))


def remote(src, dst, send, recv, peer):
    return pltpu.make_async_remote_copy(
        src_ref=src, dst_ref=dst, send_sem=send, recv_sem=recv, device_id=peer, device_id_type=MESH
    )


def begin(copies):
    for copy in copies:
        copy.start()
    return copies


def finish(copies):
    for copy in copies:
        copy.wait()


def deal(source, slots, sems, axis):
    return begin([
        remote(source(at), slots.at[k], sems.at[0, k], sems.at[1, k], peer)
        for k, at, peer in others(axis)
    ])


def share(ref, sems, axis):
    return begin([remote(ref, ref, sems.at[0, k], sems.at[1, k], peer) for k, _, peer in others(axis)])


class Relay:
    def __init__(self, sems):
        self.sems, self.direct = sems, {}
        self.square = lax.axis_size("mp") == 4
        self.blocks, self.onward = {}, {}

    @staticmethod
    def near(which):
        mm = lax.axis_index("mp")
        at = mm + 1 - 2 * lax.rem(mm, 2) if which == 0 else mm + 2 - 4 * lax.div(mm, 2)
        return at, place(mp=at)

    def across(self):
        return 3 - lax.axis_index("mp")

    def put(self, i, block, own=None):
        mine = block(lax.axis_index("mp"))
        own = mine if own is None else own
        self.blocks[i] = block
        to = [(k, peer) for k, _, peer in others("mp")]
        if self.square:
            to = [(k, self.near(k)[1]) for k in range(2)]
        self.direct[i] = begin([
            remote(own, mine, self.sems.at[i, 0, k], self.sems.at[i, 1, k], peer) for k, peer in to
        ])

    def pass_on(self, i):
        if not self.square:
            return
        which = i % 2
        self.direct[i][which].wait_recv()
        block = self.blocks[i](self.near(which)[0])
        self.onward[i] = remote(
            block, block, self.sems.at[i, 0, 2], self.sems.at[i, 1, 2], self.near(1 - which)[1]
        )
        self.onward[i].start()

    def arrived(self, i):
        for k, copy in enumerate(self.direct[i]):
            if not self.square or k != i % 2:
                copy.wait_recv()
        if self.square:
            self.onward[i].wait_recv()

    def sent(self, i):
        for copy in self.direct[i]:
            copy.wait_send()
        if self.square:
            self.onward[i].wait_send()


def share_both(all_ref, zsems, msems):
    pn, pm, mm = lax.axis_size("pass"), lax.axis_index("pass"), lax.axis_index("mp")
    zcopies = share(all_ref.at[pm, mm], zsems, "pass")
    relay = Relay(msems)
    relay.put(0, lambda at: all_ref.at[pm, at])

    def forward(j):
        zcopies[j].wait_recv()
        source = lax.rem(pm - (j + 1) + pn, pn)
        relay.put(j + 1, lambda at: all_ref.at[source, at])
        relay.pass_on(j)

    def end():
        relay.pass_on(pn - 1)
        for j in range(pn):
            relay.arrived(j)
            relay.sent(j)
        for copy in zcopies:
            copy.wait_send()

    return forward, end


def pair_sems(n):
    return pltpu.SemaphoreType.DMA((2, n))


def many_sems(m, n):
    return pltpu.SemaphoreType.DMA((m, 2, n))


def remote_call(kernel, collective_id, outs, *ins, spaces=None, out_spaces=None, scratch=()):
    vmem = pltpu.VMEM
    spaces = spaces or {}
    out_spaces = out_spaces or {}
    return pl.pallas_call(
        kernel,
        out_shape=[jax.ShapeDtypeStruct(shape, dtype) for shape, dtype in outs],
        in_specs=[pl.BlockSpec(memory_space=spaces.get(i, vmem)) for i in range(len(ins))],
        out_specs=[pl.BlockSpec(memory_space=out_spaces.get(i, vmem)) for i in range(len(outs))],
        scratch_shapes=list(scratch),
        compiler_params=pltpu.CompilerParams(
            collective_id=collective_id, has_side_effects=True, vmem_limit_bytes=VMEM_LIMIT
        ),
    )(*ins)


def home_rows(ref, chunk):
    at = pl.multiple_of(lax.axis_index("mp") * chunk, 16)
    return ref[pl.ds(at, chunk), :]


def total_of(first, slots):
    total = first.astype(F32)
    for k in range(slots.shape[0]):
        total = total + slots[k].astype(F32)
    return total


def bucket_grid(size):
    row = lax.broadcasted_iota(jnp.int32, (size, size), 0)
    col = lax.broadcasted_iota(jnp.int32, (size, size), 1)
    near = (col <= row) & (lax.div(col, ANS) == lax.div(row, ANS))
    table = bucket_table(ANS, BUCKETS)
    grid = jnp.full((size, size), -1, jnp.int32)
    for distance in range(ANS):
        grid = jnp.where(near & (row - col == distance), int(table[distance, 0]), grid)
    return grid, near, sorted({int(b) for b in table.reshape(-1)})


def self_forward(
    heads, x_ref, gain_ref, wq_ref, wk_ref, wv_ref, wo_ref, bias_ref, lens_ref,
    a1_ref, qkv_ref, p_ref, o1_ref, term_ref,
):
    x = x_ref[...].astype(F32)
    a1 = (x * rms_inverse(x) * gain_ref[0:1, :]).astype(BF16)
    a1_ref[...] = a1
    for k, w_ref in enumerate((wq_ref, wk_ref, wv_ref)):
        qkv_ref[k] = dot_nt(a1, w_ref[...]).astype(BF16)
    blocks, size = term_ref.shape[0], term_ref.shape[1]
    grid, near, used = bucket_grid(size)
    biases = []
    for h in range(heads):
        bias = jnp.full((size, size), NEGATIVE, F32)
        for b in used:
            bias = jnp.where(grid == b, bias_ref[h, b], bias)
        biases.append(bias)
    lane = lax.broadcasted_iota(jnp.int32, (1, size), 1)
    for b in range(blocks):
        alive = jnp.zeros((1, size), jnp.int32)
        for q in range(size // ANS):
            inside = (lane >= q * ANS) & (lane < q * ANS + lens_ref[b * (size // ANS) + q])
            alive = jnp.where(inside, 1, alive)
        allowed = near & (alive > 0)
        rows = pl.ds(b * size, size)
        q, k, v = qkv_ref[0, rows, :], qkv_ref[1, rows, :], qkv_ref[2, rows, :]
        for h in range(heads):
            part = slice(h * HD, (h + 1) * HD)
            s = jnp.where(allowed, dot_nt(q[:, part], k[:, part]) + biases[h], NEGATIVE)
            e = jnp.exp(s - jnp.max(s, axis=-1, keepdims=True))
            p = e / jnp.sum(e, axis=-1, keepdims=True)
            p_ref[b * heads + h] = p
            o1_ref[rows, part] = dot_nn(p.astype(BF16), v[:, part]).astype(BF16)
    for b in range(blocks):
        term_ref[b] = dot_nn(o1_ref[pl.ds(b * size, size), :], wo_ref[...]).astype(BF16)


KV_STEPS = 8


def front_kernel(
    heads, x_ref, gain_ref, wq_ref, wk_ref, wv_ref, wo_ref, bias_ref, lens_ref,
    wkc_ref, wvc_ref, wqc_ref, woc_ref, enc_ref,
    a2_ref, h_ref, a1_ref, qkv_ref, p_ref, o1_ref, wkv_ref, wq_out_ref, wo_out_ref, kv_ref,
    term, slots, enc, kv_slots, wsems, dsems, rsems, zsems, msems, own_sems, enc_sem, kv_sems,
):
    core, mm, pm = lax.axis_index("dp"), lax.axis_index("mp"), lax.axis_index("pass")
    mn, pn = lax.axis_size("mp"), lax.axis_size("pass")
    width = wkc_ref.shape[0]
    half = width // 2
    chunk = h_ref.shape[0]
    load = pltpu.make_async_copy(enc_ref, enc, enc_sem)
    load.start()
    pieces = [
        (wkc_ref, wkv_ref.at[0]), (wvc_ref, wkv_ref.at[1]), (wqc_ref, wq_out_ref), (woc_ref, wo_out_ref)
    ]

    def rows_of(source, which):
        return pl.ds(pl.multiple_of(source * width + which * half, 16), half)

    mine = pl.ds(pl.multiple_of(core * half, 16), half)
    owns = []
    for i, (shard, full) in enumerate(pieces):
        at = pl.ds(pl.multiple_of(mm * width, 16), width)
        own = pltpu.make_async_copy(shard, full.at[at], own_sems.at[i])
        own.start()
        owns.append(own)
    greet(("dp", "pass", "mp"))

    relay = Relay(wsems)

    def send_weight(i):
        shard, full = pieces[i]
        relay.put(i, lambda at: full.at[rows_of(at, core)], shard.at[mine])

    def to_other_core(i):
        full = pieces[i][1]
        relay.arrived(i)
        return begin([
            remote(
                full.at[rows_of(at, core)], full.at[rows_of(at, core)],
                dsems.at[i, 0, k], dsems.at[i, 1, k], other("dp", 1)[1],
            )
            for k, at, _ in others("mp")
        ])

    send_weight(0)
    send_weight(1)
    self_forward(
        heads, x_ref, gain_ref, wq_ref, wk_ref, wv_ref, wo_ref, bias_ref, lens_ref,
        a1_ref, qkv_ref, p_ref, o1_ref, term,
    )
    dealt = deal(lambda at: term.at[at], slots, rsems, "mp")
    relay.pass_on(0)
    relay.pass_on(1)
    for copy in dealt:
        copy.wait_recv()
    h = home_rows(x_ref, chunk).astype(F32) + total_of(term[mm], slots)
    h_ref[...] = h
    a2_ref[pm, mm] = (h * rms_inverse(h) * gain_ref[1:2, :]).astype(BF16)
    forward, end = share_both(a2_ref, zsems, msems)
    send_weight(2)
    send_weight(3)
    passed = [to_other_core(0), to_other_core(1)]
    for copies in passed:
        for copy in copies:
            copy.wait_recv()
    for own in owns:
        own.wait()
    load.wait()
    rows = enc.shape[0] // KV_STEPS

    def store(step):
        slot = lax.rem(step, 2)
        at = pl.ds(pl.multiple_of(step * rows, rows), rows)
        return pltpu.make_async_copy(kv_slots.at[slot], kv_ref.at[at], kv_sems.at[slot])

    def project(step, carry):
        slot = lax.rem(step, 2)

        @pl.when(step >= 2)
        def _():
            store(step - 2).wait()

        x = enc[pl.ds(pl.multiple_of(step * rows, rows), rows), :]
        for i in range(2):
            kv_slots[slot, :, i * MODEL_WIDTH : (i + 1) * MODEL_WIDTH] = dot_nt(x, wkv_ref[i]).astype(BF16)
        store(step).start()
        return carry

    done, onward = 0, [2, 3]
    for j in range(pn - 1):
        upto = KV_STEPS * (j + 1) // (pn - 1)
        if upto > done:
            lax.fori_loop(done, upto, project, 0)
            done = upto
        forward(j)
        if onward:
            relay.pass_on(onward.pop(0))
    for i in onward:
        relay.pass_on(i)
    passed += [to_other_core(2), to_other_core(3)]
    for step in (KV_STEPS - 2, KV_STEPS - 1):
        store(step).wait()
    end()
    for copy in dealt:
        copy.wait_send()
    for i, copies in enumerate(passed):
        relay.sent(i)
        for copy in copies:
            copy.wait_send()
            if i >= 2:
                copy.wait_recv()


PAIR = 2 * HD
PAIRS = MODEL_WIDTH // PAIR
PROWS = 2 * PADT
FLOOR = -1e29


def low_lanes(shape):
    return lax.broadcasted_iota(jnp.int32, shape, len(shape) - 1) < HD


def pair_rows(dst_ref, pad_ref, values, stat=None, stat_at=0):
    questions = dst_ref.shape[0]
    low = low_lanes((1, PADT, PAIR))
    for q in range(questions):
        rows = slice(q * ANS, (q + 1) * ANS)
        pad_ref[q, 0:ANS, :MODEL_WIDTH] = values[rows, :]
        pad_ref[q, ANS:PADT, :] = jnp.zeros((PADT - ANS, pad_ref.shape[2]), F32)
        if stat is not None:
            pad_ref[q, 0:ANS, MODEL_WIDTH:] = stat[rows, :]
    lane = lax.broadcasted_iota(jnp.int32, (1, 1, LANES), 2)
    for c in range(PAIRS):
        x = pad_ref[:, :, c * PAIR : (c + 1) * PAIR]
        both = jnp.concatenate([jnp.where(low, x, 0.0), jnp.where(low, 0.0, x)], axis=1)
        dst_ref[:, c, :, :PAIR] = both.astype(BF16)
        if stat is not None:
            s = pad_ref[:, :, MODEL_WIDTH:]
            parts = []
            for h in (2 * c, 2 * c + 1):
                at = lane - (stat_at + h)
                parts.append(s * ((at == 0) | (at == 16) | (at == 32)).astype(F32))
            dst_ref[:, c, :, PAIR:] = jnp.concatenate(parts, axis=1).astype(BF16)


def segment_mask(lens_ref, row, keys):
    lane = lax.broadcasted_iota(jnp.int32, (PROWS, keys), 1)
    cut = lens_ref[0, row] - lax.axis_index("mp") * keys
    return [lane < cut, (lane >= cut) & (lane < cut + lens_ref[1, row])]


def masked(scores, mask):
    return jnp.concatenate(
        [jnp.where(mask[s], scores[s * PROWS : (s + 1) * PROWS], NEGATIVE) for s in range(2)], axis=0
    )


def fold_pair(x, s, low):
    at = s * PROWS
    return jnp.where(low, x[at : at + PADT], x[at + PADT : at + PROWS])


def split_three(x):
    hi = x.astype(BF16).astype(F32)
    mid = (x - hi).astype(BF16).astype(F32)
    return hi, mid, x - hi - mid


def staged(rows_per, stages):
    depth = len(stages)
    for i in range(rows_per + depth - 1):
        for k in reversed(range(depth)):
            if 0 <= i - k < rows_per:
                stages[k](i - k, (i - k) % 2)


def cross_forward_kernel(
    rows_per, keys, lens_ref, owners_ref, a2_ref, wq_ref, kv_ref, out_ref,
    q_rows, pad, s_buf, p_buf, t_buf, o_acc, m_acc, l_acc, flat,
):
    g = pl.program_id(0)
    pair_rows(q_rows, pad, dot_nt(a2_ref[0], wq_ref[...]).astype(BF16).astype(F32))
    o_acc[...] = jnp.zeros_like(o_acc)
    m_acc[...] = jnp.full_like(m_acc, FLOOR)
    l_acc[...] = jnp.zeros_like(l_acc)
    low = low_lanes((PADT, PAIR))
    ones = jnp.ones((keys, PAIR), BF16)

    def row_of(r):
        return lax.axis_index("pass") * GROUP_ROWS + g * rows_per + r

    def owners_of(r):
        return [owners_ref[0, row_of(r)], owners_ref[1, row_of(r)]]

    def scores(r, slot):
        owners = owners_of(r)
        mask = segment_mask(lens_ref, row_of(r), keys)
        for c in range(PAIRS):
            k = kv_ref[r * keys : (r + 1) * keys, c * PAIR : (c + 1) * PAIR]
            qm = jnp.concatenate([q_rows[q, c] for q in owners], axis=0)
            s_buf[slot, c] = masked(dot_nt(qm, k), mask)

    def chances(r, slot):
        for c in range(PAIRS):
            s = s_buf[slot, c]
            top = jnp.maximum(jnp.max(s, axis=-1, keepdims=True), FLOOR)
            p_buf[slot, c] = jnp.exp(s - top).astype(BF16)
            top = jnp.broadcast_to(top, (2 * PROWS, PAIR))
            for i in range(2):
                t_buf[slot, c, i] = fold_pair(top, i, low)

    def values(r, slot):
        owners = owners_of(r)
        new = []
        for c in range(PAIRS):
            v = kv_ref[r * keys : (r + 1) * keys, MODEL_WIDTH + c * PAIR : MODEL_WIDTH + (c + 1) * PAIR]
            both = dot_nn(p_buf[slot, c], jnp.concatenate([v, ones], axis=1))
            new.append([
                (fold_pair(both[:, :PAIR], i, low), fold_pair(both[:, PAIR:], i, low)) for i in range(2)
            ])
        for i, q in enumerate(owners):
            for c in range(PAIRS):
                cols = slice(c * PAIR, (c + 1) * PAIR)
                o, l = new[c][i]
                m_old, m_new = m_acc[q, :, cols], t_buf[slot, c, i]
                m_both = jnp.maximum(m_old, m_new)
                a, b = jnp.exp(m_old - m_both), jnp.exp(m_new - m_both)
                o_acc[q, :, cols] = a * o_acc[q, :, cols] + b * o
                l_acc[q, :, cols] = a * l_acc[q, :, cols] + b * l
                m_acc[q, :, cols] = m_both

    staged(rows_per, [scores, chances, values])
    questions = q_rows.shape[0]
    lane = lax.broadcasted_iota(jnp.int32, (PADT, LANES), 1)
    for q in range(questions):
        l = l_acc[q]
        some = l > 0.0
        safe = jnp.where(some, l, 1.0)
        o = o_acc[q] / safe
        lse = jnp.where(some, m_acc[q] + jnp.log(safe), NEGATIVE)
        few = jnp.zeros((PADT, LANES), F32)
        for h in range(MODEL_WIDTH // HD):
            few = jnp.where(lane == h, lse[:, h * HD : h * HD + 1], few)
        hi, mid, rest = split_three(few)
        stat = hi + pltpu.roll(mid, 16, 1) + pltpu.roll(rest, 32, 1)
        flat[q * ANS : (q + 1) * ANS, :MODEL_WIDTH] = o[:ANS]
        flat[q * ANS : (q + 1) * ANS, MODEL_WIDTH:] = stat[:ANS]
    chunk = out_ref.shape[2]
    for m in range(out_ref.shape[0]):
        out_ref[m, 0] = flat[m * chunk : (m + 1) * chunk, :].astype(BF16)


def cross_forward(lens, owners, a2_all, wq, kv, mp_parts):
    groups, n_tokens, _ = a2_all.shape
    rows_per = GROUP_ROWS // groups
    keys = kv.shape[0] // GROUP_ROWS
    questions = n_tokens // ANS
    block = rows_per * keys
    padded = pltpu.VMEM((questions, PADT, MODEL_WIDTH), F32)
    return pl.pallas_call(
        functools.partial(cross_forward_kernel, rows_per, keys),
        grid_spec=pltpu.PrefetchScalarGridSpec(
            num_scalar_prefetch=2,
            grid=(groups,),
            in_specs=[
                pl.BlockSpec((1, n_tokens, MODEL_WIDTH), lambda g, *_: (g, 0, 0)),
                pl.BlockSpec((MODEL_WIDTH, MODEL_WIDTH), lambda g, *_: (0, 0)),
                pl.BlockSpec((block, 2 * MODEL_WIDTH), lambda g, *_: (g, 0)),
            ],
            out_specs=pl.BlockSpec(
                (mp_parts, 1, n_tokens // mp_parts, STATW), lambda g, *_: (0, g, 0, 0)
            ),
            scratch_shapes=[
                pltpu.VMEM((questions, PAIRS, PROWS, PAIR), BF16),
                padded,
                pltpu.VMEM((2, PAIRS, 2 * PROWS, keys), F32),
                pltpu.VMEM((2, PAIRS, 2 * PROWS, keys), BF16),
                pltpu.VMEM((2, PAIRS, 2, PADT, PAIR), F32),
                padded,
                padded,
                padded,
                pltpu.VMEM((n_tokens, STATW), F32),
            ],
        ),
        out_shape=jax.ShapeDtypeStruct((mp_parts, groups, n_tokens // mp_parts, STATW), BF16),
        compiler_params=pltpu.CompilerParams(vmem_limit_bytes=VMEM_LIMIT),
    )(lens, owners, a2_all, wq, kv)


def cross_backward_kernel(
    rows_per, keys, lens_ref, owners_ref, a2_ref, gc_ref, wq_ref, wo_ref, kv_ref, gq_ref, gkv_ref,
    q_rows, go_rows, pad, s_buf, gp_buf, p_buf, gs_buf, gq_acc, flat,
):
    g = pl.program_id(0)
    stat = gc_ref[0, :, MODEL_WIDTH:].astype(F32)
    q2 = dot_nt(a2_ref[0], wq_ref[...]).astype(BF16).astype(F32)
    pair_rows(q_rows, pad, q2, stat, 0)
    go2 = dot_nt(gc_ref[0, :, :MODEL_WIDTH], wo_ref[...]).astype(BF16).astype(F32)
    pair_rows(go_rows, pad, go2, stat, 48)
    gq_acc[...] = jnp.zeros_like(gq_acc)
    low = low_lanes((PADT, PAIR))
    minus = jnp.full((keys, LANES), -1.0, BF16)

    def row_of(r):
        return lax.axis_index("pass") * GROUP_ROWS + g * rows_per + r

    def owners_of(r):
        return [owners_ref[0, row_of(r)], owners_ref[1, row_of(r)]]

    def tile(r, c, off):
        return kv_ref[r * keys : (r + 1) * keys, off + c * PAIR : off + (c + 1) * PAIR]

    def scores(r, slot):
        owners = owners_of(r)
        mask = segment_mask(lens_ref, row_of(r), keys)
        for c in range(PAIRS):
            qm = jnp.concatenate([q_rows[q, c] for q in owners], axis=0)
            gom = jnp.concatenate([go_rows[q, c] for q in owners], axis=0)
            s = dot_nt(qm, jnp.concatenate([tile(r, c, 0), minus], axis=1))
            s_buf[slot, c] = masked(s, mask)
            gp_buf[slot, c] = dot_nt(gom, jnp.concatenate([tile(r, c, MODEL_WIDTH), minus], axis=1))

    def chances(r, slot):
        for c in range(PAIRS):
            p = jnp.exp(s_buf[slot, c])
            p_buf[slot, c] = p.astype(BF16)
            gs_buf[slot, c] = (p * gp_buf[slot, c]).astype(BF16)

    def grads(r, slot):
        owners = owners_of(r)
        new = []
        rows = slice(r * keys, (r + 1) * keys)
        for c in range(PAIRS):
            gs, p = gs_buf[slot, c], p_buf[slot, c]
            qm = jnp.concatenate([q_rows[q, c, :, :PAIR] for q in owners], axis=0)
            gom = jnp.concatenate([go_rows[q, c, :, :PAIR] for q in owners], axis=0)
            gkv_ref[rows, c * PAIR : (c + 1) * PAIR] = dot_tn(gs, qm).astype(BF16)
            gkv_ref[rows, MODEL_WIDTH + c * PAIR : MODEL_WIDTH + (c + 1) * PAIR] = dot_tn(p, gom).astype(BF16)
            gq = dot_nn(gs, tile(r, c, 0))
            new.append([fold_pair(gq, i, low) for i in range(2)])
        for i, q in enumerate(owners):
            for c in range(PAIRS):
                cols = slice(c * PAIR, (c + 1) * PAIR)
                gq_acc[q, :, cols] = gq_acc[q, :, cols] + new[c][i]

    staged(rows_per, [scores, chances, grads])
    for q in range(q_rows.shape[0]):
        flat[q * ANS : (q + 1) * ANS, :] = gq_acc[q, :ANS, :]
    chunk = gq_ref.shape[2]
    for m in range(gq_ref.shape[0]):
        gq_ref[m, 0] = flat[m * chunk : (m + 1) * chunk, :].astype(BF16)


def cross_backward(lens, owners, a2_all, gc_all, wq, wo, kv, mp_parts):
    groups, n_tokens, _ = a2_all.shape
    rows_per = GROUP_ROWS // groups
    keys = kv.shape[0] // GROUP_ROWS
    questions = n_tokens // ANS
    block = rows_per * keys
    rows = pltpu.VMEM((questions, PAIRS, PROWS, PAIR + LANES), BF16)
    whole = pl.BlockSpec((MODEL_WIDTH, MODEL_WIDTH), lambda g, *_: (0, 0))
    return pl.pallas_call(
        functools.partial(cross_backward_kernel, rows_per, keys),
        grid_spec=pltpu.PrefetchScalarGridSpec(
            num_scalar_prefetch=2,
            grid=(groups,),
            in_specs=[
                pl.BlockSpec((1, n_tokens, MODEL_WIDTH), lambda g, *_: (g, 0, 0)),
                pl.BlockSpec((1, n_tokens, STATW), lambda g, *_: (g, 0, 0)),
                whole,
                whole,
                pl.BlockSpec((block, 2 * MODEL_WIDTH), lambda g, *_: (g, 0)),
            ],
            out_specs=[
                pl.BlockSpec(
                    (mp_parts, 1, n_tokens // mp_parts, MODEL_WIDTH), lambda g, *_: (0, g, 0, 0)
                ),
                pl.BlockSpec((block, 2 * MODEL_WIDTH), lambda g, *_: (g, 0)),
            ],
            scratch_shapes=[
                rows,
                rows,
                pltpu.VMEM((questions, PADT, STATW), F32),
                pltpu.VMEM((2, PAIRS, 2 * PROWS, keys), F32),
                pltpu.VMEM((2, PAIRS, 2 * PROWS, keys), F32),
                pltpu.VMEM((2, PAIRS, 2 * PROWS, keys), BF16),
                pltpu.VMEM((2, PAIRS, 2 * PROWS, keys), BF16),
                pltpu.VMEM((questions, PADT, MODEL_WIDTH), F32),
                pltpu.VMEM((n_tokens, MODEL_WIDTH), F32),
            ],
        ),
        out_shape=[
            jax.ShapeDtypeStruct((mp_parts, groups, n_tokens // mp_parts, MODEL_WIDTH), BF16),
            jax.ShapeDtypeStruct(kv.shape, BF16),
        ],
        compiler_params=pltpu.CompilerParams(vmem_limit_bytes=VMEM_LIMIT),
    )(lens, owners, a2_all, gc_all, wq, wo, kv)


def widen(w):
    row = lax.broadcasted_iota(jnp.int32, (LANES, MODEL_WIDTH), 0)
    col = lax.broadcasted_iota(jnp.int32, (LANES, MODEL_WIDTH), 1)
    each = (row == lax.div(col, HD)).astype(BF16)
    hi = w.astype(BF16)
    low = (w - hi.astype(F32)).astype(BF16)
    return dot_nn(hi, each) + dot_nn(low, each)


def combined(parts):
    lses = []
    for part in parts:
        stat = part[:, MODEL_WIDTH:].astype(F32)
        lses.append(stat + pltpu.roll(stat, LANES - 16, 1) + pltpu.roll(stat, LANES - 32, 1))
    top = functools.reduce(jnp.maximum, lses)
    weights = [jnp.exp(x - top) for x in lses]
    total = functools.reduce(jnp.add, weights)
    out = 0.0
    for part, weight in zip(parts, weights):
        out = out + widen(weight / total) * part[:, :MODEL_WIDTH].astype(F32)
    lane = lax.broadcasted_iota(jnp.int32, total.shape, 1)
    lse = jnp.where(lane < MODEL_WIDTH // HD, top + jnp.log(total), 0.0)
    return out, lse


def packed_stat(lse, at=0):
    hi, mid, low = split_three(lse)
    parts = [hi if at == 0 else pltpu.roll(hi, at, 1)]
    parts += [pltpu.roll(mid, at + 16, 1), pltpu.roll(low, at + 32, 1)]
    return parts[0] + parts[1] + parts[2]


def deal_groups(source, slots, sems):
    pn, pm = lax.axis_size("pass"), lax.axis_index("pass")
    for step in range(pn):
        group = lax.rem(pm + 1 + step, pn)
        deal(lambda at: source.at[at, group], slots.at[step], sems.at[step], "mp")


def groups_home(source, slots, held, zslots, msems, zsems, add):
    pn, pm, mm = lax.axis_size("pass"), lax.axis_index("pass"), lax.axis_index("mp")

    def arrived(step):
        group = lax.rem(pm + 1 + step, pn)
        for k, at, peer in others("mp"):
            remote(
                source.at[at, group], slots.at[step, k], msems.at[step, 0, k], msems.at[step, 1, k], peer
            ).wait()
        held[step] = add([source[mm, group]] + [slots[step, k] for k in range(slots.shape[1])])

    def to_home(step):
        at, peer = other("pass", step + 1)
        return remote(
            held.at[step], zslots.at[step], zsems.at[0, step], zsems.at[1, step], peer
        )

    def one(step, carry):
        arrived(step)
        to_home(step).start()
        return carry

    if pn <= 4:
        for step in range(pn - 1):
            one(step, 0)
    else:
        lax.fori_loop(0, pn - 1, one, 0)
    arrived(pn - 1)
    for step in range(pn - 1):
        to_home(step).wait()
    return [held[pn - 1]] + [zslots[k] for k in range(pn - 1)]


def cross_out_kernel(
    part_ref, h_ref, wo_ref, gain_ref, h2_ref, a3_ref, o_ref, own_ref, lse_ref,
    slots, held, zslots, blocks, msems, zsems, asems, bsems,
):
    mm = lax.axis_index("mp")
    greet(("pass", "mp"))
    deal_groups(part_ref, slots, msems)

    def add(parts):
        out, lse = combined(parts)
        return jnp.concatenate([out, packed_stat(lse)], axis=1).astype(BF16)

    o, lse = combined(groups_home(part_ref, slots, held, zslots, msems, zsems, add))
    low = o.astype(BF16)
    h = h_ref[...] + dot_nn(low, wo_ref[...])
    a3_ref[mm] = (h * rms_inverse(h) * gain_ref[2:3, :]).astype(BF16)
    copies = share(a3_ref.at[mm], asems, "mp")
    h2_ref[...] = h
    o_ref[...] = o
    lse_ref[...] = lse
    width = blocks.shape[2]
    for k in range(blocks.shape[0]):
        blocks[k] = low[:, k * width : (k + 1) * width]
    own_ref[mm] = blocks[mm]
    copies += begin([
        remote(blocks.at[at], own_ref.at[mm], bsems.at[0, k], bsems.at[1, k], peer)
        for k, at, peer in others("mp")
    ])
    finish(copies)


def ffn_back_kernel(
    ga_ref, gy_ref, h_ref, gain_ref, wo_ref, o_ref, lse_ref, gw_ref, gh_ref, gc_ref, gain_out_ref, *refs
):
    pieces, (slots, gw_slot, y, rsems, zsems, msems, gw_sems) = refs[:-7], refs[-7:]
    pn, core = lax.axis_size("pass"), lax.axis_index("dp")
    mm, pm = lax.axis_index("mp"), lax.axis_index("pass")
    greet(("dp", "pass", "mp"))
    dealt = deal(lambda at: ga_ref.at[at], slots, rsems, "mp")
    swapped = remote(gw_ref.at[1 - core], gw_slot, gw_sems.at[0], gw_sems.at[1], other("dp", 1)[1])
    swapped.start()
    finish(dealt)
    gv, gain_grad = rms_back(h_ref[...], gain_ref[2:3, :], total_of(ga_ref[mm], slots))
    gain_out_ref[...] = gain_grad
    gh = home_rows(gy_ref, h_ref.shape[0]).astype(F32) + gv
    gh_ref[...] = gh
    gc = gh.astype(BF16)
    go = dot_nt(gc, wo_ref[...]).astype(BF16).astype(F32)
    row = lax.broadcasted_iota(jnp.int32, (MODEL_WIDTH, LANES), 0)
    col = lax.broadcasted_iota(jnp.int32, (MODEL_WIDTH, LANES), 1)
    each = (lax.div(row, HD) == col).astype(F32)
    delta = lax.dot_general(
        go * o_ref[...], each, (((1,), (0,)), ((), ())),
        preferred_element_type=F32, precision=lax.Precision.HIGHEST,
    )
    stat = packed_stat(lse_ref[...]) + packed_stat(delta, 48)
    gc_ref[pm, mm] = jnp.concatenate([gc, stat.astype(BF16)], axis=1)
    forward, end = share_both(gc_ref, zsems, msems)
    swapped.wait()
    used = gw_slot.shape[0]
    y[0:used, :] = (gw_ref[core].astype(F32) + gw_slot[...].astype(F32)).astype(BF16)
    fill_tail(y, used)
    rows = pieces[0].shape[0]
    for k, piece in enumerate(pieces):
        piece[...] = y[pl.ds(pl.multiple_of(lax.rem(pm + k, pn) * rows, 16), rows), :]
    for j in range(pn - 1):
        forward(j)
    end()


def sum_rows(rows, groups):
    return -(-rows // (groups * 16)) * 16


class GroupSum:
    def __init__(self, y, zslots, out, sems):
        self.y, self.zslots, self.out, self.sems = y, zslots, out, sems
        self.rows = zslots.shape[1]

    def part(self, at):
        return pl.ds(pl.multiple_of(at * self.rows, 16), self.rows)

    def dealing(self):
        return [
            remote(self.y.at[self.part(at)], self.zslots.at[k], self.sems.at[0, 0, k], self.sems.at[0, 1, k], peer)
            for k, at, peer in others("pass")
        ]

    def sharing(self):
        here = self.out.at[lax.axis_index("dp"), self.part(lax.axis_index("pass"))]
        return [
            remote(here, here, self.sems.at[1, 0, k], self.sems.at[1, 1, k], peer)
            for k, _, peer in others("pass")
        ]

    def swapping(self):
        here = self.out.at[lax.axis_index("dp")]
        return [remote(here, here, self.sems.at[2, 0, 0], self.sems.at[2, 1, 0], other("dp", 1)[1])]

    def spread(self):
        begin(self.dealing())

    def gather(self):
        finish(self.dealing())
        at = self.part(lax.axis_index("pass"))
        total = total_of(self.y[at, :], self.zslots)
        self.out[lax.axis_index("dp"), at, :] = total.astype(BF16)
        begin(self.sharing())

    def swap(self):
        finish(self.sharing())
        begin(self.swapping())

    def end(self):
        finish(self.swapping())


def fill_tail(y, used):
    if y.shape[0] > used:
        y[used:, :] = jnp.zeros((y.shape[0] - used, y.shape[1]), y.dtype)


def self_backward(
    heads, gsa, wq_ref, wk_ref, wv_ref, wo_ref, qkv_ref, p_ref, ga1_ref, gqkv_ref, bias_ref
):
    go1 = dot_nt(gsa, wo_ref[...]).astype(BF16)
    blocks, size = ga1_ref.shape[0], ga1_ref.shape[1]
    grid, _, used = bucket_grid(size)
    at_row = lax.broadcasted_iota(jnp.int32, bias_ref.shape, 0)
    at_lane = lax.broadcasted_iota(jnp.int32, bias_ref.shape, 1)
    totals = []
    for h in range(heads):
        part = slice(h * HD, (h + 1) * HD)
        total = jnp.zeros((size, size), F32)
        for b in range(blocks):
            rows = pl.ds(b * size, size)
            q, k, v = qkv_ref[0, rows, part], qkv_ref[1, rows, part], qkv_ref[2, rows, part]
            p = p_ref[b * heads + h]
            go = go1[b * size : (b + 1) * size, part]
            gp = dot_nt(go, v)
            gs = (p * (gp - jnp.sum(gp * p, axis=-1, keepdims=True))).astype(BF16)
            total = total + gs.astype(F32)
            gqkv_ref[0, rows, part] = dot_nn(gs, k).astype(BF16)
            gqkv_ref[1, rows, part] = dot_tn(gs, q).astype(BF16)
            gqkv_ref[2, rows, part] = dot_tn(p.astype(BF16), go).astype(BF16)
        totals.append(total)
    ga1 = dot_nn(gqkv_ref[0], wq_ref[...])
    ga1 = ga1 + dot_nn(gqkv_ref[1], wk_ref[...])
    ga1 = ga1 + dot_nn(gqkv_ref[2], wv_ref[...])
    for b in range(blocks):
        ga1_ref[b] = ga1[b * size : (b + 1) * size].astype(BF16)

    def bias_sums():
        bias = jnp.zeros(bias_ref.shape, F32)
        for h, total in enumerate(totals):
            for b in used:
                value = jnp.sum(jnp.where(grid == b, total, 0.0), keepdims=True)
                bias = jnp.where((at_row == h) & (at_lane == b), value, bias)
        bias_ref[...] = bias

    return bias_sums


def finish_kernel(
    heads, gq_ref, gkv_ref, enc_ref, wkv_ref, gh2_ref, h_ref, gain_ref, wq_ref,
    ws_q_ref, ws_k_ref, ws_v_ref, ws_o_ref, a1_ref, qkv_ref, p_ref, o1_ref,
    a2_ref, gc_ref, o2_ref, x_ref, ffn_gain_ref, term_ref, h2_ref, *refs,
):
    count = lax.axis_size("pass")
    gw_parts, refs = refs[:count], refs[count:]
    (
    gx_ref, out_ref, sum_k_ref, sum_c_ref, sum_s_ref, small_ref, sum_f_ref, genc_ref,
    held, slots, zslots, gkv_in, enc_in, genc_out, gw_acc, gw_kv, gw_o, gw_c, gw_s, gh1,
    blocks, gq_own, gsa_all, ga1, gqkv, bias, a2_own, gc_own,
    ga_slots, term_slots, kv_core, kv_slots, core_o, core_c, core_s,
    y_k, y_c, y_s, z_k, z_c, z_s, small, small_dp, small_z, small_m,
    msems, gzsems, asems, bsems, load_sems, in_sems, genc_sems,
    ga_sems, term_sems, out_sems, kv_dsems, kv_msems, co_sems, cc_sems, cs_sems, gx_sems,
    zk_sems, zc_sems, zs_sems, sd_sems, sz_sems, sm_sems,
    f_sems,
    ) = refs
    core, mm, pm = lax.axis_index("dp"), lax.axis_index("mp"), lax.axis_index("pass")
    pn = lax.axis_size("pass")
    chunk = h_ref.shape[0]
    width = o1_ref.shape[1]
    half = width // 2
    mine = pl.ds(pl.multiple_of(core * half, 16), half)
    theirs = pl.ds(pl.multiple_of((1 - core) * half, 16), half)
    peer = other("dp", 1)[1]
    loads = begin([
        pltpu.make_async_copy(gq_ref.at[mm], held, load_sems.at[0]),
        pltpu.make_async_copy(a2_ref.at[pm], a2_own, load_sems.at[1]),
        pltpu.make_async_copy(gc_ref.at[pm], gc_own, load_sems.at[2]),
    ])
    rows = gkv_in.shape[1]
    steps = gkv_ref.shape[0] // rows

    def step_rows(step):
        return pl.ds(pl.multiple_of(step * rows, rows), rows)

    def fetch_gkv(step, slot):
        return pltpu.make_async_copy(gkv_ref.at[step_rows(step)], gkv_in.at[slot], in_sems.at[slot, 0])

    def fetch_enc(step, slot):
        return pltpu.make_async_copy(enc_ref.at[step_rows(step)], enc_in.at[slot], in_sems.at[slot, 1])

    def store(step, slot):
        return pltpu.make_async_copy(genc_out.at[slot], genc_ref.at[step_rows(step)], genc_sems.at[slot])

    fetch_gkv(0, 0).start()
    fetch_enc(0, 0).start()
    greet(("dp", "pass", "mp"))
    for step in range(pn):
        group = lax.rem(pm + 1 + step, pn)
        deal(lambda at: gq_ref.at[at, group], slots.at[step], msems.at[step], "mp")
    finish(loads)

    def to_home(step):
        at, to = other("pass", step + 1)
        return remote(held.at[at], zslots.at[step], gzsems.at[0, step], gzsems.at[1, step], to)

    def arrived(step, carry):
        group = lax.rem(pm + 1 + step, pn)
        for k, at, to in others("mp"):
            remote(
                gq_ref.at[at, group], slots.at[step, k], msems.at[step, 0, k], msems.at[step, 1, k], to
            ).wait()
        total = held[group].astype(F32)
        for k in range(slots.shape[1]):
            total = total + slots[step, k].astype(F32)
        held[group] = total.astype(BF16)

        @pl.when(step < pn - 1)
        def _():
            to_home(step).start()

        return carry

    def arrivals(step):
        last = steps * 13 // 8
        lax.fori_loop(
            lax.min(lax.div(step * pn, last), pn), lax.min(lax.div((step + 1) * pn, last), pn), arrived, 0
        )

    parts = blocks.shape[0]

    def both_cores(copy, gw, got, y, first=0):
        copy.wait()
        for i in range(gw.shape[0]):
            at = pl.ds(pl.multiple_of(lax.axis_index("dp") * half, 16), half)
            to = (first + i) * half
            y[to : to + half, :] = (gw[i, at, :].astype(F32) + got[i].astype(F32)).astype(BF16)
        fill_tail(y, (first + gw.shape[0]) * half)

    total = gw_parts[0][...].astype(F32)
    for part in gw_parts[1:]:
        total = total + part[...].astype(F32)
    f_rows = pl.ds(pl.multiple_of(pm * total.shape[0], 16), total.shape[0])
    sum_f_ref[core, f_rows, :] = total.astype(BF16)
    f_copies = share(sum_f_ref.at[core, f_rows], f_sems.at[0], "pass")
    total = jnp.zeros((width, MODEL_WIDTH), F32)
    for k in range(parts):
        total = total + dot_tn(o2_ref[k], gc_own[k, :, :MODEL_WIDTH])
    gw_o[0] = total.astype(BF16)

    def core_copy(gw, got, sems):
        to = other("dp", 1)[1]
        off = pl.multiple_of((1 - lax.axis_index("dp")) * half, 16)
        where = (slice(None),) * (len(gw.shape) - 2) + (pl.ds(off, half),)
        return remote(gw.at[where], got, sems.at[0], sems.at[1], to)

    core_copy(gw_o, core_o, co_sems).start()
    gw_acc[...] = jnp.zeros_like(gw_acc)

    def weights(step, carry):
        slot = lax.rem(step, 2)

        @pl.when(step + 1 < steps)
        def _():
            fetch_gkv(step + 1, 1 - slot).start()
            fetch_enc(step + 1, 1 - slot).start()

        fetch_gkv(step, slot).wait()
        fetch_enc(step, slot).wait()
        for i in range(2):
            part = slice(i * MODEL_WIDTH, (i + 1) * MODEL_WIDTH)
            gw_acc[part, :] += dot_tn(gkv_in[slot, :, part], enc_in[slot])
        arrivals(step)

        @pl.when(step == 1)
        def _():
            both_cores(core_copy(gw_o, core_o, co_sems), gw_o, core_o, y_k, 2)

        return carry

    lax.fori_loop(0, steps, weights, 0)
    fetch_gkv(0, 0).start()
    for i in range(2):
        for k in range(parts):
            at = (i * parts + k) * width
            gw_kv[i, k] = gw_acc[at : at + width, :].astype(BF16)
    core_copy(gw_kv, kv_core, kv_dsems).start()

    def mine_rows():
        return pl.ds(pl.multiple_of(lax.axis_index("dp") * half, 16), half)

    def kv_copies():
        return [
            remote(gw_kv.at[:, at, mine_rows()], kv_slots.at[k], kv_msems.at[0, k], kv_msems.at[1, k], to)
            for k, at, to in others("mp")
        ]

    def encodings(step, carry):
        slot = lax.rem(step, 2)

        @pl.when(step + 1 < steps)
        def _():
            fetch_gkv(step + 1, 1 - slot).start()

        fetch_gkv(step, slot).wait()

        @pl.when(step >= 2)
        def _():
            store(step - 2, slot).wait()

        genc_out[slot] = dot_nn(gkv_in[slot], wkv_ref[...]).astype(BF16)
        store(step, slot).start()
        arrivals(steps + step)

        @pl.when(step == 1)
        def _():
            core_copy(gw_kv, kv_core, kv_dsems).wait()
            at = pl.ds(pl.multiple_of(lax.axis_index("dp") * half, 16), half)
            for i in range(2):
                for k in range(parts):
                    gw_kv[i, k, at, :] = (gw_kv[i, k, at, :].astype(F32) + kv_core[i, k].astype(F32)).astype(BF16)
            begin(kv_copies())

        @pl.when(step == steps - 2)
        def _():
            for at in range(pn - 1):
                to_home(at).wait()
            low = total_of(held[pm], zslots).astype(BF16)
            gv, cross_gain = rms_back(h_ref[...], gain_ref[1:2, :], dot_nn(low, wq_ref[...]))
            gh = gh2_ref[...] + gv
            gh1[...] = gh
            gsa_all[mm] = gh.astype(BF16)
            begin(gsa_copies())
            small[...] = jnp.zeros_like(small)
            small[1:2, :] = cross_gain
            for k in range(parts):
                blocks[k] = low[:, k * width : (k + 1) * width]
            gq_own[mm] = blocks[mm]
            begin(block_copies())

        return carry

    def gsa_copies():
        here = gsa_all.at[mm]
        return [remote(here, here, asems.at[0, k], asems.at[1, k], to) for k, _, to in others("mp")]

    def block_copies():
        return [
            remote(blocks.at[at], gq_own.at[mm], bsems.at[0, k], bsems.at[1, k], to)
            for k, at, to in others("mp")
        ]

    lax.fori_loop(0, steps, encodings, 0)
    finish(f_copies)
    f_copies = share(sum_f_ref.at[core], f_sems.at[1], "dp")
    for step in (steps - 2, steps - 1):
        store(step, step % 2).wait()
    finish(block_copies())
    total = jnp.zeros((width, MODEL_WIDTH), F32)
    for k in range(parts):
        total = total + dot_tn(gq_own[k], a2_own[k])
    gw_c[0] = total.astype(BF16)
    finish(kv_copies())
    for i in range(2):
        total = gw_kv[i, mm, mine, :].astype(F32)
        for k in range(kv_slots.shape[0]):
            total = total + kv_slots[k, i].astype(F32)
        y_k[i * half : (i + 1) * half, :] = total.astype(BF16)
    sum_k = GroupSum(y_k, z_k, sum_k_ref, zk_sems)
    sum_k.spread()
    finish(gsa_copies())
    gsa = jnp.concatenate([gsa_all[k] for k in range(parts)], axis=0)
    gw_c[1] = dot_tn(o1_ref[...], gsa).astype(BF16)
    core_copy(gw_c, core_c, cc_sems).start()
    bias_sums = self_backward(
        heads, gsa, ws_q_ref, ws_k_ref, ws_v_ref, ws_o_ref, qkv_ref, p_ref, ga1, gqkv, bias
    )
    ga_copies = deal(lambda at: ga1.at[at], ga_slots, ga_sems, "mp")
    sum_c = GroupSum(y_c, z_c, sum_c_ref, zc_sems)
    both_cores(core_copy(gw_c, core_c, cc_sems), gw_c, core_c, y_c)
    sum_c.spread()
    for k in range(3):
        gw_s[k] = dot_tn(gqkv[k], a1_ref[...]).astype(BF16)
    core_copy(gw_s, core_s, cs_sems).start()
    bias_sums()
    sum_s = GroupSum(y_s, z_s, sum_s_ref, zs_sems)
    both_cores(core_copy(gw_s, core_s, cs_sems), gw_s, core_s, y_s)
    sum_s.spread()
    finish(ga_copies)
    gv, self_gain = rms_back(
        home_rows(x_ref, chunk).astype(F32), gain_ref[0:1, :], total_of(ga1[mm], ga_slots)
    )
    gx_ref[mm] = (gh1[...] + gv).astype(BF16)
    gx_copies = share(gx_ref.at[mm], gx_sems, "mp")
    term_copies = deal(lambda at: term_ref.at[at], term_slots, term_sems, "mp")
    small[0:1, :] = self_gain
    small[2:3, :] = ffn_gain_ref[...]
    small[8:16, :LANES] = bias[...]
    sd = begin([remote(small, small_dp, sd_sems.at[0], sd_sems.at[1], peer)])
    sum_k.gather()
    sum_c.gather()
    finish(sd)
    small_z[pm] = small[...] + small_dp[...]
    sz = share(small_z.at[pm], sz_sems, "pass")
    sum_s.gather()
    finish(term_copies)
    out_ref[mm] = (h2_ref[...] + total_of(term_ref[mm], term_slots)).astype(BF16)
    out_copies = share(out_ref.at[mm], out_sems, "mp")
    finish(sz)
    total = small_z[0]
    for k in range(1, small_z.shape[0]):
        total = total + small_z[k]
    small_m[mm] = total
    sm = share(small_m.at[mm], sm_sems, "mp")
    sum_c.swap()
    finish(sm)
    gains = small_m[0]
    for k in range(1, small_m.shape[0]):
        gains = gains + small_m[k]
    small_ref[0:8, :] = gains[0:8]
    small_ref[8:16, :] = total[8:16]
    finish(gx_copies)
    sum_s.swap()
    sum_k.swap()
    finish(out_copies)
    finish(f_copies)
    sum_c.end()
    sum_s.end()
    sum_k.end()


def closing_kernel(
    k_ref, c_ref, s_ref, ffn_ref, small_ref, genc_ref, y_ref, gx_ref, *refs
):
    outs, (wide, wide_in, wide_out, sems) = refs[:17], refs[17:]
    half = wide.shape[1] // 2
    moves = [(genc_ref, outs[2]), (y_ref, outs[0]), (gx_ref, outs[1])]
    copies = begin([pltpu.make_async_copy(src, dst, sems.at[n]) for n, (src, dst) in enumerate(moves)])
    sources = [(s_ref, 0), (s_ref, 1), (s_ref, 2), (c_ref, 1), (c_ref, 0), (k_ref, 0), (k_ref, 1), (k_ref, 2)]
    for n, (ref, i) in enumerate(sources):
        for core in range(2):
            wide[n, core * half : (core + 1) * half, :] = ref[core, i * half : (i + 1) * half, :].astype(F32)
        copies += begin([pltpu.make_async_copy(wide.at[n], outs[7 + n], sems.at[3 + n])])
    for n, buffer in enumerate((wide_in, wide_out)):
        buffer[...] = ffn_ref[n, 0 : buffer.shape[0], :].astype(F32)
        copies += begin([pltpu.make_async_copy(buffer, outs[15 + n], sems.at[11 + n])])
    for n in range(3):
        outs[3 + n][...] = small_ref[n, :]
    heads, buckets = outs[6].shape
    outs[6][...] = small_ref[8 : 8 + heads, 0:buckets]
    finish(copies)


def ffn_kernel(a3_ref, w_in_ref, w_out_ref, gy_ref, term_ref, ga3_ref, gw_ref):
    a3, gy = a3_ref[...], gy_ref[...]
    u = dot_nn(a3, w_in_ref[...])
    cdf = 0.5 * (1.0 + lax.erf(u * np.float32(math.sqrt(0.5))))
    pdf = np.float32(1.0 / math.sqrt(2.0 * math.pi)) * jnp.exp(-0.5 * u * u)
    e = (u * cdf).astype(BF16)
    term_ref[...] = dot_nn(e, w_out_ref[...]).astype(BF16)
    ge = dot_nt(gy, w_out_ref[...]).astype(BF16).astype(F32)
    gu = (ge * (cdf + u * pdf)).astype(BF16)
    ga3_ref[...] = dot_nt(gu, w_in_ref[...]).astype(BF16)
    gw_ref[0] = dot_tn(a3, gu).astype(BF16)
    gw_ref[1] = dot_tn(e, gy).astype(BF16)


def on_device(
    tokens,
    encoded,
    seg_lens,
    owners,
    answer_lens,
    gain_self,
    gain_cross,
    gain_ffn,
    rel_bias,
    wq_self,
    wk_self,
    wv_self,
    wo_self,
    wq_cross,
    wk_cross,
    wv_cross,
    wo_cross,
    w_in,
    w_out,
    out_grad,
):
    groups, mp_parts = lax.axis_size("pass"), lax.axis_size("mp")
    heads = rel_bias.shape[1]
    head_cols = heads * HD
    half = head_cols // 2
    quarter = encoded.shape[1]
    n_tokens = tokens.shape[0]
    chunk = n_tokens // mp_parts
    assert w_in.shape == (MODEL_WIDTH, MODEL_WIDTH)
    rows_f = sum_rows(MODEL_WIDTH, groups)
    keys = GROUP_ROWS * quarter
    near, far = mp_parts - 1, groups - 1
    gains = jnp.stack([gain_self, gain_cross, gain_ffn])

    lens, owners = seg_lens.T, owners.T
    flat_encoded = encoded.reshape(keys, MODEL_WIDTH)
    home = (chunk, MODEL_WIDTH)
    dealt = (mp_parts, chunk, MODEL_WIDTH)
    square = (MODEL_WIDTH, MODEL_WIDTH)
    smem = pltpu.SMEM
    a2_all, h_one, a1, qkv, p1, o1, wkv, wq_full, wo_full, kv = remote_call(
        functools.partial(front_kernel, heads),
        0,
        [
            ((groups, *dealt), BF16),
            (home, F32),
            ((n_tokens, MODEL_WIDTH), BF16),
            ((3, n_tokens, head_cols), BF16),
            ((mp_parts * heads, chunk, chunk), F32),
            ((n_tokens, head_cols), BF16),
            ((2, *square), BF16),
            (square, BF16),
            (square, BF16),
            ((keys, 2 * MODEL_WIDTH), BF16),
        ],
        tokens, gains, wq_self.T, wk_self.T, wv_self.T, wo_self, rel_bias.T, answer_lens,
        wk_cross.T, wv_cross.T, wq_cross.T, wo_cross, flat_encoded,
        spaces={6: smem, 7: smem, 12: pl.ANY},
        out_spaces={9: pl.ANY},
        scratch=[
            pltpu.VMEM(dealt, BF16),
            pltpu.VMEM((near, *home), BF16),
            pltpu.VMEM((keys, MODEL_WIDTH), BF16),
            pltpu.VMEM((2, keys // KV_STEPS, 2 * MODEL_WIDTH), BF16),
            many_sems(4, max(near, 3)),
            many_sems(4, near),
            pair_sems(near),
            pair_sems(far),
            many_sems(groups, near),
            pltpu.SemaphoreType.DMA((4,)),
            pltpu.SemaphoreType.DMA,
            pltpu.SemaphoreType.DMA((2,)),
        ],
    )
    a2_all = a2_all.reshape(groups, n_tokens, MODEL_WIDTH)

    def home_scratch(width):
        return [
            pltpu.VMEM((groups, near, chunk, width), BF16),
            pltpu.VMEM((groups, chunk, width), BF16),
            pltpu.VMEM((far, chunk, width), BF16),
            pltpu.VMEM((mp_parts, chunk, head_cols), BF16),
            many_sems(groups, near),
            pair_sems(far),
            pair_sems(near),
            pair_sems(near),
        ]

    partial = cross_forward(lens, owners, a2_all, wq_full, kv, mp_parts)
    h_two, a3, o2, o2_own, lse = remote_call(
        cross_out_kernel,
        1,
        [
            (home, F32),
            (dealt, BF16),
            (home, F32),
            ((mp_parts, chunk, head_cols), BF16),
            ((chunk, LANES), F32),
        ],
        partial, h_one, wo_full, gains,
        scratch=home_scratch(STATW),
    )
    term, ga3, gw_ffn = local_call(
        ffn_kernel,
        [
            ((n_tokens, MODEL_WIDTH), BF16),
            ((n_tokens, MODEL_WIDTH), BF16),
            ((2, MODEL_WIDTH, MODEL_WIDTH), BF16),
        ],
        a3.reshape(n_tokens, MODEL_WIDTH), w_in, w_out, out_grad,
    )
    gh_two, gc_all, gain_ffn_grad, *gw_parts = remote_call(
        ffn_back_kernel,
        2,
        [
            (home, F32),
            ((groups, mp_parts, chunk, STATW), BF16),
            ((1, MODEL_WIDTH), F32),
            *[((rows_f, MODEL_WIDTH), BF16)] * groups,
        ],
        ga3.reshape(dealt), out_grad, h_two, gains, wo_full, o2, lse, gw_ffn,
        scratch=[
            pltpu.VMEM((near, *home), BF16),
            pltpu.VMEM((MODEL_WIDTH, MODEL_WIDTH), BF16),
            pltpu.VMEM((groups * rows_f, MODEL_WIDTH), BF16),
            pair_sems(near),
            pair_sems(far),
            many_sems(groups, near),
            pltpu.SemaphoreType.DMA((2,)),
        ],
    )
    gw_parts = [
        lax.ppermute(x, "pass", [(i, (i + k) % groups) for i in range(groups)]) if k else x
        for k, x in enumerate(gw_parts)
    ]
    gq, gkv = cross_backward(
        lens, owners, a2_all, gc_all.reshape(groups, n_tokens, STATW), wq_full, wo_full, kv, mp_parts
    )
    rows = {k: sum_rows(n * half, groups) for k, n in (("k", 3), ("c", 2), ("s", 3))}
    small = pltpu.VMEM((16, MODEL_WIDTH), F32)
    own = (mp_parts, chunk, head_cols)
    step = keys // (KV_STEPS if groups <= KV_STEPS else 4 * KV_STEPS)
    hbm = pl.ANY
    pair = pltpu.SemaphoreType.DMA((2,))
    grad_tokens, output, sum_k, sum_c, sum_s, small_sums, sum_f, genc = remote_call(
        functools.partial(finish_kernel, heads),
        3,
        [
            (dealt, BF16),
            (dealt, BF16),
            *[((2, groups * rows[k], MODEL_WIDTH), BF16) for k in "kcs"],
            ((16, MODEL_WIDTH), F32),
            ((2, groups * rows_f, MODEL_WIDTH), BF16),
            ((keys, MODEL_WIDTH), BF16),
        ],
        gq, gkv, flat_encoded, wkv.reshape(2 * MODEL_WIDTH, MODEL_WIDTH), gh_two, h_one, gains, wq_full,
        wq_self.T, wk_self.T, wv_self.T, wo_self, a1, qkv, p1, o1,
        a2_all.reshape(groups, *dealt), gc_all, o2_own, tokens, gain_ffn_grad, term.reshape(dealt), h_two, *gw_parts,
        spaces={0: hbm, 1: hbm, 2: hbm, 16: hbm, 17: hbm},
        out_spaces={7: hbm},
        scratch=[
            pltpu.VMEM((groups, *home), BF16),
            pltpu.VMEM((groups, near, *home), BF16),
            pltpu.VMEM((far, *home), BF16),
            pltpu.VMEM((2, step, 2 * MODEL_WIDTH), BF16),
            pltpu.VMEM((2, step, MODEL_WIDTH), BF16),
            pltpu.VMEM((2, step, MODEL_WIDTH), BF16),
            pltpu.VMEM((2 * MODEL_WIDTH, MODEL_WIDTH), F32),
            pltpu.VMEM((2, mp_parts, head_cols, MODEL_WIDTH), BF16),
            pltpu.VMEM((1, head_cols, MODEL_WIDTH), BF16),
            pltpu.VMEM((2, head_cols, MODEL_WIDTH), BF16),
            pltpu.VMEM((3, head_cols, MODEL_WIDTH), BF16),
            pltpu.VMEM(home, F32),
            pltpu.VMEM(own, BF16),
            pltpu.VMEM(own, BF16),
            pltpu.VMEM(dealt, BF16),
            pltpu.VMEM(dealt, BF16),
            pltpu.VMEM((3, n_tokens, head_cols), BF16),
            pltpu.VMEM((8, LANES), F32),
            pltpu.VMEM(dealt, BF16),
            pltpu.VMEM((mp_parts, chunk, STATW), BF16),
            pltpu.VMEM((near, *home), BF16),
            pltpu.VMEM((near, *home), BF16),
            pltpu.VMEM((2, mp_parts, half, MODEL_WIDTH), BF16),
            pltpu.VMEM((near, 2, half, MODEL_WIDTH), BF16),
            pltpu.VMEM((1, half, MODEL_WIDTH), BF16),
            pltpu.VMEM((2, half, MODEL_WIDTH), BF16),
            pltpu.VMEM((3, half, MODEL_WIDTH), BF16),
            *[pltpu.VMEM((groups * rows[k], MODEL_WIDTH), BF16) for k in "kcs"],
            *[pltpu.VMEM((far, rows[k], MODEL_WIDTH), BF16) for k in "kcs"],
            small,
            small,
            pltpu.VMEM((groups, 16, MODEL_WIDTH), F32),
            pltpu.VMEM((mp_parts, 16, MODEL_WIDTH), F32),
            many_sems(groups, near),
            pair_sems(far),
            pair_sems(near),
            pair_sems(near),
            pltpu.SemaphoreType.DMA((3,)),
            pltpu.SemaphoreType.DMA((2, 2)),
            pair,
            pair_sems(near),
            pair_sems(near),
            pair_sems(near),
            pair,
            pair_sems(near),
            pair,
            pair,
            pair,
            pair_sems(near),
            *[many_sems(3, far)] * 3,
            pair,
            pair_sems(far),
            pair_sems(near),
            many_sems(2, far),
        ],
    )
    shard = jax.ShapeDtypeStruct((head_cols, MODEL_WIDTH), F32)
    gain = jax.ShapeDtypeStruct((MODEL_WIDTH,), F32)
    y, gx, genc, gs, gc, gf, gb, *grads = pl.pallas_call(
        closing_kernel,
        out_shape=[
            *[jax.ShapeDtypeStruct(x.shape, x.dtype) for x in (output, grad_tokens, genc)],
            gain, gain, gain,
            jax.ShapeDtypeStruct((heads, BUCKETS), F32),
            *[shard] * 8,
            *[jax.ShapeDtypeStruct(square, F32)] * 2,
        ],
        in_specs=[pl.BlockSpec(memory_space=pltpu.VMEM)] * 8,
        out_specs=[pl.BlockSpec(memory_space=hbm)] * 3
        + [pl.BlockSpec(memory_space=pltpu.VMEM)] * 4
        + [pl.BlockSpec(memory_space=hbm)] * 10,
        scratch_shapes=[
            pltpu.VMEM((8, head_cols, MODEL_WIDTH), F32),
            pltpu.VMEM(square, F32),
            pltpu.VMEM(square, F32),
            pltpu.SemaphoreType.DMA((13,)),
        ],
        compiler_params=pltpu.CompilerParams(vmem_limit_bytes=VMEM_LIMIT),
    )(sum_k, sum_c, sum_s, sum_f, small_sums, genc, output, grad_tokens)

    return (
        y.reshape(n_tokens, MODEL_WIDTH),
        gx.reshape(n_tokens, MODEL_WIDTH),
        genc.reshape(GROUP_ROWS, quarter, MODEL_WIDTH),
        gs,
        gc,
        gf,
        gb.T,
        *[grads[i].T for i in range(3)],
        grads[3],
        *[grads[i].T for i in range(4, 7)],
        *grads[7:],
    )


def solution(mesh):
    tokens_in = P(("dp", "pass"), None)
    encoded_in = P(("dp", "pass"), "mp", None)
    by_column, by_row = P(None, "mp"), P("mp", None)
    weights = (by_column, by_column, by_column, by_row)
    return jax.shard_map(
        on_device,
        mesh=mesh,
        in_specs=(
            tokens_in, encoded_in, P("dp", None), P("dp", None), P(("dp", "pass")),
            P(), P(), P(), by_column,
            *weights, *weights, by_column, by_row, tokens_in,
        ),
        out_specs=(
            tokens_in, tokens_in, encoded_in, P(), P(), P(), by_column,
            *weights, *weights, by_column, by_row,
        ),
        check_vma=False,
    )
```

```python
import functools
import math

import jax
import jax.numpy as jnp
import numpy as np
from jax import lax
from jax.experimental import pallas as pl
from jax.experimental.pallas import tpu as pltpu
from jax.sharding import PartitionSpec as P

MODEL_WIDTH = 768
HD = 64
BUCKETS = 32
ANS = 20
PADT = 24
LANES = 128
STATW = MODEL_WIDTH + LANES
GROUP_ROWS = 32

EPSILON = 1e-06
NEGATIVE = -1e30
MESH = pl.DeviceIdType.MESH
VMEM_LIMIT = 61 << 20
F32 = jnp.float32
BF16 = jnp.bfloat16


def bucket_table(length, buckets):
    exact_half = buckets // 2
    result = np.zeros((length, length), np.int32)
    for target in range(length):
        for source in range(length):
            distance = max(target - source, 0)
            if distance < exact_half:
                result[target, source] = distance
            else:
                spread = int(
                    math.log(distance / exact_half)
                    / math.log(128 / exact_half)
                    * (buckets - exact_half)
                )
                result[target, source] = min(exact_half + spread, buckets - 1)
    return result


def dot_nn(a, b):
    return lax.dot_general(a, b, (((1,), (0,)), ((), ())), preferred_element_type=F32)


def dot_nt(a, b):
    return lax.dot_general(a, b, (((1,), (1,)), ((), ())), preferred_element_type=F32)


def dot_tn(a, b):
    return lax.dot_general(a, b, (((0,), (0,)), ((), ())), preferred_element_type=F32)


def rms_inverse(v):
    return lax.rsqrt(jnp.mean(v * v, axis=-1, keepdims=True) + EPSILON)


def row_of_gain(ref):
    return ref[...].reshape(1, ref.shape[0])


def rms_back(v, gains, ga):
    w = rms_inverse(v)
    gain_grad = jnp.sum(ga * v * w, axis=0, keepdims=True)
    gg = gains * ga
    gv = w * gg - v * (w * w * w) * jnp.mean(gg * v, axis=-1, keepdims=True)
    return gv, gain_grad


def local_call(kernel, outs, *ins, scratch=(), flops=0):
    return pl.pallas_call(
        kernel,
        out_shape=[jax.ShapeDtypeStruct(shape, dtype) for shape, dtype in outs],
        in_specs=[pl.BlockSpec(memory_space=pltpu.VMEM) for _ in ins],
        out_specs=[pl.BlockSpec(memory_space=pltpu.VMEM) for _ in outs],
        scratch_shapes=list(scratch),
        compiler_params=pltpu.CompilerParams(vmem_limit_bytes=VMEM_LIMIT),
        cost_estimate=pl.CostEstimate(
            flops=flops,
            bytes_accessed=sum(math.prod(x.shape) * x.dtype.itemsize for x in ins),
            transcendentals=0,
        ),
    )(*ins)


def place(**kw):
    return tuple(kw[a] if a in kw else lax.axis_index(a) for a in ("dp", "pass", "mp"))


def other(axis, k):
    n = lax.axis_size(axis)
    at = lax.rem(lax.axis_index(axis) + k, n)
    return at, place(**{axis: at})


def others(axis):
    return [(k - 1, *other(axis, k)) for k in range(1, lax.axis_size(axis))]


def greet(axes):
    barrier = pltpu.get_barrier_semaphore()
    peers = [peer for axis in axes for _, _, peer in others(axis)]
    for peer in peers:
        pl.semaphore_signal(barrier, inc=1, device_id=peer, device_id_type=MESH)
    pl.semaphore_wait(barrier, len(peers))


def remote(src, dst, send, recv, peer):
    return pltpu.make_async_remote_copy(
        src_ref=src, dst_ref=dst, send_sem=send, recv_sem=recv, device_id=peer, device_id_type=MESH
    )


def begin(copies):
    for copy in copies:
        copy.start()
    return copies


def finish(copies):
    for copy in copies:
        copy.wait()


def deal(source, slots, sems, axis):
    return begin([
        remote(source(at), slots.at[k], sems.at[0, k], sems.at[1, k], peer)
        for k, at, peer in others(axis)
    ])


def share(ref, sems, axis):
    return begin([remote(ref, ref, sems.at[0, k], sems.at[1, k], peer) for k, _, peer in others(axis)])


class Relay:
    def __init__(self, sems):
        self.sems, self.direct = sems, {}
        self.square = lax.axis_size("mp") == 4
        self.blocks, self.onward = {}, {}

    @staticmethod
    def near(which):
        mm = lax.axis_index("mp")
        at = mm + 1 - 2 * lax.rem(mm, 2) if which == 0 else mm + 2 - 4 * lax.div(mm, 2)
        return at, place(mp=at)

    def across(self):
        return 3 - lax.axis_index("mp")

    def put(self, i, block, own=None):
        mine = block(lax.axis_index("mp"))
        own = mine if own is None else own
        self.blocks[i] = block
        to = [(k, peer) for k, _, peer in others("mp")]
        if self.square:
            to = [(k, self.near(k)[1]) for k in range(2)]
        self.direct[i] = begin([
            remote(own, mine, self.sems.at[i, 0, k], self.sems.at[i, 1, k], peer) for k, peer in to
        ])

    def pass_on(self, i):
        if not self.square:
            return
        which = i % 2
        self.direct[i][which].wait_recv()
        block = self.blocks[i](self.near(which)[0])
        self.onward[i] = remote(
            block, block, self.sems.at[i, 0, 2], self.sems.at[i, 1, 2], self.near(1 - which)[1]
        )
        self.onward[i].start()

    def arrived(self, i):
        for k, copy in enumerate(self.direct[i]):
            if not self.square or k != i % 2:
                copy.wait_recv()
        if self.square:
            self.onward[i].wait_recv()

    def sent(self, i):
        for copy in self.direct[i]:
            copy.wait_send()
        if self.square:
            self.onward[i].wait_send()


def share_both(all_ref, zsems, msems):
    pn, pm, mm = lax.axis_size("pass"), lax.axis_index("pass"), lax.axis_index("mp")
    zcopies = share(all_ref.at[pm, mm], zsems, "pass")
    relay = Relay(msems)
    relay.put(0, lambda at: all_ref.at[pm, at])

    def forward(j):
        zcopies[j].wait_recv()
        source = lax.rem(pm - (j + 1) + pn, pn)
        relay.put(j + 1, lambda at: all_ref.at[source, at])
        relay.pass_on(j)

    def across():
        relay.pass_on(pn - 1)

    def end():
        for j in range(pn):
            relay.arrived(j)
            relay.sent(j)
        for copy in zcopies:
            copy.wait_send()

    return forward, across, end


def pair_sems(n):
    return pltpu.SemaphoreType.DMA((2, n))


def many_sems(m, n):
    return pltpu.SemaphoreType.DMA((m, 2, n))


def remote_call(kernel, collective_id, outs, *ins, spaces=None, out_spaces=None, scratch=()):
    vmem = pltpu.VMEM
    spaces = spaces or {}
    out_spaces = out_spaces or {}
    return pl.pallas_call(
        kernel,
        out_shape=[jax.ShapeDtypeStruct(shape, dtype) for shape, dtype in outs],
        in_specs=[pl.BlockSpec(memory_space=spaces.get(i, vmem)) for i in range(len(ins))],
        out_specs=[pl.BlockSpec(memory_space=out_spaces.get(i, vmem)) for i in range(len(outs))],
        scratch_shapes=list(scratch),
        compiler_params=pltpu.CompilerParams(
            collective_id=collective_id, has_side_effects=True, vmem_limit_bytes=VMEM_LIMIT
        ),
    )(*ins)


def home_rows(ref, chunk):
    at = pl.multiple_of(lax.axis_index("mp") * chunk, 16)
    return ref[pl.ds(at, chunk), :]


def total_of(first, slots):
    total = first.astype(F32)
    for k in range(slots.shape[0]):
        total = total + slots[k].astype(F32)
    return total


def bucket_grid(size):
    row = lax.broadcasted_iota(jnp.int32, (size, size), 0)
    col = lax.broadcasted_iota(jnp.int32, (size, size), 1)
    near = (col <= row) & (lax.div(col, ANS) == lax.div(row, ANS))
    table = bucket_table(ANS, BUCKETS)
    grid = jnp.full((size, size), -1, jnp.int32)
    for distance in range(ANS):
        grid = jnp.where(near & (row - col == distance), int(table[distance, 0]), grid)
    return grid, near, sorted({int(b) for b in table.reshape(-1)})


def self_forward(
    heads, x_ref, gain_ref, wq_ref, wk_ref, wv_ref, wo_ref, bias_ref, lens_ref,
    a1_ref, qkv_ref, p_ref, o1_ref, term_ref,
):
    x = x_ref[...].astype(F32)
    a1 = (x * rms_inverse(x) * row_of_gain(gain_ref)).astype(BF16)
    a1_ref[...] = a1
    for k, w_ref in enumerate((wq_ref, wk_ref, wv_ref)):
        qkv_ref[k] = dot_nt(a1, w_ref[...]).astype(BF16)
    blocks, size = term_ref.shape[0], term_ref.shape[1]
    grid, near, used = bucket_grid(size)
    biases = []
    for h in range(heads):
        bias = jnp.full((size, size), NEGATIVE, F32)
        for b in used:
            bias = jnp.where(grid == b, bias_ref[h, b], bias)
        biases.append(bias)
    lane = lax.broadcasted_iota(jnp.int32, (1, size), 1)
    for b in range(blocks):
        alive = jnp.zeros((1, size), jnp.int32)
        for q in range(size // ANS):
            inside = (lane >= q * ANS) & (lane < q * ANS + lens_ref[b * (size // ANS) + q])
            alive = jnp.where(inside, 1, alive)
        allowed = near & (alive > 0)
        rows = pl.ds(b * size, size)
        q, k, v = qkv_ref[0, rows, :], qkv_ref[1, rows, :], qkv_ref[2, rows, :]
        for h in range(heads):
            part = slice(h * HD, (h + 1) * HD)
            s = jnp.where(allowed, dot_nt(q[:, part], k[:, part]) + biases[h], NEGATIVE)
            e = jnp.exp(s - jnp.max(s, axis=-1, keepdims=True))
            p = e / jnp.sum(e, axis=-1, keepdims=True)
            p_ref[b * heads + h] = p
            o1_ref[rows, part] = dot_nn(p.astype(BF16), v[:, part]).astype(BF16)
    for b in range(blocks):
        term_ref[b] = dot_nn(o1_ref[pl.ds(b * size, size), :], wo_ref[...]).astype(BF16)


KV_STEPS = 8


def front_kernel(
    heads, x_ref, gain_ref, gain_cross_ref, wq_ref, wk_ref, wv_ref, wo_ref, bias_ref, lens_ref,
    wkc_ref, wvc_ref, wqc_ref, woc_ref, enc_ref,
    a2_ref, h_ref, a1_ref, qkv_ref, p_ref, o1_ref, wkv_ref, wq_out_ref, wo_out_ref, kv_ref,
    term, slots, enc, kv_slots, wsems, dsems, rsems, zsems, msems, own_sems, enc_sem, kv_sems,
):
    core, mm, pm = lax.axis_index("dp"), lax.axis_index("mp"), lax.axis_index("pass")
    mn, pn = lax.axis_size("mp"), lax.axis_size("pass")
    width = wkc_ref.shape[0]
    half = width // 2
    chunk = h_ref.shape[0]
    load = pltpu.make_async_copy(enc_ref, enc, enc_sem)
    load.start()
    pieces = [
        (wkc_ref, wkv_ref.at[0]), (wvc_ref, wkv_ref.at[1]), (wqc_ref, wq_out_ref), (woc_ref, wo_out_ref)
    ]

    def rows_of(source, which):
        return pl.ds(pl.multiple_of(source * width + which * half, 16), half)

    mine = pl.ds(pl.multiple_of(core * half, 16), half)
    owns = []
    for i, (shard, full) in enumerate(pieces):
        at = pl.ds(pl.multiple_of(mm * width, 16), width)
        own = pltpu.make_async_copy(shard, full.at[at], own_sems.at[i])
        own.start()
        owns.append(own)
    greet(("dp", "pass", "mp"))

    relay = Relay(wsems)

    def send_weight(i):
        shard, full = pieces[i]
        relay.put(i, lambda at: full.at[rows_of(at, core)], shard.at[mine])

    def to_other_core(i):
        full = pieces[i][1]
        relay.arrived(i)
        return begin([
            remote(
                full.at[rows_of(at, core)], full.at[rows_of(at, core)],
                dsems.at[i, 0, k], dsems.at[i, 1, k], other("dp", 1)[1],
            )
            for k, at, _ in others("mp")
        ])

    send_weight(0)
    send_weight(1)
    self_forward(
        heads, x_ref, gain_ref, wq_ref, wk_ref, wv_ref, wo_ref, bias_ref, lens_ref,
        a1_ref, qkv_ref, p_ref, o1_ref, term,
    )
    dealt = deal(lambda at: term.at[at], slots, rsems, "mp")
    relay.pass_on(0)
    relay.pass_on(1)
    for copy in dealt:
        copy.wait_recv()
    h = home_rows(x_ref, chunk).astype(F32) + total_of(term[mm], slots)
    h_ref[...] = h
    a2_ref[pm, mm] = (h * rms_inverse(h) * row_of_gain(gain_cross_ref)).astype(BF16)
    forward, across, end = share_both(a2_ref, zsems, msems)
    send_weight(2)
    send_weight(3)
    passed = [to_other_core(0), to_other_core(1)]
    for copies in passed:
        for copy in copies:
            copy.wait_recv()
    for own in owns:
        own.wait()
    load.wait()
    rows = enc.shape[0] // KV_STEPS

    def store(step):
        slot = lax.rem(step, 2)
        at = pl.ds(pl.multiple_of(step * rows, rows), rows)
        return pltpu.make_async_copy(kv_slots.at[slot], kv_ref.at[at], kv_sems.at[slot])

    def project(step, carry):
        slot = lax.rem(step, 2)

        @pl.when(step >= 2)
        def _():
            store(step - 2).wait()

        x = enc[pl.ds(pl.multiple_of(step * rows, rows), rows), :]
        for i in range(2):
            kv_slots[slot, :, i * MODEL_WIDTH : (i + 1) * MODEL_WIDTH] = dot_nt(x, wkv_ref[i]).astype(BF16)
        store(step).start()
        return carry

    done, onward = 0, [2, 3]
    for j in range(pn - 1):
        upto = KV_STEPS * (2 * j + 1) // (2 * pn)
        if upto > done:
            lax.fori_loop(done, upto, project, 0)
            done = upto
        forward(j)
        if onward:
            relay.pass_on(onward.pop(0))
    for i in onward:
        relay.pass_on(i)
    lax.fori_loop(done, KV_STEPS - 1, project, 0)
    across()
    lax.fori_loop(KV_STEPS - 1, KV_STEPS, project, 0)
    passed += [to_other_core(2), to_other_core(3)]
    for step in (KV_STEPS - 2, KV_STEPS - 1):
        store(step).wait()
    end()
    for copy in dealt:
        copy.wait_send()
    for i, copies in enumerate(passed):
        relay.sent(i)
        for copy in copies:
            copy.wait_send()
            if i >= 2:
                copy.wait_recv()


PAIR = 2 * HD
PAIRS = MODEL_WIDTH // PAIR
PROWS = 2 * PADT
FLOOR = -1e29


def low_lanes(shape):
    return lax.broadcasted_iota(jnp.int32, shape, len(shape) - 1) < HD


def pair_rows(dst_ref, pad_ref, values, stat=None, stat_at=0):
    questions = dst_ref.shape[0]
    low = low_lanes((1, PADT, PAIR))
    for q in range(questions):
        rows = slice(q * ANS, (q + 1) * ANS)
        pad_ref[q, 0:ANS, :MODEL_WIDTH] = values[rows, :]
        pad_ref[q, ANS:PADT, :] = jnp.zeros((PADT - ANS, pad_ref.shape[2]), F32)
        if stat is not None:
            pad_ref[q, 0:ANS, MODEL_WIDTH:] = stat[rows, :]
    lane = lax.broadcasted_iota(jnp.int32, (1, 1, LANES), 2)
    for c in range(PAIRS):
        x = pad_ref[:, :, c * PAIR : (c + 1) * PAIR]
        both = jnp.concatenate([jnp.where(low, x, 0.0), jnp.where(low, 0.0, x)], axis=1)
        dst_ref[:, c, :, :PAIR] = both.astype(BF16)
        if stat is not None:
            s = pad_ref[:, :, MODEL_WIDTH:]
            parts = []
            for h in (2 * c, 2 * c + 1):
                at = lane - (stat_at + h)
                parts.append(s * ((at == 0) | (at == 16) | (at == 32)).astype(F32))
            dst_ref[:, c, :, PAIR:] = jnp.concatenate(parts, axis=1).astype(BF16)


def segment_mask(lens_ref, row, keys):
    lane = lax.broadcasted_iota(jnp.int32, (PROWS, keys), 1)
    cut = lens_ref[0, row] - lax.axis_index("mp") * keys
    return [lane < cut, (lane >= cut) & (lane < cut + lens_ref[1, row])]


def masked(scores, mask):
    return jnp.concatenate(
        [jnp.where(mask[s], scores[s * PROWS : (s + 1) * PROWS], NEGATIVE) for s in range(2)], axis=0
    )


def fold_pair(x, s, low):
    at = s * PROWS
    return jnp.where(low, x[at : at + PADT], x[at + PADT : at + PROWS])


def split_three(x):
    hi = x.astype(BF16).astype(F32)
    mid = (x - hi).astype(BF16).astype(F32)
    return hi, mid, x - hi - mid


def staged(rows_per, stages):
    depth = len(stages)
    for i in range(rows_per + depth - 1):
        for k in reversed(range(depth)):
            if 0 <= i - k < rows_per:
                stages[k](i - k, (i - k) % 2)


def cross_forward_kernel(
    rows_per, keys, lens_ref, owners_ref, a2_ref, wq_ref, kv_ref, out_ref,
    q_rows, pad, s_buf, p_buf, t_buf, o_acc, m_acc, l_acc, flat,
):
    g = pl.program_id(0)
    pair_rows(q_rows, pad, dot_nt(a2_ref[0], wq_ref[...]).astype(BF16).astype(F32))
    o_acc[...] = jnp.zeros_like(o_acc)
    m_acc[...] = jnp.full_like(m_acc, FLOOR)
    l_acc[...] = jnp.zeros_like(l_acc)
    low = low_lanes((PADT, PAIR))
    ones = jnp.ones((keys, PAIR), BF16)

    def row_of(r):
        return lax.axis_index("pass") * GROUP_ROWS + g * rows_per + r

    def owners_of(r):
        return [owners_ref[0, row_of(r)], owners_ref[1, row_of(r)]]

    def scores(r, slot):
        owners = owners_of(r)
        mask = segment_mask(lens_ref, row_of(r), keys)
        for c in range(PAIRS):
            k = kv_ref[r * keys : (r + 1) * keys, c * PAIR : (c + 1) * PAIR]
            qm = jnp.concatenate([q_rows[q, c] for q in owners], axis=0)
            s_buf[slot, c] = masked(dot_nt(qm, k), mask)

    def chances(r, slot):
        for c in range(PAIRS):
            s = s_buf[slot, c]
            top = jnp.maximum(jnp.max(s, axis=-1, keepdims=True), FLOOR)
            p_buf[slot, c] = jnp.exp(s - top).astype(BF16)
            top = jnp.broadcast_to(top, (2 * PROWS, PAIR))
            for i in range(2):
                t_buf[slot, c, i] = fold_pair(top, i, low)

    def values(r, slot):
        owners = owners_of(r)
        new = []
        for c in range(PAIRS):
            v = kv_ref[r * keys : (r + 1) * keys, MODEL_WIDTH + c * PAIR : MODEL_WIDTH + (c + 1) * PAIR]
            both = dot_nn(p_buf[slot, c], jnp.concatenate([v, ones], axis=1))
            new.append([
                (fold_pair(both[:, :PAIR], i, low), fold_pair(both[:, PAIR:], i, low)) for i in range(2)
            ])
        for i, q in enumerate(owners):
            for c in range(PAIRS):
                cols = slice(c * PAIR, (c + 1) * PAIR)
                o, l = new[c][i]
                m_old, m_new = m_acc[q, :, cols], t_buf[slot, c, i]
                m_both = jnp.maximum(m_old, m_new)
                a, b = jnp.exp(m_old - m_both), jnp.exp(m_new - m_both)
                o_acc[q, :, cols] = a * o_acc[q, :, cols] + b * o
                l_acc[q, :, cols] = a * l_acc[q, :, cols] + b * l
                m_acc[q, :, cols] = m_both

    staged(rows_per, [scores, chances, values])
    questions = q_rows.shape[0]
    lane = lax.broadcasted_iota(jnp.int32, (PADT, LANES), 1)
    for q in range(questions):
        l = l_acc[q]
        some = l > 0.0
        safe = jnp.where(some, l, 1.0)
        o = o_acc[q] / safe
        lse = jnp.where(some, m_acc[q] + jnp.log(safe), NEGATIVE)
        few = jnp.zeros((PADT, LANES), F32)
        for h in range(MODEL_WIDTH // HD):
            few = jnp.where(lane == h, lse[:, h * HD : h * HD + 1], few)
        hi, mid, rest = split_three(few)
        stat = hi + pltpu.roll(mid, 16, 1) + pltpu.roll(rest, 32, 1)
        flat[q * ANS : (q + 1) * ANS, :MODEL_WIDTH] = o[:ANS]
        flat[q * ANS : (q + 1) * ANS, MODEL_WIDTH:] = stat[:ANS]
    chunk = out_ref.shape[2]
    for m in range(out_ref.shape[0]):
        out_ref[m, 0] = flat[m * chunk : (m + 1) * chunk, :].astype(BF16)


def cross_forward(lens, owners, a2_all, wq, kv, mp_parts):
    groups, n_tokens, _ = a2_all.shape
    rows_per = GROUP_ROWS // groups
    keys = kv.shape[0] // GROUP_ROWS
    questions = n_tokens // ANS
    block = rows_per * keys
    padded = pltpu.VMEM((questions, PADT, MODEL_WIDTH), F32)
    return pl.pallas_call(
        functools.partial(cross_forward_kernel, rows_per, keys),
        grid_spec=pltpu.PrefetchScalarGridSpec(
            num_scalar_prefetch=2,
            grid=(groups,),
            in_specs=[
                pl.BlockSpec((1, n_tokens, MODEL_WIDTH), lambda g, *_: (g, 0, 0)),
                pl.BlockSpec((MODEL_WIDTH, MODEL_WIDTH), lambda g, *_: (0, 0)),
                pl.BlockSpec((block, 2 * MODEL_WIDTH), lambda g, *_: (g, 0)),
            ],
            out_specs=pl.BlockSpec(
                (mp_parts, 1, n_tokens // mp_parts, STATW), lambda g, *_: (0, g, 0, 0)
            ),
            scratch_shapes=[
                pltpu.VMEM((questions, PAIRS, PROWS, PAIR), BF16),
                padded,
                pltpu.VMEM((2, PAIRS, 2 * PROWS, keys), F32),
                pltpu.VMEM((2, PAIRS, 2 * PROWS, keys), BF16),
                pltpu.VMEM((2, PAIRS, 2, PADT, PAIR), F32),
                padded,
                padded,
                padded,
                pltpu.VMEM((n_tokens, STATW), F32),
            ],
        ),
        out_shape=jax.ShapeDtypeStruct((mp_parts, groups, n_tokens // mp_parts, STATW), BF16),
        compiler_params=pltpu.CompilerParams(vmem_limit_bytes=VMEM_LIMIT),
    )(lens, owners, a2_all, wq, kv)


def cross_backward_kernel(
    rows_per, keys, lens_ref, owners_ref, a2_ref, gc_ref, wq_ref, wo_ref, kv_ref, gq_ref, gkv_ref,
    q_rows, go_rows, pad, s_buf, gp_buf, p_buf, gs_buf, gq_acc, flat,
):
    g = pl.program_id(0)
    stat = gc_ref[0, :, MODEL_WIDTH:].astype(F32)
    q2 = dot_nt(a2_ref[0], wq_ref[...]).astype(BF16).astype(F32)
    pair_rows(q_rows, pad, q2, stat, 0)
    go2 = dot_nt(gc_ref[0, :, :MODEL_WIDTH], wo_ref[...]).astype(BF16).astype(F32)
    pair_rows(go_rows, pad, go2, stat, 48)
    gq_acc[...] = jnp.zeros_like(gq_acc)
    low = low_lanes((PADT, PAIR))
    minus = jnp.full((keys, LANES), -1.0, BF16)

    def row_of(r):
        return lax.axis_index("pass") * GROUP_ROWS + g * rows_per + r

    def owners_of(r):
        return [owners_ref[0, row_of(r)], owners_ref[1, row_of(r)]]

    def tile(r, c, off):
        return kv_ref[r * keys : (r + 1) * keys, off + c * PAIR : off + (c + 1) * PAIR]

    def scores(r, slot):
        owners = owners_of(r)
        mask = segment_mask(lens_ref, row_of(r), keys)
        for c in range(PAIRS):
            qm = jnp.concatenate([q_rows[q, c] for q in owners], axis=0)
            gom = jnp.concatenate([go_rows[q, c] for q in owners], axis=0)
            s = dot_nt(qm, jnp.concatenate([tile(r, c, 0), minus], axis=1))
            s_buf[slot, c] = masked(s, mask)
            gp_buf[slot, c] = dot_nt(gom, jnp.concatenate([tile(r, c, MODEL_WIDTH), minus], axis=1))

    def chances(r, slot):
        for c in range(PAIRS):
            p = jnp.exp(s_buf[slot, c])
            p_buf[slot, c] = p.astype(BF16)
            gs_buf[slot, c] = (p * gp_buf[slot, c]).astype(BF16)

    def grads(r, slot):
        owners = owners_of(r)
        new = []
        rows = slice(r * keys, (r + 1) * keys)
        for c in range(PAIRS):
            gs, p = gs_buf[slot, c], p_buf[slot, c]
            qm = jnp.concatenate([q_rows[q, c, :, :PAIR] for q in owners], axis=0)
            gom = jnp.concatenate([go_rows[q, c, :, :PAIR] for q in owners], axis=0)
            gkv_ref[rows, c * PAIR : (c + 1) * PAIR] = dot_tn(gs, qm).astype(BF16)
            gkv_ref[rows, MODEL_WIDTH + c * PAIR : MODEL_WIDTH + (c + 1) * PAIR] = dot_tn(p, gom).astype(BF16)
            gq = dot_nn(gs, tile(r, c, 0))
            new.append([fold_pair(gq, i, low) for i in range(2)])
        for i, q in enumerate(owners):
            for c in range(PAIRS):
                cols = slice(c * PAIR, (c + 1) * PAIR)
                gq_acc[q, :, cols] = gq_acc[q, :, cols] + new[c][i]

    staged(rows_per, [scores, chances, grads])
    for q in range(q_rows.shape[0]):
        flat[q * ANS : (q + 1) * ANS, :] = gq_acc[q, :ANS, :]
    chunk = gq_ref.shape[2]
    for m in range(gq_ref.shape[0]):
        gq_ref[m, 0] = flat[m * chunk : (m + 1) * chunk, :].astype(BF16)


def cross_backward(lens, owners, a2_all, gc_all, wq, wo, kv, mp_parts):
    groups, n_tokens, _ = a2_all.shape
    rows_per = GROUP_ROWS // groups
    keys = kv.shape[0] // GROUP_ROWS
    questions = n_tokens // ANS
    block = rows_per * keys
    rows = pltpu.VMEM((questions, PAIRS, PROWS, PAIR + LANES), BF16)
    whole = pl.BlockSpec((MODEL_WIDTH, MODEL_WIDTH), lambda g, *_: (0, 0))
    return pl.pallas_call(
        functools.partial(cross_backward_kernel, rows_per, keys),
        grid_spec=pltpu.PrefetchScalarGridSpec(
            num_scalar_prefetch=2,
            grid=(groups,),
            in_specs=[
                pl.BlockSpec((1, n_tokens, MODEL_WIDTH), lambda g, *_: (g, 0, 0)),
                pl.BlockSpec((1, n_tokens, STATW), lambda g, *_: (g, 0, 0)),
                whole,
                whole,
                pl.BlockSpec((block, 2 * MODEL_WIDTH), lambda g, *_: (g, 0)),
            ],
            out_specs=[
                pl.BlockSpec(
                    (mp_parts, 1, n_tokens // mp_parts, MODEL_WIDTH), lambda g, *_: (0, g, 0, 0)
                ),
                pl.BlockSpec((block, 2 * MODEL_WIDTH), lambda g, *_: (g, 0)),
            ],
            scratch_shapes=[
                rows,
                rows,
                pltpu.VMEM((questions, PADT, STATW), F32),
                pltpu.VMEM((2, PAIRS, 2 * PROWS, keys), F32),
                pltpu.VMEM((2, PAIRS, 2 * PROWS, keys), F32),
                pltpu.VMEM((2, PAIRS, 2 * PROWS, keys), BF16),
                pltpu.VMEM((2, PAIRS, 2 * PROWS, keys), BF16),
                pltpu.VMEM((questions, PADT, MODEL_WIDTH), F32),
                pltpu.VMEM((n_tokens, MODEL_WIDTH), F32),
            ],
        ),
        out_shape=[
            jax.ShapeDtypeStruct((mp_parts, groups, n_tokens // mp_parts, MODEL_WIDTH), BF16),
            jax.ShapeDtypeStruct(kv.shape, BF16),
        ],
        compiler_params=pltpu.CompilerParams(vmem_limit_bytes=VMEM_LIMIT),
    )(lens, owners, a2_all, gc_all, wq, wo, kv)


def widen(w):
    row = lax.broadcasted_iota(jnp.int32, (LANES, MODEL_WIDTH), 0)
    col = lax.broadcasted_iota(jnp.int32, (LANES, MODEL_WIDTH), 1)
    each = (row == lax.div(col, HD)).astype(BF16)
    hi = w.astype(BF16)
    low = (w - hi.astype(F32)).astype(BF16)
    return dot_nn(hi, each) + dot_nn(low, each)


def combined(parts):
    lses = []
    for part in parts:
        stat = part[:, MODEL_WIDTH:].astype(F32)
        lses.append(stat + pltpu.roll(stat, LANES - 16, 1) + pltpu.roll(stat, LANES - 32, 1))
    top = functools.reduce(jnp.maximum, lses)
    weights = [jnp.exp(x - top) for x in lses]
    total = functools.reduce(jnp.add, weights)
    out = 0.0
    for part, weight in zip(parts, weights):
        out = out + widen(weight / total) * part[:, :MODEL_WIDTH].astype(F32)
    lane = lax.broadcasted_iota(jnp.int32, total.shape, 1)
    lse = jnp.where(lane < MODEL_WIDTH // HD, top + jnp.log(total), 0.0)
    return out, lse


def packed_stat(lse, at=0):
    hi, mid, low = split_three(lse)
    parts = [hi if at == 0 else pltpu.roll(hi, at, 1)]
    parts += [pltpu.roll(mid, at + 16, 1), pltpu.roll(low, at + 32, 1)]
    return parts[0] + parts[1] + parts[2]


def deal_groups(source, slots, sems):
    pn, pm = lax.axis_size("pass"), lax.axis_index("pass")
    for step in range(pn):
        group = lax.rem(pm + 1 + step, pn)
        deal(lambda at: source.at[at, group], slots.at[step], sems.at[step], "mp")


def middle_kernel(
    part_ref, h_ref, wo_ref, gain_ref, w_in_ref, w_out_ref, gy_ref,
    h2_ref, own_ref, term_ref, gh_ref, gc_ref, gain_out_ref, *refs,
):
    count = lax.axis_size("pass")
    pieces, refs = refs[:count], refs[count:]
    (
        held, slots, zslots, blocks, a3_all, ga3, gw, ga_slots, gw_slot, y, gc_home,
        msems, gsems, asems, bsems, rsems, zsems, relay_sems, gw_sems, load_sem, own_sem,
    ) = refs
    core, mm, pm = lax.axis_index("dp"), lax.axis_index("mp"), lax.axis_index("pass")
    pn = lax.axis_size("pass")
    load = pltpu.make_async_copy(part_ref.at[mm], held, load_sem)
    load.start()
    greet(("dp", "pass", "mp"))
    deal_groups(part_ref, slots, msems)
    load.wait()

    def add(parts):
        out, lse = combined(parts)
        return jnp.concatenate([out, packed_stat(lse)], axis=1).astype(BF16)

    def arrived(step):
        group = lax.rem(pm + 1 + step, pn)
        for k, at, peer in others("mp"):
            remote(
                part_ref.at[at, group], slots.at[step, k], msems.at[step, 0, k], msems.at[step, 1, k], peer
            ).wait()
        held[group] = add([held[group]] + [slots[step, k] for k in range(slots.shape[1])])

    def to_home(step):
        at, peer = other("pass", step + 1)
        return remote(held.at[at], zslots.at[step], gsems.at[0, step], gsems.at[1, step], peer)

    def one(step, carry):
        arrived(step)
        to_home(step).start()
        return carry

    if pn <= 4:
        for step in range(pn - 1):
            one(step, 0)
    else:
        lax.fori_loop(0, pn - 1, one, 0)
    arrived(pn - 1)
    for step in range(pn - 1):
        to_home(step).wait()
    o, lse = combined([held[pm]] + [zslots[k] for k in range(pn - 1)])
    low = o.astype(BF16)
    h2 = h_ref[...] + dot_nn(low, wo_ref[...])
    a3_all[mm] = (h2 * rms_inverse(h2) * row_of_gain(gain_ref)).astype(BF16)
    copies = share(a3_all.at[mm], asems, "mp")
    h2_ref[...] = h2
    width = blocks.shape[2]
    parts = blocks.shape[0]
    for k in range(parts):
        blocks[k] = low[:, k * width : (k + 1) * width]
    own_ref[mm] = blocks[mm]
    block_copies = begin([
        remote(blocks.at[at], own_ref.at[mm], bsems.at[0, k], bsems.at[1, k], peer)
        for k, at, peer in others("mp")
    ])
    gy = gy_ref[...]
    ge = dot_nt(gy, w_out_ref[...]).astype(BF16).astype(F32)
    finish(copies)
    a3 = jnp.concatenate([a3_all[k] for k in range(parts)], axis=0)
    u = dot_nn(a3, w_in_ref[...])
    cdf = 0.5 * (1.0 + lax.erf(u * np.float32(math.sqrt(0.5))))
    pdf = np.float32(1.0 / math.sqrt(2.0 * math.pi)) * jnp.exp(-0.5 * u * u)
    gu = (ge * (cdf + u * pdf)).astype(BF16)
    ga = dot_nt(gu, w_in_ref[...]).astype(BF16)
    chunk = h_ref.shape[0]
    for k in range(parts):
        ga3[k] = ga[k * chunk : (k + 1) * chunk]
    dealt = deal(lambda at: ga3.at[at], ga_slots, rsems, "mp")
    e = (u * cdf).astype(BF16)
    gw[0] = dot_tn(a3, gu).astype(BF16)
    gw[1] = dot_tn(e, gy).astype(BF16)
    swapped = remote(gw.at[1 - core], gw_slot, gw_sems.at[0], gw_sems.at[1], other("dp", 1)[1])
    swapped.start()
    term = dot_nn(e, w_out_ref[...]).astype(BF16)
    for k in range(parts):
        term_ref[k] = term[k * chunk : (k + 1) * chunk]
    finish(dealt)
    gv, gain_grad = rms_back(h2, row_of_gain(gain_ref), total_of(ga3[mm], ga_slots))
    gain_out_ref[...] = gain_grad
    gh = home_rows(gy_ref, chunk).astype(F32) + gv
    gh_ref[...] = gh
    gc = gh.astype(BF16)
    go = dot_nt(gc, wo_ref[...]).astype(BF16).astype(F32)
    row = lax.broadcasted_iota(jnp.int32, (MODEL_WIDTH, LANES), 0)
    col = lax.broadcasted_iota(jnp.int32, (MODEL_WIDTH, LANES), 1)
    each = (lax.div(row, HD) == col).astype(F32)
    delta = lax.dot_general(
        go * o, each, (((1,), (0,)), ((), ())),
        preferred_element_type=F32, precision=lax.Precision.HIGHEST,
    )
    stat = packed_stat(lse) + packed_stat(delta, 48)
    gc_home[...] = jnp.concatenate([gc, stat.astype(BF16)], axis=1)
    own = pltpu.make_async_copy(gc_home, gc_ref.at[pm, mm], own_sem)
    own.start()
    own.wait()
    forward, across, end = share_both(gc_ref, zsems, relay_sems)
    swapped.wait()
    used = gw_slot.shape[0]
    y[0:used, :] = (gw[core].astype(F32) + gw_slot[...].astype(F32)).astype(BF16)
    fill_tail(y, used)
    rows = pieces[0].shape[0]
    for k, piece in enumerate(pieces):
        piece[...] = y[pl.ds(pl.multiple_of(lax.rem(pm + k, pn) * rows, 16), rows), :]
    for j in range(pn - 1):
        forward(j)
    across()
    finish(block_copies)
    end()


def sum_rows(rows, groups):
    return -(-rows // (groups * 16)) * 16


class GroupSum:
    def __init__(self, y, zslots, out, sems):
        self.y, self.zslots, self.out, self.sems = y, zslots, out, sems
        self.rows = zslots.shape[1]

    def part(self, at):
        return pl.ds(pl.multiple_of(at * self.rows, 16), self.rows)

    def dealing(self):
        return [
            remote(self.y.at[self.part(at)], self.zslots.at[k], self.sems.at[0, 0, k], self.sems.at[0, 1, k], peer)
            for k, at, peer in others("pass")
        ]

    def sharing(self):
        here = self.out.at[lax.axis_index("dp"), self.part(lax.axis_index("pass"))]
        return [
            remote(here, here, self.sems.at[1, 0, k], self.sems.at[1, 1, k], peer)
            for k, _, peer in others("pass")
        ]

    def swapping(self):
        here = self.out.at[lax.axis_index("dp")]
        return [remote(here, here, self.sems.at[2, 0, 0], self.sems.at[2, 1, 0], other("dp", 1)[1])]

    def spread(self):
        begin(self.dealing())

    def gather(self):
        finish(self.dealing())
        at = self.part(lax.axis_index("pass"))
        total = total_of(self.y[at, :], self.zslots)
        self.out[lax.axis_index("dp"), at, :] = total.astype(BF16)
        begin(self.sharing())

    def swap(self):
        finish(self.sharing())
        begin(self.swapping())

    def end(self):
        finish(self.swapping())


def fill_tail(y, used):
    if y.shape[0] > used:
        y[used:, :] = jnp.zeros((y.shape[0] - used, y.shape[1]), y.dtype)


def self_backward(
    heads, gsa, wq_ref, wk_ref, wv_ref, wo_ref, qkv_ref, p_ref, ga1_ref, gqkv_ref, bias_ref
):
    go1 = dot_nt(gsa, wo_ref[...]).astype(BF16)
    blocks, size = ga1_ref.shape[0], ga1_ref.shape[1]
    grid, _, used = bucket_grid(size)
    at_row = lax.broadcasted_iota(jnp.int32, bias_ref.shape, 0)
    at_lane = lax.broadcasted_iota(jnp.int32, bias_ref.shape, 1)
    totals = []
    for h in range(heads):
        part = slice(h * HD, (h + 1) * HD)
        total = jnp.zeros((size, size), F32)
        for b in range(blocks):
            rows = pl.ds(b * size, size)
            q, k, v = qkv_ref[0, rows, part], qkv_ref[1, rows, part], qkv_ref[2, rows, part]
            p = p_ref[b * heads + h]
            go = go1[b * size : (b + 1) * size, part]
            gp = dot_nt(go, v)
            gs = (p * (gp - jnp.sum(gp * p, axis=-1, keepdims=True))).astype(BF16)
            total = total + gs.astype(F32)
            gqkv_ref[0, rows, part] = dot_nn(gs, k).astype(BF16)
            gqkv_ref[1, rows, part] = dot_tn(gs, q).astype(BF16)
            gqkv_ref[2, rows, part] = dot_tn(p.astype(BF16), go).astype(BF16)
        totals.append(total)
    ga1 = dot_nn(gqkv_ref[0], wq_ref[...])
    ga1 = ga1 + dot_nn(gqkv_ref[1], wk_ref[...])
    ga1 = ga1 + dot_nn(gqkv_ref[2], wv_ref[...])
    for b in range(blocks):
        ga1_ref[b] = ga1[b * size : (b + 1) * size].astype(BF16)

    def bias_sums():
        bias = jnp.zeros(bias_ref.shape, F32)
        for h, total in enumerate(totals):
            for b in used:
                value = jnp.sum(jnp.where(grid == b, total, 0.0), keepdims=True)
                bias = jnp.where((at_row == h) & (at_lane == b), value, bias)
        bias_ref[...] = bias

    return bias_sums


def finish_kernel(
    heads, gq_ref, gkv_ref, enc_ref, wkv_ref, gh2_ref, h_ref, gain_ref, gain_cross_ref, wq_ref,
    ws_q_ref, ws_k_ref, ws_v_ref, ws_o_ref, a1_ref, qkv_ref, p_ref, o1_ref,
    a2_ref, gc_ref, o2_ref, x_ref, ffn_gain_ref, term_ref, h2_ref, *refs,
):
    count = lax.axis_size("pass")
    gw_parts, refs = refs[:count], refs[count:]
    (
    gx_ref, out_ref, sum_k_ref, sum_c_ref, sum_s_ref, small_ref, sum_f_ref, genc_ref,
    held, slots, zslots, gkv_in, enc_in, genc_out, gw_acc, gw_kv, gw_o, gw_c, gw_s, gh1,
    blocks, gq_own, gsa_all, ga1, gqkv, bias, a2_own, gc_own,
    ga_slots, term_slots, kv_core, kv_slots, core_o, core_c, core_s,
    y_k, y_c, y_s, z_k, z_c, z_s, small, small_dp, small_z, small_m,
    msems, gzsems, asems, bsems, load_sems, in_sems, genc_sems,
    ga_sems, term_sems, out_sems, kv_dsems, kv_msems, co_sems, cc_sems, cs_sems, gx_sems,
    zk_sems, zc_sems, zs_sems, sd_sems, sz_sems, sm_sems,
    f_sems,
    ) = refs
    core, mm, pm = lax.axis_index("dp"), lax.axis_index("mp"), lax.axis_index("pass")
    pn = lax.axis_size("pass")
    chunk = h_ref.shape[0]
    width = o1_ref.shape[1]
    half = width // 2
    mine = pl.ds(pl.multiple_of(core * half, 16), half)
    theirs = pl.ds(pl.multiple_of((1 - core) * half, 16), half)
    peer = other("dp", 1)[1]
    loads = begin([
        pltpu.make_async_copy(gq_ref.at[mm], held, load_sems.at[0]),
        pltpu.make_async_copy(a2_ref.at[pm], a2_own, load_sems.at[1]),
        pltpu.make_async_copy(gc_ref.at[pm], gc_own, load_sems.at[2]),
    ])
    rows = gkv_in.shape[1]
    steps = gkv_ref.shape[0] // rows

    def step_rows(step):
        return pl.ds(pl.multiple_of(step * rows, rows), rows)

    def fetch_gkv(step, slot):
        return pltpu.make_async_copy(gkv_ref.at[step_rows(step)], gkv_in.at[slot], in_sems.at[slot, 0])

    def fetch_enc(step, slot):
        return pltpu.make_async_copy(enc_ref.at[step_rows(step)], enc_in.at[slot], in_sems.at[slot, 1])

    def store(step, slot):
        return pltpu.make_async_copy(genc_out.at[slot], genc_ref.at[step_rows(step)], genc_sems.at[slot])

    fetch_gkv(0, 0).start()
    fetch_enc(0, 0).start()
    greet(("dp", "pass", "mp"))
    for step in range(pn):
        group = lax.rem(pm + 1 + step, pn)
        deal(lambda at: gq_ref.at[at, group], slots.at[step], msems.at[step], "mp")
    finish(loads)

    def to_home(step):
        at, to = other("pass", step + 1)
        return remote(held.at[at], zslots.at[step], gzsems.at[0, step], gzsems.at[1, step], to)

    def arrived(step, carry):
        group = lax.rem(pm + 1 + step, pn)
        for k, at, to in others("mp"):
            remote(
                gq_ref.at[at, group], slots.at[step, k], msems.at[step, 0, k], msems.at[step, 1, k], to
            ).wait()
        total = held[group].astype(F32)
        for k in range(slots.shape[1]):
            total = total + slots[step, k].astype(F32)
        held[group] = total.astype(BF16)

        @pl.when(step < pn - 1)
        def _():
            to_home(step).start()

        return carry

    def arrivals(step):
        last = steps * 13 // 8
        lax.fori_loop(
            lax.min(lax.div(step * pn, last), pn), lax.min(lax.div((step + 1) * pn, last), pn), arrived, 0
        )

    parts = blocks.shape[0]

    def both_cores(copy, gw, got, y, first=0):
        copy.wait()
        for i in range(gw.shape[0]):
            at = pl.ds(pl.multiple_of(lax.axis_index("dp") * half, 16), half)
            to = (first + i) * half
            y[to : to + half, :] = (gw[i, at, :].astype(F32) + got[i].astype(F32)).astype(BF16)
        fill_tail(y, (first + gw.shape[0]) * half)

    total = gw_parts[0][...].astype(F32)
    for part in gw_parts[1:]:
        total = total + part[...].astype(F32)
    f_rows = pl.ds(pl.multiple_of(pm * total.shape[0], 16), total.shape[0])
    sum_f_ref[core, f_rows, :] = total.astype(BF16)
    f_copies = share(sum_f_ref.at[core, f_rows], f_sems.at[0], "pass")
    total = jnp.zeros((width, MODEL_WIDTH), F32)
    for k in range(parts):
        total = total + dot_tn(o2_ref[k], gc_own[k, :, :MODEL_WIDTH])
    gw_o[0] = total.astype(BF16)

    def core_copy(gw, got, sems):
        to = other("dp", 1)[1]
        off = pl.multiple_of((1 - lax.axis_index("dp")) * half, 16)
        where = (slice(None),) * (len(gw.shape) - 2) + (pl.ds(off, half),)
        return remote(gw.at[where], got, sems.at[0], sems.at[1], to)

    core_copy(gw_o, core_o, co_sems).start()
    gw_acc[...] = jnp.zeros_like(gw_acc)

    def weights(step, carry):
        slot = lax.rem(step, 2)

        @pl.when(step + 1 < steps)
        def _():
            fetch_gkv(step + 1, 1 - slot).start()
            fetch_enc(step + 1, 1 - slot).start()

        fetch_gkv(step, slot).wait()
        fetch_enc(step, slot).wait()
        for i in range(2):
            part = slice(i * MODEL_WIDTH, (i + 1) * MODEL_WIDTH)
            gw_acc[part, :] += dot_tn(gkv_in[slot, :, part], enc_in[slot])
        arrivals(step)

        @pl.when(step == 1)
        def _():
            both_cores(core_copy(gw_o, core_o, co_sems), gw_o, core_o, y_k, 2)

        return carry

    lax.fori_loop(0, steps, weights, 0)
    fetch_gkv(0, 0).start()
    for i in range(2):
        for k in range(parts):
            at = (i * parts + k) * width
            gw_kv[i, k] = gw_acc[at : at + width, :].astype(BF16)
    core_copy(gw_kv, kv_core, kv_dsems).start()

    def mine_rows():
        return pl.ds(pl.multiple_of(lax.axis_index("dp") * half, 16), half)

    def kv_copies():
        return [
            remote(gw_kv.at[:, at, mine_rows()], kv_slots.at[k], kv_msems.at[0, k], kv_msems.at[1, k], to)
            for k, at, to in others("mp")
        ]

    def encodings(step, carry):
        slot = lax.rem(step, 2)

        @pl.when(step + 1 < steps)
        def _():
            fetch_gkv(step + 1, 1 - slot).start()

        fetch_gkv(step, slot).wait()

        @pl.when(step >= 2)
        def _():
            store(step - 2, slot).wait()

        genc_out[slot] = dot_nn(gkv_in[slot], wkv_ref[...]).astype(BF16)
        store(step, slot).start()
        arrivals(steps + step)

        @pl.when(step == 1)
        def _():
            core_copy(gw_kv, kv_core, kv_dsems).wait()
            at = pl.ds(pl.multiple_of(lax.axis_index("dp") * half, 16), half)
            for i in range(2):
                for k in range(parts):
                    gw_kv[i, k, at, :] = (gw_kv[i, k, at, :].astype(F32) + kv_core[i, k].astype(F32)).astype(BF16)
            begin(kv_copies())

        @pl.when(step == steps - 2)
        def _():
            for at in range(pn - 1):
                to_home(at).wait()
            low = total_of(held[pm], zslots).astype(BF16)
            gv, cross_gain = rms_back(h_ref[...], row_of_gain(gain_cross_ref), dot_nn(low, wq_ref[...]))
            gh = gh2_ref[...] + gv
            gh1[...] = gh
            gsa_all[mm] = gh.astype(BF16)
            begin(gsa_copies())
            small[...] = jnp.zeros_like(small)
            small[1:2, :] = cross_gain
            for k in range(parts):
                blocks[k] = low[:, k * width : (k + 1) * width]
            gq_own[mm] = blocks[mm]
            begin(block_copies())

        return carry

    def gsa_copies():
        here = gsa_all.at[mm]
        return [remote(here, here, asems.at[0, k], asems.at[1, k], to) for k, _, to in others("mp")]

    def block_copies():
        return [
            remote(blocks.at[at], gq_own.at[mm], bsems.at[0, k], bsems.at[1, k], to)
            for k, at, to in others("mp")
        ]

    lax.fori_loop(0, steps, encodings, 0)
    finish(f_copies)
    f_copies = share(sum_f_ref.at[core], f_sems.at[1], "dp")
    for step in (steps - 2, steps - 1):
        store(step, step % 2).wait()
    finish(block_copies())
    total = jnp.zeros((width, MODEL_WIDTH), F32)
    for k in range(parts):
        total = total + dot_tn(gq_own[k], a2_own[k])
    gw_c[0] = total.astype(BF16)
    finish(kv_copies())
    for i in range(2):
        total = gw_kv[i, mm, mine, :].astype(F32)
        for k in range(kv_slots.shape[0]):
            total = total + kv_slots[k, i].astype(F32)
        y_k[i * half : (i + 1) * half, :] = total.astype(BF16)
    sum_k = GroupSum(y_k, z_k, sum_k_ref, zk_sems)
    sum_k.spread()
    finish(gsa_copies())
    gsa = jnp.concatenate([gsa_all[k] for k in range(parts)], axis=0)
    gw_c[1] = dot_tn(o1_ref[...], gsa).astype(BF16)
    core_copy(gw_c, core_c, cc_sems).start()
    bias_sums = self_backward(
        heads, gsa, ws_q_ref, ws_k_ref, ws_v_ref, ws_o_ref, qkv_ref, p_ref, ga1, gqkv, bias
    )
    ga_copies = deal(lambda at: ga1.at[at], ga_slots, ga_sems, "mp")
    sum_c = GroupSum(y_c, z_c, sum_c_ref, zc_sems)
    both_cores(core_copy(gw_c, core_c, cc_sems), gw_c, core_c, y_c)
    sum_c.spread()
    for k in range(3):
        gw_s[k] = dot_tn(gqkv[k], a1_ref[...]).astype(BF16)
    core_copy(gw_s, core_s, cs_sems).start()
    bias_sums()
    sum_s = GroupSum(y_s, z_s, sum_s_ref, zs_sems)
    both_cores(core_copy(gw_s, core_s, cs_sems), gw_s, core_s, y_s)
    sum_s.spread()
    finish(ga_copies)
    gv, self_gain = rms_back(
        home_rows(x_ref, chunk).astype(F32), row_of_gain(gain_ref), total_of(ga1[mm], ga_slots)
    )
    gx_ref[mm] = (gh1[...] + gv).astype(BF16)
    gx_copies = share(gx_ref.at[mm], gx_sems, "mp")
    term_copies = deal(lambda at: term_ref.at[at], term_slots, term_sems, "mp")
    small[0:1, :] = self_gain
    small[2:3, :] = ffn_gain_ref[...]
    small[8:16, :LANES] = bias[...]
    sd = begin([remote(small, small_dp, sd_sems.at[0], sd_sems.at[1], peer)])
    sum_k.gather()
    sum_c.gather()
    finish(sd)
    small_z[pm] = small[...] + small_dp[...]
    sz = share(small_z.at[pm], sz_sems, "pass")
    sum_s.gather()
    finish(term_copies)
    out_ref[mm] = (h2_ref[...] + total_of(term_ref[mm], term_slots)).astype(BF16)
    out_copies = share(out_ref.at[mm], out_sems, "mp")
    finish(sz)
    total = small_z[0]
    for k in range(1, small_z.shape[0]):
        total = total + small_z[k]
    small_m[mm] = total
    sm = share(small_m.at[mm], sm_sems, "mp")
    sum_c.swap()
    finish(sm)
    gains = small_m[0]
    for k in range(1, small_m.shape[0]):
        gains = gains + small_m[k]
    small_ref[0:8, :] = gains[0:8]
    small_ref[8:16, :] = total[8:16]
    finish(gx_copies)
    sum_s.swap()
    sum_k.swap()
    finish(out_copies)
    finish(f_copies)
    sum_c.end()
    sum_s.end()
    sum_k.end()


def closing_kernel(
    k_ref, c_ref, s_ref, ffn_ref, small_ref, genc_ref, y_ref, gx_ref, *refs
):
    outs, (wide, wide_in, wide_out, sems) = refs[:17], refs[17:]
    half = wide.shape[1] // 2
    moves = [(genc_ref, outs[2]), (y_ref, outs[0]), (gx_ref, outs[1])]
    copies = begin([pltpu.make_async_copy(src, dst, sems.at[n]) for n, (src, dst) in enumerate(moves)])
    sources = [(s_ref, 0), (s_ref, 1), (s_ref, 2), (c_ref, 1), (c_ref, 0), (k_ref, 0), (k_ref, 1), (k_ref, 2)]
    for n, (ref, i) in enumerate(sources):
        for core in range(2):
            wide[n, core * half : (core + 1) * half, :] = ref[core, i * half : (i + 1) * half, :].astype(F32)
        copies += begin([pltpu.make_async_copy(wide.at[n], outs[7 + n], sems.at[3 + n])])
    for n, buffer in enumerate((wide_in, wide_out)):
        buffer[...] = ffn_ref[n, 0 : buffer.shape[0], :].astype(F32)
        copies += begin([pltpu.make_async_copy(buffer, outs[15 + n], sems.at[11 + n])])
    for n in range(3):
        outs[3 + n][...] = small_ref[n, :]
    heads, buckets = outs[6].shape
    outs[6][...] = small_ref[8 : 8 + heads, 0:buckets]
    finish(copies)


def on_device(
    tokens,
    encoded,
    seg_lens,
    owners,
    answer_lens,
    gain_self,
    gain_cross,
    gain_ffn,
    rel_bias,
    wq_self,
    wk_self,
    wv_self,
    wo_self,
    wq_cross,
    wk_cross,
    wv_cross,
    wo_cross,
    w_in,
    w_out,
    out_grad,
):
    groups, mp_parts = lax.axis_size("pass"), lax.axis_size("mp")
    heads = rel_bias.shape[1]
    head_cols = heads * HD
    half = head_cols // 2
    quarter = encoded.shape[1]
    n_tokens = tokens.shape[0]
    chunk = n_tokens // mp_parts
    assert w_in.shape == (MODEL_WIDTH, MODEL_WIDTH)
    rows_f = sum_rows(MODEL_WIDTH, groups)
    keys = GROUP_ROWS * quarter
    near, far = mp_parts - 1, groups - 1

    lens, owners = seg_lens.T, owners.T
    flat_encoded = encoded.reshape(keys, MODEL_WIDTH)
    home = (chunk, MODEL_WIDTH)
    dealt = (mp_parts, chunk, MODEL_WIDTH)
    square = (MODEL_WIDTH, MODEL_WIDTH)
    smem = pltpu.SMEM
    a2_all, h_one, a1, qkv, p1, o1, wkv, wq_full, wo_full, kv = remote_call(
        functools.partial(front_kernel, heads),
        0,
        [
            ((groups, *dealt), BF16),
            (home, F32),
            ((n_tokens, MODEL_WIDTH), BF16),
            ((3, n_tokens, head_cols), BF16),
            ((mp_parts * heads, chunk, chunk), F32),
            ((n_tokens, head_cols), BF16),
            ((2, *square), BF16),
            (square, BF16),
            (square, BF16),
            ((keys, 2 * MODEL_WIDTH), BF16),
        ],
        tokens, gain_self, gain_cross, wq_self.T, wk_self.T, wv_self.T, wo_self, rel_bias.T, answer_lens,
        wk_cross.T, wv_cross.T, wq_cross.T, wo_cross, flat_encoded,
        spaces={7: smem, 8: smem, 13: pl.ANY},
        out_spaces={9: pl.ANY},
        scratch=[
            pltpu.VMEM(dealt, BF16),
            pltpu.VMEM((near, *home), BF16),
            pltpu.VMEM((keys, MODEL_WIDTH), BF16),
            pltpu.VMEM((2, keys // KV_STEPS, 2 * MODEL_WIDTH), BF16),
            many_sems(4, max(near, 3)),
            many_sems(4, near),
            pair_sems(near),
            pair_sems(far),
            many_sems(groups, near),
            pltpu.SemaphoreType.DMA((4,)),
            pltpu.SemaphoreType.DMA,
            pltpu.SemaphoreType.DMA((2,)),
        ],
    )
    a2_all = a2_all.reshape(groups, n_tokens, MODEL_WIDTH)

    partial = cross_forward(lens, owners, a2_all, wq_full, kv, mp_parts)
    gc_space = pltpu.VMEM if groups <= KV_STEPS else pl.ANY
    h_two, o2_own, term, gh_two, gc_all, gain_ffn_grad, *gw_parts = remote_call(
        middle_kernel,
        1,
        [
            (home, F32),
            ((mp_parts, chunk, head_cols), BF16),
            (dealt, BF16),
            (home, F32),
            ((groups, mp_parts, chunk, STATW), BF16),
            ((1, MODEL_WIDTH), F32),
            *[((rows_f, MODEL_WIDTH), BF16)] * groups,
        ],
        partial, h_one, wo_full, gain_ffn, w_in, w_out, out_grad,
        spaces={0: pl.ANY},
        out_spaces={4: gc_space},
        scratch=[
            pltpu.VMEM((groups, chunk, STATW), BF16),
            pltpu.VMEM((groups, near, chunk, STATW), BF16),
            pltpu.VMEM((far, chunk, STATW), BF16),
            pltpu.VMEM((mp_parts, chunk, head_cols), BF16),
            pltpu.VMEM(dealt, BF16),
            pltpu.VMEM(dealt, BF16),
            pltpu.VMEM((2, *square), BF16),
            pltpu.VMEM((near, *home), BF16),
            pltpu.VMEM(square, BF16),
            pltpu.VMEM((groups * rows_f, MODEL_WIDTH), BF16),
            pltpu.VMEM((chunk, STATW), BF16),
            many_sems(groups, near),
            pair_sems(far),
            pair_sems(near),
            pair_sems(near),
            pair_sems(near),
            pair_sems(far),
            many_sems(groups, near),
            pltpu.SemaphoreType.DMA((2,)),
            pltpu.SemaphoreType.DMA,
            pltpu.SemaphoreType.DMA,
        ],
    )
    gw_parts = [
        lax.ppermute(x, "pass", [(i, (i + k) % groups) for i in range(groups)]) if k else x
        for k, x in enumerate(gw_parts)
    ]
    gq, gkv = cross_backward(
        lens, owners, a2_all, gc_all.reshape(groups, n_tokens, STATW), wq_full, wo_full, kv, mp_parts
    )
    rows = {k: sum_rows(n * half, groups) for k, n in (("k", 3), ("c", 2), ("s", 3))}
    small = pltpu.VMEM((16, MODEL_WIDTH), F32)
    own = (mp_parts, chunk, head_cols)
    step = keys // (KV_STEPS if groups <= KV_STEPS else 4 * KV_STEPS)
    hbm = pl.ANY
    pair = pltpu.SemaphoreType.DMA((2,))
    grad_tokens, output, sum_k, sum_c, sum_s, small_sums, sum_f, genc = remote_call(
        functools.partial(finish_kernel, heads),
        3,
        [
            (dealt, BF16),
            (dealt, BF16),
            *[((2, groups * rows[k], MODEL_WIDTH), BF16) for k in "kcs"],
            ((16, MODEL_WIDTH), F32),
            ((2, groups * rows_f, MODEL_WIDTH), BF16),
            ((keys, MODEL_WIDTH), BF16),
        ],
        gq, gkv, flat_encoded, wkv.reshape(2 * MODEL_WIDTH, MODEL_WIDTH), gh_two, h_one, gain_self, gain_cross, wq_full,
        wq_self.T, wk_self.T, wv_self.T, wo_self, a1, qkv, p1, o1,
        a2_all.reshape(groups, *dealt), gc_all, o2_own, tokens, gain_ffn_grad, term, h_two, *gw_parts,
        spaces={0: hbm, 1: hbm, 2: hbm, 17: hbm, 18: hbm},
        out_spaces={7: hbm},
        scratch=[
            pltpu.VMEM((groups, *home), BF16),
            pltpu.VMEM((groups, near, *home), BF16),
            pltpu.VMEM((far, *home), BF16),
            pltpu.VMEM((2, step, 2 * MODEL_WIDTH), BF16),
            pltpu.VMEM((2, step, MODEL_WIDTH), BF16),
            pltpu.VMEM((2, step, MODEL_WIDTH), BF16),
            pltpu.VMEM((2 * MODEL_WIDTH, MODEL_WIDTH), F32),
            pltpu.VMEM((2, mp_parts, head_cols, MODEL_WIDTH), BF16),
            pltpu.VMEM((1, head_cols, MODEL_WIDTH), BF16),
            pltpu.VMEM((2, head_cols, MODEL_WIDTH), BF16),
            pltpu.VMEM((3, head_cols, MODEL_WIDTH), BF16),
            pltpu.VMEM(home, F32),
            pltpu.VMEM(own, BF16),
            pltpu.VMEM(own, BF16),
            pltpu.VMEM(dealt, BF16),
            pltpu.VMEM(dealt, BF16),
            pltpu.VMEM((3, n_tokens, head_cols), BF16),
            pltpu.VMEM((8, LANES), F32),
            pltpu.VMEM(dealt, BF16),
            pltpu.VMEM((mp_parts, chunk, STATW), BF16),
            pltpu.VMEM((near, *home), BF16),
            pltpu.VMEM((near, *home), BF16),
            pltpu.VMEM((2, mp_parts, half, MODEL_WIDTH), BF16),
            pltpu.VMEM((near, 2, half, MODEL_WIDTH), BF16),
            pltpu.VMEM((1, half, MODEL_WIDTH), BF16),
            pltpu.VMEM((2, half, MODEL_WIDTH), BF16),
            pltpu.VMEM((3, half, MODEL_WIDTH), BF16),
            *[pltpu.VMEM((groups * rows[k], MODEL_WIDTH), BF16) for k in "kcs"],
            *[pltpu.VMEM((far, rows[k], MODEL_WIDTH), BF16) for k in "kcs"],
            small,
            small,
            pltpu.VMEM((groups, 16, MODEL_WIDTH), F32),
            pltpu.VMEM((mp_parts, 16, MODEL_WIDTH), F32),
            many_sems(groups, near),
            pair_sems(far),
            pair_sems(near),
            pair_sems(near),
            pltpu.SemaphoreType.DMA((3,)),
            pltpu.SemaphoreType.DMA((2, 2)),
            pair,
            pair_sems(near),
            pair_sems(near),
            pair_sems(near),
            pair,
            pair_sems(near),
            pair,
            pair,
            pair,
            pair_sems(near),
            *[many_sems(3, far)] * 3,
            pair,
            pair_sems(far),
            pair_sems(near),
            many_sems(2, far),
        ],
    )
    shard = jax.ShapeDtypeStruct((head_cols, MODEL_WIDTH), F32)
    gain = jax.ShapeDtypeStruct((MODEL_WIDTH,), F32)
    y, gx, genc, gs, gc, gf, gb, *grads = pl.pallas_call(
        closing_kernel,
        out_shape=[
            *[jax.ShapeDtypeStruct(x.shape, x.dtype) for x in (output, grad_tokens, genc)],
            gain, gain, gain,
            jax.ShapeDtypeStruct((heads, BUCKETS), F32),
            *[shard] * 8,
            *[jax.ShapeDtypeStruct(square, F32)] * 2,
        ],
        in_specs=[pl.BlockSpec(memory_space=pltpu.VMEM)] * 8,
        out_specs=[pl.BlockSpec(memory_space=hbm)] * 3
        + [pl.BlockSpec(memory_space=pltpu.VMEM)] * 4
        + [pl.BlockSpec(memory_space=hbm)] * 10,
        scratch_shapes=[
            pltpu.VMEM((8, head_cols, MODEL_WIDTH), F32),
            pltpu.VMEM(square, F32),
            pltpu.VMEM(square, F32),
            pltpu.SemaphoreType.DMA((13,)),
        ],
        compiler_params=pltpu.CompilerParams(vmem_limit_bytes=VMEM_LIMIT),
    )(sum_k, sum_c, sum_s, sum_f, small_sums, genc, output, grad_tokens)

    return (
        y.reshape(n_tokens, MODEL_WIDTH),
        gx.reshape(n_tokens, MODEL_WIDTH),
        genc.reshape(GROUP_ROWS, quarter, MODEL_WIDTH),
        gs,
        gc,
        gf,
        gb.T,
        *[grads[i].T for i in range(3)],
        grads[3],
        *[grads[i].T for i in range(4, 7)],
        *grads[7:],
    )


def solution(mesh):
    tokens_in = P(("dp", "pass"), None)
    encoded_in = P(("dp", "pass"), "mp", None)
    by_column, by_row = P(None, "mp"), P("mp", None)
    weights = (by_column, by_column, by_column, by_row)
    return jax.shard_map(
        on_device,
        mesh=mesh,
        in_specs=(
            tokens_in, encoded_in, P("dp", None), P("dp", None), P(("dp", "pass")),
            P(), P(), P(), by_column,
            *weights, *weights, by_column, by_row, tokens_in,
        ),
        out_specs=(
            tokens_in, tokens_in, encoded_in, P(), P(), P(), by_column,
            *weights, *weights, by_column, by_row,
        ),
        check_vma=False,
    )
```

```python
import functools
import math

import jax
import jax.numpy as jnp
import numpy as np
from jax import lax
from jax.experimental import pallas as pl
from jax.experimental.pallas import tpu as pltpu
from jax.sharding import PartitionSpec as P

MODEL_WIDTH = 768
HD = 64
BUCKETS = 32
ANS = 20
PADT = 24
LANES = 128
STATW = MODEL_WIDTH + LANES
GROUP_ROWS = 32

EPSILON = 1e-06
NEGATIVE = -1e30
MESH = pl.DeviceIdType.MESH
VMEM_LIMIT = 61 << 20
F32 = jnp.float32
BF16 = jnp.bfloat16


def bucket_table(length, buckets):
    exact_half = buckets // 2
    result = np.zeros((length, length), np.int32)
    for target in range(length):
        for source in range(length):
            distance = max(target - source, 0)
            if distance < exact_half:
                result[target, source] = distance
            else:
                spread = int(
                    math.log(distance / exact_half)
                    / math.log(128 / exact_half)
                    * (buckets - exact_half)
                )
                result[target, source] = min(exact_half + spread, buckets - 1)
    return result


def dot_nn(a, b):
    return lax.dot_general(a, b, (((1,), (0,)), ((), ())), preferred_element_type=F32)


def dot_nt(a, b):
    return lax.dot_general(a, b, (((1,), (1,)), ((), ())), preferred_element_type=F32)


def dot_tn(a, b):
    return lax.dot_general(a, b, (((0,), (0,)), ((), ())), preferred_element_type=F32)


def rms_inverse(v):
    return lax.rsqrt(jnp.mean(v * v, axis=-1, keepdims=True) + EPSILON)


def row_of_gain(ref):
    return ref[...].reshape(1, ref.shape[0])


def rms_back(v, gains, ga):
    w = rms_inverse(v)
    gain_grad = jnp.sum(ga * v * w, axis=0, keepdims=True)
    gg = gains * ga
    gv = w * gg - v * (w * w * w) * jnp.mean(gg * v, axis=-1, keepdims=True)
    return gv, gain_grad


def local_call(kernel, outs, *ins, scratch=(), flops=0):
    return pl.pallas_call(
        kernel,
        out_shape=[jax.ShapeDtypeStruct(shape, dtype) for shape, dtype in outs],
        in_specs=[pl.BlockSpec(memory_space=pltpu.VMEM) for _ in ins],
        out_specs=[pl.BlockSpec(memory_space=pltpu.VMEM) for _ in outs],
        scratch_shapes=list(scratch),
        compiler_params=pltpu.CompilerParams(vmem_limit_bytes=VMEM_LIMIT),
        cost_estimate=pl.CostEstimate(
            flops=flops,
            bytes_accessed=sum(math.prod(x.shape) * x.dtype.itemsize for x in ins),
            transcendentals=0,
        ),
    )(*ins)


def place(**kw):
    return tuple(kw[a] if a in kw else lax.axis_index(a) for a in ("dp", "pass", "mp"))


def other(axis, k):
    n = lax.axis_size(axis)
    at = lax.rem(lax.axis_index(axis) + k, n)
    return at, place(**{axis: at})


def others(axis):
    return [(k - 1, *other(axis, k)) for k in range(1, lax.axis_size(axis))]


def greet(axes):
    barrier = pltpu.get_barrier_semaphore()
    peers = [peer for axis in axes for _, _, peer in others(axis)]
    for peer in peers:
        pl.semaphore_signal(barrier, inc=1, device_id=peer, device_id_type=MESH)
    pl.semaphore_wait(barrier, len(peers))


def remote(src, dst, send, recv, peer):
    return pltpu.make_async_remote_copy(
        src_ref=src, dst_ref=dst, send_sem=send, recv_sem=recv, device_id=peer, device_id_type=MESH
    )


def begin(copies):
    for copy in copies:
        copy.start()
    return copies


def finish(copies):
    for copy in copies:
        copy.wait()


def deal(source, slots, sems, axis):
    return begin([
        remote(source(at), slots.at[k], sems.at[0, k], sems.at[1, k], peer)
        for k, at, peer in others(axis)
    ])


def share(ref, sems, axis):
    return begin([remote(ref, ref, sems.at[0, k], sems.at[1, k], peer) for k, _, peer in others(axis)])


class Relay:
    def __init__(self, sems):
        self.sems, self.direct = sems, {}
        self.square = lax.axis_size("mp") == 4
        self.blocks, self.onward = {}, {}

    @staticmethod
    def near(which):
        mm = lax.axis_index("mp")
        at = mm + 1 - 2 * lax.rem(mm, 2) if which == 0 else mm + 2 - 4 * lax.div(mm, 2)
        return at, place(mp=at)

    def across(self):
        return 3 - lax.axis_index("mp")

    def put(self, i, block, own=None):
        mine = block(lax.axis_index("mp"))
        own = mine if own is None else own
        self.blocks[i] = block
        to = [(k, peer) for k, _, peer in others("mp")]
        if self.square:
            to = [(k, self.near(k)[1]) for k in range(2)]
        self.direct[i] = begin([
            remote(own, mine, self.sems.at[i, 0, k], self.sems.at[i, 1, k], peer) for k, peer in to
        ])

    def pass_on(self, i):
        if not self.square:
            return
        which = i % 2
        self.direct[i][which].wait_recv()
        block = self.blocks[i](self.near(which)[0])
        self.onward[i] = remote(
            block, block, self.sems.at[i, 0, 2], self.sems.at[i, 1, 2], self.near(1 - which)[1]
        )
        self.onward[i].start()

    def arrived(self, i):
        for k, copy in enumerate(self.direct[i]):
            if not self.square or k != i % 2:
                copy.wait_recv()
        if self.square:
            self.onward[i].wait_recv()

    def sent(self, i):
        for copy in self.direct[i]:
            copy.wait_send()
        if self.square:
            self.onward[i].wait_send()


def share_both(all_ref, zsems, msems):
    pn, pm, mm = lax.axis_size("pass"), lax.axis_index("pass"), lax.axis_index("mp")
    zcopies = share(all_ref.at[pm, mm], zsems, "pass")
    relay = Relay(msems)
    relay.put(0, lambda at: all_ref.at[pm, at])

    def forward(j):
        zcopies[j].wait_recv()
        source = lax.rem(pm - (j + 1) + pn, pn)
        relay.put(j + 1, lambda at: all_ref.at[source, at])
        relay.pass_on(j)

    def across():
        relay.pass_on(pn - 1)

    def end():
        for j in range(pn):
            relay.arrived(j)
            relay.sent(j)
        for copy in zcopies:
            copy.wait_send()

    return forward, across, end


def pair_sems(n):
    return pltpu.SemaphoreType.DMA((2, n))


def many_sems(m, n):
    return pltpu.SemaphoreType.DMA((m, 2, n))


def remote_call(kernel, collective_id, outs, *ins, spaces=None, out_spaces=None, scratch=()):
    vmem = pltpu.VMEM
    spaces = spaces or {}
    out_spaces = out_spaces or {}
    return pl.pallas_call(
        kernel,
        out_shape=[jax.ShapeDtypeStruct(shape, dtype) for shape, dtype in outs],
        in_specs=[pl.BlockSpec(memory_space=spaces.get(i, vmem)) for i in range(len(ins))],
        out_specs=[pl.BlockSpec(memory_space=out_spaces.get(i, vmem)) for i in range(len(outs))],
        scratch_shapes=list(scratch),
        compiler_params=pltpu.CompilerParams(
            collective_id=collective_id, has_side_effects=True, vmem_limit_bytes=VMEM_LIMIT
        ),
    )(*ins)


def home_rows(ref, chunk):
    at = pl.multiple_of(lax.axis_index("mp") * chunk, 16)
    return ref[pl.ds(at, chunk), :]


def total_of(first, slots):
    total = first.astype(F32)
    for k in range(slots.shape[0]):
        total = total + slots[k].astype(F32)
    return total


def bucket_grid(size):
    row = lax.broadcasted_iota(jnp.int32, (size, size), 0)
    col = lax.broadcasted_iota(jnp.int32, (size, size), 1)
    near = (col <= row) & (lax.div(col, ANS) == lax.div(row, ANS))
    table = bucket_table(ANS, BUCKETS)
    grid = jnp.full((size, size), -1, jnp.int32)
    for distance in range(ANS):
        grid = jnp.where(near & (row - col == distance), int(table[distance, 0]), grid)
    return grid, near, sorted({int(b) for b in table.reshape(-1)})


def self_forward(
    heads, x_ref, gain_ref, wq_ref, wk_ref, wv_ref, wo_ref, bias_ref, lens_ref,
    a1_ref, qkv_ref, p_ref, o1_ref, term_ref,
):
    x = x_ref[...].astype(F32)
    a1 = (x * rms_inverse(x) * row_of_gain(gain_ref)).astype(BF16)
    a1_ref[...] = a1
    for k, w_ref in enumerate((wq_ref, wk_ref, wv_ref)):
        qkv_ref[k] = dot_nt(a1, w_ref[...]).astype(BF16)
    blocks, size = term_ref.shape[0], term_ref.shape[1]
    grid, near, used = bucket_grid(size)
    biases = []
    for h in range(heads):
        bias = jnp.full((size, size), NEGATIVE, F32)
        for b in used:
            bias = jnp.where(grid == b, bias_ref[h, b], bias)
        biases.append(bias)
    lane = lax.broadcasted_iota(jnp.int32, (1, size), 1)
    for b in range(blocks):
        alive = jnp.zeros((1, size), jnp.int32)
        for q in range(size // ANS):
            inside = (lane >= q * ANS) & (lane < q * ANS + lens_ref[b * (size // ANS) + q])
            alive = jnp.where(inside, 1, alive)
        allowed = near & (alive > 0)
        rows = pl.ds(b * size, size)
        q, k, v = qkv_ref[0, rows, :], qkv_ref[1, rows, :], qkv_ref[2, rows, :]
        for h in range(heads):
            part = slice(h * HD, (h + 1) * HD)
            s = jnp.where(allowed, dot_nt(q[:, part], k[:, part]) + biases[h], NEGATIVE)
            e = jnp.exp(s - jnp.max(s, axis=-1, keepdims=True))
            p = e / jnp.sum(e, axis=-1, keepdims=True)
            p_ref[b * heads + h] = p
            o1_ref[rows, part] = dot_nn(p.astype(BF16), v[:, part]).astype(BF16)
    for b in range(blocks):
        term_ref[b] = dot_nn(o1_ref[pl.ds(b * size, size), :], wo_ref[...]).astype(BF16)


KV_STEPS = 8


def front_kernel(
    heads, x_ref, gain_ref, gain_cross_ref, wq_ref, wk_ref, wv_ref, wo_ref, bias_ref, lens_ref,
    wkc_ref, wvc_ref, wqc_ref, woc_ref, enc_ref,
    a2_ref, h_ref, a1_ref, qkv_ref, p_ref, o1_ref, wkv_ref, wq_out_ref, wo_out_ref, kv_ref,
    term, slots, enc, kv_slots, wsems, dsems, rsems, zsems, msems, own_sems, enc_sem, kv_sems,
):
    core, mm, pm = lax.axis_index("dp"), lax.axis_index("mp"), lax.axis_index("pass")
    mn, pn = lax.axis_size("mp"), lax.axis_size("pass")
    width = wkc_ref.shape[0]
    half = width // 2
    chunk = h_ref.shape[0]
    load = pltpu.make_async_copy(enc_ref, enc, enc_sem)
    load.start()
    pieces = [
        (wkc_ref, wkv_ref.at[0]), (wvc_ref, wkv_ref.at[1]), (wqc_ref, wq_out_ref), (woc_ref, wo_out_ref)
    ]

    def rows_of(source, which):
        return pl.ds(pl.multiple_of(source * width + which * half, 16), half)

    mine = pl.ds(pl.multiple_of(core * half, 16), half)
    owns = []
    for i, (shard, full) in enumerate(pieces):
        at = pl.ds(pl.multiple_of(mm * width, 16), width)
        own = pltpu.make_async_copy(shard, full.at[at], own_sems.at[i])
        own.start()
        owns.append(own)
    greet(("dp", "pass", "mp"))

    relay = Relay(wsems)

    def send_weight(i):
        shard, full = pieces[i]
        relay.put(i, lambda at: full.at[rows_of(at, core)], shard.at[mine])

    def to_other_core(i):
        full = pieces[i][1]
        relay.arrived(i)
        return begin([
            remote(
                full.at[rows_of(at, core)], full.at[rows_of(at, core)],
                dsems.at[i, 0, k], dsems.at[i, 1, k], other("dp", 1)[1],
            )
            for k, at, _ in others("mp")
        ])

    send_weight(0)
    send_weight(1)
    self_forward(
        heads, x_ref, gain_ref, wq_ref, wk_ref, wv_ref, wo_ref, bias_ref, lens_ref,
        a1_ref, qkv_ref, p_ref, o1_ref, term,
    )
    dealt = deal(lambda at: term.at[at], slots, rsems, "mp")
    relay.pass_on(0)
    relay.pass_on(1)
    for copy in dealt:
        copy.wait_recv()
    h = home_rows(x_ref, chunk).astype(F32) + total_of(term[mm], slots)
    h_ref[...] = h
    a2_ref[pm, mm] = (h * rms_inverse(h) * row_of_gain(gain_cross_ref)).astype(BF16)
    forward, across, end = share_both(a2_ref, zsems, msems)
    send_weight(2)
    send_weight(3)
    passed = [to_other_core(0), to_other_core(1)]
    for copies in passed:
        for copy in copies:
            copy.wait_recv()
    for own in owns:
        own.wait()
    load.wait()
    rows = enc.shape[0] // KV_STEPS

    def store(step):
        slot = lax.rem(step, 2)
        at = pl.ds(pl.multiple_of(step * rows, rows), rows)
        return pltpu.make_async_copy(kv_slots.at[slot], kv_ref.at[at], kv_sems.at[slot])

    def project(step, carry):
        slot = lax.rem(step, 2)

        @pl.when(step >= 2)
        def _():
            store(step - 2).wait()

        x = enc[pl.ds(pl.multiple_of(step * rows, rows), rows), :]
        for i in range(2):
            kv_slots[slot, :, i * MODEL_WIDTH : (i + 1) * MODEL_WIDTH] = dot_nt(x, wkv_ref[i]).astype(BF16)
        store(step).start()
        return carry

    done, onward = 0, [2, 3]
    for j in range(pn - 1):
        upto = KV_STEPS * (2 * j + 1) // (2 * pn)
        if upto > done:
            lax.fori_loop(done, upto, project, 0)
            done = upto
        forward(j)
        if onward:
            relay.pass_on(onward.pop(0))
    for i in onward:
        relay.pass_on(i)
    lax.fori_loop(done, KV_STEPS - 1, project, 0)
    across()
    lax.fori_loop(KV_STEPS - 1, KV_STEPS, project, 0)
    passed += [to_other_core(2), to_other_core(3)]
    for step in (KV_STEPS - 2, KV_STEPS - 1):
        store(step).wait()
    end()
    for copy in dealt:
        copy.wait_send()
    for i, copies in enumerate(passed):
        relay.sent(i)
        for copy in copies:
            copy.wait_send()
            if i >= 2:
                copy.wait_recv()


PAIR = 2 * HD
PAIRS = MODEL_WIDTH // PAIR
PROWS = 2 * PADT
FLOOR = -1e29


def low_lanes(shape):
    return lax.broadcasted_iota(jnp.int32, shape, len(shape) - 1) < HD


def pair_rows(dst_ref, pad_ref, values, stat=None, stat_at=0):
    questions = dst_ref.shape[0]
    low = low_lanes((1, PADT, PAIR))
    for q in range(questions):
        rows = slice(q * ANS, (q + 1) * ANS)
        pad_ref[q, 0:ANS, :MODEL_WIDTH] = values[rows, :]
        pad_ref[q, ANS:PADT, :] = jnp.zeros((PADT - ANS, pad_ref.shape[2]), F32)
        if stat is not None:
            pad_ref[q, 0:ANS, MODEL_WIDTH:] = stat[rows, :]
    lane = lax.broadcasted_iota(jnp.int32, (1, 1, LANES), 2)
    for c in range(PAIRS):
        x = pad_ref[:, :, c * PAIR : (c + 1) * PAIR]
        both = jnp.concatenate([jnp.where(low, x, 0.0), jnp.where(low, 0.0, x)], axis=1)
        dst_ref[:, c, :, :PAIR] = both.astype(BF16)
        if stat is not None:
            s = pad_ref[:, :, MODEL_WIDTH:]
            parts = []
            for h in (2 * c, 2 * c + 1):
                at = lane - (stat_at + h)
                parts.append(s * ((at == 0) | (at == 16) | (at == 32)).astype(F32))
            dst_ref[:, c, :, PAIR:] = jnp.concatenate(parts, axis=1).astype(BF16)


def segment_mask(lens_ref, row, keys):
    lane = lax.broadcasted_iota(jnp.int32, (PROWS, keys), 1)
    cut = lens_ref[0, row] - lax.axis_index("mp") * keys
    return [lane < cut, (lane >= cut) & (lane < cut + lens_ref[1, row])]


def masked(scores, mask):
    return jnp.concatenate(
        [jnp.where(mask[s], scores[s * PROWS : (s + 1) * PROWS], NEGATIVE) for s in range(2)], axis=0
    )


def fold_pair(x, s, low):
    at = s * PROWS
    return jnp.where(low, x[at : at + PADT], x[at + PADT : at + PROWS])


def split_three(x):
    hi = x.astype(BF16).astype(F32)
    mid = (x - hi).astype(BF16).astype(F32)
    return hi, mid, x - hi - mid


def staged(rows_per, stages):
    depth = len(stages)
    for i in range(rows_per + depth - 1):
        for k in reversed(range(depth)):
            if 0 <= i - k < rows_per:
                stages[k](i - k, (i - k) % 2)


def cross_forward_kernel(
    rows_per, keys, lens_ref, owners_ref, a2_ref, wq_ref, kv_ref, out_ref,
    q_rows, pad, s_buf, p_buf, t_buf, o_acc, m_acc, l_acc, flat,
):
    g = pl.program_id(0)
    pair_rows(q_rows, pad, dot_nt(a2_ref[0], wq_ref[...]).astype(BF16).astype(F32))
    o_acc[...] = jnp.zeros_like(o_acc)
    m_acc[...] = jnp.full_like(m_acc, FLOOR)
    l_acc[...] = jnp.zeros_like(l_acc)
    low = low_lanes((PADT, PAIR))
    ones = jnp.ones((keys, PAIR), BF16)

    def row_of(r):
        return lax.axis_index("pass") * GROUP_ROWS + g * rows_per + r

    def owners_of(r):
        return [owners_ref[0, row_of(r)], owners_ref[1, row_of(r)]]

    def scores(r, slot):
        owners = owners_of(r)
        mask = segment_mask(lens_ref, row_of(r), keys)
        for c in range(PAIRS):
            k = kv_ref[r * keys : (r + 1) * keys, c * PAIR : (c + 1) * PAIR]
            qm = jnp.concatenate([q_rows[q, c] for q in owners], axis=0)
            s_buf[slot, c] = masked(dot_nt(qm, k), mask)

    def chances(r, slot):
        for c in range(PAIRS):
            s = s_buf[slot, c]
            top = jnp.maximum(jnp.max(s, axis=-1, keepdims=True), FLOOR)
            p_buf[slot, c] = jnp.exp(s - top).astype(BF16)
            top = jnp.broadcast_to(top, (2 * PROWS, PAIR))
            for i in range(2):
                t_buf[slot, c, i] = fold_pair(top, i, low)

    def values(r, slot):
        owners = owners_of(r)
        new = []
        for c in range(PAIRS):
            v = kv_ref[r * keys : (r + 1) * keys, MODEL_WIDTH + c * PAIR : MODEL_WIDTH + (c + 1) * PAIR]
            both = dot_nn(p_buf[slot, c], jnp.concatenate([v, ones], axis=1))
            new.append([
                (fold_pair(both[:, :PAIR], i, low), fold_pair(both[:, PAIR:], i, low)) for i in range(2)
            ])
        for i, q in enumerate(owners):
            for c in range(PAIRS):
                cols = slice(c * PAIR, (c + 1) * PAIR)
                o, l = new[c][i]
                m_old, m_new = m_acc[q, :, cols], t_buf[slot, c, i]
                m_both = jnp.maximum(m_old, m_new)
                a, b = jnp.exp(m_old - m_both), jnp.exp(m_new - m_both)
                o_acc[q, :, cols] = a * o_acc[q, :, cols] + b * o
                l_acc[q, :, cols] = a * l_acc[q, :, cols] + b * l
                m_acc[q, :, cols] = m_both

    staged(rows_per, [scores, chances, values])
    questions = q_rows.shape[0]
    lane = lax.broadcasted_iota(jnp.int32, (PADT, LANES), 1)
    for q in range(questions):
        l = l_acc[q]
        some = l > 0.0
        safe = jnp.where(some, l, 1.0)
        o = o_acc[q] / safe
        lse = jnp.where(some, m_acc[q] + jnp.log(safe), NEGATIVE)
        few = jnp.zeros((PADT, LANES), F32)
        for h in range(MODEL_WIDTH // HD):
            few = jnp.where(lane == h, lse[:, h * HD : h * HD + 1], few)
        hi, mid, rest = split_three(few)
        stat = hi + pltpu.roll(mid, 16, 1) + pltpu.roll(rest, 32, 1)
        flat[q * ANS : (q + 1) * ANS, :MODEL_WIDTH] = o[:ANS]
        flat[q * ANS : (q + 1) * ANS, MODEL_WIDTH:] = stat[:ANS]
    chunk = out_ref.shape[2]
    for m in range(out_ref.shape[0]):
        out_ref[m, 0] = flat[m * chunk : (m + 1) * chunk, :].astype(BF16)


def cross_forward(lens, owners, a2_all, wq, kv, mp_parts):
    groups, n_tokens, _ = a2_all.shape
    rows_per = GROUP_ROWS // groups
    keys = kv.shape[0] // GROUP_ROWS
    questions = n_tokens // ANS
    block = rows_per * keys
    padded = pltpu.VMEM((questions, PADT, MODEL_WIDTH), F32)
    return pl.pallas_call(
        functools.partial(cross_forward_kernel, rows_per, keys),
        grid_spec=pltpu.PrefetchScalarGridSpec(
            num_scalar_prefetch=2,
            grid=(groups,),
            in_specs=[
                pl.BlockSpec((1, n_tokens, MODEL_WIDTH), lambda g, *_: (g, 0, 0)),
                pl.BlockSpec((MODEL_WIDTH, MODEL_WIDTH), lambda g, *_: (0, 0)),
                pl.BlockSpec((block, 2 * MODEL_WIDTH), lambda g, *_: (g, 0)),
            ],
            out_specs=pl.BlockSpec(
                (mp_parts, 1, n_tokens // mp_parts, STATW), lambda g, *_: (0, g, 0, 0)
            ),
            scratch_shapes=[
                pltpu.VMEM((questions, PAIRS, PROWS, PAIR), BF16),
                padded,
                pltpu.VMEM((2, PAIRS, 2 * PROWS, keys), F32),
                pltpu.VMEM((2, PAIRS, 2 * PROWS, keys), BF16),
                pltpu.VMEM((2, PAIRS, 2, PADT, PAIR), F32),
                padded,
                padded,
                padded,
                pltpu.VMEM((n_tokens, STATW), F32),
            ],
        ),
        out_shape=jax.ShapeDtypeStruct((mp_parts, groups, n_tokens // mp_parts, STATW), BF16),
        compiler_params=pltpu.CompilerParams(vmem_limit_bytes=VMEM_LIMIT),
    )(lens, owners, a2_all, wq, kv)


def cross_backward_kernel(
    rows_per, keys, lens_ref, owners_ref, a2_ref, gc_ref, wq_ref, wo_ref, kv_ref, gq_ref, gkv_ref,
    q_rows, go_rows, pad, s_buf, gp_buf, p_buf, gs_buf, gq_acc, flat,
):
    g = pl.program_id(0)
    stat = gc_ref[0, :, MODEL_WIDTH:].astype(F32)
    q2 = dot_nt(a2_ref[0], wq_ref[...]).astype(BF16).astype(F32)
    pair_rows(q_rows, pad, q2, stat, 0)
    go2 = dot_nt(gc_ref[0, :, :MODEL_WIDTH], wo_ref[...]).astype(BF16).astype(F32)
    pair_rows(go_rows, pad, go2, stat, 48)
    gq_acc[...] = jnp.zeros_like(gq_acc)
    low = low_lanes((PADT, PAIR))
    minus = jnp.full((keys, LANES), -1.0, BF16)

    def row_of(r):
        return lax.axis_index("pass") * GROUP_ROWS + g * rows_per + r

    def owners_of(r):
        return [owners_ref[0, row_of(r)], owners_ref[1, row_of(r)]]

    def tile(r, c, off):
        return kv_ref[r * keys : (r + 1) * keys, off + c * PAIR : off + (c + 1) * PAIR]

    def scores(r, slot):
        owners = owners_of(r)
        mask = segment_mask(lens_ref, row_of(r), keys)
        for c in range(PAIRS):
            qm = jnp.concatenate([q_rows[q, c] for q in owners], axis=0)
            gom = jnp.concatenate([go_rows[q, c] for q in owners], axis=0)
            s = dot_nt(qm, jnp.concatenate([tile(r, c, 0), minus], axis=1))
            s_buf[slot, c] = masked(s, mask)
            gp_buf[slot, c] = dot_nt(gom, jnp.concatenate([tile(r, c, MODEL_WIDTH), minus], axis=1))

    def chances(r, slot):
        for c in range(PAIRS):
            p = jnp.exp(s_buf[slot, c])
            p_buf[slot, c] = p.astype(BF16)
            gs_buf[slot, c] = (p * gp_buf[slot, c]).astype(BF16)

    def grads(r, slot):
        owners = owners_of(r)
        new = []
        rows = slice(r * keys, (r + 1) * keys)
        for c in range(PAIRS):
            gs, p = gs_buf[slot, c], p_buf[slot, c]
            qm = jnp.concatenate([q_rows[q, c, :, :PAIR] for q in owners], axis=0)
            gom = jnp.concatenate([go_rows[q, c, :, :PAIR] for q in owners], axis=0)
            gkv_ref[rows, c * PAIR : (c + 1) * PAIR] = dot_tn(gs, qm).astype(BF16)
            gkv_ref[rows, MODEL_WIDTH + c * PAIR : MODEL_WIDTH + (c + 1) * PAIR] = dot_tn(p, gom).astype(BF16)
            gq = dot_nn(gs, tile(r, c, 0))
            new.append([fold_pair(gq, i, low) for i in range(2)])
        for i, q in enumerate(owners):
            for c in range(PAIRS):
                cols = slice(c * PAIR, (c + 1) * PAIR)
                gq_acc[q, :, cols] = gq_acc[q, :, cols] + new[c][i]

    staged(rows_per, [scores, chances, grads])
    for q in range(q_rows.shape[0]):
        flat[q * ANS : (q + 1) * ANS, :] = gq_acc[q, :ANS, :]
    chunk = gq_ref.shape[2]
    for m in range(gq_ref.shape[0]):
        gq_ref[m, 0] = flat[m * chunk : (m + 1) * chunk, :].astype(BF16)


def cross_backward(lens, owners, a2_all, gc_all, wq, wo, kv, mp_parts):
    groups, n_tokens, _ = a2_all.shape
    rows_per = GROUP_ROWS // groups
    keys = kv.shape[0] // GROUP_ROWS
    questions = n_tokens // ANS
    block = rows_per * keys
    rows = pltpu.VMEM((questions, PAIRS, PROWS, PAIR + LANES), BF16)
    whole = pl.BlockSpec((MODEL_WIDTH, MODEL_WIDTH), lambda g, *_: (0, 0))
    return pl.pallas_call(
        functools.partial(cross_backward_kernel, rows_per, keys),
        grid_spec=pltpu.PrefetchScalarGridSpec(
            num_scalar_prefetch=2,
            grid=(groups,),
            in_specs=[
                pl.BlockSpec((1, n_tokens, MODEL_WIDTH), lambda g, *_: (g, 0, 0)),
                pl.BlockSpec((1, n_tokens, STATW), lambda g, *_: (g, 0, 0)),
                whole,
                whole,
                pl.BlockSpec((block, 2 * MODEL_WIDTH), lambda g, *_: (g, 0)),
            ],
            out_specs=[
                pl.BlockSpec(
                    (mp_parts, 1, n_tokens // mp_parts, MODEL_WIDTH), lambda g, *_: (0, g, 0, 0)
                ),
                pl.BlockSpec((block, 2 * MODEL_WIDTH), lambda g, *_: (g, 0)),
            ],
            scratch_shapes=[
                rows,
                rows,
                pltpu.VMEM((questions, PADT, STATW), F32),
                pltpu.VMEM((2, PAIRS, 2 * PROWS, keys), F32),
                pltpu.VMEM((2, PAIRS, 2 * PROWS, keys), F32),
                pltpu.VMEM((2, PAIRS, 2 * PROWS, keys), BF16),
                pltpu.VMEM((2, PAIRS, 2 * PROWS, keys), BF16),
                pltpu.VMEM((questions, PADT, MODEL_WIDTH), F32),
                pltpu.VMEM((n_tokens, MODEL_WIDTH), F32),
            ],
        ),
        out_shape=[
            jax.ShapeDtypeStruct((mp_parts, groups, n_tokens // mp_parts, MODEL_WIDTH), BF16),
            jax.ShapeDtypeStruct(kv.shape, BF16),
        ],
        compiler_params=pltpu.CompilerParams(vmem_limit_bytes=VMEM_LIMIT),
    )(lens, owners, a2_all, gc_all, wq, wo, kv)


def widen(w):
    row = lax.broadcasted_iota(jnp.int32, (LANES, MODEL_WIDTH), 0)
    col = lax.broadcasted_iota(jnp.int32, (LANES, MODEL_WIDTH), 1)
    each = (row == lax.div(col, HD)).astype(BF16)
    hi = w.astype(BF16)
    low = (w - hi.astype(F32)).astype(BF16)
    return dot_nn(hi, each) + dot_nn(low, each)


def combined(parts):
    lses = []
    for part in parts:
        stat = part[:, MODEL_WIDTH:].astype(F32)
        lses.append(stat + pltpu.roll(stat, LANES - 16, 1) + pltpu.roll(stat, LANES - 32, 1))
    top = functools.reduce(jnp.maximum, lses)
    weights = [jnp.exp(x - top) for x in lses]
    total = functools.reduce(jnp.add, weights)
    out = 0.0
    for part, weight in zip(parts, weights):
        out = out + widen(weight / total) * part[:, :MODEL_WIDTH].astype(F32)
    lane = lax.broadcasted_iota(jnp.int32, total.shape, 1)
    lse = jnp.where(lane < MODEL_WIDTH // HD, top + jnp.log(total), 0.0)
    return out, lse


def packed_stat(lse, at=0):
    hi, mid, low = split_three(lse)
    parts = [hi if at == 0 else pltpu.roll(hi, at, 1)]
    parts += [pltpu.roll(mid, at + 16, 1), pltpu.roll(low, at + 32, 1)]
    return parts[0] + parts[1] + parts[2]


def deal_groups(source, slots, sems):
    pn, pm = lax.axis_size("pass"), lax.axis_index("pass")
    for step in range(pn):
        group = lax.rem(pm + 1 + step, pn)
        deal(lambda at: source.at[at, group], slots.at[step], sems.at[step], "mp")


def middle_kernel(
    part_ref, h_ref, wo_ref, gain_ref, w_in_ref, w_out_ref, gy_ref,
    h2_ref, own_ref, term_ref, gh_ref, gc_ref, gain_out_ref, *refs,
):
    count = lax.axis_size("pass")
    pieces, refs = refs[:count], refs[count:]
    (
        held, slots, zslots, blocks, a3_all, ga3, gw, ga_slots, gw_slot, y, gc_home,
        msems, gsems, asems, bsems, rsems, zsems, relay_sems, gw_sems, load_sem, own_sem,
    ) = refs
    core, mm, pm = lax.axis_index("dp"), lax.axis_index("mp"), lax.axis_index("pass")
    pn = lax.axis_size("pass")
    load = pltpu.make_async_copy(part_ref.at[mm], held, load_sem)
    load.start()
    greet(("dp", "pass", "mp"))
    deal_groups(part_ref, slots, msems)
    load.wait()

    def add(parts):
        out, lse = combined(parts)
        return jnp.concatenate([out, packed_stat(lse)], axis=1).astype(BF16)

    def arrived(step):
        group = lax.rem(pm + 1 + step, pn)
        for k, at, peer in others("mp"):
            remote(
                part_ref.at[at, group], slots.at[step, k], msems.at[step, 0, k], msems.at[step, 1, k], peer
            ).wait()
        held[group] = add([held[group]] + [slots[step, k] for k in range(slots.shape[1])])

    def to_home(step):
        at, peer = other("pass", step + 1)
        return remote(held.at[at], zslots.at[step], gsems.at[0, step], gsems.at[1, step], peer)

    def one(step, carry):
        arrived(step)
        to_home(step).start()
        return carry

    if pn <= 4:
        for step in range(pn - 1):
            one(step, 0)
    else:
        lax.fori_loop(0, pn - 1, one, 0)
    arrived(pn - 1)
    for step in range(pn - 1):
        to_home(step).wait()
    o, lse = combined([held[pm]] + [zslots[k] for k in range(pn - 1)])
    low = o.astype(BF16)
    h2 = h_ref[...] + dot_nn(low, wo_ref[...])
    a3_all[mm] = (h2 * rms_inverse(h2) * row_of_gain(gain_ref)).astype(BF16)
    copies = share(a3_all.at[mm], asems, "mp")
    h2_ref[...] = h2
    width = blocks.shape[2]
    parts = blocks.shape[0]
    for k in range(parts):
        blocks[k] = low[:, k * width : (k + 1) * width]
    own_ref[mm] = blocks[mm]
    block_copies = begin([
        remote(blocks.at[at], own_ref.at[mm], bsems.at[0, k], bsems.at[1, k], peer)
        for k, at, peer in others("mp")
    ])
    gy = gy_ref[...]
    ge = dot_nt(gy, w_out_ref[...]).astype(BF16).astype(F32)
    finish(copies)
    a3 = jnp.concatenate([a3_all[k] for k in range(parts)], axis=0)
    u = dot_nn(a3, w_in_ref[...])
    cdf = 0.5 * (1.0 + lax.erf(u * np.float32(math.sqrt(0.5))))
    pdf = np.float32(1.0 / math.sqrt(2.0 * math.pi)) * jnp.exp(-0.5 * u * u)
    gu = (ge * (cdf + u * pdf)).astype(BF16)
    ga = dot_nt(gu, w_in_ref[...]).astype(BF16)
    chunk = h_ref.shape[0]
    for k in range(parts):
        ga3[k] = ga[k * chunk : (k + 1) * chunk]
    dealt = deal(lambda at: ga3.at[at], ga_slots, rsems, "mp")
    e = (u * cdf).astype(BF16)
    gw[0] = dot_tn(a3, gu).astype(BF16)
    gw[1] = dot_tn(e, gy).astype(BF16)
    swapped = remote(gw.at[1 - core], gw_slot, gw_sems.at[0], gw_sems.at[1], other("dp", 1)[1])
    swapped.start()
    term = dot_nn(e, w_out_ref[...]).astype(BF16)
    for k in range(parts):
        term_ref[k] = term[k * chunk : (k + 1) * chunk]
    finish(dealt)
    gv, gain_grad = rms_back(h2, row_of_gain(gain_ref), total_of(ga3[mm], ga_slots))
    gain_out_ref[...] = gain_grad
    gh = home_rows(gy_ref, chunk).astype(F32) + gv
    gh_ref[...] = gh
    gc = gh.astype(BF16)
    go = dot_nt(gc, wo_ref[...]).astype(BF16).astype(F32)
    row = lax.broadcasted_iota(jnp.int32, (MODEL_WIDTH, LANES), 0)
    col = lax.broadcasted_iota(jnp.int32, (MODEL_WIDTH, LANES), 1)
    each = (lax.div(row, HD) == col).astype(F32)
    delta = lax.dot_general(
        go * o, each, (((1,), (0,)), ((), ())),
        preferred_element_type=F32, precision=lax.Precision.HIGHEST,
    )
    stat = packed_stat(lse) + packed_stat(delta, 48)
    gc_home[...] = jnp.concatenate([gc, stat.astype(BF16)], axis=1)
    own = pltpu.make_async_copy(gc_home, gc_ref.at[pm, mm], own_sem)
    own.start()
    own.wait()
    forward, across, end = share_both(gc_ref, zsems, relay_sems)
    swapped.wait()
    used = gw_slot.shape[0]
    y[0:used, :] = (gw[core].astype(F32) + gw_slot[...].astype(F32)).astype(BF16)
    fill_tail(y, used)
    rows = pieces[0].shape[0]
    for k, piece in enumerate(pieces):
        piece[...] = y[pl.ds(pl.multiple_of(lax.rem(pm + k, pn) * rows, 16), rows), :]
    for j in range(pn - 1):
        forward(j)
    across()
    finish(block_copies)
    end()


def sum_rows(rows, groups):
    return -(-rows // (groups * 16)) * 16


class GroupSum:
    def __init__(self, y, zslots, out, sems):
        self.y, self.zslots, self.out, self.sems = y, zslots, out, sems
        self.rows = zslots.shape[1]

    def part(self, at):
        return pl.ds(pl.multiple_of(at * self.rows, 16), self.rows)

    def dealing(self):
        return [
            remote(self.y.at[self.part(at)], self.zslots.at[k], self.sems.at[0, 0, k], self.sems.at[0, 1, k], peer)
            for k, at, peer in others("pass")
        ]

    def sharing(self):
        here = self.out.at[lax.axis_index("dp"), self.part(lax.axis_index("pass"))]
        return [
            remote(here, here, self.sems.at[1, 0, k], self.sems.at[1, 1, k], peer)
            for k, _, peer in others("pass")
        ]

    def swapping(self):
        here = self.out.at[lax.axis_index("dp")]
        return [remote(here, here, self.sems.at[2, 0, 0], self.sems.at[2, 1, 0], other("dp", 1)[1])]

    def spread(self):
        begin(self.dealing())

    def gather(self):
        finish(self.dealing())
        at = self.part(lax.axis_index("pass"))
        total = total_of(self.y[at, :], self.zslots)
        self.out[lax.axis_index("dp"), at, :] = total.astype(BF16)
        begin(self.sharing())

    def swap(self):
        finish(self.sharing())
        begin(self.swapping())

    def end(self):
        finish(self.swapping())


def fill_tail(y, used):
    if y.shape[0] > used:
        y[used:, :] = jnp.zeros((y.shape[0] - used, y.shape[1]), y.dtype)


def self_backward(
    heads, gsa, wq_ref, wk_ref, wv_ref, wo_ref, qkv_ref, p_ref, ga1_ref, gqkv_ref, bias_ref
):
    go1 = dot_nt(gsa, wo_ref[...]).astype(BF16)
    blocks, size = ga1_ref.shape[0], ga1_ref.shape[1]
    grid, _, used = bucket_grid(size)
    at_row = lax.broadcasted_iota(jnp.int32, bias_ref.shape, 0)
    at_lane = lax.broadcasted_iota(jnp.int32, bias_ref.shape, 1)
    totals = []
    for h in range(heads):
        part = slice(h * HD, (h + 1) * HD)
        total = jnp.zeros((size, size), F32)
        for b in range(blocks):
            rows = pl.ds(b * size, size)
            q, k, v = qkv_ref[0, rows, part], qkv_ref[1, rows, part], qkv_ref[2, rows, part]
            p = p_ref[b * heads + h]
            go = go1[b * size : (b + 1) * size, part]
            gp = dot_nt(go, v)
            gs = (p * (gp - jnp.sum(gp * p, axis=-1, keepdims=True))).astype(BF16)
            total = total + gs.astype(F32)
            gqkv_ref[0, rows, part] = dot_nn(gs, k).astype(BF16)
            gqkv_ref[1, rows, part] = dot_tn(gs, q).astype(BF16)
            gqkv_ref[2, rows, part] = dot_tn(p.astype(BF16), go).astype(BF16)
        totals.append(total)
    ga1 = dot_nn(gqkv_ref[0], wq_ref[...])
    ga1 = ga1 + dot_nn(gqkv_ref[1], wk_ref[...])
    ga1 = ga1 + dot_nn(gqkv_ref[2], wv_ref[...])
    for b in range(blocks):
        ga1_ref[b] = ga1[b * size : (b + 1) * size].astype(BF16)

    def bias_sums():
        bias = jnp.zeros(bias_ref.shape, F32)
        for h, total in enumerate(totals):
            for b in used:
                value = jnp.sum(jnp.where(grid == b, total, 0.0), keepdims=True)
                bias = jnp.where((at_row == h) & (at_lane == b), value, bias)
        bias_ref[...] = bias

    return bias_sums


def finish_kernel(
    heads, gq_ref, gkv_ref, enc_ref, wkv_ref, gh2_ref, h_ref, gain_ref, gain_cross_ref, wq_ref,
    ws_q_ref, ws_k_ref, ws_v_ref, ws_o_ref, a1_ref, qkv_ref, p_ref, o1_ref,
    a2_ref, gc_ref, o2_ref, x_ref, ffn_gain_ref, term_ref, h2_ref, *refs,
):
    count = lax.axis_size("pass")
    gw_parts, refs = refs[:count], refs[count:]
    (
    gx_ref, out_ref, sum_k_ref, sum_c_ref, sum_s_ref, small_ref, sum_f_ref, genc_ref,
    held, slots, zslots, gkv_in, enc_in, genc_out, gw_acc, gw_kv, gw_o, gw_c, gw_s, gh1,
    blocks, gq_own, gsa_all, ga1, gqkv, bias, a2_own, gc_own,
    ga_slots, term_slots, kv_core, kv_slots, core_o, core_c, core_s,
    y_k, y_c, y_s, z_k, z_c, z_s, small, small_dp, small_z, small_m,
    msems, gzsems, asems, bsems, load_sems, in_sems, genc_sems,
    ga_sems, term_sems, out_sems, kv_dsems, kv_msems, co_sems, cc_sems, cs_sems, gx_sems,
    zk_sems, zc_sems, zs_sems, sd_sems, sz_sems, sm_sems,
    f_sems,
    ) = refs
    core, mm, pm = lax.axis_index("dp"), lax.axis_index("mp"), lax.axis_index("pass")
    pn = lax.axis_size("pass")
    chunk = h_ref.shape[0]
    width = o1_ref.shape[1]
    half = width // 2
    mine = pl.ds(pl.multiple_of(core * half, 16), half)
    theirs = pl.ds(pl.multiple_of((1 - core) * half, 16), half)
    peer = other("dp", 1)[1]
    loads = begin([
        pltpu.make_async_copy(gq_ref.at[mm], held, load_sems.at[0]),
        pltpu.make_async_copy(a2_ref.at[pm], a2_own, load_sems.at[1]),
        pltpu.make_async_copy(gc_ref.at[pm], gc_own, load_sems.at[2]),
    ])
    rows = gkv_in.shape[1]
    steps = gkv_ref.shape[0] // rows

    def step_rows(step):
        return pl.ds(pl.multiple_of(step * rows, rows), rows)

    def fetch_gkv(step, slot):
        return pltpu.make_async_copy(gkv_ref.at[step_rows(step)], gkv_in.at[slot], in_sems.at[slot, 0])

    def fetch_enc(step, slot):
        return pltpu.make_async_copy(enc_ref.at[step_rows(step)], enc_in.at[slot], in_sems.at[slot, 1])

    def store(step, slot):
        return pltpu.make_async_copy(genc_out.at[slot], genc_ref.at[step_rows(step)], genc_sems.at[slot])

    fetch_gkv(0, 0).start()
    fetch_enc(0, 0).start()
    greet(("dp", "pass", "mp"))
    for step in range(pn):
        group = lax.rem(pm + 1 + step, pn)
        deal(lambda at: gq_ref.at[at, group], slots.at[step], msems.at[step], "mp")
    finish(loads)

    def to_home(step):
        at, to = other("pass", step + 1)
        return remote(held.at[at], zslots.at[step], gzsems.at[0, step], gzsems.at[1, step], to)

    def arrived(step, carry):
        group = lax.rem(pm + 1 + step, pn)
        for k, at, to in others("mp"):
            remote(
                gq_ref.at[at, group], slots.at[step, k], msems.at[step, 0, k], msems.at[step, 1, k], to
            ).wait()
        total = held[group].astype(F32)
        for k in range(slots.shape[1]):
            total = total + slots[step, k].astype(F32)
        held[group] = total.astype(BF16)

        @pl.when(step < pn - 1)
        def _():
            to_home(step).start()

        return carry

    def arrivals(step):
        last = steps * 13 // 8
        lax.fori_loop(
            lax.min(lax.div(step * pn, last), pn), lax.min(lax.div((step + 1) * pn, last), pn), arrived, 0
        )

    parts = blocks.shape[0]

    def both_cores(copy, gw, got, y, first=0):
        copy.wait()
        for i in range(gw.shape[0]):
            at = pl.ds(pl.multiple_of(lax.axis_index("dp") * half, 16), half)
            to = (first + i) * half
            y[to : to + half, :] = (gw[i, at, :].astype(F32) + got[i].astype(F32)).astype(BF16)
        fill_tail(y, (first + gw.shape[0]) * half)

    total = gw_parts[0][...].astype(F32)
    for part in gw_parts[1:]:
        total = total + part[...].astype(F32)
    f_rows = pl.ds(pl.multiple_of(pm * total.shape[0], 16), total.shape[0])
    sum_f_ref[core, f_rows, :] = total.astype(BF16)
    f_copies = share(sum_f_ref.at[core, f_rows], f_sems.at[0], "pass")
    total = jnp.zeros((width, MODEL_WIDTH), F32)
    for k in range(parts):
        total = total + dot_tn(o2_ref[k], gc_own[k, :, :MODEL_WIDTH])
    gw_o[0] = total.astype(BF16)

    def core_copy(gw, got, sems):
        to = other("dp", 1)[1]
        off = pl.multiple_of((1 - lax.axis_index("dp")) * half, 16)
        where = (slice(None),) * (len(gw.shape) - 2) + (pl.ds(off, half),)
        return remote(gw.at[where], got, sems.at[0], sems.at[1], to)

    core_copy(gw_o, core_o, co_sems).start()
    gw_acc[...] = jnp.zeros_like(gw_acc)

    def weights(step, carry):
        slot = lax.rem(step, 2)

        @pl.when(step + 1 < steps)
        def _():
            fetch_gkv(step + 1, 1 - slot).start()
            fetch_enc(step + 1, 1 - slot).start()

        fetch_gkv(step, slot).wait()
        fetch_enc(step, slot).wait()
        for i in range(2):
            part = slice(i * MODEL_WIDTH, (i + 1) * MODEL_WIDTH)
            gw_acc[part, :] += dot_tn(gkv_in[slot, :, part], enc_in[slot])
        arrivals(step)

        @pl.when(step == 1)
        def _():
            both_cores(core_copy(gw_o, core_o, co_sems), gw_o, core_o, y_k, 2)

        return carry

    lax.fori_loop(0, steps, weights, 0)
    fetch_gkv(0, 0).start()
    for i in range(2):
        for k in range(parts):
            at = (i * parts + k) * width
            gw_kv[i, k] = gw_acc[at : at + width, :].astype(BF16)
    core_copy(gw_kv, kv_core, kv_dsems).start()

    def mine_rows():
        return pl.ds(pl.multiple_of(lax.axis_index("dp") * half, 16), half)

    def kv_copies():
        return [
            remote(gw_kv.at[:, at, mine_rows()], kv_slots.at[k], kv_msems.at[0, k], kv_msems.at[1, k], to)
            for k, at, to in others("mp")
        ]

    def encodings(step, carry):
        slot = lax.rem(step, 2)

        @pl.when(step + 1 < steps)
        def _():
            fetch_gkv(step + 1, 1 - slot).start()

        fetch_gkv(step, slot).wait()

        @pl.when(step >= 2)
        def _():
            store(step - 2, slot).wait()

        genc_out[slot] = dot_nn(gkv_in[slot], wkv_ref[...]).astype(BF16)
        store(step, slot).start()
        arrivals(steps + step)

        @pl.when(step == 1)
        def _():
            core_copy(gw_kv, kv_core, kv_dsems).wait()
            at = pl.ds(pl.multiple_of(lax.axis_index("dp") * half, 16), half)
            for i in range(2):
                for k in range(parts):
                    gw_kv[i, k, at, :] = (gw_kv[i, k, at, :].astype(F32) + kv_core[i, k].astype(F32)).astype(BF16)
            begin(kv_copies())

        @pl.when(step == steps - 2)
        def _():
            for at in range(pn - 1):
                to_home(at).wait()
            low = total_of(held[pm], zslots).astype(BF16)
            gv, cross_gain = rms_back(h_ref[...], row_of_gain(gain_cross_ref), dot_nn(low, wq_ref[...]))
            gh = gh2_ref[...] + gv
            gh1[...] = gh
            gsa_all[mm] = gh.astype(BF16)
            begin(gsa_copies())
            small[...] = jnp.zeros_like(small)
            small[1:2, :] = cross_gain
            for k in range(parts):
                blocks[k] = low[:, k * width : (k + 1) * width]
            gq_own[mm] = blocks[mm]
            begin(block_copies())

        return carry

    def gsa_copies():
        here = gsa_all.at[mm]
        return [remote(here, here, asems.at[0, k], asems.at[1, k], to) for k, _, to in others("mp")]

    def block_copies():
        return [
            remote(blocks.at[at], gq_own.at[mm], bsems.at[0, k], bsems.at[1, k], to)
            for k, at, to in others("mp")
        ]

    lax.fori_loop(0, steps, encodings, 0)
    finish(f_copies)
    f_copies = share(sum_f_ref.at[core], f_sems.at[1], "dp")
    for step in (steps - 2, steps - 1):
        store(step, step % 2).wait()
    finish(kv_copies())
    for i in range(2):
        total = gw_kv[i, mm, mine, :].astype(F32)
        for k in range(kv_slots.shape[0]):
            total = total + kv_slots[k, i].astype(F32)
        y_k[i * half : (i + 1) * half, :] = total.astype(BF16)
    sum_k = GroupSum(y_k, z_k, sum_k_ref, zk_sems)
    sum_k.spread()
    finish(gsa_copies())
    gsa = jnp.concatenate([gsa_all[k] for k in range(parts)], axis=0)
    bias_sums = self_backward(
        heads, gsa, ws_q_ref, ws_k_ref, ws_v_ref, ws_o_ref, qkv_ref, p_ref, ga1, gqkv, bias
    )
    ga_copies = deal(lambda at: ga1.at[at], ga_slots, ga_sems, "mp")
    finish(block_copies())
    total = jnp.zeros((width, MODEL_WIDTH), F32)
    for k in range(parts):
        total = total + dot_tn(gq_own[k], a2_own[k])
    gw_c[0] = total.astype(BF16)
    gw_c[1] = dot_tn(o1_ref[...], gsa).astype(BF16)
    core_copy(gw_c, core_c, cc_sems).start()
    sum_c = GroupSum(y_c, z_c, sum_c_ref, zc_sems)
    both_cores(core_copy(gw_c, core_c, cc_sems), gw_c, core_c, y_c)
    sum_c.spread()
    for k in range(3):
        gw_s[k] = dot_tn(gqkv[k], a1_ref[...]).astype(BF16)
    core_copy(gw_s, core_s, cs_sems).start()
    bias_sums()
    sum_s = GroupSum(y_s, z_s, sum_s_ref, zs_sems)
    both_cores(core_copy(gw_s, core_s, cs_sems), gw_s, core_s, y_s)
    sum_s.spread()
    finish(ga_copies)
    gv, self_gain = rms_back(
        home_rows(x_ref, chunk).astype(F32), row_of_gain(gain_ref), total_of(ga1[mm], ga_slots)
    )
    gx_ref[mm] = (gh1[...] + gv).astype(BF16)
    gx_copies = share(gx_ref.at[mm], gx_sems, "mp")
    term_copies = deal(lambda at: term_ref.at[at], term_slots, term_sems, "mp")
    small[0:1, :] = self_gain
    small[2:3, :] = ffn_gain_ref[...]
    small[8:16, :LANES] = bias[...]
    sd = begin([remote(small, small_dp, sd_sems.at[0], sd_sems.at[1], peer)])
    sum_k.gather()
    sum_c.gather()
    finish(sd)
    small_z[pm] = small[...] + small_dp[...]
    sz = share(small_z.at[pm], sz_sems, "pass")
    sum_s.gather()
    finish(term_copies)
    out_ref[mm] = (h2_ref[...] + total_of(term_ref[mm], term_slots)).astype(BF16)
    out_copies = share(out_ref.at[mm], out_sems, "mp")
    finish(sz)
    total = small_z[0]
    for k in range(1, small_z.shape[0]):
        total = total + small_z[k]
    small_m[mm] = total
    sm = share(small_m.at[mm], sm_sems, "mp")
    sum_c.swap()
    finish(sm)
    gains = small_m[0]
    for k in range(1, small_m.shape[0]):
        gains = gains + small_m[k]
    small_ref[0:8, :] = gains[0:8]
    small_ref[8:16, :] = total[8:16]
    finish(gx_copies)
    sum_s.swap()
    sum_k.swap()
    finish(out_copies)
    finish(f_copies)
    sum_c.end()
    sum_s.end()
    sum_k.end()


def closing_kernel(
    k_ref, c_ref, s_ref, ffn_ref, small_ref, genc_ref, y_ref, gx_ref, *refs
):
    outs, (wide, wide_in, wide_out, sems) = refs[:17], refs[17:]
    half = wide.shape[1] // 2
    moves = [(genc_ref, outs[2]), (y_ref, outs[0]), (gx_ref, outs[1])]
    copies = begin([pltpu.make_async_copy(src, dst, sems.at[n]) for n, (src, dst) in enumerate(moves)])
    sources = [(s_ref, 0), (s_ref, 1), (s_ref, 2), (c_ref, 1), (c_ref, 0), (k_ref, 0), (k_ref, 1), (k_ref, 2)]
    for n, (ref, i) in enumerate(sources):
        for core in range(2):
            wide[n, core * half : (core + 1) * half, :] = ref[core, i * half : (i + 1) * half, :].astype(F32)
        copies += begin([pltpu.make_async_copy(wide.at[n], outs[7 + n], sems.at[3 + n])])
    for n, buffer in enumerate((wide_in, wide_out)):
        buffer[...] = ffn_ref[n, 0 : buffer.shape[0], :].astype(F32)
        copies += begin([pltpu.make_async_copy(buffer, outs[15 + n], sems.at[11 + n])])
    for n in range(3):
        outs[3 + n][...] = small_ref[n, :]
    heads, buckets = outs[6].shape
    outs[6][...] = small_ref[8 : 8 + heads, 0:buckets]
    finish(copies)


def on_device(
    tokens,
    encoded,
    seg_lens,
    owners,
    answer_lens,
    gain_self,
    gain_cross,
    gain_ffn,
    rel_bias,
    wq_self,
    wk_self,
    wv_self,
    wo_self,
    wq_cross,
    wk_cross,
    wv_cross,
    wo_cross,
    w_in,
    w_out,
    out_grad,
):
    groups, mp_parts = lax.axis_size("pass"), lax.axis_size("mp")
    heads = rel_bias.shape[1]
    head_cols = heads * HD
    half = head_cols // 2
    quarter = encoded.shape[1]
    n_tokens = tokens.shape[0]
    chunk = n_tokens // mp_parts
    assert w_in.shape == (MODEL_WIDTH, MODEL_WIDTH)
    rows_f = sum_rows(MODEL_WIDTH, groups)
    keys = GROUP_ROWS * quarter
    near, far = mp_parts - 1, groups - 1

    lens, owners = seg_lens.T, owners.T
    flat_encoded = encoded.reshape(keys, MODEL_WIDTH)
    home = (chunk, MODEL_WIDTH)
    dealt = (mp_parts, chunk, MODEL_WIDTH)
    square = (MODEL_WIDTH, MODEL_WIDTH)
    smem = pltpu.SMEM
    a2_all, h_one, a1, qkv, p1, o1, wkv, wq_full, wo_full, kv = remote_call(
        functools.partial(front_kernel, heads),
        0,
        [
            ((groups, *dealt), BF16),
            (home, F32),
            ((n_tokens, MODEL_WIDTH), BF16),
            ((3, n_tokens, head_cols), BF16),
            ((mp_parts * heads, chunk, chunk), F32),
            ((n_tokens, head_cols), BF16),
            ((2, *square), BF16),
            (square, BF16),
            (square, BF16),
            ((keys, 2 * MODEL_WIDTH), BF16),
        ],
        tokens, gain_self, gain_cross, wq_self.T, wk_self.T, wv_self.T, wo_self, rel_bias.T, answer_lens,
        wk_cross.T, wv_cross.T, wq_cross.T, wo_cross, flat_encoded,
        spaces={7: smem, 8: smem, 13: pl.ANY},
        out_spaces={9: pl.ANY},
        scratch=[
            pltpu.VMEM(dealt, BF16),
            pltpu.VMEM((near, *home), BF16),
            pltpu.VMEM((keys, MODEL_WIDTH), BF16),
            pltpu.VMEM((2, keys // KV_STEPS, 2 * MODEL_WIDTH), BF16),
            many_sems(4, max(near, 3)),
            many_sems(4, near),
            pair_sems(near),
            pair_sems(far),
            many_sems(groups, near),
            pltpu.SemaphoreType.DMA((4,)),
            pltpu.SemaphoreType.DMA,
            pltpu.SemaphoreType.DMA((2,)),
        ],
    )
    a2_all = a2_all.reshape(groups, n_tokens, MODEL_WIDTH)

    partial = cross_forward(lens, owners, a2_all, wq_full, kv, mp_parts)
    gc_space = pltpu.VMEM if groups <= KV_STEPS else pl.ANY
    h_two, o2_own, term, gh_two, gc_all, gain_ffn_grad, *gw_parts = remote_call(
        middle_kernel,
        1,
        [
            (home, F32),
            ((mp_parts, chunk, head_cols), BF16),
            (dealt, BF16),
            (home, F32),
            ((groups, mp_parts, chunk, STATW), BF16),
            ((1, MODEL_WIDTH), F32),
            *[((rows_f, MODEL_WIDTH), BF16)] * groups,
        ],
        partial, h_one, wo_full, gain_ffn, w_in, w_out, out_grad,
        spaces={0: pl.ANY},
        out_spaces={4: gc_space},
        scratch=[
            pltpu.VMEM((groups, chunk, STATW), BF16),
            pltpu.VMEM((groups, near, chunk, STATW), BF16),
            pltpu.VMEM((far, chunk, STATW), BF16),
            pltpu.VMEM((mp_parts, chunk, head_cols), BF16),
            pltpu.VMEM(dealt, BF16),
            pltpu.VMEM(dealt, BF16),
            pltpu.VMEM((2, *square), BF16),
            pltpu.VMEM((near, *home), BF16),
            pltpu.VMEM(square, BF16),
            pltpu.VMEM((groups * rows_f, MODEL_WIDTH), BF16),
            pltpu.VMEM((chunk, STATW), BF16),
            many_sems(groups, near),
            pair_sems(far),
            pair_sems(near),
            pair_sems(near),
            pair_sems(near),
            pair_sems(far),
            many_sems(groups, near),
            pltpu.SemaphoreType.DMA((2,)),
            pltpu.SemaphoreType.DMA,
            pltpu.SemaphoreType.DMA,
        ],
    )
    gw_parts = [
        lax.ppermute(x, "pass", [(i, (i + k) % groups) for i in range(groups)]) if k else x
        for k, x in enumerate(gw_parts)
    ]
    gq, gkv = cross_backward(
        lens, owners, a2_all, gc_all.reshape(groups, n_tokens, STATW), wq_full, wo_full, kv, mp_parts
    )
    rows = {k: sum_rows(n * half, groups) for k, n in (("k", 3), ("c", 2), ("s", 3))}
    small = pltpu.VMEM((16, MODEL_WIDTH), F32)
    own = (mp_parts, chunk, head_cols)
    step = keys // (KV_STEPS if groups <= KV_STEPS else 4 * KV_STEPS)
    hbm = pl.ANY
    pair = pltpu.SemaphoreType.DMA((2,))
    grad_tokens, output, sum_k, sum_c, sum_s, small_sums, sum_f, genc = remote_call(
        functools.partial(finish_kernel, heads),
        3,
        [
            (dealt, BF16),
            (dealt, BF16),
            *[((2, groups * rows[k], MODEL_WIDTH), BF16) for k in "kcs"],
            ((16, MODEL_WIDTH), F32),
            ((2, groups * rows_f, MODEL_WIDTH), BF16),
            ((keys, MODEL_WIDTH), BF16),
        ],
        gq, gkv, flat_encoded, wkv.reshape(2 * MODEL_WIDTH, MODEL_WIDTH), gh_two, h_one, gain_self, gain_cross, wq_full,
        wq_self.T, wk_self.T, wv_self.T, wo_self, a1, qkv, p1, o1,
        a2_all.reshape(groups, *dealt), gc_all, o2_own, tokens, gain_ffn_grad, term, h_two, *gw_parts,
        spaces={0: hbm, 1: hbm, 2: hbm, 17: hbm, 18: hbm},
        out_spaces={7: hbm},
        scratch=[
            pltpu.VMEM((groups, *home), BF16),
            pltpu.VMEM((groups, near, *home), BF16),
            pltpu.VMEM((far, *home), BF16),
            pltpu.VMEM((2, step, 2 * MODEL_WIDTH), BF16),
            pltpu.VMEM((2, step, MODEL_WIDTH), BF16),
            pltpu.VMEM((2, step, MODEL_WIDTH), BF16),
            pltpu.VMEM((2 * MODEL_WIDTH, MODEL_WIDTH), F32),
            pltpu.VMEM((2, mp_parts, head_cols, MODEL_WIDTH), BF16),
            pltpu.VMEM((1, head_cols, MODEL_WIDTH), BF16),
            pltpu.VMEM((2, head_cols, MODEL_WIDTH), BF16),
            pltpu.VMEM((3, head_cols, MODEL_WIDTH), BF16),
            pltpu.VMEM(home, F32),
            pltpu.VMEM(own, BF16),
            pltpu.VMEM(own, BF16),
            pltpu.VMEM(dealt, BF16),
            pltpu.VMEM(dealt, BF16),
            pltpu.VMEM((3, n_tokens, head_cols), BF16),
            pltpu.VMEM((8, LANES), F32),
            pltpu.VMEM(dealt, BF16),
            pltpu.VMEM((mp_parts, chunk, STATW), BF16),
            pltpu.VMEM((near, *home), BF16),
            pltpu.VMEM((near, *home), BF16),
            pltpu.VMEM((2, mp_parts, half, MODEL_WIDTH), BF16),
            pltpu.VMEM((near, 2, half, MODEL_WIDTH), BF16),
            pltpu.VMEM((1, half, MODEL_WIDTH), BF16),
            pltpu.VMEM((2, half, MODEL_WIDTH), BF16),
            pltpu.VMEM((3, half, MODEL_WIDTH), BF16),
            *[pltpu.VMEM((groups * rows[k], MODEL_WIDTH), BF16) for k in "kcs"],
            *[pltpu.VMEM((far, rows[k], MODEL_WIDTH), BF16) for k in "kcs"],
            small,
            small,
            pltpu.VMEM((groups, 16, MODEL_WIDTH), F32),
            pltpu.VMEM((mp_parts, 16, MODEL_WIDTH), F32),
            many_sems(groups, near),
            pair_sems(far),
            pair_sems(near),
            pair_sems(near),
            pltpu.SemaphoreType.DMA((3,)),
            pltpu.SemaphoreType.DMA((2, 2)),
            pair,
            pair_sems(near),
            pair_sems(near),
            pair_sems(near),
            pair,
            pair_sems(near),
            pair,
            pair,
            pair,
            pair_sems(near),
            *[many_sems(3, far)] * 3,
            pair,
            pair_sems(far),
            pair_sems(near),
            many_sems(2, far),
        ],
    )
    shard = jax.ShapeDtypeStruct((head_cols, MODEL_WIDTH), F32)
    gain = jax.ShapeDtypeStruct((MODEL_WIDTH,), F32)
    y, gx, genc, gs, gc, gf, gb, *grads = pl.pallas_call(
        closing_kernel,
        out_shape=[
            *[jax.ShapeDtypeStruct(x.shape, x.dtype) for x in (output, grad_tokens, genc)],
            gain, gain, gain,
            jax.ShapeDtypeStruct((heads, BUCKETS), F32),
            *[shard] * 8,
            *[jax.ShapeDtypeStruct(square, F32)] * 2,
        ],
        in_specs=[pl.BlockSpec(memory_space=pltpu.VMEM)] * 8,
        out_specs=[pl.BlockSpec(memory_space=hbm)] * 3
        + [pl.BlockSpec(memory_space=pltpu.VMEM)] * 4
        + [pl.BlockSpec(memory_space=hbm)] * 10,
        scratch_shapes=[
            pltpu.VMEM((8, head_cols, MODEL_WIDTH), F32),
            pltpu.VMEM(square, F32),
            pltpu.VMEM(square, F32),
            pltpu.SemaphoreType.DMA((13,)),
        ],
        compiler_params=pltpu.CompilerParams(vmem_limit_bytes=VMEM_LIMIT),
    )(sum_k, sum_c, sum_s, sum_f, small_sums, genc, output, grad_tokens)

    return (
        y.reshape(n_tokens, MODEL_WIDTH),
        gx.reshape(n_tokens, MODEL_WIDTH),
        genc.reshape(GROUP_ROWS, quarter, MODEL_WIDTH),
        gs,
        gc,
        gf,
        gb.T,
        *[grads[i].T for i in range(3)],
        grads[3],
        *[grads[i].T for i in range(4, 7)],
        *grads[7:],
    )


def solution(mesh):
    tokens_in = P(("dp", "pass"), None)
    encoded_in = P(("dp", "pass"), "mp", None)
    by_column, by_row = P(None, "mp"), P("mp", None)
    weights = (by_column, by_column, by_column, by_row)
    return jax.shard_map(
        on_device,
        mesh=mesh,
        in_specs=(
            tokens_in, encoded_in, P("dp", None), P("dp", None), P(("dp", "pass")),
            P(), P(), P(), by_column,
            *weights, *weights, by_column, by_row, tokens_in,
        ),
        out_specs=(
            tokens_in, tokens_in, encoded_in, P(), P(), P(), by_column,
            *weights, *weights, by_column, by_row,
        ),
        check_vma=False,
    )
```

```python
import functools
import math

import jax
import jax.numpy as jnp
import numpy as np
from jax import lax
from jax.experimental import pallas as pl
from jax.experimental.pallas import tpu as pltpu
from jax.sharding import PartitionSpec as P

MODEL_WIDTH = 768
HD = 64
BUCKETS = 32
ANS = 20
PADT = 24
LANES = 128
STATW = MODEL_WIDTH + LANES
GROUP_ROWS = 32

EPSILON = 1e-06
NEGATIVE = -1e30
MESH = pl.DeviceIdType.MESH
VMEM_LIMIT = 61 << 20
F32 = jnp.float32
BF16 = jnp.bfloat16


def bucket_table(length, buckets):
    exact_half = buckets // 2
    result = np.zeros((length, length), np.int32)
    for target in range(length):
        for source in range(length):
            distance = max(target - source, 0)
            if distance < exact_half:
                result[target, source] = distance
            else:
                spread = int(
                    math.log(distance / exact_half)
                    / math.log(128 / exact_half)
                    * (buckets - exact_half)
                )
                result[target, source] = min(exact_half + spread, buckets - 1)
    return result


def dot_nn(a, b):
    return lax.dot_general(a, b, (((1,), (0,)), ((), ())), preferred_element_type=F32)


def dot_nt(a, b):
    return lax.dot_general(a, b, (((1,), (1,)), ((), ())), preferred_element_type=F32)


def dot_tn(a, b):
    return lax.dot_general(a, b, (((0,), (0,)), ((), ())), preferred_element_type=F32)


def rms_inverse(v):
    return lax.rsqrt(jnp.mean(v * v, axis=-1, keepdims=True) + EPSILON)


def row_of_gain(ref):
    return ref[...].reshape(1, ref.shape[0])


def rms_back(v, gains, ga):
    w = rms_inverse(v)
    gain_grad = jnp.sum(ga * v * w, axis=0, keepdims=True)
    gg = gains * ga
    gv = w * gg - v * (w * w * w) * jnp.mean(gg * v, axis=-1, keepdims=True)
    return gv, gain_grad


def local_call(kernel, outs, *ins, scratch=(), flops=0):
    return pl.pallas_call(
        kernel,
        out_shape=[jax.ShapeDtypeStruct(shape, dtype) for shape, dtype in outs],
        in_specs=[pl.BlockSpec(memory_space=pltpu.VMEM) for _ in ins],
        out_specs=[pl.BlockSpec(memory_space=pltpu.VMEM) for _ in outs],
        scratch_shapes=list(scratch),
        compiler_params=pltpu.CompilerParams(vmem_limit_bytes=VMEM_LIMIT),
        cost_estimate=pl.CostEstimate(
            flops=flops,
            bytes_accessed=sum(math.prod(x.shape) * x.dtype.itemsize for x in ins),
            transcendentals=0,
        ),
    )(*ins)


def place(**kw):
    return tuple(kw[a] if a in kw else lax.axis_index(a) for a in ("dp", "pass", "mp"))


def other(axis, k):
    n = lax.axis_size(axis)
    at = lax.rem(lax.axis_index(axis) + k, n)
    return at, place(**{axis: at})


def others(axis):
    return [(k - 1, *other(axis, k)) for k in range(1, lax.axis_size(axis))]


def greet(axes):
    barrier = pltpu.get_barrier_semaphore()
    peers = [peer for axis in axes for _, _, peer in others(axis)]
    for peer in peers:
        pl.semaphore_signal(barrier, inc=1, device_id=peer, device_id_type=MESH)
    pl.semaphore_wait(barrier, len(peers))


def remote(src, dst, send, recv, peer):
    return pltpu.make_async_remote_copy(
        src_ref=src, dst_ref=dst, send_sem=send, recv_sem=recv, device_id=peer, device_id_type=MESH
    )


def begin(copies):
    for copy in copies:
        copy.start()
    return copies


def finish(copies):
    for copy in copies:
        copy.wait()


def deal(source, slots, sems, axis):
    return begin([
        remote(source(at), slots.at[k], sems.at[0, k], sems.at[1, k], peer)
        for k, at, peer in others(axis)
    ])


def share(ref, sems, axis):
    return begin([remote(ref, ref, sems.at[0, k], sems.at[1, k], peer) for k, _, peer in others(axis)])


class Relay:
    def __init__(self, sems):
        self.sems, self.direct = sems, {}
        self.square = lax.axis_size("mp") == 4
        self.blocks, self.onward = {}, {}

    @staticmethod
    def near(which):
        mm = lax.axis_index("mp")
        at = mm + 1 - 2 * lax.rem(mm, 2) if which == 0 else mm + 2 - 4 * lax.div(mm, 2)
        return at, place(mp=at)

    def across(self):
        return 3 - lax.axis_index("mp")

    def put(self, i, block, own=None):
        mine = block(lax.axis_index("mp"))
        own = mine if own is None else own
        self.blocks[i] = block
        to = [(k, peer) for k, _, peer in others("mp")]
        if self.square:
            to = [(k, self.near(k)[1]) for k in range(2)]
        self.direct[i] = begin([
            remote(own, mine, self.sems.at[i, 0, k], self.sems.at[i, 1, k], peer) for k, peer in to
        ])

    def pass_on(self, i):
        if not self.square:
            return
        which = i % 2
        self.direct[i][which].wait_recv()
        block = self.blocks[i](self.near(which)[0])
        self.onward[i] = remote(
            block, block, self.sems.at[i, 0, 2], self.sems.at[i, 1, 2], self.near(1 - which)[1]
        )
        self.onward[i].start()

    def arrived(self, i):
        for k, copy in enumerate(self.direct[i]):
            if not self.square or k != i % 2:
                copy.wait_recv()
        if self.square:
            self.onward[i].wait_recv()

    def sent(self, i):
        for copy in self.direct[i]:
            copy.wait_send()
        if self.square:
            self.onward[i].wait_send()


def share_both(all_ref, zsems, msems):
    pn, pm, mm = lax.axis_size("pass"), lax.axis_index("pass"), lax.axis_index("mp")
    zcopies = share(all_ref.at[pm, mm], zsems, "pass")
    relay = Relay(msems)
    relay.put(0, lambda at: all_ref.at[pm, at])

    def forward(j):
        zcopies[j].wait_recv()
        source = lax.rem(pm - (j + 1) + pn, pn)
        relay.put(j + 1, lambda at: all_ref.at[source, at])
        relay.pass_on(j)

    def across():
        relay.pass_on(pn - 1)

    def end():
        for j in range(pn):
            relay.arrived(j)
            relay.sent(j)
        for copy in zcopies:
            copy.wait_send()

    return forward, across, end


def pair_sems(n):
    return pltpu.SemaphoreType.DMA((2, n))


def many_sems(m, n):
    return pltpu.SemaphoreType.DMA((m, 2, n))


def remote_call(kernel, collective_id, outs, *ins, spaces=None, out_spaces=None, scratch=()):
    vmem = pltpu.VMEM
    spaces = spaces or {}
    out_spaces = out_spaces or {}
    return pl.pallas_call(
        kernel,
        out_shape=[jax.ShapeDtypeStruct(shape, dtype) for shape, dtype in outs],
        in_specs=[pl.BlockSpec(memory_space=spaces.get(i, vmem)) for i in range(len(ins))],
        out_specs=[pl.BlockSpec(memory_space=out_spaces.get(i, vmem)) for i in range(len(outs))],
        scratch_shapes=list(scratch),
        compiler_params=pltpu.CompilerParams(
            collective_id=collective_id, has_side_effects=True, vmem_limit_bytes=VMEM_LIMIT
        ),
    )(*ins)


def home_rows(ref, chunk):
    at = pl.multiple_of(lax.axis_index("mp") * chunk, 16)
    return ref[pl.ds(at, chunk), :]


def total_of(first, slots):
    total = first.astype(F32)
    for k in range(slots.shape[0]):
        total = total + slots[k].astype(F32)
    return total


def bucket_grid(size):
    row = lax.broadcasted_iota(jnp.int32, (size, size), 0)
    col = lax.broadcasted_iota(jnp.int32, (size, size), 1)
    near = (col <= row) & (lax.div(col, ANS) == lax.div(row, ANS))
    table = bucket_table(ANS, BUCKETS)
    grid = jnp.full((size, size), -1, jnp.int32)
    for distance in range(ANS):
        grid = jnp.where(near & (row - col == distance), int(table[distance, 0]), grid)
    return grid, near, sorted({int(b) for b in table.reshape(-1)})


def self_forward(
    heads, x_ref, gain_ref, wq_ref, wk_ref, wv_ref, wo_ref, bias_ref, lens_ref,
    a1_ref, qkv_ref, p_ref, o1_ref, term_ref,
):
    x = x_ref[...].astype(F32)
    a1 = (x * rms_inverse(x) * row_of_gain(gain_ref)).astype(BF16)
    a1_ref[...] = a1
    for k, w_ref in enumerate((wq_ref, wk_ref, wv_ref)):
        qkv_ref[k] = dot_nt(a1, w_ref[...]).astype(BF16)
    blocks, size = term_ref.shape[0], term_ref.shape[1]
    grid, near, used = bucket_grid(size)
    biases = []
    for h in range(heads):
        bias = jnp.full((size, size), NEGATIVE, F32)
        for b in used:
            bias = jnp.where(grid == b, bias_ref[h, b], bias)
        biases.append(bias)
    lane = lax.broadcasted_iota(jnp.int32, (1, size), 1)
    for b in range(blocks):
        alive = jnp.zeros((1, size), jnp.int32)
        for q in range(size // ANS):
            inside = (lane >= q * ANS) & (lane < q * ANS + lens_ref[b * (size // ANS) + q])
            alive = jnp.where(inside, 1, alive)
        allowed = near & (alive > 0)
        rows = pl.ds(b * size, size)
        q, k, v = qkv_ref[0, rows, :], qkv_ref[1, rows, :], qkv_ref[2, rows, :]
        for h in range(heads):
            part = slice(h * HD, (h + 1) * HD)
            s = jnp.where(allowed, dot_nt(q[:, part], k[:, part]) + biases[h], NEGATIVE)
            e = jnp.exp(s - jnp.max(s, axis=-1, keepdims=True))
            p = e / jnp.sum(e, axis=-1, keepdims=True)
            p_ref[b * heads + h] = p
            o1_ref[rows, part] = dot_nn(p.astype(BF16), v[:, part]).astype(BF16)
    for b in range(blocks):
        term_ref[b] = dot_nn(o1_ref[pl.ds(b * size, size), :], wo_ref[...]).astype(BF16)


KV_STEPS = 8


def front_kernel(
    heads, x_ref, gain_ref, gain_cross_ref, wq_ref, wk_ref, wv_ref, wo_ref, bias_ref, lens_ref,
    wkc_ref, wvc_ref, wqc_ref, woc_ref, enc_ref,
    a2_ref, h_ref, a1_ref, qkv_ref, p_ref, o1_ref, wkv_ref, wq_out_ref, wo_out_ref, kv_ref,
    term, slots, enc, kv_slots, wsems, dsems, rsems, zsems, msems, own_sems, enc_sem, kv_sems,
):
    core, mm, pm = lax.axis_index("dp"), lax.axis_index("mp"), lax.axis_index("pass")
    mn, pn = lax.axis_size("mp"), lax.axis_size("pass")
    width = wkc_ref.shape[0]
    half = width // 2
    chunk = h_ref.shape[0]
    load = pltpu.make_async_copy(enc_ref, enc, enc_sem)
    load.start()
    pieces = [
        (wkc_ref, wkv_ref.at[0]), (wvc_ref, wkv_ref.at[1]), (wqc_ref, wq_out_ref), (woc_ref, wo_out_ref)
    ]

    def rows_of(source, which):
        return pl.ds(pl.multiple_of(source * width + which * half, 16), half)

    mine = pl.ds(pl.multiple_of(core * half, 16), half)
    owns = []
    for i, (shard, full) in enumerate(pieces):
        at = pl.ds(pl.multiple_of(mm * width, 16), width)
        own = pltpu.make_async_copy(shard, full.at[at], own_sems.at[i])
        own.start()
        owns.append(own)
    greet(("dp", "pass", "mp"))

    relay = Relay(wsems)

    def send_weight(i):
        shard, full = pieces[i]
        relay.put(i, lambda at: full.at[rows_of(at, core)], shard.at[mine])

    def to_other_core(i):
        full = pieces[i][1]
        relay.arrived(i)
        return begin([
            remote(
                full.at[rows_of(at, core)], full.at[rows_of(at, core)],
                dsems.at[i, 0, k], dsems.at[i, 1, k], other("dp", 1)[1],
            )
            for k, at, _ in others("mp")
        ])

    send_weight(0)
    send_weight(1)
    self_forward(
        heads, x_ref, gain_ref, wq_ref, wk_ref, wv_ref, wo_ref, bias_ref, lens_ref,
        a1_ref, qkv_ref, p_ref, o1_ref, term,
    )
    dealt = deal(lambda at: term.at[at], slots, rsems, "mp")
    relay.pass_on(0)
    relay.pass_on(1)
    for copy in dealt:
        copy.wait_recv()
    h = home_rows(x_ref, chunk).astype(F32) + total_of(term[mm], slots)
    h_ref[...] = h
    a2_ref[pm, mm] = (h * rms_inverse(h) * row_of_gain(gain_cross_ref)).astype(BF16)
    forward, across, end = share_both(a2_ref, zsems, msems)
    send_weight(2)
    send_weight(3)
    passed = [to_other_core(0), to_other_core(1)]
    for copies in passed:
        for copy in copies:
            copy.wait_recv()
    for own in owns:
        own.wait()
    load.wait()
    rows = enc.shape[0] // KV_STEPS

    def store(step):
        slot = lax.rem(step, 2)
        at = pl.ds(pl.multiple_of(step * rows, rows), rows)
        return pltpu.make_async_copy(kv_slots.at[slot], kv_ref.at[at], kv_sems.at[slot])

    def project(step, carry):
        slot = lax.rem(step, 2)

        @pl.when(step >= 2)
        def _():
            store(step - 2).wait()

        x = enc[pl.ds(pl.multiple_of(step * rows, rows), rows), :]
        for i in range(2):
            kv_slots[slot, :, i * MODEL_WIDTH : (i + 1) * MODEL_WIDTH] = dot_nt(x, wkv_ref[i]).astype(BF16)
        store(step).start()
        return carry

    done, onward = 0, [2, 3]
    for j in range(pn - 1):
        upto = KV_STEPS * (2 * j + 1) // (2 * pn)
        if upto > done:
            lax.fori_loop(done, upto, project, 0)
            done = upto
        forward(j)
        if onward:
            relay.pass_on(onward.pop(0))
    for i in onward:
        relay.pass_on(i)
    lax.fori_loop(done, KV_STEPS - 1, project, 0)
    across()
    lax.fori_loop(KV_STEPS - 1, KV_STEPS, project, 0)
    passed += [to_other_core(2), to_other_core(3)]
    for step in (KV_STEPS - 2, KV_STEPS - 1):
        store(step).wait()
    end()
    for copy in dealt:
        copy.wait_send()
    for i, copies in enumerate(passed):
        relay.sent(i)
        for copy in copies:
            copy.wait_send()
            if i >= 2:
                copy.wait_recv()


PAIR = 2 * HD
PAIRS = MODEL_WIDTH // PAIR
PROWS = 2 * PADT
FLOOR = -1e29


def low_lanes(shape):
    return lax.broadcasted_iota(jnp.int32, shape, len(shape) - 1) < HD


def pair_rows(dst_ref, pad_ref, values, stat=None, stat_at=0):
    questions = dst_ref.shape[0]
    low = low_lanes((1, PADT, PAIR))
    for q in range(questions):
        rows = slice(q * ANS, (q + 1) * ANS)
        pad_ref[q, 0:ANS, :MODEL_WIDTH] = values[rows, :]
        pad_ref[q, ANS:PADT, :] = jnp.zeros((PADT - ANS, pad_ref.shape[2]), F32)
        if stat is not None:
            pad_ref[q, 0:ANS, MODEL_WIDTH:] = stat[rows, :]
    lane = lax.broadcasted_iota(jnp.int32, (1, 1, LANES), 2)
    for c in range(PAIRS):
        x = pad_ref[:, :, c * PAIR : (c + 1) * PAIR]
        both = jnp.concatenate([jnp.where(low, x, 0.0), jnp.where(low, 0.0, x)], axis=1)
        dst_ref[:, c, :, :PAIR] = both.astype(BF16)
        if stat is not None:
            s = pad_ref[:, :, MODEL_WIDTH:]
            parts = []
            for h in (2 * c, 2 * c + 1):
                at = lane - (stat_at + h)
                parts.append(s * ((at == 0) | (at == 16) | (at == 32)).astype(F32))
            dst_ref[:, c, :, PAIR:] = jnp.concatenate(parts, axis=1).astype(BF16)


def segment_mask(lens_ref, row, keys):
    lane = lax.broadcasted_iota(jnp.int32, (PROWS, keys), 1)
    cut = lens_ref[0, row] - lax.axis_index("mp") * keys
    return [lane < cut, (lane >= cut) & (lane < cut + lens_ref[1, row])]


def masked(scores, mask):
    return jnp.concatenate(
        [jnp.where(mask[s], scores[s * PROWS : (s + 1) * PROWS], NEGATIVE) for s in range(2)], axis=0
    )


def fold_pair(x, s, low):
    at = s * PROWS
    return jnp.where(low, x[at : at + PADT], x[at + PADT : at + PROWS])


def split_three(x):
    hi = x.astype(BF16).astype(F32)
    mid = (x - hi).astype(BF16).astype(F32)
    return hi, mid, x - hi - mid


def staged(rows_per, stages):
    depth = len(stages)
    for i in range(rows_per + depth - 1):
        for k in reversed(range(depth)):
            if 0 <= i - k < rows_per:
                stages[k](i - k, (i - k) % 2)


def cross_forward_kernel(
    rows_per, keys, lens_ref, owners_ref, a2_ref, wq_ref, kv_ref, out_ref,
    q_rows, pad, s_buf, p_buf, t_buf, o_acc, m_acc, l_acc, flat,
):
    g = pl.program_id(0)
    pair_rows(q_rows, pad, dot_nt(a2_ref[0], wq_ref[...]).astype(BF16).astype(F32))
    o_acc[...] = jnp.zeros_like(o_acc)
    m_acc[...] = jnp.full_like(m_acc, FLOOR)
    l_acc[...] = jnp.zeros_like(l_acc)
    low = low_lanes((PADT, PAIR))
    ones = jnp.ones((keys, PAIR), BF16)

    def row_of(r):
        return lax.axis_index("pass") * GROUP_ROWS + g * rows_per + r

    def owners_of(r):
        return [owners_ref[0, row_of(r)], owners_ref[1, row_of(r)]]

    def scores(r, slot):
        owners = owners_of(r)
        mask = segment_mask(lens_ref, row_of(r), keys)
        for c in range(PAIRS):
            k = kv_ref[r * keys : (r + 1) * keys, c * PAIR : (c + 1) * PAIR]
            qm = jnp.concatenate([q_rows[q, c] for q in owners], axis=0)
            s_buf[slot, c] = masked(dot_nt(qm, k), mask)

    def chances(r, slot):
        for c in range(PAIRS):
            s = s_buf[slot, c]
            top = jnp.maximum(jnp.max(s, axis=-1, keepdims=True), FLOOR)
            p_buf[slot, c] = jnp.exp(s - top).astype(BF16)
            top = jnp.broadcast_to(top, (2 * PROWS, PAIR))
            for i in range(2):
                t_buf[slot, c, i] = fold_pair(top, i, low)

    def values(r, slot):
        owners = owners_of(r)
        new = []
        for c in range(PAIRS):
            v = kv_ref[r * keys : (r + 1) * keys, MODEL_WIDTH + c * PAIR : MODEL_WIDTH + (c + 1) * PAIR]
            both = dot_nn(p_buf[slot, c], jnp.concatenate([v, ones], axis=1))
            new.append([
                (fold_pair(both[:, :PAIR], i, low), fold_pair(both[:, PAIR:], i, low)) for i in range(2)
            ])
        for i, q in enumerate(owners):
            for c in range(PAIRS):
                cols = slice(c * PAIR, (c + 1) * PAIR)
                o, l = new[c][i]
                m_old, m_new = m_acc[q, :, cols], t_buf[slot, c, i]
                m_both = jnp.maximum(m_old, m_new)
                a, b = jnp.exp(m_old - m_both), jnp.exp(m_new - m_both)
                o_acc[q, :, cols] = a * o_acc[q, :, cols] + b * o
                l_acc[q, :, cols] = a * l_acc[q, :, cols] + b * l
                m_acc[q, :, cols] = m_both

    staged(rows_per, [scores, chances, values])
    questions = q_rows.shape[0]
    lane = lax.broadcasted_iota(jnp.int32, (PADT, LANES), 1)
    for q in range(questions):
        l = l_acc[q]
        some = l > 0.0
        safe = jnp.where(some, l, 1.0)
        o = o_acc[q] / safe
        lse = jnp.where(some, m_acc[q] + jnp.log(safe), NEGATIVE)
        few = jnp.zeros((PADT, LANES), F32)
        for h in range(MODEL_WIDTH // HD):
            few = jnp.where(lane == h, lse[:, h * HD : h * HD + 1], few)
        hi, mid, rest = split_three(few)
        stat = hi + pltpu.roll(mid, 16, 1) + pltpu.roll(rest, 32, 1)
        flat[q * ANS : (q + 1) * ANS, :MODEL_WIDTH] = o[:ANS]
        flat[q * ANS : (q + 1) * ANS, MODEL_WIDTH:] = stat[:ANS]
    chunk = out_ref.shape[2]
    for m in range(out_ref.shape[0]):
        out_ref[m, 0] = flat[m * chunk : (m + 1) * chunk, :].astype(BF16)


def cross_forward(lens, owners, a2_all, wq, kv, mp_parts):
    groups, n_tokens, _ = a2_all.shape
    rows_per = GROUP_ROWS // groups
    keys = kv.shape[0] // GROUP_ROWS
    questions = n_tokens // ANS
    block = rows_per * keys
    padded = pltpu.VMEM((questions, PADT, MODEL_WIDTH), F32)
    return pl.pallas_call(
        functools.partial(cross_forward_kernel, rows_per, keys),
        grid_spec=pltpu.PrefetchScalarGridSpec(
            num_scalar_prefetch=2,
            grid=(groups,),
            in_specs=[
                pl.BlockSpec((1, n_tokens, MODEL_WIDTH), lambda g, *_: (g, 0, 0)),
                pl.BlockSpec((MODEL_WIDTH, MODEL_WIDTH), lambda g, *_: (0, 0)),
                pl.BlockSpec((block, 2 * MODEL_WIDTH), lambda g, *_: (g, 0)),
            ],
            out_specs=pl.BlockSpec(
                (mp_parts, 1, n_tokens // mp_parts, STATW), lambda g, *_: (0, g, 0, 0)
            ),
            scratch_shapes=[
                pltpu.VMEM((questions, PAIRS, PROWS, PAIR), BF16),
                padded,
                pltpu.VMEM((2, PAIRS, 2 * PROWS, keys), F32),
                pltpu.VMEM((2, PAIRS, 2 * PROWS, keys), BF16),
                pltpu.VMEM((2, PAIRS, 2, PADT, PAIR), F32),
                padded,
                padded,
                padded,
                pltpu.VMEM((n_tokens, STATW), F32),
            ],
        ),
        out_shape=jax.ShapeDtypeStruct((mp_parts, groups, n_tokens // mp_parts, STATW), BF16),
        compiler_params=pltpu.CompilerParams(vmem_limit_bytes=VMEM_LIMIT),
    )(lens, owners, a2_all, wq, kv)


def cross_backward_kernel(
    rows_per, keys, lens_ref, owners_ref, a2_ref, gc_ref, wq_ref, wo_ref, kv_ref, gq_ref, gkv_ref,
    q_rows, go_rows, pad, s_buf, gp_buf, p_buf, gs_buf, gq_acc, flat,
):
    g = pl.program_id(0)
    stat = gc_ref[0, :, MODEL_WIDTH:].astype(F32)
    q2 = dot_nt(a2_ref[0], wq_ref[...]).astype(BF16).astype(F32)
    pair_rows(q_rows, pad, q2, stat, 0)
    go2 = dot_nt(gc_ref[0, :, :MODEL_WIDTH], wo_ref[...]).astype(BF16).astype(F32)
    pair_rows(go_rows, pad, go2, stat, 48)
    gq_acc[...] = jnp.zeros_like(gq_acc)
    low = low_lanes((PADT, PAIR))
    minus = jnp.full((keys, LANES), -1.0, BF16)

    def row_of(r):
        return lax.axis_index("pass") * GROUP_ROWS + g * rows_per + r

    def owners_of(r):
        return [owners_ref[0, row_of(r)], owners_ref[1, row_of(r)]]

    def tile(r, c, off):
        return kv_ref[r * keys : (r + 1) * keys, off + c * PAIR : off + (c + 1) * PAIR]

    def scores(r, slot):
        owners = owners_of(r)
        mask = segment_mask(lens_ref, row_of(r), keys)
        for c in range(PAIRS):
            qm = jnp.concatenate([q_rows[q, c] for q in owners], axis=0)
            gom = jnp.concatenate([go_rows[q, c] for q in owners], axis=0)
            s = dot_nt(qm, jnp.concatenate([tile(r, c, 0), minus], axis=1))
            s_buf[slot, c] = masked(s, mask)
            gp_buf[slot, c] = dot_nt(gom, jnp.concatenate([tile(r, c, MODEL_WIDTH), minus], axis=1))

    def chances(r, slot):
        for c in range(PAIRS):
            p = jnp.exp(s_buf[slot, c])
            p_buf[slot, c] = p.astype(BF16)
            gs_buf[slot, c] = (p * gp_buf[slot, c]).astype(BF16)

    def grads(r, slot):
        owners = owners_of(r)
        new = []
        rows = slice(r * keys, (r + 1) * keys)
        for c in range(PAIRS):
            gs, p = gs_buf[slot, c], p_buf[slot, c]
            qm = jnp.concatenate([q_rows[q, c, :, :PAIR] for q in owners], axis=0)
            gom = jnp.concatenate([go_rows[q, c, :, :PAIR] for q in owners], axis=0)
            gkv_ref[rows, c * PAIR : (c + 1) * PAIR] = dot_tn(gs, qm).astype(BF16)
            gkv_ref[rows, MODEL_WIDTH + c * PAIR : MODEL_WIDTH + (c + 1) * PAIR] = dot_tn(p, gom).astype(BF16)
            gq = dot_nn(gs, tile(r, c, 0))
            new.append([fold_pair(gq, i, low) for i in range(2)])
        for i, q in enumerate(owners):
            for c in range(PAIRS):
                cols = slice(c * PAIR, (c + 1) * PAIR)
                gq_acc[q, :, cols] = gq_acc[q, :, cols] + new[c][i]

    staged(rows_per, [scores, chances, grads])
    for q in range(q_rows.shape[0]):
        flat[q * ANS : (q + 1) * ANS, :] = gq_acc[q, :ANS, :]
    chunk = gq_ref.shape[2]
    for m in range(gq_ref.shape[0]):
        gq_ref[m, 0] = flat[m * chunk : (m + 1) * chunk, :].astype(BF16)


def cross_backward(lens, owners, a2_all, gc_all, wq, wo, kv, mp_parts):
    groups, n_tokens, _ = a2_all.shape
    rows_per = GROUP_ROWS // groups
    keys = kv.shape[0] // GROUP_ROWS
    questions = n_tokens // ANS
    block = rows_per * keys
    rows = pltpu.VMEM((questions, PAIRS, PROWS, PAIR + LANES), BF16)
    whole = pl.BlockSpec((MODEL_WIDTH, MODEL_WIDTH), lambda g, *_: (0, 0))
    return pl.pallas_call(
        functools.partial(cross_backward_kernel, rows_per, keys),
        grid_spec=pltpu.PrefetchScalarGridSpec(
            num_scalar_prefetch=2,
            grid=(groups,),
            in_specs=[
                pl.BlockSpec((1, n_tokens, MODEL_WIDTH), lambda g, *_: (g, 0, 0)),
                pl.BlockSpec((1, n_tokens, STATW), lambda g, *_: (g, 0, 0)),
                whole,
                whole,
                pl.BlockSpec((block, 2 * MODEL_WIDTH), lambda g, *_: (g, 0)),
            ],
            out_specs=[
                pl.BlockSpec(
                    (mp_parts, 1, n_tokens // mp_parts, MODEL_WIDTH), lambda g, *_: (0, g, 0, 0)
                ),
                pl.BlockSpec((block, 2 * MODEL_WIDTH), lambda g, *_: (g, 0)),
            ],
            scratch_shapes=[
                rows,
                rows,
                pltpu.VMEM((questions, PADT, STATW), F32),
                pltpu.VMEM((2, PAIRS, 2 * PROWS, keys), F32),
                pltpu.VMEM((2, PAIRS, 2 * PROWS, keys), F32),
                pltpu.VMEM((2, PAIRS, 2 * PROWS, keys), BF16),
                pltpu.VMEM((2, PAIRS, 2 * PROWS, keys), BF16),
                pltpu.VMEM((questions, PADT, MODEL_WIDTH), F32),
                pltpu.VMEM((n_tokens, MODEL_WIDTH), F32),
            ],
        ),
        out_shape=[
            jax.ShapeDtypeStruct((mp_parts, groups, n_tokens // mp_parts, MODEL_WIDTH), BF16),
            jax.ShapeDtypeStruct(kv.shape, BF16),
        ],
        compiler_params=pltpu.CompilerParams(vmem_limit_bytes=VMEM_LIMIT),
    )(lens, owners, a2_all, gc_all, wq, wo, kv)


def widen(w):
    row = lax.broadcasted_iota(jnp.int32, (LANES, MODEL_WIDTH), 0)
    col = lax.broadcasted_iota(jnp.int32, (LANES, MODEL_WIDTH), 1)
    each = (row == lax.div(col, HD)).astype(BF16)
    hi = w.astype(BF16)
    low = (w - hi.astype(F32)).astype(BF16)
    return dot_nn(hi, each) + dot_nn(low, each)


def combined(parts):
    lses = []
    for part in parts:
        stat = part[:, MODEL_WIDTH:].astype(F32)
        lses.append(stat + pltpu.roll(stat, LANES - 16, 1) + pltpu.roll(stat, LANES - 32, 1))
    top = functools.reduce(jnp.maximum, lses)
    weights = [jnp.exp(x - top) for x in lses]
    total = functools.reduce(jnp.add, weights)
    out = 0.0
    for part, weight in zip(parts, weights):
        out = out + widen(weight / total) * part[:, :MODEL_WIDTH].astype(F32)
    lane = lax.broadcasted_iota(jnp.int32, total.shape, 1)
    lse = jnp.where(lane < MODEL_WIDTH // HD, top + jnp.log(total), 0.0)
    return out, lse


def packed_stat(lse, at=0):
    hi, mid, low = split_three(lse)
    parts = [hi if at == 0 else pltpu.roll(hi, at, 1)]
    parts += [pltpu.roll(mid, at + 16, 1), pltpu.roll(low, at + 32, 1)]
    return parts[0] + parts[1] + parts[2]


def deal_groups(source, slots, sems):
    pn, pm = lax.axis_size("pass"), lax.axis_index("pass")
    for step in range(pn):
        group = lax.rem(pm + 1 + step, pn)
        deal(lambda at: source.at[at, group], slots.at[step], sems.at[step], "mp")


def middle_kernel(
    part_ref, h_ref, wo_ref, gain_ref, w_in_ref, w_out_ref, gy_ref,
    h2_ref, own_ref, term_ref, gh_ref, gc_ref, gain_out_ref, *refs,
):
    count = lax.axis_size("pass")
    pieces, refs = refs[:count], refs[count:]
    (
        held, slots, zslots, blocks, a3_all, ga3, gw, ga_slots, gw_slot, y, gc_home,
        msems, gsems, asems, bsems, rsems, zsems, relay_sems, gw_sems, load_sem, own_sem,
    ) = refs
    core, mm, pm = lax.axis_index("dp"), lax.axis_index("mp"), lax.axis_index("pass")
    pn = lax.axis_size("pass")
    load = pltpu.make_async_copy(part_ref.at[mm], held, load_sem)
    load.start()
    greet(("dp", "pass", "mp"))
    deal_groups(part_ref, slots, msems)
    load.wait()

    def add(parts):
        out, lse = combined(parts)
        return jnp.concatenate([out, packed_stat(lse)], axis=1).astype(BF16)

    def arrived(step):
        group = lax.rem(pm + 1 + step, pn)
        for k, at, peer in others("mp"):
            remote(
                part_ref.at[at, group], slots.at[step, k], msems.at[step, 0, k], msems.at[step, 1, k], peer
            ).wait()
        held[group] = add([held[group]] + [slots[step, k] for k in range(slots.shape[1])])

    def to_home(step):
        at, peer = other("pass", step + 1)
        return remote(held.at[at], zslots.at[step], gsems.at[0, step], gsems.at[1, step], peer)

    def one(step, carry):
        arrived(step)
        to_home(step).start()
        return carry

    if pn <= 4:
        for step in range(pn - 1):
            one(step, 0)
    else:
        lax.fori_loop(0, pn - 1, one, 0)
    arrived(pn - 1)
    for step in range(pn - 1):
        to_home(step).wait()
    o, lse = combined([held[pm]] + [zslots[k] for k in range(pn - 1)])
    low = o.astype(BF16)
    h2 = h_ref[...] + dot_nn(low, wo_ref[...])
    a3_all[mm] = (h2 * rms_inverse(h2) * row_of_gain(gain_ref)).astype(BF16)
    copies = share(a3_all.at[mm], asems, "mp")
    h2_ref[...] = h2
    width = blocks.shape[2]
    parts = blocks.shape[0]
    for k in range(parts):
        blocks[k] = low[:, k * width : (k + 1) * width]
    own_ref[mm] = blocks[mm]
    block_copies = begin([
        remote(blocks.at[at], own_ref.at[mm], bsems.at[0, k], bsems.at[1, k], peer)
        for k, at, peer in others("mp")
    ])
    gy = gy_ref[...]
    ge = dot_nt(gy, w_out_ref[...]).astype(BF16).astype(F32)
    finish(copies)
    a3 = jnp.concatenate([a3_all[k] for k in range(parts)], axis=0)
    u = dot_nn(a3, w_in_ref[...])
    cdf = 0.5 * (1.0 + lax.erf(u * np.float32(math.sqrt(0.5))))
    pdf = np.float32(1.0 / math.sqrt(2.0 * math.pi)) * jnp.exp(-0.5 * u * u)
    gu = (ge * (cdf + u * pdf)).astype(BF16)
    ga = dot_nt(gu, w_in_ref[...]).astype(BF16)
    chunk = h_ref.shape[0]
    for k in range(parts):
        ga3[k] = ga[k * chunk : (k + 1) * chunk]
    dealt = deal(lambda at: ga3.at[at], ga_slots, rsems, "mp")
    e = (u * cdf).astype(BF16)
    gw[0] = dot_tn(a3, gu).astype(BF16)
    gw[1] = dot_tn(e, gy).astype(BF16)
    swapped = remote(gw.at[1 - core], gw_slot, gw_sems.at[0], gw_sems.at[1], other("dp", 1)[1])
    swapped.start()
    term = dot_nn(e, w_out_ref[...]).astype(BF16)
    for k in range(parts):
        term_ref[k] = term[k * chunk : (k + 1) * chunk]
    finish(dealt)
    gv, gain_grad = rms_back(h2, row_of_gain(gain_ref), total_of(ga3[mm], ga_slots))
    gain_out_ref[...] = gain_grad
    gh = home_rows(gy_ref, chunk).astype(F32) + gv
    gh_ref[...] = gh
    gc = gh.astype(BF16)
    go = dot_nt(gc, wo_ref[...]).astype(BF16).astype(F32)
    row = lax.broadcasted_iota(jnp.int32, (MODEL_WIDTH, LANES), 0)
    col = lax.broadcasted_iota(jnp.int32, (MODEL_WIDTH, LANES), 1)
    each = (lax.div(row, HD) == col).astype(F32)
    delta = lax.dot_general(
        go * o, each, (((1,), (0,)), ((), ())),
        preferred_element_type=F32, precision=lax.Precision.HIGHEST,
    )
    stat = packed_stat(lse) + packed_stat(delta, 48)
    gc_home[...] = jnp.concatenate([gc, stat.astype(BF16)], axis=1)
    own = pltpu.make_async_copy(gc_home, gc_ref.at[pm, mm], own_sem)
    own.start()
    own.wait()
    forward, across, end = share_both(gc_ref, zsems, relay_sems)
    swapped.wait()
    used = gw_slot.shape[0]
    y[0:used, :] = (gw[core].astype(F32) + gw_slot[...].astype(F32)).astype(BF16)
    fill_tail(y, used)
    rows = pieces[0].shape[0]
    for k, piece in enumerate(pieces):
        piece[...] = y[pl.ds(pl.multiple_of(lax.rem(pm + k, pn) * rows, 16), rows), :]
    for j in range(pn - 1):
        forward(j)
    across()
    finish(block_copies)
    end()


def sum_rows(rows, groups):
    return -(-rows // (groups * 16)) * 16


class GroupSum:
    def __init__(self, y, zslots, out, sems):
        self.y, self.zslots, self.out, self.sems = y, zslots, out, sems
        self.rows = zslots.shape[1]

    def part(self, at):
        return pl.ds(pl.multiple_of(at * self.rows, 16), self.rows)

    def dealing(self):
        return [
            remote(self.y.at[self.part(at)], self.zslots.at[k], self.sems.at[0, 0, k], self.sems.at[0, 1, k], peer)
            for k, at, peer in others("pass")
        ]

    def sharing(self):
        here = self.out.at[lax.axis_index("dp"), self.part(lax.axis_index("pass"))]
        return [
            remote(here, here, self.sems.at[1, 0, k], self.sems.at[1, 1, k], peer)
            for k, _, peer in others("pass")
        ]

    def swapping(self):
        here = self.out.at[lax.axis_index("dp")]
        return [remote(here, here, self.sems.at[2, 0, 0], self.sems.at[2, 1, 0], other("dp", 1)[1])]

    def spread(self):
        begin(self.dealing())

    def gather(self):
        finish(self.dealing())
        at = self.part(lax.axis_index("pass"))
        total = total_of(self.y[at, :], self.zslots)
        self.out[lax.axis_index("dp"), at, :] = total.astype(BF16)
        begin(self.sharing())

    def swap(self):
        finish(self.sharing())
        begin(self.swapping())

    def end(self):
        finish(self.swapping())


def fill_tail(y, used):
    if y.shape[0] > used:
        y[used:, :] = jnp.zeros((y.shape[0] - used, y.shape[1]), y.dtype)


def self_backward(
    heads, gsa, wq_ref, wk_ref, wv_ref, wo_ref, qkv_ref, p_ref, ga1_ref, gqkv_ref, bias_ref
):
    go1 = dot_nt(gsa, wo_ref[...]).astype(BF16)
    blocks, size = ga1_ref.shape[0], ga1_ref.shape[1]
    grid, _, used = bucket_grid(size)
    at_row = lax.broadcasted_iota(jnp.int32, bias_ref.shape, 0)
    at_lane = lax.broadcasted_iota(jnp.int32, bias_ref.shape, 1)
    totals = []
    for h in range(heads):
        part = slice(h * HD, (h + 1) * HD)
        total = jnp.zeros((size, size), F32)
        for b in range(blocks):
            rows = pl.ds(b * size, size)
            q, k, v = qkv_ref[0, rows, part], qkv_ref[1, rows, part], qkv_ref[2, rows, part]
            p = p_ref[b * heads + h]
            go = go1[b * size : (b + 1) * size, part]
            gp = dot_nt(go, v)
            gs = (p * (gp - jnp.sum(gp * p, axis=-1, keepdims=True))).astype(BF16)
            total = total + gs.astype(F32)
            gqkv_ref[0, rows, part] = dot_nn(gs, k).astype(BF16)
            gqkv_ref[1, rows, part] = dot_tn(gs, q).astype(BF16)
            gqkv_ref[2, rows, part] = dot_tn(p.astype(BF16), go).astype(BF16)
        totals.append(total)
    ga1 = dot_nn(gqkv_ref[0], wq_ref[...])
    ga1 = ga1 + dot_nn(gqkv_ref[1], wk_ref[...])
    ga1 = ga1 + dot_nn(gqkv_ref[2], wv_ref[...])
    for b in range(blocks):
        ga1_ref[b] = ga1[b * size : (b + 1) * size].astype(BF16)

    def bias_sums():
        bias = jnp.zeros(bias_ref.shape, F32)
        for h, total in enumerate(totals):
            for b in used:
                value = jnp.sum(jnp.where(grid == b, total, 0.0), keepdims=True)
                bias = jnp.where((at_row == h) & (at_lane == b), value, bias)
        bias_ref[...] = bias

    return bias_sums


def finish_kernel(
    heads, gq_ref, gkv_ref, enc_ref, wkv_ref, gh2_ref, h_ref, gain_ref, gain_cross_ref, wq_ref,
    ws_q_ref, ws_k_ref, ws_v_ref, ws_o_ref, a1_ref, qkv_ref, p_ref, o1_ref,
    a2_ref, gc_ref, o2_ref, x_ref, ffn_gain_ref, term_ref, h2_ref, *refs,
):
    count = lax.axis_size("pass")
    gw_parts, refs = refs[:count], refs[count:]
    (
    gx_ref, out_ref, sum_k_ref, sum_c_ref, sum_s_ref, small_ref, sum_f_ref, genc_ref,
    held, slots, zslots, gkv_in, enc_in, genc_out, gw_acc, gw_kv, gw_o, gw_c, gw_s, gh1,
    blocks, gq_own, gsa_all, ga1, gqkv, bias, a2_own, gc_own,
    ga_slots, term_slots, kv_core, kv_slots, core_o, core_c, core_s,
    y_k, y_c, y_s, z_k, z_c, z_s, small, small_dp, small_z, small_m,
    msems, gzsems, asems, bsems, load_sems, in_sems, genc_sems,
    ga_sems, term_sems, out_sems, kv_dsems, kv_msems, co_sems, cc_sems, cs_sems, gx_sems,
    zk_sems, zc_sems, zs_sems, sd_sems, sz_sems, sm_sems,
    f_sems,
    ) = refs
    core, mm, pm = lax.axis_index("dp"), lax.axis_index("mp"), lax.axis_index("pass")
    pn = lax.axis_size("pass")
    chunk = h_ref.shape[0]
    width = o1_ref.shape[1]
    half = width // 2
    mine = pl.ds(pl.multiple_of(core * half, 16), half)
    theirs = pl.ds(pl.multiple_of((1 - core) * half, 16), half)
    peer = other("dp", 1)[1]
    loads = begin([
        pltpu.make_async_copy(gq_ref.at[mm], held, load_sems.at[0]),
        pltpu.make_async_copy(a2_ref.at[pm], a2_own, load_sems.at[1]),
        pltpu.make_async_copy(gc_ref.at[pm], gc_own, load_sems.at[2]),
    ])
    rows = gkv_in.shape[1]
    steps = gkv_ref.shape[0] // rows

    def step_rows(step):
        return pl.ds(pl.multiple_of(step * rows, rows), rows)

    def fetch_gkv(step, slot):
        return pltpu.make_async_copy(gkv_ref.at[step_rows(step)], gkv_in.at[slot], in_sems.at[slot, 0])

    def fetch_enc(step, slot):
        return pltpu.make_async_copy(enc_ref.at[step_rows(step)], enc_in.at[slot], in_sems.at[slot, 1])

    def store(step, slot):
        return pltpu.make_async_copy(genc_out.at[slot], genc_ref.at[step_rows(step)], genc_sems.at[slot])

    fetch_gkv(0, 0).start()
    fetch_enc(0, 0).start()
    greet(("dp", "pass", "mp"))
    for step in range(pn):
        group = lax.rem(pm + 1 + step, pn)
        deal(lambda at: gq_ref.at[at, group], slots.at[step], msems.at[step], "mp")
    finish(loads)

    def to_home(step):
        at, to = other("pass", step + 1)
        return remote(held.at[at], zslots.at[step], gzsems.at[0, step], gzsems.at[1, step], to)

    def arrived(step, carry):
        group = lax.rem(pm + 1 + step, pn)
        for k, at, to in others("mp"):
            remote(
                gq_ref.at[at, group], slots.at[step, k], msems.at[step, 0, k], msems.at[step, 1, k], to
            ).wait()
        total = held[group].astype(F32)
        for k in range(slots.shape[1]):
            total = total + slots[step, k].astype(F32)
        held[group] = total.astype(BF16)

        @pl.when(step < pn - 1)
        def _():
            to_home(step).start()

        return carry

    def arrivals(step):
        last = steps * 13 // 8
        lax.fori_loop(
            lax.min(lax.div(step * pn, last), pn), lax.min(lax.div((step + 1) * pn, last), pn), arrived, 0
        )

    parts = blocks.shape[0]

    def both_cores(copy, gw, got, y, first=0):
        copy.wait()
        for i in range(gw.shape[0]):
            at = pl.ds(pl.multiple_of(lax.axis_index("dp") * half, 16), half)
            to = (first + i) * half
            y[to : to + half, :] = (gw[i, at, :].astype(F32) + got[i].astype(F32)).astype(BF16)
        fill_tail(y, (first + gw.shape[0]) * half)

    total = gw_parts[0][...].astype(F32)
    for part in gw_parts[1:]:
        total = total + part[...].astype(F32)
    f_rows = pl.ds(pl.multiple_of(pm * total.shape[0], 16), total.shape[0])
    sum_f_ref[core, f_rows, :] = total.astype(BF16)
    f_copies = share(sum_f_ref.at[core, f_rows], f_sems.at[0], "pass")
    total = jnp.zeros((width, MODEL_WIDTH), F32)
    for k in range(parts):
        total = total + dot_tn(o2_ref[k], gc_own[k, :, :MODEL_WIDTH])
    gw_o[0] = total.astype(BF16)

    def core_copy(gw, got, sems):
        to = other("dp", 1)[1]
        off = pl.multiple_of((1 - lax.axis_index("dp")) * half, 16)
        where = (slice(None),) * (len(gw.shape) - 2) + (pl.ds(off, half),)
        return remote(gw.at[where], got, sems.at[0], sems.at[1], to)

    core_copy(gw_o, core_o, co_sems).start()
    gw_acc[...] = jnp.zeros_like(gw_acc)

    def weights(step, carry):
        slot = lax.rem(step, 2)

        @pl.when(step + 1 < steps)
        def _():
            fetch_gkv(step + 1, 1 - slot).start()
            fetch_enc(step + 1, 1 - slot).start()

        fetch_gkv(step, slot).wait()
        fetch_enc(step, slot).wait()
        for i in range(2):
            part = slice(i * MODEL_WIDTH, (i + 1) * MODEL_WIDTH)
            gw_acc[part, :] += dot_tn(gkv_in[slot, :, part], enc_in[slot])
        arrivals(step)

        @pl.when(step == 1)
        def _():
            both_cores(core_copy(gw_o, core_o, co_sems), gw_o, core_o, y_k, 2)

        return carry

    lax.fori_loop(0, steps, weights, 0)
    fetch_gkv(0, 0).start()
    for i in range(2):
        for k in range(parts):
            at = (i * parts + k) * width
            gw_kv[i, k] = gw_acc[at : at + width, :].astype(BF16)
    core_copy(gw_kv, kv_core, kv_dsems).start()

    def mine_rows():
        return pl.ds(pl.multiple_of(lax.axis_index("dp") * half, 16), half)

    def kv_copies():
        return [
            remote(gw_kv.at[:, at, mine_rows()], kv_slots.at[k], kv_msems.at[0, k], kv_msems.at[1, k], to)
            for k, at, to in others("mp")
        ]

    def encodings(step, carry):
        slot = lax.rem(step, 2)

        @pl.when(step + 1 < steps)
        def _():
            fetch_gkv(step + 1, 1 - slot).start()

        fetch_gkv(step, slot).wait()

        @pl.when(step >= 2)
        def _():
            store(step - 2, slot).wait()

        genc_out[slot] = dot_nn(gkv_in[slot], wkv_ref[...]).astype(BF16)
        store(step, slot).start()
        arrivals(steps + step)

        @pl.when(step == 1)
        def _():
            core_copy(gw_kv, kv_core, kv_dsems).wait()
            at = pl.ds(pl.multiple_of(lax.axis_index("dp") * half, 16), half)
            for i in range(2):
                for k in range(parts):
                    gw_kv[i, k, at, :] = (gw_kv[i, k, at, :].astype(F32) + kv_core[i, k].astype(F32)).astype(BF16)
            begin(kv_copies())

        @pl.when(step == steps - 2)
        def _():
            for at in range(pn - 1):
                to_home(at).wait()
            low = total_of(held[pm], zslots).astype(BF16)
            gv, cross_gain = rms_back(h_ref[...], row_of_gain(gain_cross_ref), dot_nn(low, wq_ref[...]))
            gh = gh2_ref[...] + gv
            gh1[...] = gh
            gsa_all[mm] = gh.astype(BF16)
            begin(gsa_copies())
            small[...] = jnp.zeros_like(small)
            small[1:2, :] = cross_gain
            for k in range(parts):
                blocks[k] = low[:, k * width : (k + 1) * width]
            gq_own[mm] = blocks[mm]
            begin(block_copies())

        return carry

    def gsa_copies():
        here = gsa_all.at[mm]
        return [remote(here, here, asems.at[0, k], asems.at[1, k], to) for k, _, to in others("mp")]

    def block_copies():
        return [
            remote(blocks.at[at], gq_own.at[mm], bsems.at[0, k], bsems.at[1, k], to)
            for k, at, to in others("mp")
        ]

    lax.fori_loop(0, steps, encodings, 0)
    finish(f_copies)
    f_copies = share(sum_f_ref.at[core], f_sems.at[1], "dp")
    for step in (steps - 2, steps - 1):
        store(step, step % 2).wait()
    finish(kv_copies())
    for i in range(2):
        total = gw_kv[i, mm, mine, :].astype(F32)
        for k in range(kv_slots.shape[0]):
            total = total + kv_slots[k, i].astype(F32)
        y_k[i * half : (i + 1) * half, :] = total.astype(BF16)
    sum_k = GroupSum(y_k, z_k, sum_k_ref, zk_sems)
    sum_k.spread()
    finish(gsa_copies())
    gsa = jnp.concatenate([gsa_all[k] for k in range(parts)], axis=0)
    bias_sums = self_backward(
        heads, gsa, ws_q_ref, ws_k_ref, ws_v_ref, ws_o_ref, qkv_ref, p_ref, ga1, gqkv, bias
    )
    ga_copies = deal(lambda at: ga1.at[at], ga_slots, ga_sems, "mp")
    finish(block_copies())
    total = jnp.zeros((width, MODEL_WIDTH), F32)
    for k in range(parts):
        total = total + dot_tn(gq_own[k], a2_own[k])
    gw_c[0] = total.astype(BF16)
    gw_c[1] = dot_tn(o1_ref[...], gsa).astype(BF16)
    core_copy(gw_c, core_c, cc_sems).start()
    sum_c = GroupSum(y_c, z_c, sum_c_ref, zc_sems)
    both_cores(core_copy(gw_c, core_c, cc_sems), gw_c, core_c, y_c)
    sum_c.spread()
    for k in range(3):
        gw_s[k] = dot_tn(gqkv[k], a1_ref[...]).astype(BF16)
    core_copy(gw_s, core_s, cs_sems).start()
    bias_sums()
    sum_s = GroupSum(y_s, z_s, sum_s_ref, zs_sems)
    both_cores(core_copy(gw_s, core_s, cs_sems), gw_s, core_s, y_s)
    sum_s.spread()
    finish(ga_copies)
    gv, self_gain = rms_back(
        home_rows(x_ref, chunk).astype(F32), row_of_gain(gain_ref), total_of(ga1[mm], ga_slots)
    )
    gx_ref[mm] = (gh1[...] + gv).astype(BF16)
    gx_copies = share(gx_ref.at[mm], gx_sems, "mp")
    term_copies = deal(lambda at: term_ref.at[at], term_slots, term_sems, "mp")
    small[0:1, :] = self_gain
    small[2:3, :] = ffn_gain_ref[...]
    small[8:16, :LANES] = bias[...]
    sd = begin([remote(small, small_dp, sd_sems.at[0], sd_sems.at[1], peer)])
    sum_k.gather()
    sum_c.gather()
    finish(sd)
    small_z[pm] = small[...] + small_dp[...]
    sz = share(small_z.at[pm], sz_sems, "pass")
    sum_s.gather()
    finish(term_copies)
    out_ref[mm] = (h2_ref[...] + total_of(term_ref[mm], term_slots)).astype(BF16)
    out_copies = share(out_ref.at[mm], out_sems, "mp")
    finish(sz)
    total = small_z[0]
    for k in range(1, small_z.shape[0]):
        total = total + small_z[k]
    small_m[mm] = total
    sm = share(small_m.at[mm], sm_sems, "mp")
    sum_k.swap()
    sum_c.swap()
    finish(sm)
    gains = small_m[0]
    for k in range(1, small_m.shape[0]):
        gains = gains + small_m[k]
    small_ref[0:8, :] = gains[0:8]
    small_ref[8:16, :] = total[8:16]
    finish(gx_copies)
    sum_s.swap()
    finish(out_copies)
    finish(f_copies)
    sum_c.end()
    sum_s.end()
    sum_k.end()


def closing_kernel(
    k_ref, c_ref, s_ref, ffn_ref, small_ref, genc_ref, y_ref, gx_ref, *refs
):
    outs, (wide, wide_in, wide_out, sems) = refs[:17], refs[17:]
    half = wide.shape[1] // 2
    moves = [(genc_ref, outs[2]), (y_ref, outs[0]), (gx_ref, outs[1])]
    copies = begin([pltpu.make_async_copy(src, dst, sems.at[n]) for n, (src, dst) in enumerate(moves)])
    sources = [(s_ref, 0), (s_ref, 1), (s_ref, 2), (c_ref, 1), (c_ref, 0), (k_ref, 0), (k_ref, 1), (k_ref, 2)]
    for n, (ref, i) in enumerate(sources):
        for core in range(2):
            wide[n, core * half : (core + 1) * half, :] = ref[core, i * half : (i + 1) * half, :].astype(F32)
        copies += begin([pltpu.make_async_copy(wide.at[n], outs[7 + n], sems.at[3 + n])])
    for n, buffer in enumerate((wide_in, wide_out)):
        buffer[...] = ffn_ref[n, 0 : buffer.shape[0], :].astype(F32)
        copies += begin([pltpu.make_async_copy(buffer, outs[15 + n], sems.at[11 + n])])
    for n in range(3):
        outs[3 + n][...] = small_ref[n, :]
    heads, buckets = outs[6].shape
    outs[6][...] = small_ref[8 : 8 + heads, 0:buckets]
    finish(copies)


def on_device(
    tokens,
    encoded,
    seg_lens,
    owners,
    answer_lens,
    gain_self,
    gain_cross,
    gain_ffn,
    rel_bias,
    wq_self,
    wk_self,
    wv_self,
    wo_self,
    wq_cross,
    wk_cross,
    wv_cross,
    wo_cross,
    w_in,
    w_out,
    out_grad,
):
    groups, mp_parts = lax.axis_size("pass"), lax.axis_size("mp")
    heads = rel_bias.shape[1]
    head_cols = heads * HD
    half = head_cols // 2
    quarter = encoded.shape[1]
    n_tokens = tokens.shape[0]
    chunk = n_tokens // mp_parts
    assert w_in.shape == (MODEL_WIDTH, MODEL_WIDTH)
    rows_f = sum_rows(MODEL_WIDTH, groups)
    keys = GROUP_ROWS * quarter
    near, far = mp_parts - 1, groups - 1

    lens, owners = seg_lens.T, owners.T
    flat_encoded = encoded.reshape(keys, MODEL_WIDTH)
    home = (chunk, MODEL_WIDTH)
    dealt = (mp_parts, chunk, MODEL_WIDTH)
    square = (MODEL_WIDTH, MODEL_WIDTH)
    smem = pltpu.SMEM
    a2_all, h_one, a1, qkv, p1, o1, wkv, wq_full, wo_full, kv = remote_call(
        functools.partial(front_kernel, heads),
        0,
        [
            ((groups, *dealt), BF16),
            (home, F32),
            ((n_tokens, MODEL_WIDTH), BF16),
            ((3, n_tokens, head_cols), BF16),
            ((mp_parts * heads, chunk, chunk), F32),
            ((n_tokens, head_cols), BF16),
            ((2, *square), BF16),
            (square, BF16),
            (square, BF16),
            ((keys, 2 * MODEL_WIDTH), BF16),
        ],
        tokens, gain_self, gain_cross, wq_self.T, wk_self.T, wv_self.T, wo_self, rel_bias.T, answer_lens,
        wk_cross.T, wv_cross.T, wq_cross.T, wo_cross, flat_encoded,
        spaces={7: smem, 8: smem, 13: pl.ANY},
        out_spaces={9: pl.ANY},
        scratch=[
            pltpu.VMEM(dealt, BF16),
            pltpu.VMEM((near, *home), BF16),
            pltpu.VMEM((keys, MODEL_WIDTH), BF16),
            pltpu.VMEM((2, keys // KV_STEPS, 2 * MODEL_WIDTH), BF16),
            many_sems(4, max(near, 3)),
            many_sems(4, near),
            pair_sems(near),
            pair_sems(far),
            many_sems(groups, near),
            pltpu.SemaphoreType.DMA((4,)),
            pltpu.SemaphoreType.DMA,
            pltpu.SemaphoreType.DMA((2,)),
        ],
    )
    a2_all = a2_all.reshape(groups, n_tokens, MODEL_WIDTH)

    partial = cross_forward(lens, owners, a2_all, wq_full, kv, mp_parts)
    gc_space = pltpu.VMEM if groups <= KV_STEPS else pl.ANY
    h_two, o2_own, term, gh_two, gc_all, gain_ffn_grad, *gw_parts = remote_call(
        middle_kernel,
        1,
        [
            (home, F32),
            ((mp_parts, chunk, head_cols), BF16),
            (dealt, BF16),
            (home, F32),
            ((groups, mp_parts, chunk, STATW), BF16),
            ((1, MODEL_WIDTH), F32),
            *[((rows_f, MODEL_WIDTH), BF16)] * groups,
        ],
        partial, h_one, wo_full, gain_ffn, w_in, w_out, out_grad,
        spaces={0: pl.ANY},
        out_spaces={4: gc_space},
        scratch=[
            pltpu.VMEM((groups, chunk, STATW), BF16),
            pltpu.VMEM((groups, near, chunk, STATW), BF16),
            pltpu.VMEM((far, chunk, STATW), BF16),
            pltpu.VMEM((mp_parts, chunk, head_cols), BF16),
            pltpu.VMEM(dealt, BF16),
            pltpu.VMEM(dealt, BF16),
            pltpu.VMEM((2, *square), BF16),
            pltpu.VMEM((near, *home), BF16),
            pltpu.VMEM(square, BF16),
            pltpu.VMEM((groups * rows_f, MODEL_WIDTH), BF16),
            pltpu.VMEM((chunk, STATW), BF16),
            many_sems(groups, near),
            pair_sems(far),
            pair_sems(near),
            pair_sems(near),
            pair_sems(near),
            pair_sems(far),
            many_sems(groups, near),
            pltpu.SemaphoreType.DMA((2,)),
            pltpu.SemaphoreType.DMA,
            pltpu.SemaphoreType.DMA,
        ],
    )
    gw_parts = [
        lax.ppermute(x, "pass", [(i, (i + k) % groups) for i in range(groups)]) if k else x
        for k, x in enumerate(gw_parts)
    ]
    gq, gkv = cross_backward(
        lens, owners, a2_all, gc_all.reshape(groups, n_tokens, STATW), wq_full, wo_full, kv, mp_parts
    )
    rows = {k: sum_rows(n * half, groups) for k, n in (("k", 3), ("c", 2), ("s", 3))}
    small = pltpu.VMEM((16, MODEL_WIDTH), F32)
    own = (mp_parts, chunk, head_cols)
    step = keys // (KV_STEPS if groups <= KV_STEPS else 4 * KV_STEPS)
    hbm = pl.ANY
    pair = pltpu.SemaphoreType.DMA((2,))
    grad_tokens, output, sum_k, sum_c, sum_s, small_sums, sum_f, genc = remote_call(
        functools.partial(finish_kernel, heads),
        3,
        [
            (dealt, BF16),
            (dealt, BF16),
            *[((2, groups * rows[k], MODEL_WIDTH), BF16) for k in "kcs"],
            ((16, MODEL_WIDTH), F32),
            ((2, groups * rows_f, MODEL_WIDTH), BF16),
            ((keys, MODEL_WIDTH), BF16),
        ],
        gq, gkv, flat_encoded, wkv.reshape(2 * MODEL_WIDTH, MODEL_WIDTH), gh_two, h_one, gain_self, gain_cross, wq_full,
        wq_self.T, wk_self.T, wv_self.T, wo_self, a1, qkv, p1, o1,
        a2_all.reshape(groups, *dealt), gc_all, o2_own, tokens, gain_ffn_grad, term, h_two, *gw_parts,
        spaces={0: hbm, 1: hbm, 2: hbm, 17: hbm, 18: hbm},
        out_spaces={7: hbm},
        scratch=[
            pltpu.VMEM((groups, *home), BF16),
            pltpu.VMEM((groups, near, *home), BF16),
            pltpu.VMEM((far, *home), BF16),
            pltpu.VMEM((2, step, 2 * MODEL_WIDTH), BF16),
            pltpu.VMEM((2, step, MODEL_WIDTH), BF16),
            pltpu.VMEM((2, step, MODEL_WIDTH), BF16),
            pltpu.VMEM((2 * MODEL_WIDTH, MODEL_WIDTH), F32),
            pltpu.VMEM((2, mp_parts, head_cols, MODEL_WIDTH), BF16),
            pltpu.VMEM((1, head_cols, MODEL_WIDTH), BF16),
            pltpu.VMEM((2, head_cols, MODEL_WIDTH), BF16),
            pltpu.VMEM((3, head_cols, MODEL_WIDTH), BF16),
            pltpu.VMEM(home, F32),
            pltpu.VMEM(own, BF16),
            pltpu.VMEM(own, BF16),
            pltpu.VMEM(dealt, BF16),
            pltpu.VMEM(dealt, BF16),
            pltpu.VMEM((3, n_tokens, head_cols), BF16),
            pltpu.VMEM((8, LANES), F32),
            pltpu.VMEM(dealt, BF16),
            pltpu.VMEM((mp_parts, chunk, STATW), BF16),
            pltpu.VMEM((near, *home), BF16),
            pltpu.VMEM((near, *home), BF16),
            pltpu.VMEM((2, mp_parts, half, MODEL_WIDTH), BF16),
            pltpu.VMEM((near, 2, half, MODEL_WIDTH), BF16),
            pltpu.VMEM((1, half, MODEL_WIDTH), BF16),
            pltpu.VMEM((2, half, MODEL_WIDTH), BF16),
            pltpu.VMEM((3, half, MODEL_WIDTH), BF16),
            *[pltpu.VMEM((groups * rows[k], MODEL_WIDTH), BF16) for k in "kcs"],
            *[pltpu.VMEM((far, rows[k], MODEL_WIDTH), BF16) for k in "kcs"],
            small,
            small,
            pltpu.VMEM((groups, 16, MODEL_WIDTH), F32),
            pltpu.VMEM((mp_parts, 16, MODEL_WIDTH), F32),
            many_sems(groups, near),
            pair_sems(far),
            pair_sems(near),
            pair_sems(near),
            pltpu.SemaphoreType.DMA((3,)),
            pltpu.SemaphoreType.DMA((2, 2)),
            pair,
            pair_sems(near),
            pair_sems(near),
            pair_sems(near),
            pair,
            pair_sems(near),
            pair,
            pair,
            pair,
            pair_sems(near),
            *[many_sems(3, far)] * 3,
            pair,
            pair_sems(far),
            pair_sems(near),
            many_sems(2, far),
        ],
    )
    shard = jax.ShapeDtypeStruct((head_cols, MODEL_WIDTH), F32)
    gain = jax.ShapeDtypeStruct((MODEL_WIDTH,), F32)
    y, gx, genc, gs, gc, gf, gb, *grads = pl.pallas_call(
        closing_kernel,
        out_shape=[
            *[jax.ShapeDtypeStruct(x.shape, x.dtype) for x in (output, grad_tokens, genc)],
            gain, gain, gain,
            jax.ShapeDtypeStruct((heads, BUCKETS), F32),
            *[shard] * 8,
            *[jax.ShapeDtypeStruct(square, F32)] * 2,
        ],
        in_specs=[pl.BlockSpec(memory_space=pltpu.VMEM)] * 8,
        out_specs=[pl.BlockSpec(memory_space=hbm)] * 3
        + [pl.BlockSpec(memory_space=pltpu.VMEM)] * 4
        + [pl.BlockSpec(memory_space=hbm)] * 10,
        scratch_shapes=[
            pltpu.VMEM((8, head_cols, MODEL_WIDTH), F32),
            pltpu.VMEM(square, F32),
            pltpu.VMEM(square, F32),
            pltpu.SemaphoreType.DMA((13,)),
        ],
        compiler_params=pltpu.CompilerParams(vmem_limit_bytes=VMEM_LIMIT),
    )(sum_k, sum_c, sum_s, sum_f, small_sums, genc, output, grad_tokens)

    return (
        y.reshape(n_tokens, MODEL_WIDTH),
        gx.reshape(n_tokens, MODEL_WIDTH),
        genc.reshape(GROUP_ROWS, quarter, MODEL_WIDTH),
        gs,
        gc,
        gf,
        gb.T,
        *[grads[i].T for i in range(3)],
        grads[3],
        *[grads[i].T for i in range(4, 7)],
        *grads[7:],
    )


def solution(mesh):
    tokens_in = P(("dp", "pass"), None)
    encoded_in = P(("dp", "pass"), "mp", None)
    by_column, by_row = P(None, "mp"), P("mp", None)
    weights = (by_column, by_column, by_column, by_row)
    return jax.shard_map(
        on_device,
        mesh=mesh,
        in_specs=(
            tokens_in, encoded_in, P("dp", None), P("dp", None), P(("dp", "pass")),
            P(), P(), P(), by_column,
            *weights, *weights, by_column, by_row, tokens_in,
        ),
        out_specs=(
            tokens_in, tokens_in, encoded_in, P(), P(), P(), by_column,
            *weights, *weights, by_column, by_row,
        ),
        check_vma=False,
    )
```
